32 devices in a mesh: dp: 4 (over y, x), fsdp: 8 (over z, core).
Axes of the slice: x: 2, y: 2, z: 4, core: 2. Of those that a mesh axis runs over, the one named last changes fastest.
Arguments:
- inputs: bfloat16 [16384, 512], P(('dp', 'fsdp')), may hold values from -6 to 6
- lengths: int32 [32, 3], P(('dp', 'fsdp')), may hold values from 0 to 512, as said below
- filters: bfloat16 [24, 512], replicated
- cotangent: bfloat16 [16384, 512], P(('dp', 'fsdp')), may hold values from -12 to 12
- mixer_weight: float32 [13824, 512], P(('dp', 'fsdp')), may hold values from -0.0546875 to 0.0546875
- gate_up_weight: float32 [4096, 512], P(('dp', 'fsdp')), may hold values from -0.25 to 0.25
- down_weight: float32 [2048, 512], P(('dp', 'fsdp')), may hold values from -0.125 to 0.125
- norm_gains: float32 [2, 512], P(None, ('dp', 'fsdp'))
- mixer_first: float32 [13824, 512], P(('dp', 'fsdp')), may hold values from -0.00021362305 to 0.00021362305
- gate_up_first: float32 [4096, 512], P(('dp', 'fsdp')), may hold values from -7.6293945e-05 to 7.6293945e-05
- down_first: float32 [2048, 512], P(('dp', 'fsdp')), may hold values from -0.00015258789 to 0.00015258789
- gains_first: float32 [2, 512], P(None, ('dp', 'fsdp')), may hold values from -0.00021362305 to 0.00021362305
- mixer_second: float32 [13824, 512], P(('dp', 'fsdp')), may hold values from 5.1835567e-09 to 2.053862e-08
- gate_up_second: float32 [4096, 512], P(('dp', 'fsdp')), may hold values from 8.313251e-10 to 3.3253005e-09
- down_second: float32 [2048, 512], P(('dp', 'fsdp')), may hold values from 3.3253005e-09 to 1.3301202e-08
- gains_second: float32 [2, 512], P(None, ('dp', 'fsdp')), may hold values from 5.1835567e-09 to 2.053862e-08
- mixer_average: float32 [13824, 512], P(('dp', 'fsdp')), may hold values from -0.0546875 to 0.0546875
Outputs:
- output: bfloat16 [16384, 512], P(('dp', 'fsdp'))
- input_grad: float32 [16384, 512], P(('dp', 'fsdp'))
- grad_norm: float32 [], replicated
- mixer_new: float32 [13824, 512], P(('dp', 'fsdp'))
- gate_up_new: float32 [4096, 512], P(('dp', 'fsdp'))
- down_new: float32 [2048, 512], P(('dp', 'fsdp'))
- gains_new: float32 [2, 512], P(None, ('dp', 'fsdp'))
- mixer_first_new: float32 [13824, 512], P(('dp', 'fsdp'))
- gate_up_first_new: float32 [4096, 512], P(('dp', 'fsdp'))
- down_first_new: float32 [2048, 512], P(('dp', 'fsdp'))
- gains_first_new: float32 [2, 512], P(None, ('dp', 'fsdp'))
- mixer_second_new: float32 [13824, 512], P(('dp', 'fsdp'))
- gate_up_second_new: float32 [4096, 512], P(('dp', 'fsdp'))
- down_second_new: float32 [2048, 512], P(('dp', 'fsdp'))
- gains_second_new: float32 [2, 512], P(None, ('dp', 'fsdp'))
- mixer_average_new: float32 [13824, 512], P(('dp', 'fsdp'))
The draws below stay inside these ranges and needn't reach their ends.
Inputs may be any that keep to these rules, and one draw needn't show every extreme that they name: Each row is one device's documents: either 512, 0, 0, or two lengths from 128 to 192 and a third from 0 to 128. Some row is of the first kind.
All inputs are finite; a program needn't handle non-finite values.
Results may differ from the reference program's by a relative error of at most 0.01.
Values may be sent and summed in bfloat16 or wider, within the bound.
No kernel may reach another device: no remote copies, remote signals or barrier semaphores. Data moves between devices by JAX's collectives and lax.ppermute only.
A program may use at most 192 MiB of HBM per device.

```python
import math
import jax
import jax.numpy as jnp
from jax import lax

D = 512
FILTERS = 24
AR_ORDER = 3
FF = 2048
STEP = 10
SLOTS = 512
TOKENS = 16384
PARAMS = 10224640
DEVICES = 32


def draw_lengths(key, part):
    key = jax.random.fold_in(key, 11)
    keys = jax.random.split(key, 5)
    first = jax.random.randint(keys[0], (DEVICES,), SLOTS // 4, 3 * SLOTS // 8 + 1)
    second = jax.random.randint(keys[1], (DEVICES,), SLOTS // 4, 3 * SLOTS // 8 + 1)
    third = jax.random.randint(keys[2], (DEVICES,), 0, SLOTS // 4 + 1)
    flagged = jax.random.randint(keys[3], (DEVICES,), 0, 8) == 0
    forced = jax.random.randint(keys[4], (), 0, DEVICES)
    whole = flagged | (jnp.arange(DEVICES) == forced)
    nothing = jnp.zeros((DEVICES,), jnp.int32)
    short_rows = jnp.stack([first, second, third], axis=1)
    long_rows = jnp.stack([jnp.full((DEVICES,), SLOTS, jnp.int32), nothing, nothing], axis=1)
    return jnp.where(whole[:, None], long_rows, short_rows).astype(jnp.int32)


def draw_filters(key, part):
    key = jax.random.fold_in(key, 12)
    keys = jax.random.split(key, 2)
    base = jax.random.normal(keys[0], (FILTERS, SLOTS), jnp.float32)
    spread = jnp.exp(jax.random.uniform(keys[1], (FILTERS, 1), jnp.float32, math.log(0.5), math.log(2.0)))
    return (base * spread * SLOTS ** (-0.5)).astype(jnp.bfloat16)


def draw_norm_gains(key, part):
    key = jax.random.fold_in(key, 13)
    rise = jnp.linspace(0.5, 1.5, D)
    factor = jax.random.uniform(key, (2, D), jnp.float32, 0.8, 1.25)
    return rise[None, :] * factor


def raised(drawn, stream_key, source, target, parts, factor):
    def block_of(dim):
        return (jnp.arange(drawn.shape[dim]) // (drawn.shape[dim] // parts)).reshape((-1,) + (1,) * (drawn.ndim - 1 - dim))

    near = jax.random.permutation(stream_key, parts)[block_of(target)]
    other_side = (block_of(target) + parts // 2) % parts
    return jnp.where((block_of(source) == near) | (block_of(source) == other_side), factor * drawn, drawn)


def block_levels(own_key, dims, cuts, smallest, largest):
    def one(position, blocks):
        draws = jax.random.uniform(jax.random.fold_in(jax.random.fold_in(own_key, 6), position), (blocks,), jnp.float32, smallest / len(cuts), largest / len(cuts))
        return jnp.repeat(jnp.exp(draws), dims[position] // blocks).reshape((-1,) + (1,) * (len(dims) - position - 1))

    loudness = one(*cuts[0])
    for cut in cuts[1:]:
        loudness = loudness * one(*cut)
    return loudness


def gaussian(rng, shape, scale, limit, pieces=(), kind=jnp.bfloat16):
    loudness = block_levels(rng, shape, pieces, -0.22, 0.18) if pieces else 1.0
    entries = jax.random.normal(rng, shape, jnp.float32) * scale * loudness
    return jnp.minimum(jnp.maximum(entries, -limit), limit).astype(kind)


def gaussian_with(own_key, dims, scale, reach, cuts, heavy, kind=jnp.bfloat16):
    values = scale * jax.random.normal(own_key, dims, jnp.float32)
    if cuts:
        values = values * block_levels(own_key, dims, cuts, -0.22, 0.18)
    return jnp.clip(raised(values, jax.random.fold_in(own_key, 3), *heavy), -reach, reach).astype(kind)


def setup_inputs(seed: int = 0) -> dict:
    streams_of = jax.random.split(jax.random.key(seed), 18)
    return {
        "inputs": gaussian(streams_of[0], (TOKENS, D), 1.0, 6.0, ((0, 32),)),
        "lengths": draw_lengths(jax.random.fold_in(streams_of[17], 71), 0),
        "filters": draw_filters(jax.random.fold_in(streams_of[17], 71), 0),
        "cotangent": gaussian_with(streams_of[3], (TOKENS, D), 1.0, 12.0, ((0, 32),), (0, 1, 32, 2.75)),
        "mixer_weight": gaussian(streams_of[4], ((FILTERS + AR_ORDER) * D, D), (D * (FILTERS + AR_ORDER)) ** -0.5, 0.0546875, ((0, 32),), jnp.float32),
        "gate_up_weight": gaussian(streams_of[5], (2 * FF, D), D ** -0.5, 0.25, ((0, 32),), jnp.float32),
        "down_weight": gaussian(streams_of[6], (FF, D), FF ** -0.5, 0.125, ((0, 32),), jnp.float32),
        "norm_gains": draw_norm_gains(jax.random.fold_in(streams_of[17], 71), 0),
        "mixer_first": gaussian(streams_of[8], ((FILTERS + AR_ORDER) * D, D), (0.11 / PARAMS ** 0.5), 0.00021362305, ((0, 32),), jnp.float32),
        "gate_up_first": gaussian(streams_of[9], (2 * FF, D), (0.044 / PARAMS ** 0.5), 7.62939453125e-05, ((0, 32),), jnp.float32),
        "down_first": gaussian(streams_of[10], (FF, D), (0.088 / PARAMS ** 0.5), 0.00015258789, ((0, 32),), jnp.float32),
        "gains_first": gaussian(streams_of[11], (2, D), (0.11 / PARAMS ** 0.5), 0.00021362305, ((1, 32),), jnp.float32),
        "mixer_second": jnp.clip(jnp.exp(math.log(2.0538619693866167e-08) - 1.3768156 * jax.random.uniform(streams_of[12], ((FILTERS + AR_ORDER) * D, D), jnp.float32) ** block_levels(streams_of[12], ((FILTERS + AR_ORDER) * D, D), ((0, 32),), -0.2, 0.2)), 5.183556694987601e-09, 2.0538619693866167e-08),
        "gate_up_second": jnp.clip(jnp.exp(math.log(3.3253004794175922e-09) - 1.3862944 * jax.random.uniform(streams_of[13], (2 * FF, D), jnp.float32) ** block_levels(streams_of[13], (2 * FF, D), ((0, 32),), -0.2, 0.2)), 8.313251198543981e-10, 3.3253004794175922e-09),
        "down_second": jnp.clip(jnp.exp(math.log(1.3301201917670369e-08) - 1.3862944 * jax.random.uniform(streams_of[14], (FF, D), jnp.float32) ** block_levels(streams_of[14], (FF, D), ((0, 32),), -0.2, 0.2)), 3.3253004794175922e-09, 1.3301201917670369e-08),
        "gains_second": jnp.clip(jnp.exp(math.log(2.0538619693866167e-08) - 1.3768156 * jax.random.uniform(streams_of[15], (2, D), jnp.float32) ** block_levels(streams_of[15], (2, D), ((1, 32),), -0.2, 0.2)), 5.183556694987601e-09, 2.0538619693866167e-08),
        "mixer_average": gaussian(streams_of[16], ((FILTERS + AR_ORDER) * D, D), (D * (FILTERS + AR_ORDER)) ** -0.5, 0.0546875, ((0, 32),), jnp.float32),
    }


NORM_EPS = 1e-05
CLIP_LIMIT = 1.0
BETA_ONE = 0.9
BETA_TWO = 0.95
ADAM_EPS = 1e-08
RATE_MATRIX = 0.03
RATE_GAIN = 0.5
DECAY_MATRIX = 0.1
AVERAGE_KEEP = 0.9
HIGH = lax.Precision.HIGHEST

@jax.custom_vjp
def low(v):
    return lax.optimization_barrier(v.astype(jnp.bfloat16)).astype(jnp.float32)

@jax.custom_vjp
def low_back(v):
    return v

def low_keep(v):
    return (low(v), None)

def low_pass(kept, grad):
    return (grad,)

def back_keep(v):
    return (v, None)

def back_low(kept, grad):
    return (low(grad),)
low.defvjp(low_keep, low_pass)
low_back.defvjp(back_keep, back_low)

def layout(lengths, slots):
    ends = jnp.cumsum(lengths, axis=-1).astype(jnp.int32)
    place = jnp.arange(slots, dtype=jnp.int32)
    return lax.optimization_barrier(jnp.sum((place[:, None] >= ends[..., None, :]).astype(jnp.int32), axis=-1)).astype(jnp.int32)

def group_forward(source, segment, mixer_low, gate_up_low, down_low, gains_low, filt):
    slots = source.shape[0]
    scale_one = lax.rsqrt(lax.optimization_barrier(jnp.mean(source * source, axis=-1, keepdims=True)) + NORM_EPS)
    normed = low(source * scale_one * gains_low[0])
    projected = low(low_back(jnp.dot(normed, mixer_low.T, precision=HIGH))).reshape(slots, FILTERS + AR_ORDER, D)
    live = segment < 3
    same = (segment[:, None] == segment[None, :]) & live[:, None]
    place = jnp.arange(slots, dtype=jnp.int32)
    offset = place[:, None] - place[None, :]
    keep = same & (offset >= 0)
    clipped = jnp.clip(offset, 0, slots - 1)

    def one_filter(index):
        table = jnp.where(keep, jnp.take(filt[index], clipped), 0.0)
        return jnp.dot(table, projected[:, index, :], precision=HIGH)
    mixed = lax.optimization_barrier(jnp.sum(lax.map(jax.checkpoint(one_filter), jnp.arange(FILTERS, dtype=jnp.int32)), axis=0))
    for lag in range(AR_ORDER):
        column = projected[:, FILTERS + lag, :]
        allowed = live
        if lag > 0:
            column = jnp.concatenate([jnp.zeros((lag, D), jnp.float32), column[:slots - lag]], axis=0)
            earlier = jnp.concatenate([jnp.full((lag,), -1, jnp.int32), segment[:slots - lag]])
            allowed = (earlier == segment) & live
        mixed = mixed + jnp.where(allowed[:, None], column, 0.0)
    hidden = source + low_back(mixed)
    scale_two = lax.rsqrt(lax.optimization_barrier(jnp.mean(hidden * hidden, axis=-1, keepdims=True)) + NORM_EPS)
    normed_two = low(hidden * scale_two * gains_low[1])
    gate_up = low_back(jnp.dot(normed_two, gate_up_low.T, precision=HIGH))
    act = low(jax.nn.silu(gate_up[:, :FF]) * gate_up[:, FF:])
    return hidden + jnp.dot(act, down_low, precision=HIGH)

def adam_step(weight, grad, first, second, rate, decay):
    first_new = BETA_ONE * first + (1.0 - BETA_ONE) * grad
    second_new = BETA_TWO * second + (1.0 - BETA_TWO) * grad * grad
    corr_one = 1.0 - BETA_ONE ** STEP
    corr_two = 1.0 - BETA_TWO ** STEP
    update = first_new / corr_one / (jnp.sqrt(second_new / corr_two) + ADAM_EPS)
    return (weight - rate * (update + decay * weight), first_new, second_new)

def reference(inputs, lengths, filters, cotangent, mixer_weight, gate_up_weight, down_weight, norm_gains, mixer_first, gate_up_first, down_first, gains_first, mixer_second, gate_up_second, down_second, gains_second, mixer_average):
    groups = lengths.shape[0]
    segment = layout(lengths, SLOTS)
    filt = filters.astype(jnp.float32)

    def forward(source, first_weight, second_weight, third_weight, gain_weight):
        mixer_low = low(first_weight)
        gate_up_low = low(second_weight)
        down_low = low(third_weight)
        gains_low = low(gain_weight)

        def one_group(carry, item):
            return (carry, jax.checkpoint(group_forward)(item[0], item[1], mixer_low, gate_up_low, down_low, gains_low, filt))
        unused, result = lax.scan(one_group, jnp.float32(0.0), (source, segment))
        return result
    source = inputs.astype(jnp.float32).reshape(groups, SLOTS, D)
    result, pullback = jax.vjp(forward, source, mixer_weight, gate_up_weight, down_weight, norm_gains)
    live = (segment < 3)[..., None]
    back = jnp.where(live, cotangent.astype(jnp.float32).reshape(groups, SLOTS, D), 0.0)
    grad_input, grad_mixer, grad_gate_up, grad_down, grad_gains = pullback(back)
    total = jnp.sum(grad_mixer * grad_mixer) + jnp.sum(grad_gate_up * grad_gate_up) + jnp.sum(grad_down * grad_down) + jnp.sum(grad_gains * grad_gains)
    grad_norm = jnp.sqrt(total)
    factor = CLIP_LIMIT / jnp.maximum(grad_norm, CLIP_LIMIT)
    mixer_new, mixer_first_new, mixer_second_new = adam_step(mixer_weight, grad_mixer * factor, mixer_first, mixer_second, RATE_MATRIX, DECAY_MATRIX)
    gate_up_new, gate_up_first_new, gate_up_second_new = adam_step(gate_up_weight, grad_gate_up * factor, gate_up_first, gate_up_second, RATE_MATRIX, DECAY_MATRIX)
    down_new, down_first_new, down_second_new = adam_step(down_weight, grad_down * factor, down_first, down_second, RATE_MATRIX, DECAY_MATRIX)
    gains_new, gains_first_new, gains_second_new = adam_step(norm_gains, grad_gains * factor, gains_first, gains_second, RATE_GAIN, 0.0)
    mixer_average_new = AVERAGE_KEEP * mixer_average + (1.0 - AVERAGE_KEEP) * mixer_new
    return (result.reshape(TOKENS, D).astype(jnp.bfloat16), grad_input.reshape(TOKENS, D), grad_norm, mixer_new, gate_up_new, down_new, gains_new, mixer_first_new, gate_up_first_new, down_first_new, gains_first_new, mixer_second_new, gate_up_second_new, down_second_new, gains_second_new, mixer_average_new)
```

```python
import math

import jax
import jax.numpy as jnp
import numpy as np
from jax import lax
from jax.experimental import pallas as pl
from jax.experimental.pallas import tpu as pltpu
from jax.sharding import PartitionSpec as P

bf = jnp.bfloat16
f32 = jnp.float32
FILTERS = 24
AR_ORDER = 3
STEP = 10
NORM_EPS = 1e-05
CLIP_LIMIT = 1.0
BETA_ONE = 0.9
BETA_TWO = 0.95
ADAM_EPS = 1e-08
RATE_MATRIX = 0.03
RATE_GAIN = 0.5
DECAY_MATRIX = 0.1
AVERAGE_KEEP = 0.9
CHIPS = ("d0", "d1", "z")
EVERY = CHIPS + ("core",)
NT=(((1,),(1,)),((),())); NN=(((1,),(0,)),((),())); TN=(((0,),(0,)),((),()))
def dot(a,b,d=NN): return lax.dot_general(a,b,d,preferred_element_type=f32)

def seg_of(place, ends_ref, g):
    return sum((place >= ends_ref[g, j]).astype(jnp.int32) for j in range(3))

def causal_mask(ends_ref, g, n, transposed):
    col = lax.broadcasted_iota(jnp.int32, (n, 1), 0); row = lax.broadcasted_iota(jnp.int32, (1, n), 1)
    sc, sr = seg_of(col, ends_ref, g), seg_of(row, ends_ref, g)
    order = (col <= row) if transposed else (col >= row)
    return ((sc == sr) & (sc < 3) & order).astype(f32).astype(bf)

def strip(row, sub):
    x = jnp.broadcast_to(row, (sub, row.shape[-1]))
    return pltpu.roll(x, 0, 1, stride=1, stride_axis=0).astype(bf)

def u_kernel(ends_ref, taps_ref, hat_ref, u_ref, mask, table):
    n = mask.shape[1]; q = n//4; h = n//2; w = hat_ref.shape[2]; per = taps_ref.shape[1]
    @pl.when(pl.program_id(0) == 0)
    def _():
        for g in range(2): mask[g] = causal_mask(ends_ref, g, n, False)
        table[...] = jnp.zeros_like(table)
    for j in range(per):
        s = strip(taps_ref[0, j:j+1, :], q)
        for g in range(2):
            for i in range(4):
                table[g, i*q:(i+1)*q, :(i+1)*q] = s[:, (3-i)*q:] * mask[g, i*q:(i+1)*q, :(i+1)*q]
            u_ref[0, g*n:g*n+h, j*w:(j+1)*w] = dot(table[g, :h, :h], hat_ref[g, :h]).astype(bf)
            u_ref[0, g*n+h:(g+1)*n, j*w:(j+1)*w] = dot(table[g, h:, :], hat_ref[g]).astype(bf)

def u_call(ends, taps, hat, per=3):
    steps = taps.shape[0]//per; n=hat.shape[1]; w=hat.shape[2]
    return pl.pallas_call(u_kernel, grid=(steps,),
        in_specs=[pl.BlockSpec(memory_space=pltpu.SMEM), pl.BlockSpec((1,per,n), lambda i:(i,0,0)), pl.BlockSpec((2,n,w), lambda i:(0,0,0))],
        out_specs=pl.BlockSpec((1,2*n,per*w), lambda i:(i,0,0)),
        out_shape=jax.ShapeDtypeStruct((steps,2*n,per*w), bf),
        scratch_shapes=[pltpu.VMEM((2,n,n),bf), pltpu.VMEM((2,n,n),bf)],
        compiler_params=pltpu.CompilerParams(vmem_limit_bytes=56<<20), name="spread")(ends, taps.reshape(steps,per,n), hat)

def mix_kernel(gain_ref, u_ref, w_ref, m_ref, wide):
    per = wide.shape[1]//w_ref.shape[1]; w=w_ref.shape[1]; d=wide.shape[0]
    for j in range(per):
        wide[:, j*w:(j+1)*w] = (w_ref[j*d:(j+1)*d].astype(f32)*gain_ref[...]).astype(bf)
    r = dot(u_ref[0], wide[...], NT)
    @pl.when(pl.program_id(0) == 0)
    def _(): m_ref[...] = r
    @pl.when(pl.program_id(0) > 0)
    def _(): m_ref[...] += r

def mix_call(gain, u, w):
    steps, t, pw = u.shape; width = w.shape[1]; per = pw//width; d = w.shape[0]//(steps*per)
    return pl.pallas_call(mix_kernel, grid=(steps,),
        in_specs=[pl.BlockSpec((1,width), lambda i:(0,0)), pl.BlockSpec((1,t,pw), lambda i:(i,0,0)), pl.BlockSpec((per*d,width), lambda i:(i,0))],
        out_specs=pl.BlockSpec((t,d), lambda i:(0,0)), out_shape=jax.ShapeDtypeStruct((t,d), f32),
        scratch_shapes=[pltpu.VMEM((d,pw),bf)],
        compiler_params=pltpu.CompilerParams(vmem_limit_bytes=56<<20), name="mix")(gain, u, w)

def dw_kernel(gain_ref, gt_ref, u_ref, o_ref):
    w = gain_ref.shape[1]; d = gt_ref.shape[0]; per = u_ref.shape[2]//w
    r = dot(gt_ref[...], u_ref[0])
    for j in range(per):
        o_ref[j*d:(j+1)*d, :] = (r[:, j*w:(j+1)*w]*gain_ref[...]).astype(bf)

def dw_call(gain, gt, u):
    steps, t, pw = u.shape; w = gain.shape[1]; per = pw//w; d = gt.shape[0]
    return pl.pallas_call(dw_kernel, grid=(steps,),
        in_specs=[pl.BlockSpec((1,w), lambda i:(0,0)), pl.BlockSpec((d,t), lambda i:(0,0)), pl.BlockSpec((1,t,pw), lambda i:(i,0,0))],
        out_specs=pl.BlockSpec((per*d,w), lambda i:(i,0)), out_shape=jax.ShapeDtypeStruct((steps*per*d,w), bf),
        compiler_params=pltpu.CompilerParams(vmem_limit_bytes=56<<20), name="mixer_grad")(gain, gt, u)

def back_kernel(ends_ref, taps_ref, g_ref, w_ref, o_ref, mask, tlo, thi, tb, vlo, vhi):
    n = mask.shape[1]; q=n//4; h=n//2; w=w_ref.shape[1]; per=taps_ref.shape[1]; d=g_ref.shape[1]
    @pl.when(pl.program_id(0) == 0)
    def _():
        for g in range(2): mask[g] = causal_mask(ends_ref, g, n, True)
        tlo[...] = jnp.zeros_like(tlo); tb[...] = jnp.zeros_like(tb)
        o_ref[...] = jnp.zeros_like(o_ref)
    for j in range(per):
        v = dot(g_ref[...], w_ref[j*d:(j+1)*d]).astype(bf)
        for g in range(2):
            vlo[g, j*h:(j+1)*h] = v[g*n:g*n+h]
            vhi[g, j*h:(j+1)*h] = v[g*n+h:(g+1)*n]
        s = strip(taps_ref[0, j:j+1, :], q)
        for g in range(2):
            m = mask[g]
            tlo[g, 0:q, j*h:j*h+q] = s[:, :q]*m[0:q, 0:q]
            tlo[g, 0:q, j*h+q:j*h+h] = s[:, q:2*q]*m[0:q, q:2*q]
            tlo[g, q:h, j*h+q:j*h+h] = s[:, :q]*m[q:h, q:h]
            thi[g, 0:q, j*h:j*h+h] = s[:, 2*q:4*q]*m[0:q, h:]
            thi[g, q:h, j*h:j*h+h] = s[:, q:3*q]*m[q:h, h:]
            tb[g, 0:q, j*h:j*h+h] = s[:, 0:2*q]*m[h:h+q, h:]
            tb[g, q:h, j*h+q:j*h+h] = s[:, 0:q]*m[h+q:, h+q:]
    for g in range(2):
        o_ref[g*n:g*n+h] += dot(tlo[g], vlo[g]) + dot(thi[g], vhi[g])
        o_ref[g*n+h:(g+1)*n] += dot(tb[g], vhi[g])

def back_call(ends, taps, g, w, per=3):
    steps = taps.shape[0]//per; n = taps.shape[1]; t, d = g.shape; width = w.shape[1]
    sc = lambda *s: pltpu.VMEM(s, bf)
    return pl.pallas_call(back_kernel, grid=(steps,),
        in_specs=[pl.BlockSpec(memory_space=pltpu.SMEM), pl.BlockSpec((1,per,n), lambda i:(i,0,0)), pl.BlockSpec((t,d), lambda i:(0,0)), pl.BlockSpec((per*d,width), lambda i:(i,0))],
        out_specs=pl.BlockSpec((t,width), lambda i:(0,0)), out_shape=jax.ShapeDtypeStruct((t,width), f32),
        scratch_shapes=[sc(2,n,n), sc(2,n//2,per*n//2), sc(2,n//2,per*n//2), sc(2,n//2,per*n//2), sc(2,per*n//2,width), sc(2,per*n//2,width)],
        compiler_params=pltpu.CompilerParams(vmem_limit_bytes=56<<20), name="spread_back")(ends, taps.reshape(steps,per,n), g, w)

def ffn_kernel(n2_ref, back_ref, wg_ref, wu_ref, wd_ref, br_ref, gt_ref, dgu_ref, dd_ref):
    n2, bk = n2_ref[...], back_ref[...]
    wg, wu, wd = wg_ref[...], wu_ref[...], wd_ref[...]
    gate = dot(n2, wg, NT); up = dot(n2, wu, NT)
    ga = dot(bk, wd, NT)
    sig = 1.0/(1.0+jnp.exp(-gate)); sw = gate*sig
    act = (sw*up).astype(bf)
    gg = (ga*up*(sig*(1.0+gate*(1.0-sig)))).astype(bf); gu = (ga*sw).astype(bf)
    br = dot(act, wd); gt = dot(gg, wg) + dot(gu, wu)
    @pl.when(pl.program_id(0) == 0)
    def _(): br_ref[...] = br; gt_ref[...] = gt
    @pl.when(pl.program_id(0) > 0)
    def _(): br_ref[...] += br; gt_ref[...] += gt
    dd_ref[...] = dot(act, bk, TN).astype(bf)
    dgu_ref[0] = dot(gg, n2, TN).astype(bf)
    dgu_ref[1] = dot(gu, n2, TN).astype(bf)

def ffn_call(n2, back, wgu, wd, chunk=256):
    t, d = n2.shape; u = wd.shape[0]; steps = u//chunk
    full = pl.BlockSpec((t,d), lambda i:(0,0)); row = pl.BlockSpec((chunk,d), lambda i:(i,0)); row2 = pl.BlockSpec((chunk,d), lambda i:(i+steps,0))
    S = jax.ShapeDtypeStruct
    return pl.pallas_call(ffn_kernel, grid=(steps,), in_specs=[full,full,row,row2,row],
        out_specs=[full,full,pl.BlockSpec((2,chunk,d), lambda i:(0,i,0)),row], out_shape=[S((t,d),f32),S((t,d),f32),S((2,u,d),bf),S((u,d),bf)],
        compiler_params=pltpu.CompilerParams(vmem_limit_bytes=56<<20), name="ffn")(n2, back, wgu, wgu, wd)


def adam_step(weight, grad, first, second, rate, decay):
    first_new = BETA_ONE * first + (1.0 - BETA_ONE) * grad
    second_new = BETA_TWO * second + (1.0 - BETA_TWO) * grad * grad
    corr_one = 1.0 - BETA_ONE**STEP
    corr_two = 1.0 - BETA_TWO**STEP
    update = first_new / corr_one / (jnp.sqrt(second_new / corr_two) + ADAM_EPS)
    return (weight - rate * (update + decay * weight), first_new, second_new)


def swap(v):
    return lax.ppermute(v, "core", [(0, 1), (1, 0)])


def join(mine, other, core, axis=0):
    return jnp.where(
        core == 0,
        jnp.concatenate([mine, other], axis=axis),
        jnp.concatenate([other, mine], axis=axis),
    )


def part(v, index, axis=0):
    size = v.shape[axis] // 2
    return lax.dynamic_slice_in_dim(v, index * size, size, axis)


def trade(v, core, axis=0):
    return join(part(v, core, axis), swap(part(v, 1 - core, axis)), core)


def add_trade(v, core):
    return part(v, core) + swap(part(v, 1 - core))


def body(
    inputs, lengths, filters, cotangent, mixer_weight, gate_up_weight, down_weight, norm_gains,
    mixer_first, gate_up_first, down_first, gains_first,
    mixer_second, gate_up_second, down_second, gains_second, mixer_average,
):
    slots, width = inputs.shape
    core = lax.axis_index("core")
    gather = lambda v: lax.all_gather(v, CHIPS, axis=0, tiled=True)
    scatter = lambda v: lax.psum_scatter(v, CHIPS, scatter_dimension=0, tiled=True)

    mixer_all = gather(trade(mixer_weight.astype(bf), core, 1))
    gate_up_all = gather(trade(gate_up_weight.astype(bf), core))
    down_all = gather(down_weight.astype(bf))
    gains = lax.all_gather(norm_gains.astype(bf), EVERY, axis=1, tiled=True).astype(f32)

    ends = jnp.cumsum(lengths, axis=-1).astype(jnp.int32)
    ends_both = join(ends, swap(ends), core)
    place = jnp.arange(slots, dtype=jnp.int32)
    live = place < ends[0, -1]
    back = jnp.where(live[:, None], cotangent, jnp.zeros((), bf))
    back_both = join(back, swap(back), core)
    taps = jnp.concatenate([filters.astype(f32), jnp.eye(AR_ORDER, slots, dtype=f32)])
    taps_turned = jnp.roll(taps[:, ::-1], 1 - slots // 4, axis=1)

    source = inputs.astype(f32)
    scale_one = lax.rsqrt(jnp.mean(source * source, axis=-1, keepdims=True) + NORM_EPS)
    hat_one = source * scale_one
    hat_both = trade(hat_one.astype(bf), core, 1).reshape(2, slots, width // 2)
    spread = u_call(ends_both, taps_turned, hat_both)
    gain_half = part(gains[0:1], core, 1)
    mixed = add_trade(mix_call(gain_half, spread, mixer_all), core)

    hidden = source + mixed
    scale_two = lax.rsqrt(jnp.mean(hidden * hidden, axis=-1, keepdims=True) + NORM_EPS)
    hat_two = hidden * scale_two
    normed_two = (hat_two * gains[1]).astype(bf)
    normed_both = join(normed_two, swap(normed_two), core)
    branch, grad_two, grad_gate_up, grad_down = ffn_call(normed_both, back_both, gate_up_all, down_all)
    output = (hidden + add_trade(branch, core)).astype(bf)
    grad_two = add_trade(grad_two, core)
    weighted_two = grad_two * gains[1]
    grad_hidden = back.astype(f32) + scale_two * (
        weighted_two - hat_two * jnp.mean(weighted_two * hat_two, axis=-1, keepdims=True)
    )
    grad_low = grad_hidden.astype(bf)
    grad_both = join(grad_low, swap(grad_low), core)
    grad_mixer = dw_call(gain_half, grad_both.T, spread)

    shard_gate_up = trade(scatter(grad_gate_up.reshape(-1, width)).astype(f32), core)
    shard_down = scatter(grad_down).astype(f32)
    pair = scatter(grad_mixer).astype(f32)
    shard_mixer = join(part(pair, core), swap(part(pair, 1 - core)), core, 1)

    grad_half = back_call(ends_both, taps, grad_both, mixer_all)
    grad_one = join(part(grad_half, core), swap(part(grad_half, 1 - core)), core, 1)
    weighted_one = grad_one * gains[0]
    input_grad = grad_hidden + scale_one * (
        weighted_one - hat_one * jnp.mean(weighted_one * hat_one, axis=-1, keepdims=True)
    )
    grad_gains = jnp.stack([jnp.sum(grad_one * hat_one, axis=0), jnp.sum(grad_two * hat_two, axis=0)])
    shard_gains = lax.psum_scatter(grad_gains, EVERY, scatter_dimension=1, tiled=True)

    squares = (
        jnp.sum(shard_mixer * shard_mixer)
        + jnp.sum(shard_gate_up * shard_gate_up)
        + jnp.sum(shard_down * shard_down)
        + jnp.sum(shard_gains * shard_gains)
    )
    grad_norm = jnp.sqrt(lax.psum(squares, EVERY))
    factor = CLIP_LIMIT / jnp.maximum(grad_norm, CLIP_LIMIT)
    mixer_new, mixer_first_new, mixer_second_new = adam_step(
        mixer_weight, shard_mixer * factor, mixer_first, mixer_second, RATE_MATRIX, DECAY_MATRIX
    )
    gate_up_new, gate_up_first_new, gate_up_second_new = adam_step(
        gate_up_weight, shard_gate_up * factor, gate_up_first, gate_up_second, RATE_MATRIX, DECAY_MATRIX
    )
    down_new, down_first_new, down_second_new = adam_step(
        down_weight, shard_down * factor, down_first, down_second, RATE_MATRIX, DECAY_MATRIX
    )
    gains_new, gains_first_new, gains_second_new = adam_step(
        norm_gains, shard_gains * factor, gains_first, gains_second, RATE_GAIN, 0.0
    )
    mixer_average_new = AVERAGE_KEEP * mixer_average + (1.0 - AVERAGE_KEEP) * mixer_new
    return (
        output, input_grad, grad_norm, mixer_new, gate_up_new, down_new, gains_new,
        mixer_first_new, gate_up_first_new, down_first_new, gains_first_new,
        mixer_second_new, gate_up_second_new, down_second_new, gains_second_new, mixer_average_new,
    )


def solution(mesh):
    outer, inner = mesh.shape["dp"], mesh.shape["fsdp"]
    side = math.isqrt(outer)
    if side * side != outer:
        side = 1
    split = jax.sharding.Mesh(
        np.asarray(mesh.devices).reshape(side, outer // side, inner // 2, 2), EVERY
    )
    rows, columns, whole = P(EVERY, None), P(None, EVERY), P()
    return jax.shard_map(
        body,
        mesh=split,
        in_specs=(
            rows, rows, whole, rows, rows, rows, rows, columns,
            rows, rows, rows, columns, rows, rows, rows, columns, rows,
        ),
        out_specs=(
            rows, rows, whole, rows, rows, rows, columns, rows, rows, rows, columns,
            rows, rows, rows, columns, rows,
        ),
        check_vma=False,
    )
```

```python
import functools
import math

import jax
import jax.numpy as jnp
import numpy as np
from jax import lax
from jax.experimental import pallas as pl
from jax.experimental.pallas import tpu as pltpu
from jax.sharding import PartitionSpec as P

bf = jnp.bfloat16
f32 = jnp.float32
FILTERS = 24
AR_ORDER = 3
FF = 2048
STEP = 10
NORM_EPS = 1e-05
CLIP_LIMIT = 1.0
BETA_ONE = 0.9
BETA_TWO = 0.95
ADAM_EPS = 1e-08
RATE_MATRIX = 0.03
RATE_GAIN = 0.5
DECAY_MATRIX = 0.1
AVERAGE_KEEP = 0.9
CHIPS = ("d0", "d1", "z")
EVERY = CHIPS + ("core",)


NT = (((1,), (1,)), ((), ()))
NN = (((1,), (0,)), ((), ()))
TN = (((0,), (0,)), ((), ()))


def dot(a, b, dims=NN):
    return lax.dot_general(a, b, dims, preferred_element_type=f32)


def call(kernel, name, flops, moved, **options):
    return pl.pallas_call(
        kernel,
        name=name,
        compiler_params=pltpu.CompilerParams(vmem_limit_bytes=56 << 20),
        cost_estimate=pl.CostEstimate(flops=flops, bytes_accessed=moved, transcendentals=0),
        **options,
    )


def smem():
    return pl.BlockSpec(memory_space=pltpu.SMEM)


def anywhere():
    return pl.BlockSpec(memory_space=pl.ANY)


def segment_of(place, ends_ref, group):
    return sum((place >= ends_ref[group, j]).astype(jnp.int32) for j in range(3))


def causal_mask(ends_ref, group, n, transposed):
    down = lax.broadcasted_iota(jnp.int32, (n, 1), 0)
    along = lax.broadcasted_iota(jnp.int32, (1, n), 1)
    one, two = segment_of(down, ends_ref, group), segment_of(along, ends_ref, group)
    order = (down <= along) if transposed else (down >= along)
    return ((one == two) & (one < 3) & order).astype(f32).astype(bf)


def diagonals(row, count):
    wide = jnp.broadcast_to(row, (count, row.shape[-1]))
    return pltpu.roll(wide, 0, 1, stride=1, stride_axis=0).astype(bf)


def spread_kernel(ends_ref, taps_ref, hat_ref, u_ref, mask, table):
    n = mask.shape[1]
    q, h, w = n // 4, n // 2, hat_ref.shape[2] // 2
    per = taps_ref.shape[1]

    @pl.when(pl.program_id(0) == 0)
    def _():
        for g in range(2):
            mask[g] = causal_mask(ends_ref, g, n, False)
        table[...] = jnp.zeros_like(table)

    for j in range(per):
        strip = diagonals(taps_ref[0, j : j + 1, :], q)
        for g in range(2):
            for i in range(4):
                rows, cols = slice(i * q, (i + 1) * q), slice(0, (i + 1) * q)
                table[g, rows, cols] = strip[:, (3 - i) * q :] * mask[g, rows, cols]
            upper = dot(table[g, :h, :h], hat_ref[g, :h]).astype(bf)
            lower = dot(table[g, h:, :], hat_ref[g]).astype(bf)
            for side in range(2):
                cols = slice(side * w, (side + 1) * w)
                u_ref[side, g * n : g * n + h, j * w : (j + 1) * w] = upper[:, cols]
                u_ref[side, g * n + h : (g + 1) * n, j * w : (j + 1) * w] = lower[:, cols]


def spread_call(ends, taps, hat, per=3):
    count, n = taps.shape
    w = hat.shape[2] // 2
    return call(
        spread_kernel, "spread", 12 * 10**9, 16 * 10**6,
        grid=(count // per,),
        in_specs=[
            smem(),
            pl.BlockSpec((1, per, n), lambda i: (i, 0, 0)),
            pl.BlockSpec((2, n, 2 * w), lambda i: (0, 0, 0)),
        ],
        out_specs=pl.BlockSpec((2, 2 * n, per * w), lambda i: (0, 0, i)),
        out_shape=jax.ShapeDtypeStruct((2, 2 * n, count * w), bf),
        scratch_shapes=[pltpu.VMEM((2, n, n), bf), pltpu.VMEM((2, n, n), bf)],
    )(ends, taps.reshape(count // per, per, n), hat)


def piece_copies(where_ref, piece_refs, held, sem, columns):
    copies, at = [], 0
    for ref in piece_refs:
        blocks, rows = ref.shape[0], ref.shape[1]
        for b in range(blocks):
            start = pl.multiple_of(where_ref[at] * rows, math.gcd(rows, 512))
            copies.append(pltpu.make_async_copy(ref.at[b], held.at[pl.ds(start, rows), columns], sem.at[at]))
            at += 1
    return copies


def mix_kernel(count, width, first, where_ref, gain_ref, u_ref, *refs):
    pieces, refs = refs[:count], refs[count:]
    before, (m_ref, held, wide, sem) = refs[: 0 if first else 1], refs[0 if first else 1 :]
    w = held.shape[1]
    filters = held.shape[0] // width

    @pl.when(pl.program_id(0) == 0)
    def _():
        copies = piece_copies(where_ref, pieces, held, sem, slice(0, w))
        for c in copies:
            c.start()
        for c in copies:
            c.wait()
        for k in range(filters):
            wide[:, k * w : (k + 1) * w] = (held[k * width : (k + 1) * width].astype(f32) * gain_ref[...]).astype(bf)

    result = dot(u_ref[0], wide[...], NT)
    m_ref[...] = result if first else result + before[0][...]


def mix_call(where, gain, u, side, pieces, before=None, parts=2):
    rows, depth = u.shape[1:]
    w = gain.shape[1]
    total = sum(p.shape[0] * p.shape[1] for p in pieces)
    width = total // (depth // w)
    step = rows // parts
    out = pl.BlockSpec((step, width), lambda i: (i, 0))
    extra = () if before is None else (before,)
    return call(
        functools.partial(mix_kernel, len(pieces), width, before is None),
        "mix", 2 * rows * depth * width, 2 * (rows * depth + total * w) + 4 * rows * width,
        grid=(parts,),
        in_specs=[smem(), pl.BlockSpec((1, w), lambda i: (0, 0)), pl.BlockSpec((1, step, depth), lambda i: (side, i, 0))]
        + [anywhere() for _ in pieces] + [out for _ in extra],
        out_specs=out,
        out_shape=jax.ShapeDtypeStruct((rows, width), f32),
        scratch_shapes=[
            pltpu.VMEM((total, w), bf), pltpu.VMEM((width, depth), bf),
            pltpu.SemaphoreType.DMA((where.shape[0],)),
        ],
    )(where, gain, u, *pieces, *extra)


def grad_kernel(gain_ref, turned_ref, u_ref, o_ref):
    w, width = gain_ref.shape[1], turned_ref.shape[0]
    result = dot(turned_ref[...], u_ref[0])
    for j in range(result.shape[1] // w):
        o_ref[j * width : (j + 1) * width, :] = (result[:, j * w : (j + 1) * w] * gain_ref[...]).astype(bf)


def grad_call(gain, turned, u, side, per=9):
    rows, depth = u.shape[1:]
    w, width = gain.shape[1], turned.shape[0]
    count = depth // w
    return call(
        grad_kernel, "mixer_grad", 2 * rows * depth * width, 2 * (rows * depth + count * width * w),
        grid=(count // per,),
        in_specs=[
            pl.BlockSpec((1, w), lambda i: (0, 0)),
            pl.BlockSpec((width, rows), lambda i: (0, 0)),
            pl.BlockSpec((1, rows, per * w), lambda i: (side, 0, i)),
        ],
        out_specs=pl.BlockSpec((per * width, w), lambda i: (i, 0)),
        out_shape=jax.ShapeDtypeStruct((count * width, w), bf),
    )(gain, turned, u)


def back_kernel(count, where_ref, ends_ref, taps_ref, g_ref, *refs):
    sides, (o_ref, held, mask, low_low, low_high, high, v_low, v_high, sem) = refs[: 2 * count], refs[2 * count :]
    n = mask.shape[1]
    q, h, d = n // 4, n // 2, g_ref.shape[1]
    per = taps_ref.shape[1]
    w = held.shape[1] // 2
    step = pl.program_id(0)

    @pl.when(step == 0)
    def _():
        copies = []
        for side in range(2):
            copies += piece_copies(
                where_ref, sides[side * count : (side + 1) * count], held, sem.at[side],
                slice(side * w, (side + 1) * w),
            )
        for c in copies:
            c.start()
        for g in range(2):
            mask[g] = causal_mask(ends_ref, g, n, True)
        low_low[...] = jnp.zeros_like(low_low)
        high[...] = jnp.zeros_like(high)
        o_ref[...] = jnp.zeros_like(o_ref)
        for c in copies:
            c.wait()

    for j in range(per):
        at = pl.multiple_of((step * per + j) * d, d)
        v = dot(g_ref[...], held[pl.ds(at, d), :]).astype(bf)
        for g in range(2):
            v_low[g, j * h : (j + 1) * h] = v[g * n : g * n + h]
            v_high[g, j * h : (j + 1) * h] = v[g * n + h : (g + 1) * n]
        s = diagonals(taps_ref[0, j : j + 1, :], q)
        a = j * h
        for g in range(2):
            m = mask[g]
            low_low[g, 0:q, a : a + q] = s[:, :q] * m[0:q, 0:q]
            low_low[g, 0:q, a + q : a + h] = s[:, q : 2 * q] * m[0:q, q : 2 * q]
            low_low[g, q:h, a + q : a + h] = s[:, :q] * m[q:h, q:h]
            low_high[g, 0:q, a : a + h] = s[:, 2 * q : 4 * q] * m[0:q, h:]
            low_high[g, q:h, a : a + h] = s[:, q : 3 * q] * m[q:h, h:]
            high[g, 0:q, a : a + h] = s[:, 0 : 2 * q] * m[h : h + q, h:]
            high[g, q:h, a + q : a + h] = s[:, 0:q] * m[h + q :, h + q :]
    for g in range(2):
        o_ref[g * n : g * n + h] += dot(low_low[g], v_low[g]) + dot(low_high[g], v_high[g])
        o_ref[g * n + h : (g + 1) * n] += dot(high[g], v_high[g])


def back_call(where, ends, taps, g, sides, per=3):
    count, n = taps.shape
    rows, d = g.shape
    pieces = [p for side in sides for p in side]
    total = sum(p.shape[0] * p.shape[1] for p in sides[0])
    width = 2 * sides[0][0].shape[-1]
    scratch = lambda *s: pltpu.VMEM(s, bf)
    return call(
        functools.partial(back_kernel, len(sides[0])), "spread_back",
        2 * rows * width * (total + count * n), 2 * total * width + 10**7,
        grid=(count // per,),
        in_specs=[
            smem(), smem(), pl.BlockSpec((1, per, n), lambda i: (i, 0, 0)), pl.BlockSpec((rows, d), lambda i: (0, 0)),
        ] + [anywhere() for _ in pieces],
        out_specs=pl.BlockSpec((rows, width), lambda i: (0, 0)),
        out_shape=jax.ShapeDtypeStruct((rows, width), f32),
        scratch_shapes=[
            scratch(total, width), scratch(2, n, n), scratch(2, n // 2, per * n // 2),
            scratch(2, n // 2, per * n // 2), scratch(2, n // 2, per * n // 2),
            scratch(2, per * n // 2, width), scratch(2, per * n // 2, width),
            pltpu.SemaphoreType.DMA((2, where.shape[0])),
        ],
    )(where, ends, taps.reshape(count // per, per, n), g, *pieces)


def flat(v):
    return v.reshape(-1, v.shape[-1])


def ffn_kernel(normed_ref, back_ref, gate_ref, up_ref, down_ref, branch_ref, two_ref, grads_ref):
    normed, back = normed_ref[...], back_ref[...]
    w_gate, w_up, w_down = flat(gate_ref[...]), flat(up_ref[...]), flat(down_ref[...])
    step = pl.program_id(0)
    gate, up = dot(normed, w_gate, NT), dot(normed, w_up, NT)
    grad_act = dot(back, w_down, NT)
    sigma = 1.0 / (1.0 + jnp.exp(-gate))
    swish = gate * sigma
    act = (swish * up).astype(bf)
    grad_gate = (grad_act * up * (sigma * (1.0 + gate * (1.0 - sigma)))).astype(bf)
    grad_up = (grad_act * swish).astype(bf)
    branch = dot(act, w_down)
    two = dot(grad_gate, w_gate) + dot(grad_up, w_up)

    @pl.when(step == 0)
    def _():
        branch_ref[...] = branch
        two_ref[...] = two

    @pl.when(step > 0)
    def _():
        branch_ref[...] += branch
        two_ref[...] += two

    half = grads_ref.shape[0] // 2
    chips, units, width = gate_ref.shape
    down_chips, down_units = down_ref.shape[0], down_ref.shape[1]
    put = lambda v: v.astype(bf).reshape(chips, units, width)
    grads_ref[pl.ds(step * chips, chips), 0:units] = put(dot(grad_gate, normed, TN))
    grads_ref[pl.ds(half + step * chips, chips), 0:units] = put(dot(grad_up, normed, TN))
    grads_ref[pl.ds(step * down_chips, down_chips), units : units + down_units] = (
        dot(act, back, TN).astype(bf).reshape(down_chips, down_units, width)
    )


def ffn_call(normed, back, packed, units, chunk=256):
    rows, d = normed.shape
    chips = packed.shape[0]
    own = chunk // units
    steps = chips // 2 // own
    full = pl.BlockSpec((rows, d), lambda i: (0, 0))
    shape = jax.ShapeDtypeStruct
    return call(
        ffn_kernel, "ffn", 10**10, 10**7,
        grid=(steps,),
        in_specs=[
            full, full,
            pl.BlockSpec((own, units, d), lambda i: (i, 0, 0)),
            pl.BlockSpec((own, units, d), lambda i: (i + steps, 0, 0)),
            pl.BlockSpec((2 * own, units // 2, d), lambda i: (i, 2, 0)),
        ],
        out_specs=[full, full, pl.BlockSpec((chips, units + units // 2, d), lambda i: (0, 0, 0))],
        out_shape=[shape((rows, d), f32), shape((rows, d), f32), shape((chips, units + units // 2, d), bf)],
    )(normed, back, packed, packed, packed)


def adam_step(weight, grad, first, second, rate, decay):
    first_new = BETA_ONE * first + (1.0 - BETA_ONE) * grad
    second_new = BETA_TWO * second + (1.0 - BETA_TWO) * grad * grad
    corr_one = 1.0 - BETA_ONE**STEP
    corr_two = 1.0 - BETA_TWO**STEP
    update = first_new / corr_one / (jnp.sqrt(second_new / corr_two) + ADAM_EPS)
    return (weight - rate * (update + decay * weight), first_new, second_new)


def flip(v, axis, bits=1):
    size = lax.axis_size(axis)
    return lax.ppermute(v, axis, [(i, i ^ bits) for i in range(size)])


def swap(v):
    return flip(v, "core")


def join(mine, other, core, axis=0):
    return jnp.where(
        core == 0,
        jnp.concatenate([mine, other], axis=axis),
        jnp.concatenate([other, mine], axis=axis),
    )


def part(v, index, axis=0):
    size = v.shape[axis] // 2
    return lax.dynamic_slice_in_dim(v, index * size, size, axis)


def trade(v, core, axis=0):
    return join(part(v, core, axis), swap(part(v, 1 - core, axis)), core)


def add_trade(v, core):
    return part(v, core) + swap(part(v, 1 - core))


class Whole:
    def __init__(self):
        self.chips = lax.axis_size("d0") * lax.axis_size("d1") * lax.axis_size("z")

    def gather(self, block):
        return [lax.all_gather(block, CHIPS, axis=0, tiled=True)[None]]

    def where(self):
        return jnp.zeros((1,), jnp.int32)

    def scatter(self, grad):
        return lax.psum_scatter(grad, CHIPS, scatter_dimension=0, tiled=True).astype(f32)

    def total(self, v):
        return lax.psum(v, EVERY)


class Cube(Whole):
    def __init__(self):
        super().__init__()
        self.size = lax.axis_size("z")
        self.y, self.x, self.z = (lax.axis_index(a) for a in CHIPS)

    def gather(self, block):
        line = jnp.stack([block] + [flip(block, "z", s) for s in range(1, self.size)])
        half = self.size // 2
        from_x, from_y = flip(line, "d1"), flip(line, "d0")
        return [line, from_x, from_y, flip(from_y[:half], "d1"), flip(from_x[half:], "d0")]

    def where(self):
        places = []
        for dy, dx in ((0, 0), (0, 1), (1, 0), (1, 1)):
            for s in range(self.size):
                places.append((((self.y ^ dy) * 2 + (self.x ^ dx)) * self.size) + (self.z ^ s))
        return jnp.stack(places).astype(jnp.int32)

    def scatter(self, grad):
        rows = grad.shape[0] // self.chips
        blocks = grad.reshape(2, 2, self.size, rows, grad.shape[1])
        half = self.size // 2

        def pick(dy, dx):
            return lax.dynamic_slice(blocks, (self.y ^ dy, self.x ^ dx, 0, 0, 0), (1, 1) + blocks.shape[2:])[0, 0]

        far, to_x, to_y, own = pick(1, 1), pick(0, 1), pick(1, 0), pick(0, 0)
        by_x, by_y = flip(far[:half], "d1"), flip(far[half:], "d0")
        low = lambda v: v.astype(bf)
        wide = lambda v: v.astype(f32)
        to_y = jnp.concatenate([low(wide(to_y[:half]) + wide(by_x)), to_y[half:]])
        to_x = jnp.concatenate([to_x[:half], low(wide(to_x[half:]) + wide(by_y))])
        line = wide(own) + wide(flip(to_x, "d1")) + wide(flip(to_y, "d0"))
        at = lambda s: lax.dynamic_index_in_dim(line, self.z ^ s, 0, keepdims=False)
        result = at(0)
        for s in range(1, self.size):
            result = result + wide(flip(low(at(s)), "z", s))
        return result

    def total(self, v):
        for axis, bits in (("core", 1), ("d1", 1), ("d0", 1)):
            v = v + flip(v, axis, bits)
        bits = 1
        while bits < self.size:
            v = v + flip(v, "z", bits)
            bits *= 2
        return v


def body(
    inputs, lengths, filters, cotangent, mixer_weight, gate_up_weight, down_weight, norm_gains,
    mixer_first, gate_up_first, down_first, gains_first,
    mixer_second, gate_up_second, down_second, gains_second, mixer_average,
):
    slots, width = inputs.shape
    core = lax.axis_index("core")
    depth = lax.axis_size("z")
    cube = lax.axis_size("d0") == 2 and lax.axis_size("d1") == 2 and depth & (depth - 1) == 0 and depth > 1
    links = Cube() if cube else Whole()
    chips = links.chips
    units = gate_up_weight.shape[0]
    own_gains = norm_gains.shape[1]
    spot = (lax.axis_index("d0") * lax.axis_size("d1") + lax.axis_index("d1")) * depth + lax.axis_index("z")

    mixer_block = trade(mixer_weight.astype(bf), core, 1)
    quarter = mixer_block.shape[1] // 2
    sides = [links.gather(mixer_block[:, s * quarter : (s + 1) * quarter]) for s in range(2)]
    gains_low = norm_gains.astype(bf)
    gains_row = join(gains_low, swap(gains_low), core, 1)
    gains_row = jnp.pad(gains_row, ((0, 14), (0, width - 2 * own_gains)))
    block = jnp.concatenate([trade(gate_up_weight.astype(bf), core), down_weight.astype(bf), gains_row])
    packed = lax.all_gather(block, CHIPS, axis=0, tiled=False)
    gains = packed[:, units + units // 2 :, : 2 * own_gains][:, :2]
    gains = gains.transpose(1, 0, 2).reshape(2, width).astype(f32)
    groups = 2 * FF // 256
    if chips != groups:
        gate_up_all = packed[:, :units].reshape(groups, -1, width)
        down_all = packed[:, units : units + units // 2].reshape(groups, -1, width)
        packed = jnp.concatenate([gate_up_all, down_all], axis=1)

    ends = jnp.cumsum(lengths, axis=-1).astype(jnp.int32)
    ends_both = join(ends, swap(ends), core)
    place = jnp.arange(slots, dtype=jnp.int32)
    live = place < ends[0, -1]
    back = jnp.where(live[:, None], cotangent, jnp.zeros((), bf))
    back_both = join(back, swap(back), core)
    taps = jnp.concatenate([filters.astype(f32), jnp.eye(AR_ORDER, slots, dtype=f32)])
    taps_turned = jnp.roll(taps[:, ::-1], 1 - slots // 4, axis=1)

    source = inputs.astype(f32)
    scale_one = lax.rsqrt(jnp.mean(source * source, axis=-1, keepdims=True) + NORM_EPS)
    hat_one = source * scale_one
    hat_both = trade(hat_one.astype(bf), core, 1).reshape(2, slots, width // 2)
    spread = spread_call(ends_both, taps_turned, hat_both)
    gain_half = part(gains[0:1], core, 1)
    gain_sides = [gain_half[:, s * quarter : (s + 1) * quarter] for s in range(2)]
    where = links.where()
    mixed = mix_call(where, gain_sides[0], spread, 0, sides[0])
    mixed = mix_call(where, gain_sides[1], spread, 1, sides[1], mixed)
    mixed = add_trade(mixed, core)

    hidden = source + mixed
    scale_two = lax.rsqrt(jnp.mean(hidden * hidden, axis=-1, keepdims=True) + NORM_EPS)
    hat_two = hidden * scale_two
    normed_two = (hat_two * gains[1]).astype(bf)
    normed_both = join(normed_two, swap(normed_two), core)
    branch, grad_two, grad_ffn = ffn_call(normed_both, back_both, packed, 2 * FF // groups // 2)
    if chips == groups:
        shard_ffn = lax.psum_scatter(flat(grad_ffn), CHIPS, scatter_dimension=0, tiled=True).astype(f32)
        shard_gate_up, shard_down = shard_ffn[:units], shard_ffn[units:]
    else:
        wide = 2 * FF // groups // 2
        shard_gate_up = Whole().scatter(flat(grad_ffn[:, :wide]))
        shard_down = Whole().scatter(flat(grad_ffn[:, wide:]))
    shard_gate_up = trade(shard_gate_up, core)

    grad_two = add_trade(grad_two, core)
    weighted_two = grad_two * gains[1]
    grad_hidden = back.astype(f32) + scale_two * (
        weighted_two - hat_two * jnp.mean(weighted_two * hat_two, axis=-1, keepdims=True)
    )
    grad_low = grad_hidden.astype(bf)
    grad_both = join(grad_low, swap(grad_low), core)
    turned = grad_both.T
    pairs = [links.scatter(grad_call(gain_sides[s], turned, spread, s)) for s in range(2)]
    pair = jnp.concatenate(pairs, axis=1)
    shard_mixer = join(part(pair, core), swap(part(pair, 1 - core)), core, 1)

    output = (hidden + add_trade(branch, core)).astype(bf)
    grad_half = back_call(where, ends_both, taps, grad_both, sides)
    grad_one = join(part(grad_half, core), swap(part(grad_half, 1 - core)), core, 1)
    weighted_one = grad_one * gains[0]
    input_grad = grad_hidden + scale_one * (
        weighted_one - hat_one * jnp.mean(weighted_one * hat_one, axis=-1, keepdims=True)
    )
    grad_gains = jnp.stack([jnp.sum(grad_one * hat_one, axis=0), jnp.sum(grad_two * hat_two, axis=0)])
    grad_gains = links.total(grad_gains)
    shard_gains = lax.dynamic_slice_in_dim(grad_gains, (spot * 2 + core) * own_gains, own_gains, 1)

    squares = (
        jnp.sum(shard_mixer * shard_mixer)
        + jnp.sum(shard_gate_up * shard_gate_up)
        + jnp.sum(shard_down * shard_down)
        + jnp.sum(shard_gains * shard_gains)
    )
    grad_norm = jnp.sqrt(links.total(squares))
    factor = CLIP_LIMIT / jnp.maximum(grad_norm, CLIP_LIMIT)
    mixer_new, mixer_first_new, mixer_second_new = adam_step(
        mixer_weight, shard_mixer * factor, mixer_first, mixer_second, RATE_MATRIX, DECAY_MATRIX
    )
    gate_up_new, gate_up_first_new, gate_up_second_new = adam_step(
        gate_up_weight, shard_gate_up * factor, gate_up_first, gate_up_second, RATE_MATRIX, DECAY_MATRIX
    )
    down_new, down_first_new, down_second_new = adam_step(
        down_weight, shard_down * factor, down_first, down_second, RATE_MATRIX, DECAY_MATRIX
    )
    gains_new, gains_first_new, gains_second_new = adam_step(
        norm_gains, shard_gains * factor, gains_first, gains_second, RATE_GAIN, 0.0
    )
    mixer_average_new = AVERAGE_KEEP * mixer_average + (1.0 - AVERAGE_KEEP) * mixer_new
    return (
        output, input_grad, grad_norm, mixer_new, gate_up_new, down_new, gains_new,
        mixer_first_new, gate_up_first_new, down_first_new, gains_first_new,
        mixer_second_new, gate_up_second_new, down_second_new, gains_second_new, mixer_average_new,
    )


def solution(mesh):
    outer, inner = mesh.shape["dp"], mesh.shape["fsdp"]
    side = math.isqrt(outer)
    if side * side != outer:
        side = 1
    split = jax.sharding.Mesh(
        np.asarray(mesh.devices).reshape(side, outer // side, inner // 2, 2), EVERY
    )
    rows, columns, whole = P(EVERY, None), P(None, EVERY), P()
    return jax.shard_map(
        body,
        mesh=split,
        in_specs=(
            rows, rows, whole, rows, rows, rows, rows, columns,
            rows, rows, rows, columns, rows, rows, rows, columns, rows,
        ),
        out_specs=(
            rows, rows, whole, rows, rows, rows, columns, rows, rows, rows, columns,
            rows, rows, rows, columns, rows,
        ),
        check_vma=False,
    )
```

```python
import functools
import math

import jax
import jax.numpy as jnp
import numpy as np
from jax import lax
from jax.experimental import pallas as pl
from jax.experimental.pallas import tpu as pltpu
from jax.sharding import PartitionSpec as P

bf = jnp.bfloat16
f32 = jnp.float32
FILTERS = 24
AR_ORDER = 3
FF = 2048
STEP = 10
NORM_EPS = 1e-05
CLIP_LIMIT = 1.0
BETA_ONE = 0.9
BETA_TWO = 0.95
ADAM_EPS = 1e-08
RATE_MATRIX = 0.03
RATE_GAIN = 0.5
DECAY_MATRIX = 0.1
AVERAGE_KEEP = 0.9
CHIPS = ("d0", "d1", "z")
EVERY = CHIPS + ("core",)


NT = (((1,), (1,)), ((), ()))
NN = (((1,), (0,)), ((), ()))
TN = (((0,), (0,)), ((), ()))


def dot(a, b, dims=NN):
    return lax.dot_general(a, b, dims, preferred_element_type=f32)


class Chain:
    def __init__(self):
        self.token = None

    def call(self, kernel, name, args, in_specs, out_specs, out_shape, waits=(), through=(), **options):
        count, single = len(args), not isinstance(out_shape, (list, tuple)) and not through
        if single:
            out_specs, out_shape = [out_specs], [out_shape]
        made = len(out_shape)
        aliases = options.pop("input_output_aliases", {})
        aliases = {**aliases, **{count + i: made + i for i in range(len(through))}}
        last = tuple(through) + tuple(waits) + (() if self.token is None else (self.token,))

        def whole(*refs):
            first = count + len(last)
            kernel(*refs[:count], *refs[first : first + made], *refs[first + made + len(through) + 1 :])

        *outs, self.token = pl.pallas_call(
            whole,
            name=name,
            in_specs=list(in_specs) + [anywhere() for _ in last],
            out_specs=list(out_specs) + [anywhere() for _ in through] + [anywhere()],
            out_shape=list(out_shape) + [shaped(v.shape, v.dtype) for v in through] + [shaped((8, 128), f32)],
            input_output_aliases=aliases,
            compiler_params=pltpu.CompilerParams(vmem_limit_bytes=64 << 20),
            cost_estimate=pl.CostEstimate(flops=1, bytes_accessed=1, transcendentals=0),
            **options,
        )(*args, *last)
        return outs[0] if single else outs

    def pause(self, *waits):
        self.call(lambda: None, "pause", (), [], [], [], waits=waits)


def smem():
    return pl.BlockSpec(memory_space=pltpu.SMEM)


def anywhere():
    return pl.BlockSpec(memory_space=pl.ANY)


def fixed(*shape):
    return pl.BlockSpec(shape, lambda i: (0,) * len(shape))


NOTE = 16


def shaped(shape, dtype):
    return jax.ShapeDtypeStruct(tuple(shape), dtype)


def segment_of(place, ends_ref, group):
    return sum((place >= ends_ref[group, j]).astype(jnp.int32) for j in range(3))


def causal_mask(ends_ref, group, n, transposed):
    down = lax.broadcasted_iota(jnp.int32, (n, 1), 0)
    along = lax.broadcasted_iota(jnp.int32, (1, n), 1)
    one, two = segment_of(down, ends_ref, group), segment_of(along, ends_ref, group)
    order = (down <= along) if transposed else (down >= along)
    return ((one == two) & (one < 3) & order).astype(f32).astype(bf)


def diagonals(row, count):
    wide = jnp.broadcast_to(row, (count, row.shape[-1]))
    return pltpu.roll(wide, 0, 1, stride=1, stride_axis=0).astype(bf)


def spread_kernel(lengths_ref, came_ref, taps_ref, own_ref, other_ref, *refs):
    u_ref, mask, table, ends = refs[-4:]
    n = mask.shape[1]
    q, h, w = n // 4, n // 2, own_ref.shape[1] // 2
    per = taps_ref.shape[1]

    @pl.when(pl.program_id(0) == 0)
    def _():
        find_ends(ends, lengths_ref, came_ref)
        for g in range(2):
            mask[g] = causal_mask(ends, g, n, False)
        table[...] = jnp.zeros_like(table)

    for j in range(per):
        strip = diagonals(taps_ref[0, j : j + 1, :], q)
        for g, tokens in enumerate((own_ref, other_ref)):
            for i in range(4):
                rows, cols = slice(i * q, (i + 1) * q), slice(0, (i + 1) * q)
                table[g, rows, cols] = strip[:, (3 - i) * q :] * mask[g, rows, cols]
            upper = dot(table[g, :h, :h], tokens[:h]).astype(bf)
            lower = dot(table[g, h:, :], tokens[...]).astype(bf)
            for side in range(2):
                cols = slice(side * w, (side + 1) * w)
                u_ref[side, g * n : g * n + h, j * w : (j + 1) * w] = upper[:, cols]
                u_ref[side, g * n + h : (g + 1) * n, j * w : (j + 1) * w] = lower[:, cols]


def find_ends(ends, lengths_ref, came_ref):
    for g, ref in enumerate((lengths_ref, came_ref)):
        total = ref[0, 0]
        ends[g, 0] = total
        for j in range(1, 3):
            total = total + ref[0, j]
            ends[g, j] = total


def spread_call(chain, lengths, taps, own, other, first, steps, into=None):
    blocks, per, n = taps.shape
    w = own.shape[1] // 2
    args = [*lengths, taps, own, other]
    specs = [smem()] * 2 + [pl.BlockSpec((1, per, n), lambda i: (i + first, 0, 0)), fixed(n, 2 * w), fixed(n, 2 * w)]
    options = {}
    if into is not None:
        options = dict(input_output_aliases={len(args): 0})
        args, specs = args + [into], specs + [anywhere()]
    return chain.call(
        spread_kernel, "spread", args, specs,
        pl.BlockSpec((2, 2 * n, per * w), lambda i: (0, 0, i + first)),
        shaped((2, 2 * n, blocks * per * w), bf),
        grid=(steps,),
        scratch_shapes=[pltpu.VMEM((2, n, n), bf), pltpu.VMEM((2, n, n), bf), pltpu.SMEM((2, 3), jnp.int32)],
        **options,
    )


def run_copies(copies):
    for c in copies:
        c.start()
    for c in copies:
        c.wait()


def chip_of(spot_ref, slot, size):
    if isinstance(slot, int):
        return slot
    dy, dx, dz, fixed_z = slot
    return ((spot_ref[0] ^ dy) * 2 + (spot_ref[1] ^ dx)) * size + (dz if fixed_z else spot_ref[2] ^ dz)


def collect(spot_ref, pieces, plan, size, held, sem, columns):
    copies = []
    for at, (piece, row, rows, slot, half) in enumerate(plan):
        place = chip_of(spot_ref, slot, size)
        if half is not None:
            place = place * 2 + (spot_ref[3] ^ half)
        start = pl.multiple_of(place * rows, math.gcd(rows, 512))
        copies.append(
            pltpu.make_async_copy(pieces[piece].at[pl.ds(row, rows)], held.at[pl.ds(start, rows), columns], sem.at[at])
        )
    return copies


def mix_kernel(count, plan, notes, size, width, side, spot_ref, u_ref, *refs):
    pieces, refs = refs[:count], refs[count:]
    first = side == 0
    before, refs = refs[: 0 if first else 2], refs[0 if first else 2 :]
    if notes:
        own_ref, other_ref, gains_ref, held, wide, sem, tiles = refs
    else:
        gains_ref, own_ref, other_ref, held, wide, sem = refs
    w = held.shape[1]
    filters = held.shape[0] // width
    step = pl.program_id(0)

    @pl.when(step == 0)
    def _():
        copies = collect(spot_ref, pieces, plan, size, held, sem, slice(0, w))
        for at, (piece, row, slot) in enumerate(notes):
            copies.append(
                pltpu.make_async_copy(
                    pieces[piece].at[pl.ds(row, NOTE)], tiles.at[chip_of(spot_ref, slot, size)], sem.at[len(plan) + at]
                )
            )
        run_copies(copies)
        if notes:
            lanes = width // len(notes)
            for b in range(width // 128):
                block = jnp.zeros((NOTE, 128), f32)
                for j in range(128 // lanes):
                    tile = tiles[b * (128 // lanes) + j].astype(f32)
                    block = block + (pltpu.roll(tile, j * lanes, 1) if j else tile)
                gains_ref[:, b * 128 : (b + 1) * 128] = block
        gain = gains_ref[0:1, pl.ds(pl.multiple_of((spot_ref[3] * 2 + side) * w, w), w)]
        for k in range(filters):
            wide[:, k * w : (k + 1) * w] = (held[k * width : (k + 1) * width].astype(f32) * gain).astype(bf)

    result = dot(u_ref[0], wide[...], NT)
    for g, out in enumerate((own_ref, other_ref)):

        @pl.when(step == g)
        def _():
            out[...] = result if first else result + before[g][...]


def mix_call(chain, spot, u, side, pieces, plan, notes, gains, size, width, before=()):
    rows, depth = u.shape[1:]
    w = pieces[0].shape[-1]
    total = depth // w * width
    step = rows // 2
    out = fixed(step, width)
    note = fixed(NOTE, width)
    given = () if notes else (gains,)
    return chain.call(
        functools.partial(mix_kernel, len(pieces), plan, notes, size, width, side), "mix",
        (spot, u, *pieces, *before, *given),
        [smem(), pl.BlockSpec((1, step, depth), lambda i: (side, i, 0))] + [anywhere() for _ in pieces]
        + [out for _ in before] + [note for _ in given],
        [out, out] + [note for _ in range(1 - len(given))],
        [shaped((step, width), f32)] * 2 + [shaped((NOTE, width), f32) for _ in range(1 - len(given))],
        grid=(2,),
        scratch_shapes=[
            pltpu.VMEM((total, w), bf), pltpu.VMEM((width, depth), bf), pltpu.SemaphoreType.DMA((len(plan) + len(notes),)),
        ] + [pltpu.VMEM((len(notes), NOTE, 128), bf)] * (1 - len(given)),
    )


def hidden_kernel(source_ref, own_ref, came_ref, gain_ref, hidden_ref, normed_ref):
    hidden = source_ref[...].astype(f32) + (own_ref[...] + came_ref[...])
    scale = lax.rsqrt(jnp.mean(hidden * hidden, axis=-1, keepdims=True) + NORM_EPS)
    hidden_ref[...] = hidden
    normed_ref[...] = (hidden * scale * gain_ref[1:2]).astype(bf)


def hidden_call(chain, source, own, came, gain, parts=4):
    rows, width = source.shape
    block = pl.BlockSpec((rows // parts, width), lambda i: (i, 0))
    return chain.call(
        hidden_kernel, "hidden", (source, own, came, gain), [block, block, block, fixed(NOTE, width)],
        [block, block], [shaped((rows, width), f32), shaped((rows, width), bf)],
        grid=(parts,),
    )


def norm_back(grad, hat, scale, gain):
    weighted = grad * gain
    return scale * (weighted - hat * jnp.mean(weighted * hat, axis=-1, keepdims=True))


def add_rows(ref, values, step):
    total = jnp.sum(values, axis=0, keepdims=True)

    @pl.when(step == 0)
    def _():
        ref[...] = total

    @pl.when(step > 0)
    def _():
        ref[...] += total


def turn_kernel(lengths_ref, hidden_ref, back_ref, own_ref, came_ref, gain_ref, grad_ref, low_ref, gains_ref):
    hidden = hidden_ref[...]
    scale = lax.rsqrt(jnp.mean(hidden * hidden, axis=-1, keepdims=True) + NORM_EPS)
    hat = hidden * scale
    two = own_ref[...] + came_ref[...]
    back = live_rows(back_ref[...].astype(f32), lengths_ref, pl.program_id(0) * hidden.shape[0])
    grad = back + norm_back(two, hat, scale, gain_ref[1:2])
    grad_ref[...] = grad
    low_ref[...] = grad.astype(bf)
    add_rows(gains_ref, two * hat, pl.program_id(0))


def turn_call(chain, lengths, hidden, back, own, came, gain, parts=4):
    rows, width = hidden.shape
    block = pl.BlockSpec((rows // parts, width), lambda i: (i, 0))
    return chain.call(
        turn_kernel, "turn", (lengths, hidden, back, own, came, gain), [smem()] + [block] * 4 + [fixed(NOTE, width)],
        [block, block, fixed(1, width)],
        [shaped((rows, width), f32), shaped((rows, width), bf), shaped((1, width), f32)],
        grid=(parts,),
    )


def output_kernel(hidden_ref, own_ref, came_ref, out_ref):
    out_ref[...] = (hidden_ref[...] + (own_ref[...] + came_ref[...])).astype(bf)


def output_call(chain, hidden, own, came, parts=4):
    rows, width = hidden.shape
    block = pl.BlockSpec((rows // parts, width), lambda i: (i, 0))
    return chain.call(
        output_kernel, "output", (hidden, own, came), [block] * 3, block, shaped((rows, width), bf), grid=(parts,),
    )


def last_kernel(spot_ref, grad_ref, source_ref, own_ref, came_ref, gain_ref, out_ref, gains_ref, one):
    half = own_ref.shape[1]
    core = spot_ref[3]
    one[:, pl.ds(pl.multiple_of(core * half, half), half)] = own_ref[...]
    one[:, pl.ds(pl.multiple_of((1 - core) * half, half), half)] = came_ref[...]
    source = source_ref[...].astype(f32)
    scale = lax.rsqrt(jnp.mean(source * source, axis=-1, keepdims=True) + NORM_EPS)
    hat = source * scale
    grad = one[...]
    out_ref[...] = grad_ref[...] + norm_back(grad, hat, scale, gain_ref[0:1])
    add_rows(gains_ref, grad * hat, pl.program_id(0))


def last_call(chain, spot, grad_hidden, source, own, came, gain, waits, parts=4):
    rows, width = source.shape
    block = pl.BlockSpec((rows // parts, width), lambda i: (i, 0))
    thin = pl.BlockSpec((rows // parts, width // 2), lambda i: (i, 0))
    return chain.call(
        last_kernel, "last", (spot, grad_hidden, source, own, came, gain),
        [smem(), block, block, thin, thin, fixed(NOTE, width)],
        [block, fixed(1, width)], [shaped((rows, width), f32), shaped((1, width), f32)],
        grid=(parts,),
        scratch_shapes=[pltpu.VMEM((rows // parts, width), f32)],
        waits=waits,
    )


def grad_kernel(slots, size, side, spot_ref, gains_ref, own_ref, other_ref, u_ref, *refs):
    outs, (turned, held, sem) = refs[:-3], refs[-3:]
    n, width = own_ref.shape
    w = held.shape[1]
    per = u_ref.shape[2] // w
    step = pl.program_id(0)

    @pl.when(step == 0)
    def _():
        turned[:, :n] = own_ref[...].T
        turned[:, n:] = other_ref[...].T

    gain = gains_ref[0:1, pl.ds(pl.multiple_of((spot_ref[3] * 2 + side) * w, w), w)]
    result = dot(turned[...], u_ref[0])
    for j in range(per):
        at = pl.multiple_of((step * per + j) * width, width)
        held[pl.ds(at, width), :] = (result[:, j * w : (j + 1) * w] * gain).astype(bf)

    @pl.when(step == pl.num_programs(0) - 1)
    def _():
        rows = held.shape[0] // len(slots)
        copies, at = [], 0
        for ref in outs:
            for b in range(ref.shape[0] // rows):
                start = pl.multiple_of(chip_of(spot_ref, slots[at], size) * rows, math.gcd(rows, 512))
                copies.append(
                    pltpu.make_async_copy(held.at[pl.ds(start, rows)], ref.at[pl.ds(b * rows, rows)], sem.at[at])
                )
                at += 1
        run_copies(copies)


def grad_call(chain, spot, gains, own, other, u, side, w, blocks, slots, size, per=9):
    rows, depth = u.shape[1:]
    n, width = own.shape
    count = depth // w
    each = count * width // len(slots)
    return chain.call(
        functools.partial(grad_kernel, slots, size, side), "mixer_grad", (spot, gains, own, other, u),
        [smem(), fixed(NOTE, width), fixed(n, width), fixed(n, width), pl.BlockSpec((1, rows, per * w), lambda i: (side, 0, i))],
        [anywhere() for _ in blocks], [shaped((b * each, w), bf) for b in blocks],
        grid=(count // per,),
        scratch_shapes=[
            pltpu.VMEM((width, rows), bf), pltpu.VMEM((count * width, w), bf), pltpu.SemaphoreType.DMA((len(slots),)),
        ],
    )


def back_kernel(count, plans, size, first, spot_ref, lengths_ref, came_ref, taps_ref, own_ref, other_ref, *refs):
    sides, refs = refs[: 2 * count], refs[2 * count :]
    before, refs = refs[: 2 if first else 0], refs[2 if first else 0 :]
    own_out, other_out, held, mask, low_low, low_high, high, v_low, v_high, ends, sem = refs
    n = mask.shape[1]
    q, h, d = n // 4, n // 2, own_ref.shape[1]
    per = taps_ref.shape[1]
    w = held.shape[1] // 2
    step = pl.program_id(0)

    @pl.when(step == 0)
    def _():
        copies = []
        for side in range(2):
            copies += collect(
                spot_ref, sides[side * count : (side + 1) * count], plans[side], size, held, sem.at[side],
                slice(side * w, (side + 1) * w),
            )
        for c in copies:
            c.start()
        find_ends(ends, lengths_ref, came_ref)
        for g in range(2):
            mask[g] = causal_mask(ends, g, n, True)
        low_low[...] = jnp.zeros_like(low_low)
        high[...] = jnp.zeros_like(high)
        for g, ref in enumerate((own_out, other_out)):
            ref[...] = before[g][...] if first else jnp.zeros_like(ref)
        for c in copies:
            c.wait()

    for j in range(per):
        at = pl.multiple_of(((step + first) * per + j) * d, d)
        weight = held[pl.ds(at, d), :]
        s = diagonals(taps_ref[0, j : j + 1, :], q)
        a = j * h
        for g, grad in enumerate((own_ref, other_ref)):
            v = dot(grad[...], weight).astype(bf)
            v_low[g, a : a + h] = v[:h]
            v_high[g, a : a + h] = v[h:]
            m = mask[g]
            low_low[g, 0:q, a : a + q] = s[:, :q] * m[0:q, 0:q]
            low_low[g, 0:q, a + q : a + h] = s[:, q : 2 * q] * m[0:q, q : 2 * q]
            low_low[g, q:h, a + q : a + h] = s[:, :q] * m[q:h, q:h]
            low_high[g, 0:q, a : a + h] = s[:, 2 * q : 4 * q] * m[0:q, h:]
            low_high[g, q:h, a : a + h] = s[:, q : 3 * q] * m[q:h, h:]
            high[g, 0:q, a : a + h] = s[:, 0 : 2 * q] * m[h : h + q, h:]
            high[g, q:h, a + q : a + h] = s[:, 0:q] * m[h + q :, h + q :]
    for g, out in enumerate((own_out, other_out)):
        out[:h] += dot(low_low[g], v_low[g]) + dot(low_high[g], v_high[g])
        out[h:] += dot(high[g], v_high[g])


def back_call(chain, spot, lengths, taps, own, other, sides, plans, size, first, steps, before=()):
    blocks, per, n = taps.shape
    rows, d = own.shape
    pieces = [p for side in sides for p in side]
    total = blocks * per * d
    width = 2 * sides[0][0].shape[-1]
    scratch = lambda *s: pltpu.VMEM(s, bf)
    return chain.call(
        functools.partial(back_kernel, len(sides[0]), plans, size, first), "spread_back",
        (spot, *lengths, taps, own, other, *pieces, *before),
        [smem()] * 3 + [pl.BlockSpec((1, per, n), lambda i: (i + first, 0, 0)), fixed(rows, d), fixed(rows, d)]
        + [anywhere() for _ in pieces] + [fixed(rows, width) for _ in before],
        [fixed(rows, width)] * 2, [shaped((rows, width), f32)] * 2,
        grid=(steps,),
        scratch_shapes=[
            scratch(total, width), scratch(2, n, n), scratch(2, n // 2, per * n // 2),
            scratch(2, n // 2, per * n // 2), scratch(2, n // 2, per * n // 2),
            scratch(2, per * n // 2, width), scratch(2, per * n // 2, width),
            pltpu.SMEM((2, 3), jnp.int32), pltpu.SemaphoreType.DMA((2, len(plans[0]))),
        ],
    )


def flat(v):
    return v.reshape(-1, v.shape[-1])


def ffn_kernel(count, outs, steps, slots, size, crossed, spot_ref, lengths_ref, came_ref, *refs):
    turned = spot_ref[3] if crossed else 0
    tokens, pieces, refs = refs[:4], refs[4 : 4 + count], refs[4 + count :]
    results, grads, (held, dealt, normed, back, sem) = refs[:4], refs[4 : 4 + outs], refs[4 + outs :]
    n = tokens[0].shape[0]
    chips, units, width = held.shape[0], held.shape[1] * 2 // 3, held.shape[2]
    own, half = chips // 2 // steps, units // 2
    step = pl.program_id(0)

    @pl.when(step == 0)
    def _():
        copies, at = [], 0
        for ref in pieces:
            for b in range(ref.shape[0]):
                chip = chip_of(spot_ref, slots[at], size)
                copies.append(
                    pltpu.make_async_copy(ref.at[b, pl.ds(0, units)], held.at[chip, pl.ds(0, units)], sem.at[0, at])
                )
                copies.append(
                    pltpu.make_async_copy(
                        ref.at[b, pl.ds(units, half)], held.at[chip ^ turned, pl.ds(units, half)], sem.at[1, at]
                    )
                )
                at += 1
        for c in copies:
            c.start()
        normed[:n], normed[n:] = tokens[0][...], tokens[1][...]
        back[:n] = live_rows(tokens[2][...].astype(f32), lengths_ref).astype(bf)
        back[n:] = live_rows(tokens[3][...].astype(f32), came_ref).astype(bf)
        for c in copies:
            c.wait()

    w_gate = flat(held[pl.ds(step * own, own), 0:units])
    w_up = flat(held[pl.ds(chips // 2 + step * own, own), 0:units])
    w_down = flat(held[pl.ds(step * 2 * own, 2 * own), units : units + half])
    gate, up = dot(normed[...], w_gate, NT), dot(normed[...], w_up, NT)
    grad_act = dot(back[...], w_down, NT)
    sigma = 1.0 / (1.0 + jnp.exp(-gate))
    swish = gate * sigma
    act = (swish * up).astype(bf)
    grad_gate = (grad_act * up * (sigma * (1.0 + gate * (1.0 - sigma)))).astype(bf)
    grad_up = (grad_act * swish).astype(bf)
    branch = dot(act, w_down)
    two = dot(grad_gate, w_gate) + dot(grad_up, w_up)
    values = (branch[:n], branch[n:], two[:n], two[n:])

    @pl.when(step == 0)
    def _():
        for ref, value in zip(results, values):
            ref[...] = value

    @pl.when(step > 0)
    def _():
        for ref, value in zip(results, values):
            ref[...] += value

    put = lambda v: v.astype(bf).reshape(own, units, width)
    dealt[pl.ds(step * own, own), 0:units] = put(dot(grad_gate, normed[...], TN))
    dealt[pl.ds(chips // 2 + step * own, own), 0:units] = put(dot(grad_up, normed[...], TN))
    grad_down = dot(act, back[...], TN).astype(bf)
    for b in range(2 * own):
        dealt[(step * 2 * own + b) ^ turned, units : units + half] = grad_down[b * half : (b + 1) * half]

    @pl.when(step == steps - 1)
    def _():
        copies, at = [], 0
        for ref in grads:
            for b in range(ref.shape[0]):
                copies.append(
                    pltpu.make_async_copy(dealt.at[chip_of(spot_ref, slots[at], size)], ref.at[b], sem.at[0, at])
                )
                at += 1
        run_copies(copies)


def ffn_call(chain, spot, lengths, tokens, pieces, blocks, slots, size, crossed, chunk=256):
    n, d = tokens[0].shape
    chips, rows = len(slots), pieces[0].shape[1]
    units = rows * 2 // 3
    steps = chips // 2 * units // chunk
    return chain.call(
        functools.partial(ffn_kernel, len(pieces), len(blocks), steps, slots, size, crossed), "ffn",
        (spot, *lengths, *tokens, *pieces),
        [smem()] * 3 + [fixed(n, d)] * 4 + [anywhere() for _ in pieces],
        [fixed(n, d)] * 4 + [anywhere() for _ in blocks],
        [shaped((n, d), f32)] * 4 + [shaped((b, rows, d), bf) for b in blocks],
        grid=(steps,),
        scratch_shapes=[
            pltpu.VMEM((chips, rows, d), bf), pltpu.VMEM((chips, rows, d), bf),
            pltpu.VMEM((2 * n, d), bf), pltpu.VMEM((2 * n, d), bf), pltpu.SemaphoreType.DMA((2, chips)),
        ],
    )


def normed_kernel(spot_ref, own_ref, other_ref, own_out, other_out, full):
    half = own_out.shape[1]
    cols = pl.ds(pl.multiple_of(spot_ref[3] * half, half), half)
    for ref, out in ((own_ref, own_out), (other_ref, other_out)):
        source = ref[...].astype(f32)
        scale = lax.rsqrt(jnp.mean(source * source, axis=-1, keepdims=True) + NORM_EPS)
        full[...] = (source * scale).astype(bf)
        out[...] = full[:, cols]


def normed_call(chain, spot, own, other, parts=2):
    rows, width = own.shape
    block = pl.BlockSpec((rows // parts, width), lambda i: (i, 0))
    thin = pl.BlockSpec((rows // parts, width // 2), lambda i: (i, 0))
    return chain.call(
        normed_kernel, "normed", (spot, own, other), [smem(), block, block],
        [thin] * 2, [shaped((rows, width // 2), bf)] * 2,
        grid=(parts,), scratch_shapes=[pltpu.VMEM((rows // parts, width), bf)],
    )


def live_rows(values, lengths_ref, first=0):
    total = lengths_ref[0, 0] + lengths_ref[0, 1] + lengths_ref[0, 2]
    place = lax.broadcasted_iota(jnp.int32, (values.shape[0], 1), 0) + first
    return jnp.where(place < total, values, jnp.zeros((), values.dtype))


def pack_kernel(
    spot_ref, mixer_ref, gate_up_ref, down_ref, gains_ref, mixer_mine, mixer_theirs, gate_mine, gate_theirs, down_low, note
):
    half, units, core = mixer_mine.shape[1], gate_mine.shape[0], spot_ref[3]
    for ref, cols, rows, c in ((mixer_mine, half, units, core), (mixer_theirs, half, units, 1 - core)):
        ref[...] = mixer_ref[:, pl.ds(pl.multiple_of(c * half, half), half)].astype(bf)
    for ref, c in ((gate_mine, core), (gate_theirs, 1 - core)):
        ref[:units] = gate_up_ref[pl.ds(pl.multiple_of(c * units, units), units), :].astype(bf)
    count, own = gains_ref.shape
    note[...] = jnp.zeros_like(note)
    note[:count, :own] = gains_ref[...].astype(bf)
    gate_theirs[units:] = jnp.zeros((note.shape[0], gate_theirs.shape[1]), bf)
    gate_theirs[units:, : note.shape[1]] = note[...]
    down_low[...] = down_ref[...].astype(bf)


def pack_call(chain, spot, mixer, gate_up, down, gains):
    (rows, width), (units, _), (half, _) = mixer.shape, gate_up.shape, down.shape
    shapes = [(rows, width // 2)] * 2 + [(units // 2, width), (units // 2 + NOTE, width), (half, width), (NOTE, 128)]
    return chain.call(
        pack_kernel, "pack", (spot, mixer, gate_up, down, gains),
        [smem(), fixed(rows, width), fixed(units, width), fixed(half, width), fixed(*gains.shape)],
        [fixed(*s) for s in shapes], [shaped(s, bf) for s in shapes], grid=(1,),
    )


def block_kernel(own_gains, spot_ref, mine_ref, came_ref, note_ref, gate_ref, all_ref, copies_ref):
    rows, w = mine_ref.shape[0], all_ref.shape[1]
    mine = note_ref[...].astype(f32)
    came = gate_ref[gate_ref.shape[0] - NOTE :, :w].astype(f32)
    turned = lambda v: pltpu.roll(v, own_gains, 1)
    note = jnp.where(spot_ref[3] == 0, mine + turned(came), came + turned(mine)).astype(bf)
    at = 0
    for side in range(2):
        cols = slice(side * w, (side + 1) * w)
        all_ref[at : at + rows] = mine_ref[:, cols]
        all_ref[at + rows : at + 2 * rows] = came_ref[:, cols]
        all_ref[at + 2 * rows : at + 2 * rows + NOTE] = note
        at += 2 * rows + NOTE
    count = 2 * rows + NOTE
    for c in range(copies_ref.shape[0] // count):
        copies_ref[c * count : (c + 1) * count] = all_ref[:count]


def block_call(chain, spot, mine, came, note, gate_came, own_gains, copies, waits):
    rows, width = mine.shape
    w = width // 2
    each = 2 * rows + NOTE
    return chain.call(
        functools.partial(block_kernel, own_gains), "block", (spot, mine, came, note, gate_came),
        [smem()] + [fixed(*v.shape) for v in (mine, came, note, gate_came)],
        [fixed(2 * each, w), fixed(copies * each, w)], [shaped((2 * each, w), bf), shaped((copies * each, w), bf)],
        grid=(1,), waits=waits,
    )


def stack_kernel(count, moves, spot_ref, *refs):
    for i, a, rows, o, b in moves:
        if not isinstance(a, int):
            stride, distance, first = a
            a = pl.multiple_of((spot_ref[2] ^ distance) * stride + first, NOTE)
        refs[count + o][b : b + rows] = refs[i][pl.ds(a, rows)]


def stack_call(chain, spot, arrays, rows, moves, waits=()):
    like = {o: arrays[i] for i, _, _, o, _ in moves}
    shapes = [(r,) + like[o].shape[1:] for o, r in enumerate(rows)]
    return chain.call(
        functools.partial(stack_kernel, len(arrays), moves), "stack", (spot, *arrays),
        [smem()] + [fixed(*v.shape) for v in arrays],
        [fixed(*s) for s in shapes], [shaped(s, like[o].dtype) for o, s in enumerate(shapes)], grid=(1,), waits=waits,
    )


def corner_kernel(cut, extra, x_ref, y_ref, to_x_ref, to_y_ref):
    rows = x_ref.shape[0]
    to_x_ref[:cut] = y_ref[:cut]
    if extra:
        to_x_ref[cut:] = y_ref[rows - extra :]
    to_y_ref[...] = x_ref[cut : rows - extra]


def corner_call(chain, from_x, from_y, extra):
    total, width = from_x.shape
    cut = (total - extra) // 2
    shapes = [(cut + extra, width), (cut, width)]
    return chain.call(
        functools.partial(corner_kernel, cut, extra), "corner", (from_x, from_y), [fixed(total, width)] * 2,
        [fixed(*s) for s in shapes], [shaped(s, bf) for s in shapes], grid=(1,),
    )


def near_kernel(to_x_ref, to_y_ref, by_x_ref, by_y_ref, new_x_ref, new_y_ref):
    new_x_ref[...] = (to_x_ref[...].astype(f32) + by_y_ref[...].astype(f32)).astype(bf)
    new_y_ref[...] = (to_y_ref[...].astype(f32) + by_x_ref[...].astype(f32)).astype(bf)


def near_call(chain, to_x, to_y, by_x, by_y, parts=2, **options):
    rows, width = by_x.shape
    block = (rows // parts, width)
    low, high = pl.BlockSpec(block, lambda i: (i, 0)), pl.BlockSpec(block, lambda i: (i + parts, 0))
    return chain.call(
        near_kernel, "near", (to_x, to_y, by_x, by_y), [high, low, low, low], [high, low],
        [shaped(to_x.shape, bf), shaped(to_y.shape, bf)], grid=(parts,), input_output_aliases={0: 0, 1: 1}, **options,
    )


def line_kernel(count, *refs):
    parts, refs = refs[:count], refs[count:]
    total = parts[0][...].astype(f32)
    for ref in parts[1:]:
        total = total + ref[...].astype(f32)
    if len(refs) == 1:
        refs[0][...] = total.astype(bf)
        return
    for s, ref in enumerate(refs):

        @pl.when(pl.program_id(0) == s)
        def _():
            ref[...] = total.astype(ref.dtype)


def line_call(chain, parts, size, apart, **options):
    quarters = 4 if len(parts) == 1 else 1
    rows, width = parts[0].shape[0] // quarters // size, parts[0].shape[1]
    block = pl.BlockSpec((rows, width), lambda i: (i, 0))
    ins = [pl.BlockSpec((rows, width), lambda i, q=q: (i + q * size, 0)) for q in range(quarters)]
    ins = ins if quarters > 1 else [block] * len(parts)
    parts = parts * quarters
    if apart:
        specs = [fixed(rows, width)] * size
        shapes = [shaped((rows, width), f32)] + [shaped((rows, width), bf)] * (size - 1)
    else:
        specs, shapes = [block], [shaped((size * rows, width), bf)]
    return chain.call(
        functools.partial(line_kernel, len(parts)), "line", parts, ins, specs, shapes, grid=(size,), **options
    )


def finish_kernel(cuts, count, note, spot_ref, first_ref, *refs):
    came, more, outs, squares_ref, total = (
        refs[:count], refs[count : -len(cuts) - 2], refs[-len(cuts) - 2 : -2], refs[-2], refs[-1]
    )
    rows = total.shape[0]
    result = first_ref[:rows].astype(f32)
    for b in range(1, first_ref.shape[0] // rows):
        result = result + first_ref[b * rows : (b + 1) * rows].astype(f32)
    for ref in came:
        result = result + ref[...].astype(f32)
    total[...] = result
    squares = jnp.sum(result * result, axis=0, keepdims=True)
    if note:
        whole = jnp.sum(squares, axis=1, keepdims=True)
        for ref in more[:-1]:
            whole = whole + jnp.sum(ref[...], axis=1, keepdims=True)
        gains = more[-1][...]
        whole = whole + jnp.sum(jnp.sum(gains * gains, axis=1, keepdims=True), axis=0, keepdims=True)
        squares = jnp.broadcast_to(whole, squares_ref.shape)
    squares_ref[...] = squares
    for ref, start in zip(outs, cuts):
        rows = ref.shape[0]
        if not isinstance(start, int):
            start = pl.multiple_of((spot_ref[3] ^ start[0]) * rows, rows & -rows)
        ref[...] = total[pl.ds(start, rows), :]


def finish_call(chain, spot, first, came, blocks, cuts, note=0, more=()):
    rows, width = first.shape[0] // blocks, first.shape[1]
    shapes = [(r, width) for _, r in cuts] + [(note, 128) if note else (1, width)]
    return chain.call(
        functools.partial(finish_kernel, [c for c, _ in cuts], len(came), note), "finish", (spot, first, *came, *more),
        [smem(), fixed(*first.shape)] + [fixed(rows, width)] * len(came) + [fixed(*v.shape) for v in more],
        [fixed(*s) for s in shapes], [shaped(s, f32) for s in shapes],
        grid=(1,), scratch_shapes=[pltpu.VMEM((rows, width), f32)],
    )


def adam_step(weight, grad, first, second, rate, decay):
    first_new = BETA_ONE * first + (1.0 - BETA_ONE) * grad
    second_new = BETA_TWO * second + (1.0 - BETA_TWO) * grad * grad
    corr_one = 1.0 - BETA_ONE**STEP
    corr_two = 1.0 - BETA_TWO**STEP
    update = first_new / corr_one / (jnp.sqrt(second_new / corr_two) + ADAM_EPS)
    return (weight - rate * (update + decay * weight), first_new, second_new)


def adam_kernel(spot_ref, note_ref, *refs):
    ins, outs, wide, tall = refs[:21], refs[21:35], refs[35], refs[36]
    mixer, gate_up, down, gains, parts = ins[:4], ins[4:7], ins[7:10], ins[10:13], ins[13:]
    mixer_out, gate_up_out, down_out, gains_out, norm_out = outs[:4], outs[4:7], outs[7:10], outs[10:13], outs[13]
    core, quarter = spot_ref[3], parts[0].shape[1]
    norm = jnp.sqrt(jnp.sum(note_ref[...], axis=0, keepdims=True)[:, :1])
    factor = CLIP_LIMIT / jnp.maximum(norm, CLIP_LIMIT)

    for s in range(2):
        mine = pl.multiple_of(core * 2 * quarter, quarter) + s * quarter
        came = pl.multiple_of((1 - core) * 2 * quarter, quarter) + s * quarter
        wide[:, pl.ds(pl.multiple_of(mine, quarter), quarter)] = parts[s][...]
        wide[:, pl.ds(pl.multiple_of(came, quarter), quarter)] = parts[2 + s][...]
    old, first, second, average = (r[...] for r in mixer)
    new, first, second = adam_step(old, wide[...] * factor, first, second, RATE_MATRIX, DECAY_MATRIX)
    average = AVERAGE_KEEP * average + (1.0 - AVERAGE_KEEP) * new
    for ref, value in zip(mixer_out, (new, first, second, average)):
        ref[...] = value

    @pl.when(pl.program_id(0) == 0)
    def _():
        half = parts[4].shape[0]
        tall[pl.ds(pl.multiple_of(core * half, half), half), :] = parts[4][...]
        tall[pl.ds(pl.multiple_of((1 - core) * half, half), half), :] = parts[5][...]
        for olds, news, grad, rate, decay in (
            (gate_up, gate_up_out, tall[...], RATE_MATRIX, DECAY_MATRIX),
            (down, down_out, parts[6][...], RATE_MATRIX, DECAY_MATRIX),
            (gains, gains_out, parts[7][...], RATE_GAIN, 0.0),
        ):
            old, first, second = (r[...] for r in olds)
            scale = factor if rate == RATE_MATRIX else factor[:, :1]
            for ref, value in zip(news, adam_step(old, grad * scale, first, second, rate, decay)):
                ref[...] = value
        norm_out[...] = norm


def adam_call(chain, spot, note, mixer, gate_up, down, gains, parts, blocks=6):
    rows, width = mixer[0].shape
    step = rows // blocks
    block = pl.BlockSpec((step, width), lambda i: (i, 0))
    piece = pl.BlockSpec((step, parts[0].shape[1]), lambda i: (i, 0))
    whole = lambda v: fixed(*v.shape)
    others = [*gate_up, *down, *gains]
    shapes = [v.shape for v in (*mixer, *others)] + [(1, 1)]
    return chain.call(
        adam_kernel, "adam", (spot, note, *mixer, *others, *parts),
        [smem(), whole(note)] + [block] * 4 + [whole(v) for v in others] + [piece] * 4
        + [whole(v) for v in parts[4:]],
        [block] * 4 + [whole(v) for v in others] + [fixed(1, 1)], [shaped(s, f32) for s in shapes],
        grid=(blocks,),
        scratch_shapes=[pltpu.VMEM((step, width), f32), pltpu.VMEM(gate_up[0].shape, f32)],
    )


def flip(v, axis, bits=1):
    size = lax.axis_size(axis)
    return lax.ppermute(v, axis, [(i, i ^ bits) for i in range(size)])


def swap(v):
    return flip(v, "core")


def join(mine, other, core, axis=0):
    return jnp.where(
        core == 0,
        jnp.concatenate([mine, other], axis=axis),
        jnp.concatenate([other, mine], axis=axis),
    )


def part(v, index, axis=0):
    size = v.shape[axis] // 2
    return lax.dynamic_slice_in_dim(v, index * size, size, axis)


def low(v):
    return v.astype(bf)


def wide(v):
    return v.astype(f32)


class Whole:
    crossed = False
    mixer_slots = ((0,), (0,))
    mixer_blocks = (1,)

    def __init__(self, spot, groups):
        self.spot, self.core = spot, spot[3]
        self.size = lax.axis_size("z")
        self.chips = lax.axis_size("d0") * lax.axis_size("d1") * self.size
        self.ffn_slots, self.ffn_blocks = tuple(range(groups)), (groups,)

    def gather(self, chain, mixer, gate_up, down, gains, waits):
        def trade(v, axis):
            return join(part(v, self.core, axis), swap(part(v, 1 - self.core, axis)), self.core)

        everything = lambda v: lax.all_gather(v, CHIPS, axis=0, tiled=True)
        mixer_block = trade(low(mixer), 1)
        w, groups = mixer_block.shape[1] // 2, len(self.ffn_slots)
        sides = []
        for s in range(2):
            whole = everything(mixer_block[:, s * w : (s + 1) * w])
            sides.append(([whole], ((0, 0, whole.shape[0], 0, None),), ()))
        ffn = [everything(v).reshape(groups, -1, v.shape[1]) for v in (trade(low(gate_up), 0), low(down))]
        ffn = [jnp.concatenate(ffn, axis=1)]
        gains = lax.all_gather(wide(low(gains)), EVERY, axis=1, tiled=True)
        yield jnp.pad(gains, ((0, NOTE - 2), (0, 0)))
        while True:
            yield sides, ffn

    def scatter(self, chain, parts, cuts, groups=1, apart=False):
        grads = parts[0].reshape(groups, -1, parts[0].shape[-1])
        rows = grads.shape[1] * 2 // 3
        if groups > 1:
            shards = [grads[:, :rows], grads[:, rows:]]
        else:
            shards = [grads]
        shards = [wide(lax.psum_scatter(flat(v), CHIPS, scatter_dimension=0, tiled=True)) for v in shards]
        outs = [part(shards[0], self.core), part(shards[0], 1 - self.core)] + shards[1:]
        squares = sum(jnp.sum(v * v, axis=0, keepdims=True) for v in shards)
        if groups == 1:
            yield
            yield ()
        through = yield
        yield (), through
        yield
        yield outs + [squares]

    def scatter_gains(self, grad):
        return lax.psum_scatter(grad, EVERY, scatter_dimension=1, tiled=True)

    def total(self, v):
        return lax.psum(v, EVERY)


class Cube(Whole):
    crossed = True
    near = ((0, 0), (0, 1), (1, 0), (1, 1))

    def __init__(self, spot, groups):
        super().__init__(spot, groups)
        slots = lambda fixed_z: tuple((y, x, s, fixed_z) for y, x in self.near for s in range(self.size))
        self.mixer_slots = slots(True), slots(False)
        self.mixer_blocks = (self.size,) * 3 + (self.size // 2,) * 2

    def lines(self, block):
        return [flip(block, "z", s) for s in range(1, self.size)]

    def gather(self, chain, mixer, gate_up, down, gains, waits):
        spot = self.spot
        mixer_mine, mixer_theirs, gate_mine, gate_theirs, down_low, note = pack_call(
            chain, spot, mixer, gate_up, down, gains
        )
        gate_came = swap(gate_theirs)
        size = self.size
        own, block = block_call(
            chain, spot, mixer_mine, swap(mixer_theirs), note, gate_came, gains.shape[1], size, waits
        )
        line = self.along_z(block)
        own_x, own_y = flip(own, "d1"), flip(own, "d0")
        yield None
        rows = own.shape[0] // 2 - NOTE
        half = rows // 2
        sides = []

        def spread_out(line):
            return line, flip(line, "d1"), flip(line, "d0")

        def turn_corner(from_x, from_y, extra=0):
            to_x, to_y = corner_call(chain, from_x, from_y, extra)
            return flip(to_x, "d1"), flip(to_y, "d0")

        def plan(side):
            found = [(p, side * (rows + NOTE) + h * half, half, near + (0, False), h) for p, near in enumerate(self.near[:3]) for h in range(2)]
            found += [(3, h * half, half, (1, 1, 0, False), h) for h in range(2)]
            last = (size - 1) * 2
            for at in range(last):
                s, h = at // 2 + 1, at % 2
                found += [(4 + p, at * half, half, near + (s, False), h) for p, near in enumerate(self.near[:3])]
                found.append((7 + (at >= last // 2), at % (last // 2) * half, half, (1, 1, s, False), h))
            return tuple(found)

        corner = turn_corner(own_x, own_y)
        yield
        chain.pause(*corner)
        others, line_rows = range(1, size), (size - 1) * rows
        moves = [(0, (rows + NOTE, s, 0), rows, 0, (s - 1) * rows) for s in others]
        moves += [(0, (rows + NOTE, s, rows), NOTE, 0, line_rows + (s - 1) * NOTE) for s in others]
        moves += [(1, rows + NOTE, rows, 1, s * rows) for s in range(size)]
        line, block = stack_call(
            chain, spot, (line, own), (line_rows + (size - 1) * NOTE, size * rows), tuple(moves)
        )
        first = spread_out(line)
        line = self.along_z(block)
        yield
        first_corner = turn_corner(*first[1:], (size - 1) * NOTE)
        chain.pause(*first_corner)
        notes = [(p, rows, near + (0, False)) for p, near in enumerate(self.near)]
        for s in others:
            notes += [(4 + p, line_rows + (s - 1) * NOTE, near + (s, False)) for p, near in enumerate(self.near[:3])]
            notes.append((7, line_rows // 2 + (s - 1) * NOTE, (1, 1, s, False)))
        sides.append(([own, own_x, own_y, corner[0], *first, *first_corner], plan(0), tuple(notes)))
        units, count = gate_mine.shape[0], down_low.shape[0]
        ffn_rows = 2 * units + count
        moves = [(0, (rows, s, 0), rows, 0, (s - 1) * rows) for s in others]
        for s in range(size):
            at = s * ffn_rows
            moves += [(1, 0, units, 1, at), (2, 0, units, 1, at + units), (3, 0, count, 1, at + 2 * units)]
        line, block = stack_call(
            chain, spot, (line, gate_mine, gate_came, down_low), (line_rows, size * ffn_rows), tuple(moves)
        )
        second = spread_out(line)
        line = self.along_z(block)
        yield sides, None
        second_corner = turn_corner(*second[1:])
        chain.pause(*second_corner)
        sides.append(([own, own_x, own_y, corner[1], *second, *second_corner], plan(1), ()))
        count = size * ffn_rows
        (block,) = stack_call(
            chain, spot, (line,), (4 * count,), tuple((0, 0, count, 0, c * count) for c in range(4))
        )
        ffn = lax.all_to_all(block, ("d0", "d1"), 0, 0, tiled=True)
        yield sides, [ffn.reshape(-1, ffn_rows, ffn.shape[-1])]

    def along_z(self, v):
        return lax.all_to_all(v, "z", 0, 0, tiled=True)

    def scatter(self, chain, parts, cuts, groups=1, apart=False):
        if groups > 1:
            came = (lax.all_to_all(flat(parts[0]), ("d0", "d1"), 0, 0, tiled=True),)
        else:
            own, to_x, to_y, far_low, far_high = (flat(v) for v in parts)
            by_x, by_y = flip(far_low, "d1"), flip(far_high, "d0")
            yield
            to_x, to_y = yield near_call(chain, to_x, to_y, by_x, by_y)
            came = own, flip(to_x, "d1"), flip(to_y, "d0")
        through = yield
        outs = line_call(chain, came, self.size, apart, through=through)
        count = self.size if apart else 1
        first, *rest = yield outs[:count], outs[count:]
        if apart:
            came = [flip(v, "z", s + 1) for s, v in enumerate(rest)]
        else:
            first, came = self.along_z(first), ()
        more = yield
        yield finish_call(
            chain, self.spot, first, came, 1 if apart else self.size, cuts, 2 * self.chips if more else 0, more or ()
        )

    def everyone(self, rows):
        count, length = rows.shape
        rows = jnp.pad(rows, ((0, 0), (0, -length % 128)))
        return lax.all_to_all(rows, EVERY, 0, 0, tiled=True)[:, :length]

    def scatter_gains(self, grad):
        devices = 2 * self.chips
        rows = grad.reshape(2, devices, -1).transpose(1, 0, 2).reshape(devices, -1)
        return jnp.sum(self.everyone(rows), axis=0).reshape(2, -1)


def body(
    inputs, lengths, filters, cotangent, mixer_weight, gate_up_weight, down_weight, norm_gains,
    mixer_first, gate_up_first, down_first, gains_first,
    mixer_second, gate_up_second, down_second, gains_second, mixer_average,
):
    slots, width = inputs.shape
    size = lax.axis_size("z")
    groups = 2 * FF // 256
    cube = lax.axis_size("d0") == 2 and lax.axis_size("d1") == 2 and size == 4
    spot = jnp.stack([lax.axis_index(a) for a in EVERY]).astype(jnp.int32)
    core = spot[3]
    links = (Cube if cube else Whole)(spot, groups)
    units = gate_up_weight.shape[0]
    chain = Chain()

    sums = lengths, swap(lengths)
    source_other, cotangent_other = swap(inputs), swap(cotangent)
    taps = jnp.concatenate([wide(filters), jnp.eye(AR_ORDER, slots, dtype=f32)])
    taps_turned = jnp.roll(taps[:, ::-1], 1 - slots // 4, axis=1)
    taps, taps_turned = (v.reshape(-1, 3, slots) for v in (taps, taps_turned))

    weights = links.gather(
        chain, mixer_weight, gate_up_weight, down_weight, norm_gains, (sums[1], source_other, cotangent_other)
    )
    gains = next(weights)
    tokens = normed_call(chain, spot, inputs, source_other)
    blocks = taps.shape[0]
    cuts, spread = (0, blocks * 5 // 9, blocks * 7 // 9, blocks), None
    for at in range(3):
        spread = spread_call(chain, sums, taps_turned, *tokens, cuts[at], cuts[at + 1] - cuts[at], spread)
        sides = next(weights)
    sides, _ = sides
    quarter = sides[0][0][0].shape[1]
    *mixed, gains = (*mix_call(chain, spot, spread, 0, *sides[0], gains, size, width), gains)[:3]
    sides, ffn = next(weights)
    mixed_own, mixed_other = mix_call(chain, spot, spread, 1, *sides[1], gains, size, width, mixed)

    hidden, normed_two = hidden_call(chain, inputs, mixed_own, swap(mixed_other), gains)
    tokens = (normed_two, swap(normed_two), cotangent, cotangent_other)
    branch_own, branch_other, two_own, two_other, *grad_ffn = ffn_call(
        chain, spot, sums, tokens, ffn, links.ffn_blocks, links.ffn_slots, size, links.crossed
    )
    ffn_sum = links.scatter(chain, grad_ffn, ((0, units // 2), (units // 2, units // 2), (units, units // 2)), groups)
    next(ffn_sum)
    grad_hidden, grad_low, gains_two = turn_call(
        chain, lengths, hidden, cotangent, two_own, swap(two_other), gains
    )
    grad_other = swap(grad_low)
    output = output_call(chain, hidden, branch_own, swap(branch_other))
    rows = mixer_weight.shape[0]
    cuts = (((0,), rows), ((1,), rows))
    grads_of = lambda s: grad_call(
        chain, spot, gains, grad_low, grad_other, spread, s, quarter, links.mixer_blocks, links.mixer_slots[s], size
    )
    first_sum = links.scatter(chain, grads_of(0), cuts)
    next(first_sum)
    second_sum = links.scatter(chain, grads_of(1), cuts, apart=True)
    next(second_sum)
    early = blocks // 2
    backward = lambda *how: back_call(
        chain, spot, sums, taps, grad_low, grad_other, [s[0] for s in sides], [s[1] for s in sides], size, *how
    )
    one = backward(0, early)
    outs, held = ffn_sum.send(next(first_sum))
    first_sum.send(held)
    ffn_sum.send(outs)
    second_sum.send(next(second_sum))
    one_own, one_other = backward(early, blocks - early, one)
    gate_up_mine, gate_up_theirs, shard_down, *squares = ffn_sum.send(())
    gate_up_came = swap(gate_up_theirs)
    outs, held = first_sum.send(())
    first_sum.send(outs)
    input_grad, gains_one = last_call(
        chain, spot, grad_hidden, inputs, one_own, swap(one_other), gains, (gate_up_came,)
    )
    first_mine, first_theirs, square = first_sum.send(())
    first_came = swap(first_theirs)
    squares.append(square)
    outs, held = second_sum.send((gains_one, gains_two))
    second_sum.send(outs)
    shard_gains = links.scatter_gains(jnp.concatenate(held))
    chain.pause(first_came)
    second_mine, second_theirs, note = second_sum.send((*squares, shard_gains))
    second_came = swap(second_theirs)
    mixer = mixer_weight, mixer_first, mixer_second, mixer_average
    gate_up, down = (gate_up_weight, gate_up_first, gate_up_second), (down_weight, down_first, down_second)
    gain = norm_gains, gains_first, gains_second
    if cube:
        (
            mixer_new, mixer_first_new, mixer_second_new, mixer_average_new, gate_up_new, gate_up_first_new,
            gate_up_second_new, down_new, down_first_new, down_second_new, gains_new, gains_first_new, gains_second_new,
            grad_norm,
        ) = adam_call(
            chain, spot, links.everyone(note), mixer, gate_up, down, gain,
            (first_mine, second_mine, first_came, second_came, gate_up_mine, gate_up_came, shard_down, shard_gains),
        )
        grad_norm = grad_norm[0, 0]
    else:
        squares = sum(jnp.sum(v) for v in (*squares, note)) + jnp.sum(shard_gains * shard_gains)
        grad_norm = jnp.sqrt(links.total(squares))
        factor = CLIP_LIMIT / jnp.maximum(grad_norm, CLIP_LIMIT)
        shard_mixer = join(
            jnp.concatenate([first_mine, second_mine], axis=1), jnp.concatenate([first_came, second_came], axis=1), core, 1
        )
        shard_gate_up = join(gate_up_mine, gate_up_came, core)
        step = lambda old, grad: adam_step(old[0], grad * factor, old[1], old[2], RATE_MATRIX, DECAY_MATRIX)
        mixer_new, mixer_first_new, mixer_second_new = step(mixer, shard_mixer)
        gate_up_new, gate_up_first_new, gate_up_second_new = step(gate_up, shard_gate_up)
        down_new, down_first_new, down_second_new = step(down, shard_down)
        gains_new, gains_first_new, gains_second_new = adam_step(
            gain[0], shard_gains * factor, gain[1], gain[2], RATE_GAIN, 0.0
        )
        mixer_average_new = AVERAGE_KEEP * mixer_average + (1.0 - AVERAGE_KEEP) * mixer_new
    return (
        output, input_grad, grad_norm, mixer_new, gate_up_new, down_new, gains_new,
        mixer_first_new, gate_up_first_new, down_first_new, gains_first_new,
        mixer_second_new, gate_up_second_new, down_second_new, gains_second_new, mixer_average_new,
    )


def solution(mesh):
    outer, inner = mesh.shape["dp"], mesh.shape["fsdp"]
    side = math.isqrt(outer)
    if side * side != outer:
        side = 1
    split = jax.sharding.Mesh(
        np.asarray(mesh.devices).reshape(side, outer // side, inner // 2, 2), EVERY
    )
    rows, columns, whole = P(EVERY, None), P(None, EVERY), P()
    return jax.shard_map(
        body,
        mesh=split,
        in_specs=(
            rows, rows, whole, rows, rows, rows, rows, columns,
            rows, rows, rows, columns, rows, rows, rows, columns, rows,
        ),
        out_specs=(
            rows, rows, whole, rows, rows, rows, columns, rows, rows, rows, columns,
            rows, rows, rows, columns, rows,
        ),
        check_vma=False,
    )
```

```python
import functools
import math

import jax
import jax.numpy as jnp
import numpy as np
from jax import lax
from jax.experimental import pallas as pl
from jax.experimental.pallas import tpu as pltpu
from jax.sharding import PartitionSpec as P

bf = jnp.bfloat16
f32 = jnp.float32
FILTERS = 24
AR_ORDER = 3
FF = 2048
STEP = 10
NORM_EPS = 1e-05
CLIP_LIMIT = 1.0
BETA_ONE = 0.9
BETA_TWO = 0.95
ADAM_EPS = 1e-08
RATE_MATRIX = 0.03
RATE_GAIN = 0.5
DECAY_MATRIX = 0.1
AVERAGE_KEEP = 0.9
CHIPS = ("d0", "d1", "z")
EVERY = CHIPS + ("core",)


NT = (((1,), (1,)), ((), ()))
NN = (((1,), (0,)), ((), ()))
TN = (((0,), (0,)), ((), ()))


def dot(a, b, dims=NN):
    return lax.dot_general(a, b, dims, preferred_element_type=f32)


class Chain:
    def __init__(self):
        self.token = None

    def call(self, kernel, name, args, in_specs, out_specs, out_shape, waits=(), through=(), **options):
        count, single = len(args), not isinstance(out_shape, (list, tuple)) and not through
        if single:
            out_specs, out_shape = [out_specs], [out_shape]
        made = len(out_shape)
        aliases = options.pop("input_output_aliases", {})
        aliases = {**aliases, **{count + i: made + i for i in range(len(through))}}
        last = tuple(through) + tuple(waits) + (() if self.token is None else (self.token,))

        def whole(*refs):
            first = count + len(last)
            kernel(*refs[:count], *refs[first : first + made], *refs[first + made + len(through) + 1 :])

        *outs, self.token = pl.pallas_call(
            whole,
            name=name,
            in_specs=list(in_specs) + [anywhere() for _ in last],
            out_specs=list(out_specs) + [anywhere() for _ in through] + [anywhere()],
            out_shape=list(out_shape) + [shaped(v.shape, v.dtype) for v in through] + [shaped((8, 128), f32)],
            input_output_aliases=aliases,
            compiler_params=pltpu.CompilerParams(vmem_limit_bytes=64 << 20),
            cost_estimate=pl.CostEstimate(flops=1, bytes_accessed=1, transcendentals=0),
            **options,
        )(*args, *last)
        return outs[0] if single else outs

    def pause(self, waits=(), through=()):
        return self.call(lambda: None, "pause", (), [], [], [], waits=waits, through=through)


def smem():
    return pl.BlockSpec(memory_space=pltpu.SMEM)


def anywhere():
    return pl.BlockSpec(memory_space=pl.ANY)


def fixed(*shape):
    return pl.BlockSpec(shape, lambda i: (0,) * len(shape))


NOTE = 16


def shaped(shape, dtype):
    return jax.ShapeDtypeStruct(tuple(shape), dtype)


def segment_of(place, ends_ref, group):
    return sum((place >= ends_ref[group, j]).astype(jnp.int32) for j in range(3))


def causal_mask(ends_ref, group, n, transposed):
    down = lax.broadcasted_iota(jnp.int32, (n, 1), 0)
    along = lax.broadcasted_iota(jnp.int32, (1, n), 1)
    one, two = segment_of(down, ends_ref, group), segment_of(along, ends_ref, group)
    order = (down <= along) if transposed else (down >= along)
    return ((one == two) & (one < 3) & order).astype(f32).astype(bf)


def diagonals(row, count):
    wide = jnp.broadcast_to(row, (count, row.shape[-1]))
    return pltpu.roll(wide, 0, 1, stride=1, stride_axis=0).astype(bf)


def spread_kernel(lengths_ref, came_ref, taps_ref, own_ref, other_ref, *refs):
    u_ref, mask, table, ends = refs[-4:]
    n = mask.shape[1]
    q, h, w = n // 4, n // 2, own_ref.shape[1] // 2
    per = taps_ref.shape[1]

    @pl.when(pl.program_id(0) == 0)
    def _():
        find_ends(ends, lengths_ref, came_ref)
        for g in range(2):
            mask[g] = causal_mask(ends, g, n, False)
        table[...] = jnp.zeros_like(table)

    for j in range(per):
        strip = diagonals(taps_ref[0, j : j + 1, :], q)
        for g, tokens in enumerate((own_ref, other_ref)):
            for i in range(4):
                rows, cols = slice(i * q, (i + 1) * q), slice(0, (i + 1) * q)
                table[g, rows, cols] = strip[:, (3 - i) * q :] * mask[g, rows, cols]
            upper = dot(table[g, :h, :h], tokens[:h]).astype(bf)
            lower = dot(table[g, h:, :], tokens[...]).astype(bf)
            for side in range(2):
                cols = slice(side * w, (side + 1) * w)
                u_ref[side, g * n : g * n + h, j * w : (j + 1) * w] = upper[:, cols]
                u_ref[side, g * n + h : (g + 1) * n, j * w : (j + 1) * w] = lower[:, cols]


def find_ends(ends, lengths_ref, came_ref):
    for g, ref in enumerate((lengths_ref, came_ref)):
        total = ref[0, 0]
        ends[g, 0] = total
        for j in range(1, 3):
            total = total + ref[0, j]
            ends[g, j] = total


def spread_call(chain, lengths, taps, own, other, first, steps, into=None):
    blocks, per, n = taps.shape
    w = own.shape[1] // 2
    args = [*lengths, taps, own, other]
    specs = [smem()] * 2 + [pl.BlockSpec((1, per, n), lambda i: (i + first, 0, 0)), fixed(n, 2 * w), fixed(n, 2 * w)]
    options = {}
    if into is not None:
        options = dict(input_output_aliases={len(args): 0})
        args, specs = args + [into], specs + [anywhere()]
    return chain.call(
        spread_kernel, "spread", args, specs,
        pl.BlockSpec((2, 2 * n, per * w), lambda i: (0, 0, i + first)),
        shaped((2, 2 * n, blocks * per * w), bf),
        grid=(steps,),
        scratch_shapes=[pltpu.VMEM((2, n, n), bf), pltpu.VMEM((2, n, n), bf), pltpu.SMEM((2, 3), jnp.int32)],
        **options,
    )


def run_copies(copies):
    for c in copies:
        c.start()
    for c in copies:
        c.wait()


def chip_of(spot_ref, slot, size):
    if isinstance(slot, int):
        return slot
    dy, dx, dz, fixed_z = slot
    return ((spot_ref[0] ^ dy) * 2 + (spot_ref[1] ^ dx)) * size + (dz if fixed_z else spot_ref[2] ^ dz)


def collect(spot_ref, pieces, plan, size, held, sem, columns):
    copies = []
    for at, (piece, row, rows, slot, half) in enumerate(plan):
        place = chip_of(spot_ref, slot, size)
        if half is not None:
            place = place * 2 + (spot_ref[3] ^ half)
        start = pl.multiple_of(place * rows, math.gcd(rows, 512))
        copies.append(
            pltpu.make_async_copy(pieces[piece].at[pl.ds(row, rows)], held.at[pl.ds(start, rows), columns], sem.at[at])
        )
    return copies


def mix_kernel(count, plan, notes, size, width, side, spot_ref, u_ref, *refs):
    pieces, refs = refs[:count], refs[count:]
    first = side == 0
    before, refs = refs[: 0 if first else 2], refs[0 if first else 2 :]
    if notes:
        own_ref, other_ref, gains_ref, held, wide, sem, tiles = refs
    else:
        gains_ref, own_ref, other_ref, held, wide, sem = refs
    w = held.shape[1]
    filters = held.shape[0] // width
    step = pl.program_id(0)

    @pl.when(step == 0)
    def _():
        copies = collect(spot_ref, pieces, plan, size, held, sem, slice(0, w))
        for at, (piece, row, slot) in enumerate(notes):
            copies.append(
                pltpu.make_async_copy(
                    pieces[piece].at[pl.ds(row, NOTE)], tiles.at[chip_of(spot_ref, slot, size)], sem.at[len(plan) + at]
                )
            )
        run_copies(copies)
        if notes:
            lanes = width // len(notes)
            for b in range(width // 128):
                block = jnp.zeros((NOTE, 128), f32)
                for j in range(128 // lanes):
                    tile = tiles[b * (128 // lanes) + j].astype(f32)
                    block = block + (pltpu.roll(tile, j * lanes, 1) if j else tile)
                gains_ref[:, b * 128 : (b + 1) * 128] = block
        gain = gains_ref[0:1, pl.ds(pl.multiple_of((spot_ref[3] * 2 + side) * w, w), w)]
        for k in range(filters):
            wide[:, k * w : (k + 1) * w] = (held[k * width : (k + 1) * width].astype(f32) * gain).astype(bf)

    result = dot(u_ref[0], wide[...], NT)
    for g, out in enumerate((own_ref, other_ref)):

        @pl.when(step == g)
        def _():
            out[...] = (result if first else result + before[g][...]).astype(out.dtype)


def mix_call(chain, spot, u, side, pieces, plan, notes, gains, size, width, before=()):
    rows, depth = u.shape[1:]
    w = pieces[0].shape[-1]
    total = depth // w * width
    step = rows // 2
    out = fixed(step, width)
    note = fixed(NOTE, width)
    given = () if notes else (gains,)
    return chain.call(
        functools.partial(mix_kernel, len(pieces), plan, notes, size, width, side), "mix",
        (spot, u, *pieces, *before, *given),
        [smem(), pl.BlockSpec((1, step, depth), lambda i: (side, i, 0))] + [anywhere() for _ in pieces]
        + [out for _ in before] + [note for _ in given],
        [out, out] + [note for _ in range(1 - len(given))],
        [shaped((step, width), f32), shaped((step, width), bf if before else f32)]
        + [shaped((NOTE, width), f32) for _ in range(1 - len(given))],
        grid=(2,),
        scratch_shapes=[
            pltpu.VMEM((total, w), bf), pltpu.VMEM((width, depth), bf), pltpu.SemaphoreType.DMA((len(plan) + len(notes),)),
        ] + [pltpu.VMEM((len(notes), NOTE, 128), bf)] * (1 - len(given)),
    )


def hidden_kernel(source_ref, own_ref, came_ref, gain_ref, hidden_ref, *normed_refs):
    hidden = source_ref[...].astype(f32) + (own_ref[...] + came_ref[...].astype(f32))
    scale = lax.rsqrt(jnp.mean(hidden * hidden, axis=-1, keepdims=True) + NORM_EPS)
    hidden_ref[...] = hidden
    normed = (hidden * scale * gain_ref[1:2]).astype(bf)
    width = normed_refs[0].shape[1]
    for i, ref in enumerate(normed_refs):
        ref[...] = normed[:, i * width : (i + 1) * width]


def hidden_call(chain, source, own, came, gain, parts=4):
    rows, width = source.shape
    block = pl.BlockSpec((rows // parts, width), lambda i: (i, 0))
    thin = pl.BlockSpec((rows // parts, width // 2), lambda i: (i, 0))
    return chain.call(
        hidden_kernel, "hidden", (source, own, came, gain), [block, block, block, fixed(NOTE, width)],
        [block, thin, thin], [shaped((rows, width), f32)] + [shaped((rows, width // 2), bf)] * 2,
        grid=(parts,),
    )


def norm_back(grad, hat, scale, gain):
    weighted = grad * gain
    return scale * (weighted - hat * jnp.mean(weighted * hat, axis=-1, keepdims=True))


def add_rows(ref, values, step):
    total = jnp.sum(values, axis=0, keepdims=True)

    @pl.when(step == 0)
    def _():
        ref[...] = total

    @pl.when(step > 0)
    def _():
        ref[...] += total


def turn_kernel(lengths_ref, hidden_ref, back_ref, own_ref, came_ref, gain_ref, grad_ref, low_ref, gains_ref):
    hidden = hidden_ref[...]
    scale = lax.rsqrt(jnp.mean(hidden * hidden, axis=-1, keepdims=True) + NORM_EPS)
    hat = hidden * scale
    two = own_ref[...] + came_ref[...]
    back = live_rows(back_ref[...].astype(f32), lengths_ref, pl.program_id(0) * hidden.shape[0])
    grad = back + norm_back(two, hat, scale, gain_ref[1:2])
    grad_ref[...] = grad
    low_ref[...] = grad.astype(bf)
    add_rows(gains_ref, two * hat, pl.program_id(0))


def turn_call(chain, lengths, hidden, back, own, came, gain, parts=4):
    rows, width = hidden.shape
    block = pl.BlockSpec((rows // parts, width), lambda i: (i, 0))
    return chain.call(
        turn_kernel, "turn", (lengths, hidden, back, own, came, gain), [smem()] + [block] * 4 + [fixed(NOTE, width)],
        [block, block, fixed(1, width)],
        [shaped((rows, width), f32), shaped((rows, width), bf), shaped((1, width), f32)],
        grid=(parts,),
    )


def output_kernel(hidden_ref, own_ref, came_ref, out_ref):
    out_ref[...] = (hidden_ref[...] + (own_ref[...] + came_ref[...])).astype(bf)


def output_call(chain, hidden, own, came, parts=4):
    rows, width = hidden.shape
    block = pl.BlockSpec((rows // parts, width), lambda i: (i, 0))
    return chain.call(
        output_kernel, "output", (hidden, own, came), [block] * 3, block, shaped((rows, width), bf), grid=(parts,),
    )


def last_kernel(spot_ref, grad_ref, source_ref, own_ref, came_ref, gain_ref, out_ref, gains_ref, one):
    half = own_ref.shape[1]
    core = spot_ref[3]
    one[:, pl.ds(pl.multiple_of(core * half, half), half)] = own_ref[...]
    one[:, pl.ds(pl.multiple_of((1 - core) * half, half), half)] = came_ref[...]
    source = source_ref[...].astype(f32)
    scale = lax.rsqrt(jnp.mean(source * source, axis=-1, keepdims=True) + NORM_EPS)
    hat = source * scale
    grad = one[...]
    out_ref[...] = grad_ref[...] + norm_back(grad, hat, scale, gain_ref[0:1])
    add_rows(gains_ref, grad * hat, pl.program_id(0))


def last_call(chain, spot, grad_hidden, source, own, came, gain, waits, parts=4):
    rows, width = source.shape
    block = pl.BlockSpec((rows // parts, width), lambda i: (i, 0))
    thin = pl.BlockSpec((rows // parts, width // 2), lambda i: (i, 0))
    return chain.call(
        last_kernel, "last", (spot, grad_hidden, source, own, came, gain),
        [smem(), block, block, thin, thin, fixed(NOTE, width)],
        [block, fixed(1, width)], [shaped((rows, width), f32), shaped((1, width), f32)],
        grid=(parts,),
        scratch_shapes=[pltpu.VMEM((rows // parts, width), f32)],
        waits=waits,
    )


def grad_kernel(slots, size, side, spot_ref, gains_ref, own_ref, other_ref, u_ref, *refs):
    outs, (turned, held, sem) = refs[:-3], refs[-3:]
    n, width = own_ref.shape
    w = held.shape[1]
    per = u_ref.shape[2] // w
    step = pl.program_id(0)

    @pl.when(step == 0)
    def _():
        turned[:, :n] = own_ref[...].T
        turned[:, n:] = other_ref[...].T

    gain = gains_ref[0:1, pl.ds(pl.multiple_of((spot_ref[3] * 2 + side) * w, w), w)]
    result = dot(turned[...], u_ref[0])
    for j in range(per):
        at = pl.multiple_of((step * per + j) * width, width)
        held[pl.ds(at, width), :] = (result[:, j * w : (j + 1) * w] * gain).astype(bf)

    @pl.when(step == pl.num_programs(0) - 1)
    def _():
        rows = held.shape[0] // len(slots)
        copies, at = [], 0
        for ref in outs:
            for b in range(ref.shape[0] // rows):
                start = pl.multiple_of(chip_of(spot_ref, slots[at], size) * rows, math.gcd(rows, 512))
                copies.append(
                    pltpu.make_async_copy(held.at[pl.ds(start, rows)], ref.at[pl.ds(b * rows, rows)], sem.at[at])
                )
                at += 1
        run_copies(copies)


def grad_call(chain, spot, gains, own, other, u, side, w, blocks, slots, size, per=9):
    rows, depth = u.shape[1:]
    n, width = own.shape
    count = depth // w
    each = count * width // len(slots)
    return chain.call(
        functools.partial(grad_kernel, slots, size, side), "mixer_grad", (spot, gains, own, other, u),
        [smem(), fixed(NOTE, width), fixed(n, width), fixed(n, width), pl.BlockSpec((1, rows, per * w), lambda i: (side, 0, i))],
        [anywhere() for _ in blocks], [shaped((b * each, w), bf) for b in blocks],
        grid=(count // per,),
        scratch_shapes=[
            pltpu.VMEM((width, rows), bf), pltpu.VMEM((count * width, w), bf), pltpu.SemaphoreType.DMA((len(slots),)),
        ],
    )


def back_kernel(count, plans, size, first, spot_ref, lengths_ref, came_ref, taps_ref, own_ref, other_ref, *refs):
    sides, refs = refs[: 2 * count], refs[2 * count :]
    before, refs = refs[: 2 if first else 0], refs[2 if first else 0 :]
    own_out, other_out, held, mask, low_low, low_high, high, v_low, v_high, ends, sem = refs
    n = mask.shape[1]
    q, h, d = n // 4, n // 2, own_ref.shape[1]
    per = taps_ref.shape[1]
    w = held.shape[1] // 2
    step = pl.program_id(0)

    @pl.when(step == 0)
    def _():
        copies = []
        for side in range(2):
            copies += collect(
                spot_ref, sides[side * count : (side + 1) * count], plans[side], size, held, sem.at[side],
                slice(side * w, (side + 1) * w),
            )
        for c in copies:
            c.start()
        find_ends(ends, lengths_ref, came_ref)
        for g in range(2):
            mask[g] = causal_mask(ends, g, n, True)
        low_low[...] = jnp.zeros_like(low_low)
        high[...] = jnp.zeros_like(high)
        for g, ref in enumerate((own_out, other_out)):
            ref[...] = before[g][...] if first else jnp.zeros_like(ref)
        for c in copies:
            c.wait()

    for j in range(per):
        at = pl.multiple_of(((step + first) * per + j) * d, d)
        weight = held[pl.ds(at, d), :]
        s = diagonals(taps_ref[0, j : j + 1, :], q)
        a = j * h
        for g, grad in enumerate((own_ref, other_ref)):
            v = dot(grad[...], weight).astype(bf)
            v_low[g, a : a + h] = v[:h]
            v_high[g, a : a + h] = v[h:]
            m = mask[g]
            low_low[g, 0:q, a : a + q] = s[:, :q] * m[0:q, 0:q]
            low_low[g, 0:q, a + q : a + h] = s[:, q : 2 * q] * m[0:q, q : 2 * q]
            low_low[g, q:h, a + q : a + h] = s[:, :q] * m[q:h, q:h]
            low_high[g, 0:q, a : a + h] = s[:, 2 * q : 4 * q] * m[0:q, h:]
            low_high[g, q:h, a : a + h] = s[:, q : 3 * q] * m[q:h, h:]
            high[g, 0:q, a : a + h] = s[:, 0 : 2 * q] * m[h : h + q, h:]
            high[g, q:h, a + q : a + h] = s[:, 0:q] * m[h + q :, h + q :]
    for g, out in enumerate((own_out, other_out)):
        out[:h] += dot(low_low[g], v_low[g]) + dot(low_high[g], v_high[g])
        out[h:] += dot(high[g], v_high[g])


def back_call(chain, spot, lengths, taps, own, other, sides, plans, size, first, steps, before=()):
    blocks, per, n = taps.shape
    rows, d = own.shape
    pieces = [p for side in sides for p in side]
    total = blocks * per * d
    width = 2 * sides[0][0].shape[-1]
    scratch = lambda *s: pltpu.VMEM(s, bf)
    return chain.call(
        functools.partial(back_kernel, len(sides[0]), plans, size, first), "spread_back",
        (spot, *lengths, taps, own, other, *pieces, *before),
        [smem()] * 3 + [pl.BlockSpec((1, per, n), lambda i: (i + first, 0, 0)), fixed(rows, d), fixed(rows, d)]
        + [anywhere() for _ in pieces] + [fixed(rows, width) for _ in before],
        [fixed(rows, width)] * 2, [shaped((rows, width), f32)] * 2,
        grid=(steps,),
        scratch_shapes=[
            scratch(total, width), scratch(2, n, n), scratch(2, n // 2, per * n // 2),
            scratch(2, n // 2, per * n // 2), scratch(2, n // 2, per * n // 2),
            scratch(2, per * n // 2, width), scratch(2, per * n // 2, width),
            pltpu.SMEM((2, 3), jnp.int32), pltpu.SemaphoreType.DMA((2, len(plans[0]))),
        ],
    )


def flat(v):
    return v.reshape(-1, v.shape[-1])


def ffn_kernel(count, outs, steps, slots, out_slots, size, crossed, spot_ref, lengths_ref, came_ref, *refs):
    turned = spot_ref[3] if crossed else 0
    tokens, pieces, refs = refs[:6], refs[6 : 6 + count], refs[6 + count :]
    results, grads, (held, dealt, normed, back, sem) = refs[:4], refs[4 : 4 + outs], refs[4 + outs :]
    n = tokens[0].shape[0]
    chips, units, width = held.shape[0], held.shape[1] * 2 // 3, held.shape[2]
    own, half = chips // 2 // steps, units // 2
    step = pl.program_id(0)

    @pl.when(step == 0)
    def _():
        copies, at = [], 0
        for ref in pieces:
            for b in range(ref.shape[0]):
                chip = chip_of(spot_ref, slots[at], size)
                copies.append(
                    pltpu.make_async_copy(ref.at[b, pl.ds(0, units)], held.at[chip, pl.ds(0, units)], sem.at[0, at])
                )
                copies.append(
                    pltpu.make_async_copy(
                        ref.at[b, pl.ds(units, half)], held.at[chip ^ turned, pl.ds(units, half)], sem.at[1, at]
                    )
                )
                at += 1
        for c in copies:
            c.start()
        half_width = tokens[0].shape[1]
        for i in range(2):
            cols = slice(i * half_width, (i + 1) * half_width)
            normed[:n, cols], normed[n:, cols] = tokens[i][...], tokens[2 + i][...]
        back[:n] = live_rows(tokens[4][...].astype(f32), lengths_ref).astype(bf)
        back[n:] = live_rows(tokens[5][...].astype(f32), came_ref).astype(bf)
        for c in copies:
            c.wait()

    w_gate = flat(held[pl.ds(step * own, own), 0:units])
    w_up = flat(held[pl.ds(chips // 2 + step * own, own), 0:units])
    w_down = flat(held[pl.ds(step * 2 * own, 2 * own), units : units + half])
    gate, up = dot(normed[...], w_gate, NT), dot(normed[...], w_up, NT)
    grad_act = dot(back[...], w_down, NT)
    sigma = 1.0 / (1.0 + jnp.exp(-gate))
    swish = gate * sigma
    act = (swish * up).astype(bf)
    grad_gate = (grad_act * up * (sigma * (1.0 + gate * (1.0 - sigma)))).astype(bf)
    grad_up = (grad_act * swish).astype(bf)
    branch = dot(act, w_down)
    two = dot(grad_gate, w_gate) + dot(grad_up, w_up)
    values = (branch[:n], branch[n:], two[:n], two[n:])

    @pl.when(step == 0)
    def _():
        for ref, value in zip(results, values):
            ref[...] = value

    @pl.when(step > 0)
    def _():
        for ref, value in zip(results, values):
            ref[...] += value

    put = lambda v: v.astype(bf).reshape(own, units, width)
    dealt[pl.ds(step * own, own), 0:units] = put(dot(grad_gate, normed[...], TN))
    dealt[pl.ds(chips // 2 + step * own, own), 0:units] = put(dot(grad_up, normed[...], TN))
    grad_down = dot(act, back[...], TN).astype(bf)
    for b in range(2 * own):
        dealt[(step * 2 * own + b) ^ turned, units : units + half] = grad_down[b * half : (b + 1) * half]

    @pl.when(step == steps - 1)
    def _():
        copies, at = [], 0
        for ref in grads:
            for b in range(ref.shape[0]):
                copies.append(
                    pltpu.make_async_copy(dealt.at[chip_of(spot_ref, out_slots[at], size)], ref.at[b], sem.at[0, at])
                )
                at += 1
        run_copies(copies)


def ffn_call(chain, spot, lengths, tokens, pieces, blocks, slots, out_slots, size, crossed, chunk=256):
    n, d = tokens[-1].shape
    chips, rows = len(slots), pieces[0].shape[1]
    units = rows * 2 // 3
    steps = chips // 2 * units // chunk
    return chain.call(
        functools.partial(ffn_kernel, len(pieces), len(blocks), steps, slots, out_slots, size, crossed), "ffn",
        (spot, *lengths, *tokens, *pieces),
        [smem()] * 3 + [fixed(*v.shape) for v in tokens] + [anywhere() for _ in pieces],
        [fixed(n, d)] * 4 + [anywhere() for _ in blocks],
        [shaped((n, d), f32)] * 4 + [shaped((b, rows, d), bf) for b in blocks],
        grid=(steps,),
        scratch_shapes=[
            pltpu.VMEM((chips, rows, d), bf), pltpu.VMEM((chips, rows, d), bf),
            pltpu.VMEM((2 * n, d), bf), pltpu.VMEM((2 * n, d), bf), pltpu.SemaphoreType.DMA((2, chips)),
        ],
    )


def normed_kernel(spot_ref, own_ref, other_ref, own_out, other_out, full):
    half = own_out.shape[1]
    cols = pl.ds(pl.multiple_of(spot_ref[3] * half, half), half)
    for ref, out in ((own_ref, own_out), (other_ref, other_out)):
        source = ref[...].astype(f32)
        scale = lax.rsqrt(jnp.mean(source * source, axis=-1, keepdims=True) + NORM_EPS)
        full[...] = (source * scale).astype(bf)
        out[...] = full[:, cols]


def normed_call(chain, spot, own, other, parts=2):
    rows, width = own.shape
    block = pl.BlockSpec((rows // parts, width), lambda i: (i, 0))
    thin = pl.BlockSpec((rows // parts, width // 2), lambda i: (i, 0))
    return chain.call(
        normed_kernel, "normed", (spot, own, other), [smem(), block, block],
        [thin] * 2, [shaped((rows, width // 2), bf)] * 2,
        grid=(parts,), scratch_shapes=[pltpu.VMEM((rows // parts, width), bf)],
    )


def live_rows(values, lengths_ref, first=0):
    total = lengths_ref[0, 0] + lengths_ref[0, 1] + lengths_ref[0, 2]
    place = lax.broadcasted_iota(jnp.int32, (values.shape[0], 1), 0) + first
    return jnp.where(place < total, values, jnp.zeros((), values.dtype))


def pack_kernel(
    spot_ref, mixer_ref, gate_up_ref, down_ref, gains_ref, mixer_mine, mixer_theirs, gate_mine, gate_theirs, down_low, note
):
    half, units, core = mixer_mine.shape[1], gate_mine.shape[0], spot_ref[3]
    for ref, cols, rows, c in ((mixer_mine, half, units, core), (mixer_theirs, half, units, 1 - core)):
        ref[...] = mixer_ref[:, pl.ds(pl.multiple_of(c * half, half), half)].astype(bf)
    for ref, c in ((gate_mine, core), (gate_theirs, 1 - core)):
        ref[:units] = gate_up_ref[pl.ds(pl.multiple_of(c * units, units), units), :].astype(bf)
    count, own = gains_ref.shape
    note[...] = jnp.zeros_like(note)
    note[:count, :own] = gains_ref[...].astype(bf)
    gate_theirs[units:] = jnp.zeros((note.shape[0], gate_theirs.shape[1]), bf)
    gate_theirs[units:, : note.shape[1]] = note[...]
    down_low[...] = down_ref[...].astype(bf)


def pack_call(chain, spot, mixer, gate_up, down, gains):
    (rows, width), (units, _), (half, _) = mixer.shape, gate_up.shape, down.shape
    shapes = [(rows, width // 2)] * 2 + [(units // 2, width), (units // 2 + NOTE, width), (half, width), (NOTE, 128)]
    return chain.call(
        pack_kernel, "pack", (spot, mixer, gate_up, down, gains),
        [smem(), fixed(rows, width), fixed(units, width), fixed(half, width), fixed(*gains.shape)],
        [fixed(*s) for s in shapes], [shaped(s, bf) for s in shapes], grid=(1,),
    )


def block_kernel(own_gains, spot_ref, mine_ref, came_ref, note_ref, gate_ref, all_ref, copies_ref):
    rows, w = mine_ref.shape[0], all_ref.shape[1]
    mine = note_ref[...].astype(f32)
    came = gate_ref[gate_ref.shape[0] - NOTE :, :w].astype(f32)
    turned = lambda v: pltpu.roll(v, own_gains, 1)
    note = jnp.where(spot_ref[3] == 0, mine + turned(came), came + turned(mine)).astype(bf)
    at = 0
    for side in range(2):
        cols = slice(side * w, (side + 1) * w)
        all_ref[at : at + rows] = mine_ref[:, cols]
        all_ref[at + rows : at + 2 * rows] = came_ref[:, cols]
        all_ref[at + 2 * rows : at + 2 * rows + NOTE] = note
        at += 2 * rows + NOTE
    count = 2 * rows + NOTE
    for c in range(copies_ref.shape[0] // count):
        copies_ref[c * count : (c + 1) * count] = all_ref[:count]


def block_call(chain, spot, mine, came, note, gate_came, own_gains, copies, waits):
    rows, width = mine.shape
    w = width // 2
    each = 2 * rows + NOTE
    return chain.call(
        functools.partial(block_kernel, own_gains), "block", (spot, mine, came, note, gate_came),
        [smem()] + [fixed(*v.shape) for v in (mine, came, note, gate_came)],
        [fixed(2 * each, w), fixed(copies * each, w)], [shaped((2 * each, w), bf), shaped((copies * each, w), bf)],
        grid=(1,), waits=waits,
    )


def stack_kernel(count, moves, spot_ref, *refs):
    for i, a, rows, o, b in moves:
        if not isinstance(a, int):
            stride, distance, first = a
            a = pl.multiple_of((spot_ref[2] ^ distance) * stride + first, NOTE)
        refs[count + o][b : b + rows] = refs[i][pl.ds(a, rows)]


def stack_call(chain, spot, arrays, rows, moves, waits=()):
    like = {o: arrays[i] for i, _, _, o, _ in moves}
    shapes = [(r,) + like[o].shape[1:] for o, r in enumerate(rows)]
    return chain.call(
        functools.partial(stack_kernel, len(arrays), moves), "stack", (spot, *arrays),
        [smem()] + [fixed(*v.shape) for v in arrays],
        [fixed(*s) for s in shapes], [shaped(s, like[o].dtype) for o, s in enumerate(shapes)], grid=(1,), waits=waits,
    )


def corner_kernel(cut, extra, x_ref, y_ref, to_x_ref, to_y_ref):
    rows = x_ref.shape[0]
    to_x_ref[:cut] = y_ref[:cut]
    if extra:
        to_x_ref[cut:] = y_ref[rows - extra :]
    to_y_ref[...] = x_ref[cut : rows - extra]


def corner_call(chain, from_x, from_y, extra):
    total, width = from_x.shape
    cut = (total - extra) // 2
    shapes = [(cut + extra, width), (cut, width)]
    return chain.call(
        functools.partial(corner_kernel, cut, extra), "corner", (from_x, from_y), [fixed(total, width)] * 2,
        [fixed(*s) for s in shapes], [shaped(s, bf) for s in shapes], grid=(1,),
    )


def near_kernel(to_x_ref, to_y_ref, by_x_ref, by_y_ref, new_x_ref, new_y_ref):
    new_x_ref[...] = (to_x_ref[...].astype(f32) + by_y_ref[...].astype(f32)).astype(bf)
    new_y_ref[...] = (to_y_ref[...].astype(f32) + by_x_ref[...].astype(f32)).astype(bf)


def near_call(chain, to_x, to_y, by_x, by_y, parts=2, **options):
    rows, width = by_x.shape
    block = (rows // parts, width)
    low, high = pl.BlockSpec(block, lambda i: (i, 0)), pl.BlockSpec(block, lambda i: (i + parts, 0))
    return chain.call(
        near_kernel, "near", (to_x, to_y, by_x, by_y), [high, low, low, low], [high, low],
        [shaped(to_x.shape, bf), shaped(to_y.shape, bf)], grid=(parts,), input_output_aliases={0: 0, 1: 1}, **options,
    )


def line_kernel(count, *refs):
    parts, refs = refs[:count], refs[count:]
    total = parts[0][...].astype(f32)
    for ref in parts[1:]:
        total = total + ref[...].astype(f32)
    if len(refs) == 1:
        refs[0][...] = total.astype(bf)
        return
    for s, ref in enumerate(refs):

        @pl.when(pl.program_id(0) == s)
        def _():
            ref[...] = total.astype(ref.dtype)


def line_call(chain, parts, size, apart, **options):
    quarters = 4 if len(parts) == 1 else 1
    rows, width = parts[0].shape[0] // quarters // size, parts[0].shape[1]
    block = pl.BlockSpec((rows, width), lambda i: (i, 0))
    ins = [pl.BlockSpec((rows, width), lambda i, q=q: (i + q * size, 0)) for q in range(quarters)]
    ins = ins if quarters > 1 else [block] * len(parts)
    parts = parts * quarters
    if apart:
        specs = [fixed(rows, width)] * size
        shapes = [shaped((rows, width), f32)] + [shaped((rows, width), bf)] * (size - 1)
    else:
        specs, shapes = [block], [shaped((size * rows, width), bf)]
    return chain.call(
        functools.partial(line_kernel, len(parts)), "line", parts, ins, specs, shapes, grid=(size,), **options
    )


def finish_kernel(cuts, count, note, spot_ref, first_ref, *refs):
    came, more, outs, squares_ref, total = (
        refs[:count], refs[count : -len(cuts) - 2], refs[-len(cuts) - 2 : -2], refs[-2], refs[-1]
    )
    rows = total.shape[0]
    result = first_ref[:rows].astype(f32)
    for b in range(1, first_ref.shape[0] // rows):
        result = result + first_ref[b * rows : (b + 1) * rows].astype(f32)
    for ref in came:
        result = result + ref[...].astype(f32)
    total[...] = result
    squares = jnp.sum(result * result, axis=0, keepdims=True)
    if note:
        whole = jnp.sum(squares, axis=1, keepdims=True)
        for ref in more[:-1]:
            whole = whole + jnp.sum(ref[...], axis=1, keepdims=True)
        gains = jnp.sum(more[-1][...], axis=0, keepdims=True)
        squares = jnp.broadcast_to(whole + jnp.sum(gains * gains, axis=1, keepdims=True), squares_ref.shape)
    squares_ref[...] = squares
    for ref, start in zip(outs, cuts):
        rows = ref.shape[0]
        if not isinstance(start, int):
            start = pl.multiple_of((spot_ref[3] ^ start[0]) * rows, rows & -rows)
        ref[...] = total[pl.ds(start, rows), :]


def finish_call(chain, spot, first, came, blocks, cuts, note=0, more=(), waits=()):
    rows, width = first.shape[0] // blocks, first.shape[1]
    shapes = [(r, width) for _, r in cuts] + [(note, 128) if note else (1, width)]
    return chain.call(
        functools.partial(finish_kernel, [c for c, _ in cuts], len(came), note), "finish", (spot, first, *came, *more),
        [smem(), fixed(*first.shape)] + [fixed(rows, width)] * len(came) + [fixed(*v.shape) for v in more],
        [fixed(*s) for s in shapes], [shaped(s, f32) for s in shapes],
        grid=(1,), scratch_shapes=[pltpu.VMEM((rows, width), f32)], waits=waits,
    )


def adam_step(weight, grad, first, second, rate, decay):
    first_new = BETA_ONE * first + (1.0 - BETA_ONE) * grad
    second_new = BETA_TWO * second + (1.0 - BETA_TWO) * grad * grad
    corr_one = 1.0 - BETA_ONE**STEP
    corr_two = 1.0 - BETA_TWO**STEP
    update = first_new / corr_one / (jnp.sqrt(second_new / corr_two) + ADAM_EPS)
    return (weight - rate * (update + decay * weight), first_new, second_new)


def adam_kernel(spot_ref, note_ref, *refs):
    ins, outs, wide, tall = refs[:21], refs[21:35], refs[35], refs[36]
    mixer, gate_up, down, gains, parts = ins[:4], ins[4:7], ins[7:10], ins[10:13], ins[13:]
    mixer_out, gate_up_out, down_out, gains_out, norm_out = outs[:4], outs[4:7], outs[7:10], outs[10:13], outs[13]
    core, quarter = spot_ref[3], parts[0].shape[1]
    norm = jnp.sqrt(jnp.sum(note_ref[...], axis=0, keepdims=True)[:, :1])
    factor = CLIP_LIMIT / jnp.maximum(norm, CLIP_LIMIT)

    for s in range(2):
        mine = pl.multiple_of(core * 2 * quarter, quarter) + s * quarter
        came = pl.multiple_of((1 - core) * 2 * quarter, quarter) + s * quarter
        wide[:, pl.ds(pl.multiple_of(mine, quarter), quarter)] = parts[s][...]
        wide[:, pl.ds(pl.multiple_of(came, quarter), quarter)] = parts[2 + s][...]
    old, first, second, average = (r[...] for r in mixer)
    new, first, second = adam_step(old, wide[...] * factor, first, second, RATE_MATRIX, DECAY_MATRIX)
    average = AVERAGE_KEEP * average + (1.0 - AVERAGE_KEEP) * new
    for ref, value in zip(mixer_out, (new, first, second, average)):
        ref[...] = value

    @pl.when(pl.program_id(0) == 0)
    def _():
        half = parts[4].shape[0]
        tall[pl.ds(pl.multiple_of(core * half, half), half), :] = parts[4][...]
        tall[pl.ds(pl.multiple_of((1 - core) * half, half), half), :] = parts[5][...]
        own = gains[0].shape[1]
        sums = jnp.sum(parts[7][...], axis=0, keepdims=True)
        gain_grad = jnp.concatenate([sums[:, :own], sums[:, own : 2 * own]])
        for olds, news, grad, rate, decay in (
            (gate_up, gate_up_out, tall[...], RATE_MATRIX, DECAY_MATRIX),
            (down, down_out, parts[6][...], RATE_MATRIX, DECAY_MATRIX),
            (gains, gains_out, gain_grad, RATE_GAIN, 0.0),
        ):
            old, first, second = (r[...] for r in olds)
            scale = factor if rate == RATE_MATRIX else factor[:, :1]
            for ref, value in zip(news, adam_step(old, grad * scale, first, second, rate, decay)):
                ref[...] = value
        norm_out[...] = norm


def adam_call(chain, spot, note, mixer, gate_up, down, gains, parts, blocks=6):
    rows, width = mixer[0].shape
    step = rows // blocks
    block = pl.BlockSpec((step, width), lambda i: (i, 0))
    piece = pl.BlockSpec((step, parts[0].shape[1]), lambda i: (i, 0))
    whole = lambda v: fixed(*v.shape)
    others = [*gate_up, *down, *gains]
    shapes = [v.shape for v in (*mixer, *others)] + [(1, 1)]
    return chain.call(
        adam_kernel, "adam", (spot, note, *mixer, *others, *parts),
        [smem(), whole(note)] + [block] * 4 + [whole(v) for v in others] + [piece] * 4
        + [whole(v) for v in parts[4:]],
        [block] * 4 + [whole(v) for v in others] + [fixed(1, 1)], [shaped(s, f32) for s in shapes],
        grid=(blocks,),
        scratch_shapes=[pltpu.VMEM((step, width), f32), pltpu.VMEM(gate_up[0].shape, f32)],
    )


def flip(v, axis, bits=1):
    size = lax.axis_size(axis)
    return lax.ppermute(v, axis, [(i, i ^ bits) for i in range(size)])


def swap(v):
    return flip(v, "core")


def join(mine, other, core, axis=0):
    return jnp.where(
        core == 0,
        jnp.concatenate([mine, other], axis=axis),
        jnp.concatenate([other, mine], axis=axis),
    )


def part(v, index, axis=0):
    size = v.shape[axis] // 2
    return lax.dynamic_slice_in_dim(v, index * size, size, axis)


def low(v):
    return v.astype(bf)


def wide(v):
    return v.astype(f32)


class Whole:
    crossed = False
    mixer_slots = ((0,), (0,))
    mixer_blocks = (1,)

    def __init__(self, spot, groups):
        self.spot, self.core = spot, spot[3]
        self.size = lax.axis_size("z")
        self.chips = lax.axis_size("d0") * lax.axis_size("d1") * self.size
        self.ffn_in = self.ffn_out = tuple(range(groups))
        self.ffn_blocks = (groups,)

    def gather(self, chain, mixer, gate_up, down, gains, waits):
        def trade(v, axis):
            return join(part(v, self.core, axis), swap(part(v, 1 - self.core, axis)), self.core)

        everything = lambda v: lax.all_gather(v, CHIPS, axis=0, tiled=True)
        mixer_block = trade(low(mixer), 1)
        w, groups = mixer_block.shape[1] // 2, len(self.ffn_in)
        sides = []
        for s in range(2):
            whole = everything(mixer_block[:, s * w : (s + 1) * w])
            sides.append(([whole], ((0, 0, whole.shape[0], 0, None),), ()))
        ffn = [everything(v).reshape(groups, -1, v.shape[1]) for v in (trade(low(gate_up), 0), low(down))]
        ffn = [jnp.concatenate(ffn, axis=1)]
        gains = lax.all_gather(wide(low(gains)), EVERY, axis=1, tiled=True)
        yield jnp.pad(gains, ((0, NOTE - 2), (0, 0)))
        while True:
            yield sides, ffn

    def scatter(self, chain, parts, cuts, groups=1, apart=False):
        grads = parts[0].reshape(groups, -1, parts[0].shape[-1])
        rows = grads.shape[1] * 2 // 3
        if groups > 1:
            shards = [grads[:, :rows], grads[:, rows:]]
        else:
            shards = [grads]
        shards = [wide(lax.psum_scatter(flat(v), CHIPS, scatter_dimension=0, tiled=True)) for v in shards]
        outs = [part(shards[0], self.core), part(shards[0], 1 - self.core)] + shards[1:]
        squares = sum(jnp.sum(v * v, axis=0, keepdims=True) for v in shards)
        if groups == 1:
            yield
            yield ()
        through = yield
        yield (), through
        yield
        yield outs + [squares]

    def spread_gains(self, grad):
        return lax.psum_scatter(grad, EVERY, scatter_dimension=1, tiled=True)

    def total(self, v):
        return lax.psum(v, EVERY)


class Cube(Whole):
    crossed = True
    near = ((0, 0), (0, 1), (1, 0), (1, 1))

    def __init__(self, spot, groups):
        super().__init__(spot, groups)
        slots = lambda fixed_z: tuple((y, x, s, fixed_z) for y, x in self.near for s in range(self.size))
        self.mixer_slots = slots(False), slots(False)
        self.ffn_in = slots(True)
        self.ffn_out = tuple(yx * self.size + z for z in range(self.size) for yx in range(4))
        self.mixer_blocks = (self.size,) * 3 + (self.size // 2,) * 2

    def lines(self, block):
        return [flip(block, "z", s) for s in range(1, self.size)]

    def gather(self, chain, mixer, gate_up, down, gains, waits):
        spot = self.spot
        mixer_mine, mixer_theirs, gate_mine, gate_theirs, down_low, note = pack_call(
            chain, spot, mixer, gate_up, down, gains
        )
        gate_came = swap(gate_theirs)
        size = self.size
        own, block = block_call(
            chain, spot, mixer_mine, swap(mixer_theirs), note, gate_came, gains.shape[1], size, waits
        )
        line = self.along_z(block)
        own_x, own_y = flip(own, "d1"), flip(own, "d0")
        yield None
        rows = own.shape[0] // 2 - NOTE
        half = rows // 2
        sides = []

        def spread_out(line):
            return line, flip(line, "d1"), flip(line, "d0")

        def turn_corner(from_x, from_y, extra=0):
            to_x, to_y = corner_call(chain, from_x, from_y, extra)
            return flip(to_x, "d1"), flip(to_y, "d0")

        def plan(side):
            found = [(p, side * (rows + NOTE) + h * half, half, near + (0, False), h) for p, near in enumerate(self.near[:3]) for h in range(2)]
            found += [(3, h * half, half, (1, 1, 0, False), h) for h in range(2)]
            last = (size - 1) * 2
            for at in range(last):
                s, h = at // 2 + 1, at % 2
                found += [(4 + p, at * half, half, near + (s, False), h) for p, near in enumerate(self.near[:3])]
                found.append((7 + (at >= last // 2), at % (last // 2) * half, half, (1, 1, s, False), h))
            return tuple(found)

        corner = turn_corner(own_x, own_y)
        yield
        chain.pause(corner)
        others, line_rows = range(1, size), (size - 1) * rows
        moves = [(0, (rows + NOTE, s, 0), rows, 0, (s - 1) * rows) for s in others]
        moves += [(0, (rows + NOTE, s, rows), NOTE, 0, line_rows + (s - 1) * NOTE) for s in others]
        moves += [(1, rows + NOTE, rows, 1, s * rows) for s in range(size)]
        line, block = stack_call(
            chain, spot, (line, own), (line_rows + (size - 1) * NOTE, size * rows), tuple(moves)
        )
        first = spread_out(line)
        line = self.along_z(block)
        yield
        first_corner = turn_corner(*first[1:], (size - 1) * NOTE)
        notes = [(p, rows, near + (0, False)) for p, near in enumerate(self.near)]
        for s in others:
            notes += [(4 + p, line_rows + (s - 1) * NOTE, near + (s, False)) for p, near in enumerate(self.near[:3])]
            notes.append((7, line_rows // 2 + (s - 1) * NOTE, (1, 1, s, False)))
        sides.append(([own, own_x, own_y, corner[0], *first, *first_corner], plan(0), tuple(notes)))
        units, count = gate_mine.shape[0], down_low.shape[0]
        ffn_rows = 2 * units + count
        moves = [(0, (rows, s, 0), rows, 0, (s - 1) * rows) for s in others]
        for s in range(size):
            at = s * ffn_rows
            moves += [(1, 0, units, 1, at), (2, 0, units, 1, at + units), (3, 0, count, 1, at + 2 * units)]
        line, block = stack_call(
            chain, spot, (line, gate_mine, gate_came, down_low), (line_rows, size * ffn_rows), tuple(moves)
        )
        across, line = line, self.along_z(block)
        second = spread_out(*chain.pause(first_corner, (across,)))
        yield sides, None
        second_corner = turn_corner(*second[1:])
        sides.append(([own, own_x, own_y, corner[1], *second, *second_corner], plan(1), ()))
        ffn = spread_out(*chain.pause(second_corner, (line,)))
        yield sides, None
        ffn = (*ffn, *turn_corner(*ffn[1:]))
        yield sides, [v.reshape(-1, ffn_rows, v.shape[-1]) for v in ffn]

    def along_z(self, v):
        return lax.all_to_all(v, "z", 0, 0, tiled=True)

    def scatter(self, chain, parts, cuts, groups=1, apart=False):
        if groups > 1:
            came = (self.along_z(flat(parts[0])),)
        else:
            own, to_x, to_y, far_low, far_high = (flat(v) for v in parts)
            by_x, by_y = flip(far_low, "d1"), flip(far_high, "d0")
            yield
            to_x, to_y = yield near_call(chain, to_x, to_y, by_x, by_y)
            came = own, flip(to_x, "d1"), flip(to_y, "d0")
        through = yield
        outs = line_call(chain, came, self.size, apart, through=through or ())
        count = self.size if apart else 1
        first, *rest = yield outs[:count], outs[count:]
        if apart:
            came = [flip(v, "z", s + 1) for s, v in enumerate(rest)]
        elif groups > 1:
            first, came = lax.all_to_all(first, ("d0", "d1"), 0, 0, tiled=True), ()
        else:
            first, came = self.along_z(first), ()
        more, waits = yield
        yield finish_call(
            chain, self.spot, first, came, 1 if apart else self.size, cuts, 2 * self.chips if more else 0, more, waits
        )

    def spread_gains(self, grad):
        devices = 2 * self.chips
        rows = grad.reshape(2, devices, -1).transpose(1, 0, 2).reshape(devices, -1)
        return self.everyone(jnp.pad(rows, ((0, 0), (0, -rows.shape[1] % 128))))

    def everyone(self, rows):
        return lax.all_to_all(rows, EVERY, 0, 0, tiled=True)


def body(
    inputs, lengths, filters, cotangent, mixer_weight, gate_up_weight, down_weight, norm_gains,
    mixer_first, gate_up_first, down_first, gains_first,
    mixer_second, gate_up_second, down_second, gains_second, mixer_average,
):
    slots, width = inputs.shape
    size = lax.axis_size("z")
    groups = 2 * FF // 256
    cube = lax.axis_size("d0") == 2 and lax.axis_size("d1") == 2 and size == 4
    spot = jnp.stack([lax.axis_index(a) for a in EVERY]).astype(jnp.int32)
    core = spot[3]
    links = (Cube if cube else Whole)(spot, groups)
    units = gate_up_weight.shape[0]
    chain = Chain()

    sums = lengths, swap(lengths)
    source_other, cotangent_other = swap(inputs), swap(cotangent)
    taps = jnp.concatenate([wide(filters), jnp.eye(AR_ORDER, slots, dtype=f32)])
    taps_turned = jnp.roll(taps[:, ::-1], 1 - slots // 4, axis=1)
    taps, taps_turned = (v.reshape(-1, 3, slots) for v in (taps, taps_turned))

    weights = links.gather(
        chain, mixer_weight, gate_up_weight, down_weight, norm_gains, (sums[1], source_other, cotangent_other)
    )
    gains = next(weights)
    tokens = normed_call(chain, spot, inputs, source_other)
    blocks = taps.shape[0]
    cuts, spread = (0, blocks // 3, blocks * 2 // 3, blocks), None
    for at in range(3):
        spread = spread_call(chain, sums, taps_turned, *tokens, cuts[at], cuts[at + 1] - cuts[at], spread)
        sides = next(weights)
    sides, _ = sides
    quarter = sides[0][0][0].shape[1]
    *mixed, gains = (*mix_call(chain, spot, spread, 0, *sides[0], gains, size, width), gains)[:3]
    sides, _ = next(weights)
    mixed_own, mixed_other = mix_call(chain, spot, spread, 1, *sides[1], gains, size, width, mixed)
    _, ffn = next(weights)

    hidden, *normed_two = hidden_call(chain, inputs, mixed_own, swap(mixed_other), gains)
    tokens = (*normed_two, *(swap(v) for v in normed_two), cotangent, cotangent_other)
    branch_own, branch_other, two_own, two_other, *grad_ffn = ffn_call(
        chain, spot, sums, tokens, ffn, links.ffn_blocks, links.ffn_in, links.ffn_out, size, links.crossed
    )
    ffn_sum = links.scatter(chain, grad_ffn, ((0, units // 2), (units // 2, units // 2), (units, units // 2)), groups)
    next(ffn_sum)
    grad_hidden, grad_low, gains_two = turn_call(
        chain, lengths, hidden, cotangent, two_own, swap(two_other), gains
    )
    grad_other = swap(grad_low)
    rows = mixer_weight.shape[0]
    cuts = (((0,), rows), ((1,), rows))
    grads_of = lambda s: grad_call(
        chain, spot, gains, grad_low, grad_other, spread, s, quarter, links.mixer_blocks, links.mixer_slots[s], size
    )
    first_sum = links.scatter(chain, grads_of(0), cuts, apart=True)
    next(first_sum)
    second_sum = links.scatter(chain, grads_of(1), cuts, apart=True)
    next(second_sum)
    one = ()
    backward = lambda at, one: back_call(
        chain, spot, sums, taps, grad_low, grad_other, [s[0] for s in sides], [s[1] for s in sides], size,
        at * (blocks // 3), blocks // 3, one,
    )
    one = backward(0, one)
    held = next(first_sum), next(second_sum)
    count = len(held[0])
    held = chain.pause(through=(*held[0], *held[1])) if cube else ()
    first_sum.send(held[:count])
    second_sum.send(held[count:])
    one = backward(1, one)
    one_own, one_other = backward(2, one)
    outs, _ = first_sum.send(())
    first_sum.send(outs)
    outs, _ = ffn_sum.send(())
    ffn_sum.send(outs)
    outs, _ = second_sum.send(())
    first_mine, first_theirs, square = first_sum.send(((), ()))
    one_other, first_theirs, branch_other, *outs = chain.pause(
        through=(one_other, first_theirs, branch_other, *outs)
    )
    second_sum.send(outs)
    gate_up_mine, gate_up_theirs, shard_down, *squares = ffn_sum.send(((), ()))
    input_grad, gains_one = last_call(
        chain, spot, grad_hidden, inputs, one_own, swap(one_other), gains, ()
    )
    squares.append(square)
    shard_gains = links.spread_gains(jnp.concatenate([gains_one, gains_two]))
    output = output_call(chain, hidden, branch_own, swap(branch_other))
    gate_up_came, first_came = swap(gate_up_theirs), swap(first_theirs)
    second_mine, second_theirs, note = second_sum.send(((*squares, shard_gains), ()))
    second_came = swap(second_theirs)
    mixer = mixer_weight, mixer_first, mixer_second, mixer_average
    gate_up, down = (gate_up_weight, gate_up_first, gate_up_second), (down_weight, down_first, down_second)
    gain = norm_gains, gains_first, gains_second
    if cube:
        (
            mixer_new, mixer_first_new, mixer_second_new, mixer_average_new, gate_up_new, gate_up_first_new,
            gate_up_second_new, down_new, down_first_new, down_second_new, gains_new, gains_first_new, gains_second_new,
            grad_norm,
        ) = adam_call(
            chain, spot, links.everyone(note), mixer, gate_up, down, gain,
            (first_mine, second_mine, first_came, second_came, gate_up_mine, gate_up_came, shard_down, shard_gains),
        )
        grad_norm = grad_norm[0, 0]
    else:
        squares = sum(jnp.sum(v) for v in (*squares, note)) + jnp.sum(shard_gains * shard_gains)
        grad_norm = jnp.sqrt(links.total(squares))
        factor = CLIP_LIMIT / jnp.maximum(grad_norm, CLIP_LIMIT)
        shard_mixer = join(
            jnp.concatenate([first_mine, second_mine], axis=1), jnp.concatenate([first_came, second_came], axis=1), core, 1
        )
        shard_gate_up = join(gate_up_mine, gate_up_came, core)
        step = lambda old, grad: adam_step(old[0], grad * factor, old[1], old[2], RATE_MATRIX, DECAY_MATRIX)
        mixer_new, mixer_first_new, mixer_second_new = step(mixer, shard_mixer)
        gate_up_new, gate_up_first_new, gate_up_second_new = step(gate_up, shard_gate_up)
        down_new, down_first_new, down_second_new = step(down, shard_down)
        gains_new, gains_first_new, gains_second_new = adam_step(
            gain[0], shard_gains * factor, gain[1], gain[2], RATE_GAIN, 0.0
        )
        mixer_average_new = AVERAGE_KEEP * mixer_average + (1.0 - AVERAGE_KEEP) * mixer_new
    return (
        output, input_grad, grad_norm, mixer_new, gate_up_new, down_new, gains_new,
        mixer_first_new, gate_up_first_new, down_first_new, gains_first_new,
        mixer_second_new, gate_up_second_new, down_second_new, gains_second_new, mixer_average_new,
    )


def solution(mesh):
    outer, inner = mesh.shape["dp"], mesh.shape["fsdp"]
    side = math.isqrt(outer)
    if side * side != outer:
        side = 1
    split = jax.sharding.Mesh(
        np.asarray(mesh.devices).reshape(side, outer // side, inner // 2, 2), EVERY
    )
    rows, columns, whole = P(EVERY, None), P(None, EVERY), P()
    return jax.shard_map(
        body,
        mesh=split,
        in_specs=(
            rows, rows, whole, rows, rows, rows, rows, columns,
            rows, rows, rows, columns, rows, rows, rows, columns, rows,
        ),
        out_specs=(
            rows, rows, whole, rows, rows, rows, columns, rows, rows, rows, columns,
            rows, rows, rows, columns, rows,
        ),
        check_vma=False,
    )
```

```python
import functools
import math

import jax
import jax.numpy as jnp
import numpy as np
from jax import lax
from jax.experimental import pallas as pl
from jax.experimental.pallas import tpu as pltpu
from jax.sharding import PartitionSpec as P

bf = jnp.bfloat16
f32 = jnp.float32
FILTERS = 24
AR_ORDER = 3
FF = 2048
STEP = 10
NORM_EPS = 1e-05
CLIP_LIMIT = 1.0
BETA_ONE = 0.9
BETA_TWO = 0.95
ADAM_EPS = 1e-08
RATE_MATRIX = 0.03
RATE_GAIN = 0.5
DECAY_MATRIX = 0.1
AVERAGE_KEEP = 0.9
CHIPS = ("d0", "d1", "z")
EVERY = CHIPS + ("core",)


NT = (((1,), (1,)), ((), ()))
NN = (((1,), (0,)), ((), ()))
TN = (((0,), (0,)), ((), ()))


def dot(a, b, dims=NN):
    return lax.dot_general(a, b, dims, preferred_element_type=f32)


class Chain:
    def __init__(self):
        self.token = None

    def call(self, kernel, name, args, in_specs, out_specs, out_shape, waits=(), through=(), **options):
        count, single = len(args), not isinstance(out_shape, (list, tuple)) and not through
        if single:
            out_specs, out_shape = [out_specs], [out_shape]
        made = len(out_shape)
        aliases = options.pop("input_output_aliases", {})
        aliases = {**aliases, **{count + i: made + i for i in range(len(through))}}
        last = tuple(through) + tuple(waits) + (() if self.token is None else (self.token,))

        def whole(*refs):
            first = count + len(last)
            kernel(*refs[:count], *refs[first : first + made], *refs[first + made + len(through) + 1 :])

        *outs, self.token = pl.pallas_call(
            whole,
            name=name,
            in_specs=list(in_specs) + [anywhere() for _ in last],
            out_specs=list(out_specs) + [anywhere() for _ in through] + [anywhere()],
            out_shape=list(out_shape) + [shaped(v.shape, v.dtype) for v in through] + [shaped((8, 128), f32)],
            input_output_aliases=aliases,
            compiler_params=pltpu.CompilerParams(vmem_limit_bytes=64 << 20),
            cost_estimate=pl.CostEstimate(flops=1, bytes_accessed=1, transcendentals=0),
            **options,
        )(*args, *last)
        return outs[0] if single else outs

    def pause(self, waits=(), through=()):
        return self.call(lambda: None, "pause", (), [], [], [], waits=waits, through=through)


def smem():
    return pl.BlockSpec(memory_space=pltpu.SMEM)


def anywhere():
    return pl.BlockSpec(memory_space=pl.ANY)


def fixed(*shape):
    return pl.BlockSpec(shape, lambda i: (0,) * len(shape))


NOTE = 16


def shaped(shape, dtype):
    return jax.ShapeDtypeStruct(tuple(shape), dtype)


def segment_of(place, ends_ref, group):
    return sum((place >= ends_ref[group, j]).astype(jnp.int32) for j in range(3))


def causal_mask(ends_ref, group, n, transposed):
    down = lax.broadcasted_iota(jnp.int32, (n, 1), 0)
    along = lax.broadcasted_iota(jnp.int32, (1, n), 1)
    one, two = segment_of(down, ends_ref, group), segment_of(along, ends_ref, group)
    order = (down <= along) if transposed else (down >= along)
    return ((one == two) & (one < 3) & order).astype(f32).astype(bf)


def diagonals(row, count):
    wide = jnp.broadcast_to(row, (count, row.shape[-1]))
    return pltpu.roll(wide, 0, 1, stride=1, stride_axis=0).astype(bf)


def spread_kernel(lengths_ref, came_ref, taps_ref, own_ref, other_ref, *refs):
    u_ref, mask, table, ends = refs[-4:]
    n = mask.shape[1]
    q, h, w = n // 4, n // 2, own_ref.shape[1] // 2
    per = taps_ref.shape[1]

    @pl.when(pl.program_id(0) == 0)
    def _():
        find_ends(ends, lengths_ref, came_ref)
        for g in range(2):
            mask[g] = causal_mask(ends, g, n, False)
        table[...] = jnp.zeros_like(table)

    for j in range(per):
        strip = diagonals(taps_ref[0, j : j + 1, :], q)
        for g, tokens in enumerate((own_ref, other_ref)):
            for i in range(4):
                rows, cols = slice(i * q, (i + 1) * q), slice(0, (i + 1) * q)
                table[g, rows, cols] = strip[:, (3 - i) * q :] * mask[g, rows, cols]
            upper = dot(table[g, :h, :h], tokens[:h]).astype(bf)
            lower = dot(table[g, h:, :], tokens[...]).astype(bf)
            for side in range(2):
                cols = slice(side * w, (side + 1) * w)
                u_ref[side, g * n : g * n + h, j * w : (j + 1) * w] = upper[:, cols]
                u_ref[side, g * n + h : (g + 1) * n, j * w : (j + 1) * w] = lower[:, cols]


def find_ends(ends, lengths_ref, came_ref):
    for g, ref in enumerate((lengths_ref, came_ref)):
        total = ref[0, 0]
        ends[g, 0] = total
        for j in range(1, 3):
            total = total + ref[0, j]
            ends[g, j] = total


def spread_call(chain, lengths, taps, own, other, first, steps, into=None):
    blocks, per, n = taps.shape
    w = own.shape[1] // 2
    args = [*lengths, taps, own, other]
    specs = [smem()] * 2 + [pl.BlockSpec((1, per, n), lambda i: (i + first, 0, 0)), fixed(n, 2 * w), fixed(n, 2 * w)]
    options = {}
    if into is not None:
        options = dict(input_output_aliases={len(args): 0})
        args, specs = args + [into], specs + [anywhere()]
    return chain.call(
        spread_kernel, "spread", args, specs,
        pl.BlockSpec((2, 2 * n, per * w), lambda i: (0, 0, i + first)),
        shaped((2, 2 * n, blocks * per * w), bf),
        grid=(steps,),
        scratch_shapes=[pltpu.VMEM((2, n, n), bf), pltpu.VMEM((2, n, n), bf), pltpu.SMEM((2, 3), jnp.int32)],
        **options,
    )


def run_copies(copies):
    for c in copies:
        c.start()
    for c in copies:
        c.wait()


def chip_of(spot_ref, slot, size):
    if isinstance(slot, int):
        return slot
    dy, dx, dz, fixed_z = slot
    return ((spot_ref[0] ^ dy) * 2 + (spot_ref[1] ^ dx)) * size + (dz if fixed_z else spot_ref[2] ^ dz)


def collect(spot_ref, pieces, plan, size, held, sem, columns):
    copies = []
    for at, (piece, row, rows, slot, half) in enumerate(plan):
        place = chip_of(spot_ref, slot, size)
        if half is not None:
            place = place * 2 + (spot_ref[3] ^ half)
        start = pl.multiple_of(place * rows, math.gcd(rows, 512))
        copies.append(
            pltpu.make_async_copy(pieces[piece].at[pl.ds(row, rows)], held.at[pl.ds(start, rows), columns], sem.at[at])
        )
    return copies


def mix_kernel(count, plan, notes, size, width, side, spot_ref, u_ref, *refs):
    pieces, refs = refs[:count], refs[count:]
    first = side == 0
    before, refs = refs[: 0 if first else 2], refs[0 if first else 2 :]
    if not notes:
        gains_ref, refs = refs[0], refs[1:]
    own_ref, other_ref, w_ref, *refs = refs
    if notes:
        gains_ref, refs = refs[0], refs[1:]
    held, u, sem, u_sem, *refs = refs
    tiles = sums = refs[0] if refs else None
    w = held.shape[1]
    filters = held.shape[0] // width
    rows = own_ref.shape[0]
    copies = collect(spot_ref, pieces, plan, size, held, sem, slice(0, w))
    for at, (piece, row, slot) in enumerate(notes):
        copies.append(
            pltpu.make_async_copy(
                pieces[piece].at[pl.ds(row, NOTE)], tiles.at[chip_of(spot_ref, slot, size)], sem.at[len(plan) + at]
            )
        )
    third = filters // 3
    cols = [pl.ds(t * third * w, third * w) for t in range(3)]
    loads = [pltpu.make_async_copy(u_ref.at[side, :, c], u.at[:, c], u_sem.at[t]) for t, c in enumerate(cols)]
    adds = [pltpu.make_async_copy(ref, sums.at[g], u_sem.at[4 + g]) for g, ref in enumerate(before)]
    for c in copies + loads + adds:
        c.start()
    for c in copies:
        c.wait()
    give = pltpu.make_async_copy(held, w_ref, u_sem.at[3])
    give.start()
    if notes:
        lanes = width // len(notes)
        for b in range(width // 128):
            block = jnp.zeros((NOTE, 128), f32)
            for j in range(128 // lanes):
                tile = tiles[b * (128 // lanes) + j].astype(f32)
                block = block + (pltpu.roll(tile, j * lanes, 1) if j else tile)
            gains_ref[:, b * 128 : (b + 1) * 128] = block
    gain = gains_ref[0:1, pl.ds(pl.multiple_of((spot_ref[3] * 2 + side) * w, w), w)]
    result = None
    for t in range(3):
        wide = jnp.concatenate(
            [(held[k * width : (k + 1) * width].astype(f32) * gain).astype(bf) for k in range(t * third, (t + 1) * third)],
            axis=1,
        )
        loads[t].wait()
        part = dot(u[:, cols[t]], wide, NT)
        result = part if t == 0 else result + part
    for g, out in enumerate((own_ref, other_ref)):
        mine = result[g * rows : (g + 1) * rows]
        if not first:
            adds[g].wait()
            mine = mine + sums[g]
        out[...] = mine.astype(out.dtype)
    give.wait()


def mix_call(chain, spot, u, side, pieces, plan, notes, gains, size, width, before=()):
    rows, depth = u.shape[1:]
    w = pieces[0].shape[-1]
    total = depth // w * width
    step = rows // 2
    out = fixed(step, width)
    note = fixed(NOTE, width)
    given = () if notes else (gains,)
    made = 1 - len(given)
    return chain.call(
        functools.partial(mix_kernel, len(pieces), plan, notes, size, width, side), "mix",
        (spot, u, *pieces, *before, *given),
        [smem(), anywhere()] + [anywhere() for _ in (*pieces, *before)] + [note for _ in given],
        [out, out, anywhere()] + [note] * made,
        [shaped((step, width), f32), shaped((step, width), bf if before else f32), shaped((total, w), bf)]
        + [shaped((NOTE, width), f32)] * made,
        grid=(1,),
        scratch_shapes=[
            pltpu.VMEM((total, w), bf), pltpu.VMEM((rows, depth), bf),
            pltpu.SemaphoreType.DMA((len(plan) + len(notes),)), pltpu.SemaphoreType.DMA((6,)),
        ] + [pltpu.VMEM((len(notes), NOTE, 128), bf)] * made + [pltpu.VMEM((2, step, width), f32)] * min(1, len(before)),
    )


def hidden_kernel(source_ref, own_ref, came_ref, gain_ref, hidden_ref, *normed_refs):
    hidden = source_ref[...].astype(f32) + (own_ref[...] + came_ref[...].astype(f32))
    scale = lax.rsqrt(jnp.mean(hidden * hidden, axis=-1, keepdims=True) + NORM_EPS)
    hidden_ref[...] = hidden
    normed = (hidden * scale * gain_ref[1:2]).astype(bf)
    width = normed_refs[0].shape[1]
    for i, ref in enumerate(normed_refs):
        ref[...] = normed[:, i * width : (i + 1) * width]


def hidden_call(chain, source, own, came, gain, parts=2):
    rows, width = source.shape
    block = pl.BlockSpec((rows // parts, width), lambda i: (i, 0))
    thin = pl.BlockSpec((rows // parts, width // 2), lambda i: (i, 0))
    return chain.call(
        hidden_kernel, "hidden", (source, own, came, gain), [block, block, block, fixed(NOTE, width)],
        [block, thin, thin], [shaped((rows, width), f32)] + [shaped((rows, width // 2), bf)] * 2,
        grid=(parts,),
    )


def norm_back(grad, hat, scale, gain):
    weighted = grad * gain
    return scale * (weighted - hat * jnp.mean(weighted * hat, axis=-1, keepdims=True))


def add_rows(ref, values, step):
    total = jnp.sum(values, axis=0, keepdims=True)

    @pl.when(step == 0)
    def _():
        ref[...] = total

    @pl.when(step > 0)
    def _():
        ref[...] += total


def turn_kernel(lengths_ref, hidden_ref, back_ref, own_ref, came_ref, gain_ref, grad_ref, low_ref, gains_ref):
    hidden = hidden_ref[...]
    scale = lax.rsqrt(jnp.mean(hidden * hidden, axis=-1, keepdims=True) + NORM_EPS)
    hat = hidden * scale
    two = own_ref[...] + came_ref[...].astype(f32)
    back = live_rows(back_ref[...].astype(f32), lengths_ref, pl.program_id(0) * hidden.shape[0])
    grad = back + norm_back(two, hat, scale, gain_ref[1:2])
    grad_ref[...] = grad
    low_ref[...] = grad.astype(bf)
    add_rows(gains_ref, two * hat, pl.program_id(0))


def turn_call(chain, lengths, hidden, back, own, came, gain, parts=2):
    rows, width = hidden.shape
    block = pl.BlockSpec((rows // parts, width), lambda i: (i, 0))
    return chain.call(
        turn_kernel, "turn", (lengths, hidden, back, own, came, gain), [smem()] + [block] * 4 + [fixed(NOTE, width)],
        [block, block, fixed(1, width)],
        [shaped((rows, width), f32), shaped((rows, width), bf), shaped((1, width), f32)],
        grid=(parts,),
    )


def output_kernel(hidden_ref, own_ref, came_ref, out_ref):
    out_ref[...] = (hidden_ref[...] + (own_ref[...] + came_ref[...].astype(f32))).astype(bf)


def output_call(chain, hidden, own, came, parts=2):
    rows, width = hidden.shape
    block = pl.BlockSpec((rows // parts, width), lambda i: (i, 0))
    return chain.call(
        output_kernel, "output", (hidden, own, came), [block] * 3, block, shaped((rows, width), bf), grid=(parts,),
    )


def last_kernel(spot_ref, grad_ref, source_ref, own_ref, came_ref, gain_ref, out_ref, gains_ref, one):
    half = own_ref.shape[1]
    core = spot_ref[3]
    one[:, pl.ds(pl.multiple_of(core * half, half), half)] = own_ref[...]
    one[:, pl.ds(pl.multiple_of((1 - core) * half, half), half)] = came_ref[...]
    source = source_ref[...].astype(f32)
    scale = lax.rsqrt(jnp.mean(source * source, axis=-1, keepdims=True) + NORM_EPS)
    hat = source * scale
    grad = one[...]
    out_ref[...] = grad_ref[...] + norm_back(grad, hat, scale, gain_ref[0:1])
    add_rows(gains_ref, grad * hat, pl.program_id(0))


def last_call(chain, spot, grad_hidden, source, own, came, gain, waits, parts=2):
    rows, width = source.shape
    block = pl.BlockSpec((rows // parts, width), lambda i: (i, 0))
    thin = pl.BlockSpec((rows // parts, width // 2), lambda i: (i, 0))
    return chain.call(
        last_kernel, "last", (spot, grad_hidden, source, own, came, gain),
        [smem(), block, block, thin, thin, fixed(NOTE, width)],
        [block, fixed(1, width)], [shaped((rows, width), f32), shaped((1, width), f32)],
        grid=(parts,),
        scratch_shapes=[pltpu.VMEM((rows // parts, width), f32)],
        waits=waits,
    )


def grad_kernel(slots, size, side, spot_ref, gains_ref, own_ref, other_ref, u_ref, *refs):
    outs, (turned, held, sem) = refs[:-3], refs[-3:]
    n, width = own_ref.shape
    w = held.shape[1]
    per = u_ref.shape[2] // w
    step = pl.program_id(0)

    @pl.when(step == 0)
    def _():
        turned[:, :n] = own_ref[...].T
        turned[:, n:] = other_ref[...].T

    gain = gains_ref[0:1, pl.ds(pl.multiple_of((spot_ref[3] * 2 + side) * w, w), w)]
    result = dot(turned[...], u_ref[0])
    for j in range(per):
        at = pl.multiple_of((step * per + j) * width, width)
        held[pl.ds(at, width), :] = (result[:, j * w : (j + 1) * w] * gain).astype(bf)

    @pl.when(step == pl.num_programs(0) - 1)
    def _():
        rows = held.shape[0] // len(slots)
        copies, at = [], 0
        for ref in outs:
            for b in range(ref.shape[0] // rows):
                start = pl.multiple_of(chip_of(spot_ref, slots[at], size) * rows, math.gcd(rows, 512))
                copies.append(
                    pltpu.make_async_copy(held.at[pl.ds(start, rows)], ref.at[pl.ds(b * rows, rows)], sem.at[at])
                )
                at += 1
        run_copies(copies)


def grad_call(chain, spot, gains, own, other, u, side, w, blocks, slots, size, per=9):
    rows, depth = u.shape[1:]
    n, width = own.shape
    count = depth // w
    each = count * width // len(slots)
    return chain.call(
        functools.partial(grad_kernel, slots, size, side), "mixer_grad", (spot, gains, own, other, u),
        [smem(), fixed(NOTE, width), fixed(n, width), fixed(n, width), pl.BlockSpec((1, rows, per * w), lambda i: (side, 0, i))],
        [anywhere() for _ in blocks], [shaped((b * each, w), bf) for b in blocks],
        grid=(count // per,),
        scratch_shapes=[
            pltpu.VMEM((width, rows), bf), pltpu.VMEM((count * width, w), bf), pltpu.SemaphoreType.DMA((len(slots),)),
        ],
    )


def back_kernel(first, spot_ref, lengths_ref, came_ref, taps_ref, own_ref, other_ref, left_ref, right_ref, *refs):
    before, refs = refs[: 2 if first else 0], refs[2 if first else 0 :]
    own_out, other_out, mask, low_low, low_high, high, v_low, v_high, ends = refs
    n = mask.shape[1]
    q, h, d = n // 4, n // 2, own_ref.shape[1]
    per = taps_ref.shape[1]

    @pl.when(pl.program_id(0) == 0)
    def _():
        find_ends(ends, lengths_ref, came_ref)
        for g in range(2):
            mask[g] = causal_mask(ends, g, n, True)
        low_low[...] = jnp.zeros_like(low_low)
        high[...] = jnp.zeros_like(high)
        for g, ref in enumerate((own_out, other_out)):
            ref[...] = before[g][...] if first else jnp.zeros_like(ref)

    for j in range(per):
        weight = jnp.concatenate([left_ref[j * d : (j + 1) * d], right_ref[j * d : (j + 1) * d]], axis=1)
        s = diagonals(taps_ref[0, j : j + 1, :], q)
        a = j * h
        for g, grad in enumerate((own_ref, other_ref)):
            v = dot(grad[...], weight).astype(bf)
            v_low[g, a : a + h] = v[:h]
            v_high[g, a : a + h] = v[h:]
            m = mask[g]
            low_low[g, 0:q, a : a + q] = s[:, :q] * m[0:q, 0:q]
            low_low[g, 0:q, a + q : a + h] = s[:, q : 2 * q] * m[0:q, q : 2 * q]
            low_low[g, q:h, a + q : a + h] = s[:, :q] * m[q:h, q:h]
            low_high[g, 0:q, a : a + h] = s[:, 2 * q : 4 * q] * m[0:q, h:]
            low_high[g, q:h, a : a + h] = s[:, q : 3 * q] * m[q:h, h:]
            high[g, 0:q, a : a + h] = s[:, 0 : 2 * q] * m[h : h + q, h:]
            high[g, q:h, a + q : a + h] = s[:, 0:q] * m[h + q :, h + q :]
    for g, out in enumerate((own_out, other_out)):
        out[:h] += dot(low_low[g], v_low[g]) + dot(low_high[g], v_high[g])
        out[h:] += dot(high[g], v_high[g])


def back_call(chain, spot, lengths, taps, own, other, weights, first, steps, before=()):
    blocks, per, n = taps.shape
    rows, d = own.shape
    w = weights[0].shape[1]
    width = 2 * w
    scratch = lambda *s: pltpu.VMEM(s, bf)
    weight = pl.BlockSpec((per * d, w), lambda i: (i + first, 0))
    return chain.call(
        functools.partial(back_kernel, first), "spread_back", (spot, *lengths, taps, own, other, *weights, *before),
        [smem()] * 3 + [pl.BlockSpec((1, per, n), lambda i: (i + first, 0, 0)), fixed(rows, d), fixed(rows, d)]
        + [weight, weight] + [fixed(rows, width) for _ in before],
        [fixed(rows, width)] * 2, [shaped((rows, width), f32)] * 2,
        grid=(steps,),
        scratch_shapes=[
            scratch(2, n, n), scratch(2, n // 2, per * n // 2),
            scratch(2, n // 2, per * n // 2), scratch(2, n // 2, per * n // 2),
            scratch(2, per * n // 2, width), scratch(2, per * n // 2, width), pltpu.SMEM((2, 3), jnp.int32),
        ],
    )


def flat(v):
    return v.reshape(-1, v.shape[-1])


def ffn_kernel(count, outs, steps, slots, out_slots, size, crossed, spot_ref, lengths_ref, came_ref, *refs):
    turned = spot_ref[3] if crossed else 0
    tokens, pieces, refs = refs[:6], refs[6 : 6 + count], refs[6 + count :]
    results, grads, (held, dealt, normed, back, sums, sem) = refs[:4], refs[4 : 4 + outs], refs[4 + outs :]
    n = tokens[0].shape[0]
    chips, units, width = held.shape[0], held.shape[1] * 2 // 3, held.shape[2]
    own, half = chips // 2 // steps, units // 2
    step = pl.program_id(0)

    @pl.when(step == 0)
    def _():
        copies, at = [], 0
        for ref in pieces:
            for b in range(ref.shape[0]):
                chip = chip_of(spot_ref, slots[at], size)
                copies.append(
                    pltpu.make_async_copy(ref.at[b, pl.ds(0, units)], held.at[chip, pl.ds(0, units)], sem.at[0, at])
                )
                copies.append(
                    pltpu.make_async_copy(
                        ref.at[b, pl.ds(units, half)], held.at[chip ^ turned, pl.ds(units, half)], sem.at[1, at]
                    )
                )
                at += 1
        for c in copies:
            c.start()
        half_width = tokens[0].shape[1]
        for i in range(2):
            cols = slice(i * half_width, (i + 1) * half_width)
            normed[:n, cols], normed[n:, cols] = tokens[i][...], tokens[2 + i][...]
        back[:n] = live_rows(tokens[4][...].astype(f32), lengths_ref).astype(bf)
        back[n:] = live_rows(tokens[5][...].astype(f32), came_ref).astype(bf)
        for c in copies:
            c.wait()

    w_gate = flat(held[pl.ds(step * own, own), 0:units])
    w_up = flat(held[pl.ds(chips // 2 + step * own, own), 0:units])
    w_down = flat(held[pl.ds(step * 2 * own, 2 * own), units : units + half])
    gate, up = dot(normed[...], w_gate, NT), dot(normed[...], w_up, NT)
    grad_act = dot(back[...], w_down, NT)
    sigma = 1.0 / (1.0 + jnp.exp(-gate))
    swish = gate * sigma
    act = (swish * up).astype(bf)
    grad_gate = (grad_act * up * (sigma * (1.0 + gate * (1.0 - sigma)))).astype(bf)
    grad_up = (grad_act * swish).astype(bf)
    branch = dot(act, w_down)
    two = dot(jnp.concatenate([grad_gate, grad_up], axis=1), jnp.concatenate([w_gate, w_up], axis=0))
    for i, value in enumerate((branch, two)):
        if steps > 1:

            @pl.when(step == 0)
            def _():
                sums[i] = value

            @pl.when((step > 0) & (step < steps - 1))
            def _():
                sums[i] += value

        @pl.when(step == steps - 1)
        def _():
            total = value + sums[i] if steps > 1 else value
            results[2 * i][...] = total[:n]
            results[2 * i + 1][...] = total[n:].astype(bf)

    put = lambda v: v.astype(bf).reshape(own, units, width)
    dealt[pl.ds(step * own, own), 0:units] = put(dot(grad_gate, normed[...], TN))
    dealt[pl.ds(chips // 2 + step * own, own), 0:units] = put(dot(grad_up, normed[...], TN))
    grad_down = dot(act, back[...], TN).astype(bf)
    for b in range(2 * own):
        dealt[(step * 2 * own + b) ^ turned, units : units + half] = grad_down[b * half : (b + 1) * half]

    @pl.when(step == steps - 1)
    def _():
        copies, at = [], 0
        for ref in grads:
            for b in range(ref.shape[0]):
                copies.append(
                    pltpu.make_async_copy(dealt.at[chip_of(spot_ref, out_slots[at], size)], ref.at[b], sem.at[0, at])
                )
                at += 1
        run_copies(copies)


def ffn_call(chain, spot, lengths, tokens, pieces, blocks, slots, out_slots, size, crossed, chunk=1024):
    n, d = tokens[-1].shape
    chips, rows = len(slots), pieces[0].shape[1]
    units = rows * 2 // 3
    steps = chips // 2 * units // chunk
    return chain.call(
        functools.partial(ffn_kernel, len(pieces), len(blocks), steps, slots, out_slots, size, crossed), "ffn",
        (spot, *lengths, *tokens, *pieces),
        [smem()] * 3 + [fixed(*v.shape) for v in tokens] + [anywhere() for _ in pieces],
        [fixed(n, d)] * 4 + [anywhere() for _ in blocks],
        [shaped((n, d), f32), shaped((n, d), bf)] * 2 + [shaped((b, rows, d), bf) for b in blocks],
        grid=(steps,),
        scratch_shapes=[
            pltpu.VMEM((chips, rows, d), bf), pltpu.VMEM((chips, rows, d), bf),
            pltpu.VMEM((2 * n, d), bf), pltpu.VMEM((2 * n, d), bf), pltpu.VMEM((2, 2 * n, d), f32),
            pltpu.SemaphoreType.DMA((2, chips)),
        ],
    )


def normed_kernel(spot_ref, own_ref, other_ref, own_out, other_out, full):
    half = own_out.shape[1]
    cols = pl.ds(pl.multiple_of(spot_ref[3] * half, half), half)
    for ref, out in ((own_ref, own_out), (other_ref, other_out)):
        source = ref[...].astype(f32)
        scale = lax.rsqrt(jnp.mean(source * source, axis=-1, keepdims=True) + NORM_EPS)
        full[...] = (source * scale).astype(bf)
        out[...] = full[:, cols]


def normed_call(chain, spot, own, other, parts=2):
    rows, width = own.shape
    block = pl.BlockSpec((rows // parts, width), lambda i: (i, 0))
    thin = pl.BlockSpec((rows // parts, width // 2), lambda i: (i, 0))
    return chain.call(
        normed_kernel, "normed", (spot, own, other), [smem(), block, block],
        [thin] * 2, [shaped((rows, width // 2), bf)] * 2,
        grid=(parts,), scratch_shapes=[pltpu.VMEM((rows // parts, width), bf)],
    )


def live_rows(values, lengths_ref, first=0):
    total = lengths_ref[0, 0] + lengths_ref[0, 1] + lengths_ref[0, 2]
    place = lax.broadcasted_iota(jnp.int32, (values.shape[0], 1), 0) + first
    return jnp.where(place < total, values, jnp.zeros((), values.dtype))


def pack_kernel(
    spot_ref, mixer_ref, gate_up_ref, down_ref, gains_ref, mixer_mine, mixer_theirs, gate_mine, gate_theirs, down_low, note
):
    half, units, core = mixer_mine.shape[1], gate_mine.shape[0], spot_ref[3]
    for ref, cols, rows, c in ((mixer_mine, half, units, core), (mixer_theirs, half, units, 1 - core)):
        ref[...] = mixer_ref[:, pl.ds(pl.multiple_of(c * half, half), half)].astype(bf)
    for ref, c in ((gate_mine, core), (gate_theirs, 1 - core)):
        ref[:units] = gate_up_ref[pl.ds(pl.multiple_of(c * units, units), units), :].astype(bf)
    count, own = gains_ref.shape
    note[...] = jnp.zeros_like(note)
    note[:count, :own] = gains_ref[...].astype(bf)
    gate_theirs[units:] = jnp.zeros((note.shape[0], gate_theirs.shape[1]), bf)
    gate_theirs[units:, : note.shape[1]] = note[...]
    down_low[...] = down_ref[...].astype(bf)


def pack_call(chain, spot, mixer, gate_up, down, gains):
    (rows, width), (units, _), (half, _) = mixer.shape, gate_up.shape, down.shape
    shapes = [(rows, width // 2)] * 2 + [(units // 2, width), (units // 2 + NOTE, width), (half, width), (NOTE, 128)]
    return chain.call(
        pack_kernel, "pack", (spot, mixer, gate_up, down, gains),
        [smem(), fixed(rows, width), fixed(units, width), fixed(half, width), fixed(*gains.shape)],
        [fixed(*s) for s in shapes], [shaped(s, bf) for s in shapes], grid=(1,),
    )


def block_kernel(own_gains, spot_ref, mine_ref, came_ref, note_ref, gate_ref, all_ref, copies_ref):
    rows, w = mine_ref.shape[0], all_ref.shape[1]
    mine = note_ref[...].astype(f32)
    came = gate_ref[gate_ref.shape[0] - NOTE :, :w].astype(f32)
    turned = lambda v: pltpu.roll(v, own_gains, 1)
    note = jnp.where(spot_ref[3] == 0, mine + turned(came), came + turned(mine)).astype(bf)
    at = 0
    for side in range(2):
        cols = slice(side * w, (side + 1) * w)
        all_ref[at : at + rows] = mine_ref[:, cols]
        all_ref[at + rows : at + 2 * rows] = came_ref[:, cols]
        all_ref[at + 2 * rows : at + 2 * rows + NOTE] = note
        at += 2 * rows + NOTE
    count = 2 * rows + NOTE
    for c in range(copies_ref.shape[0] // count):
        copies_ref[c * count : (c + 1) * count] = all_ref[:count]


def block_call(chain, spot, mine, came, note, gate_came, own_gains, copies, waits):
    rows, width = mine.shape
    w = width // 2
    each = 2 * rows + NOTE
    return chain.call(
        functools.partial(block_kernel, own_gains), "block", (spot, mine, came, note, gate_came),
        [smem()] + [fixed(*v.shape) for v in (mine, came, note, gate_came)],
        [fixed(2 * each, w), fixed(copies * each, w)], [shaped((2 * each, w), bf), shaped((copies * each, w), bf)],
        grid=(1,), waits=waits,
    )


def stack_kernel(count, moves, spot_ref, *refs):
    for i, a, rows, o, b in moves:
        if not isinstance(a, int):
            stride, distance, first = a
            a = pl.multiple_of((spot_ref[2] ^ distance) * stride + first, NOTE)
        refs[count + o][b : b + rows] = refs[i][pl.ds(a, rows)]


def stack_call(chain, spot, arrays, rows, moves, waits=()):
    like = {o: arrays[i] for i, _, _, o, _ in moves}
    shapes = [(r,) + like[o].shape[1:] for o, r in enumerate(rows)]
    return chain.call(
        functools.partial(stack_kernel, len(arrays), moves), "stack", (spot, *arrays),
        [smem()] + [fixed(*v.shape) for v in arrays],
        [fixed(*s) for s in shapes], [shaped(s, like[o].dtype) for o, s in enumerate(shapes)], grid=(1,), waits=waits,
    )


def corner_kernel(cut, extra, x_ref, y_ref, to_x_ref, to_y_ref):
    rows = x_ref.shape[0]
    to_x_ref[:cut] = y_ref[:cut]
    if extra:
        to_x_ref[cut:] = y_ref[rows - extra :]
    to_y_ref[...] = x_ref[cut : rows - extra]


def corner_call(chain, from_x, from_y, extra):
    total, width = from_x.shape
    cut = (total - extra) // 2
    shapes = [(cut + extra, width), (cut, width)]
    return chain.call(
        functools.partial(corner_kernel, cut, extra), "corner", (from_x, from_y), [fixed(total, width)] * 2,
        [fixed(*s) for s in shapes], [shaped(s, bf) for s in shapes], grid=(1,),
    )


def near_kernel(to_x_ref, to_y_ref, by_x_ref, by_y_ref, new_x_ref, new_y_ref):
    new_x_ref[...] = (to_x_ref[...].astype(f32) + by_y_ref[...].astype(f32)).astype(bf)
    new_y_ref[...] = (to_y_ref[...].astype(f32) + by_x_ref[...].astype(f32)).astype(bf)


def near_call(chain, to_x, to_y, by_x, by_y, parts=2, **options):
    rows, width = by_x.shape
    block = (rows // parts, width)
    low, high = pl.BlockSpec(block, lambda i: (i, 0)), pl.BlockSpec(block, lambda i: (i + parts, 0))
    return chain.call(
        near_kernel, "near", (to_x, to_y, by_x, by_y), [high, low, low, low], [high, low],
        [shaped(to_x.shape, bf), shaped(to_y.shape, bf)], grid=(parts,), input_output_aliases={0: 0, 1: 1}, **options,
    )


def line_kernel(count, *refs):
    parts, refs = refs[:count], refs[count:]
    rows = refs[-1].shape[0]

    def total(at):
        result = parts[0][pl.ds(at, rows)].astype(f32)
        for ref in parts[1:]:
            result = result + ref[pl.ds(at, rows)].astype(f32)
        return result

    for s, ref in enumerate(refs):
        ref[...] = total(s * rows).astype(ref.dtype)


def line_call(chain, parts, size, apart, **options):
    quarters = 4 if len(parts) == 1 else 1
    rows, width = parts[0].shape[0] // quarters // size, parts[0].shape[1]
    if apart:
        ins = [fixed(size * rows, width)] * len(parts)
        specs = [fixed(rows, width)] * size
        shapes = [shaped((rows, width), f32)] + [shaped((rows, width), bf)] * (size - 1)
        steps = 1
    else:
        steps = 2
        half = size * rows // steps
        ins = [pl.BlockSpec((half, width), lambda i, q=q: (i + q * steps, 0)) for q in range(quarters)]
        specs, shapes = [pl.BlockSpec((half, width), lambda i: (i, 0))], [shaped((size * rows, width), bf)]
    parts = parts * quarters
    return chain.call(
        functools.partial(line_kernel, len(parts)), "line", parts, ins, specs, shapes, grid=(steps,), **options
    )


def finish_kernel(cuts, count, note, spot_ref, first_ref, *refs):
    came, more, outs, squares_ref, total = (
        refs[:count], refs[count : -len(cuts) - 2], refs[-len(cuts) - 2 : -2], refs[-2], refs[-1]
    )
    rows = total.shape[0]
    result = first_ref[:rows].astype(f32)
    for b in range(1, first_ref.shape[0] // rows):
        result = result + first_ref[b * rows : (b + 1) * rows].astype(f32)
    for ref in came:
        result = result + ref[...].astype(f32)
    total[...] = result
    squares = jnp.sum(result * result, axis=0, keepdims=True)
    if note:
        whole = jnp.sum(squares, axis=1, keepdims=True)
        for ref in more[:-1]:
            whole = whole + jnp.sum(ref[...], axis=1, keepdims=True)
        gains = jnp.sum(more[-1][...], axis=0, keepdims=True)
        squares = jnp.broadcast_to(whole + jnp.sum(gains * gains, axis=1, keepdims=True), squares_ref.shape)
    squares_ref[...] = squares
    for ref, start in zip(outs, cuts):
        rows = ref.shape[0]
        if not isinstance(start, int):
            start = pl.multiple_of((spot_ref[3] ^ start[0]) * rows, rows & -rows)
        ref[...] = total[pl.ds(start, rows), :]


def finish_call(chain, spot, first, came, blocks, cuts, note=0, more=(), waits=()):
    rows, width = first.shape[0] // blocks, first.shape[1]
    shapes = [(r, width) for _, r in cuts] + [(note, 128) if note else (1, width)]
    return chain.call(
        functools.partial(finish_kernel, [c for c, _ in cuts], len(came), note), "finish", (spot, first, *came, *more),
        [smem(), fixed(*first.shape)] + [fixed(rows, width)] * len(came) + [fixed(*v.shape) for v in more],
        [fixed(*s) for s in shapes], [shaped(s, f32) for s in shapes],
        grid=(1,), scratch_shapes=[pltpu.VMEM((rows, width), f32)], waits=waits,
    )


def adam_step(weight, grad, first, second, rate, decay):
    first_new = BETA_ONE * first + (1.0 - BETA_ONE) * grad
    second_new = BETA_TWO * second + (1.0 - BETA_TWO) * grad * grad
    corr_one = 1.0 - BETA_ONE**STEP
    corr_two = 1.0 - BETA_TWO**STEP
    update = first_new / corr_one / (jnp.sqrt(second_new / corr_two) + ADAM_EPS)
    return (weight - rate * (update + decay * weight), first_new, second_new)


def adam_kernel(spot_ref, note_ref, *refs):
    ins, outs, wide, tall = refs[:21], refs[21:35], refs[35], refs[36]
    mixer, gate_up, down, gains, parts = ins[:4], ins[4:7], ins[7:10], ins[10:13], ins[13:]
    mixer_out, gate_up_out, down_out, gains_out, norm_out = outs[:4], outs[4:7], outs[7:10], outs[10:13], outs[13]
    core, quarter = spot_ref[3], parts[0].shape[1]
    norm = jnp.sqrt(jnp.sum(note_ref[...], axis=0, keepdims=True)[:, :1])
    factor = CLIP_LIMIT / jnp.maximum(norm, CLIP_LIMIT)

    for s in range(2):
        mine = pl.multiple_of(core * 2 * quarter, quarter) + s * quarter
        came = pl.multiple_of((1 - core) * 2 * quarter, quarter) + s * quarter
        wide[:, pl.ds(pl.multiple_of(mine, quarter), quarter)] = parts[s][...]
        wide[:, pl.ds(pl.multiple_of(came, quarter), quarter)] = parts[2 + s][...]
    old, first, second, average = (r[...] for r in mixer)
    new, first, second = adam_step(old, wide[...] * factor, first, second, RATE_MATRIX, DECAY_MATRIX)
    average = AVERAGE_KEEP * average + (1.0 - AVERAGE_KEEP) * new
    for ref, value in zip(mixer_out, (new, first, second, average)):
        ref[...] = value

    @pl.when(pl.program_id(0) == 0)
    def _():
        half = parts[4].shape[0]
        tall[pl.ds(pl.multiple_of(core * half, half), half), :] = parts[4][...]
        tall[pl.ds(pl.multiple_of((1 - core) * half, half), half), :] = parts[5][...]
        own = gains[0].shape[1]
        sums = jnp.sum(parts[7][...], axis=0, keepdims=True)
        gain_grad = jnp.concatenate([sums[:, :own], sums[:, own : 2 * own]])
        for olds, news, grad, rate, decay in (
            (gate_up, gate_up_out, tall[...], RATE_MATRIX, DECAY_MATRIX),
            (down, down_out, parts[6][...], RATE_MATRIX, DECAY_MATRIX),
            (gains, gains_out, gain_grad, RATE_GAIN, 0.0),
        ):
            old, first, second = (r[...] for r in olds)
            scale = factor if rate == RATE_MATRIX else factor[:, :1]
            for ref, value in zip(news, adam_step(old, grad * scale, first, second, rate, decay)):
                ref[...] = value
        norm_out[...] = norm


def adam_call(chain, spot, note, mixer, gate_up, down, gains, parts, blocks=1):
    rows, width = mixer[0].shape
    step = rows // blocks
    block = pl.BlockSpec((step, width), lambda i: (i, 0))
    piece = pl.BlockSpec((step, parts[0].shape[1]), lambda i: (i, 0))
    whole = lambda v: fixed(*v.shape)
    others = [*gate_up, *down, *gains]
    shapes = [v.shape for v in (*mixer, *others)] + [(1, 1)]
    return chain.call(
        adam_kernel, "adam", (spot, note, *mixer, *others, *parts),
        [smem(), whole(note)] + [block] * 4 + [whole(v) for v in others] + [piece] * 4
        + [whole(v) for v in parts[4:]],
        [block] * 4 + [whole(v) for v in others] + [fixed(1, 1)], [shaped(s, f32) for s in shapes],
        grid=(blocks,),
        scratch_shapes=[pltpu.VMEM((step, width), f32), pltpu.VMEM(gate_up[0].shape, f32)],
    )


def flip(v, axis, bits=1):
    size = lax.axis_size(axis)
    return lax.ppermute(v, axis, [(i, i ^ bits) for i in range(size)])


def swap(v):
    return flip(v, "core")


def join(mine, other, core, axis=0):
    return jnp.where(
        core == 0,
        jnp.concatenate([mine, other], axis=axis),
        jnp.concatenate([other, mine], axis=axis),
    )


def part(v, index, axis=0):
    size = v.shape[axis] // 2
    return lax.dynamic_slice_in_dim(v, index * size, size, axis)


def low(v):
    return v.astype(bf)


def wide(v):
    return v.astype(f32)


class Whole:
    crossed = False
    mixer_slots = ((0,), (0,))
    mixer_blocks = (1,)

    def __init__(self, spot, groups):
        self.spot, self.core = spot, spot[3]
        self.size = lax.axis_size("z")
        self.chips = lax.axis_size("d0") * lax.axis_size("d1") * self.size
        self.ffn_in = self.ffn_out = tuple(range(groups))
        self.ffn_blocks = (groups,)

    def gather(self, chain, mixer, gate_up, down, gains, waits):
        def trade(v, axis):
            return join(part(v, self.core, axis), swap(part(v, 1 - self.core, axis)), self.core)

        everything = lambda v: lax.all_gather(v, CHIPS, axis=0, tiled=True)
        mixer_block = trade(low(mixer), 1)
        w, groups = mixer_block.shape[1] // 2, len(self.ffn_in)
        sides = []
        for s in range(2):
            whole = everything(mixer_block[:, s * w : (s + 1) * w])
            sides.append(([whole], ((0, 0, whole.shape[0], 0, None),), ()))
        ffn = [everything(v).reshape(groups, -1, v.shape[1]) for v in (trade(low(gate_up), 0), low(down))]
        ffn = [jnp.concatenate(ffn, axis=1)]
        gains = lax.all_gather(wide(low(gains)), EVERY, axis=1, tiled=True)
        yield jnp.pad(gains, ((0, NOTE - 2), (0, 0)))
        while True:
            yield sides, ffn

    def scatter(self, chain, parts, cuts, groups=1, apart=False):
        grads = parts[0].reshape(groups, -1, parts[0].shape[-1])
        rows = grads.shape[1] * 2 // 3
        if groups > 1:
            shards = [grads[:, :rows], grads[:, rows:]]
        else:
            shards = [grads]
        shards = [wide(lax.psum_scatter(flat(v), CHIPS, scatter_dimension=0, tiled=True)) for v in shards]
        outs = [part(shards[0], self.core), part(shards[0], 1 - self.core)] + shards[1:]
        squares = sum(jnp.sum(v * v, axis=0, keepdims=True) for v in shards)
        if groups == 1:
            yield
            yield ()
        through = yield ()
        yield (), through
        yield
        yield outs + [squares]

    def spread_gains(self, grad):
        return lax.psum_scatter(grad, EVERY, scatter_dimension=1, tiled=True)

    def total(self, v):
        return lax.psum(v, EVERY)


class Cube(Whole):
    crossed = True
    near = ((0, 0), (0, 1), (1, 0), (1, 1))

    def __init__(self, spot, groups):
        super().__init__(spot, groups)
        slots = lambda fixed_z: tuple((y, x, s, fixed_z) for y, x in self.near for s in range(self.size))
        self.mixer_slots = slots(False), slots(False)
        self.ffn_in = slots(True)
        self.ffn_out = tuple(yx * self.size + z for z in range(self.size) for yx in range(4))
        self.mixer_blocks = (self.size,) * 3 + (self.size // 2,) * 2

    def lines(self, block):
        return [flip(block, "z", s) for s in range(1, self.size)]

    def gather(self, chain, mixer, gate_up, down, gains, waits):
        spot = self.spot
        mixer_mine, mixer_theirs, gate_mine, gate_theirs, down_low, note = pack_call(
            chain, spot, mixer, gate_up, down, gains
        )
        gate_came = swap(gate_theirs)
        size = self.size
        own, block = block_call(
            chain, spot, mixer_mine, swap(mixer_theirs), note, gate_came, gains.shape[1], size, waits
        )
        line = self.along_z(block)
        own_x, own_y = flip(own, "d1"), flip(own, "d0")
        yield None
        rows = own.shape[0] // 2 - NOTE
        half = rows // 2
        sides = []

        def spread_out(line):
            return line, flip(line, "d1"), flip(line, "d0")

        def turn_corner(from_x, from_y, extra=0):
            to_x, to_y = corner_call(chain, from_x, from_y, extra)
            return flip(to_x, "d1"), flip(to_y, "d0")

        def plan(side):
            found = [(p, side * (rows + NOTE) + h * half, half, near + (0, False), h) for p, near in enumerate(self.near[:3]) for h in range(2)]
            found += [(3, h * half, half, (1, 1, 0, False), h) for h in range(2)]
            last = (size - 1) * 2
            for at in range(last):
                s, h = at // 2 + 1, at % 2
                found += [(4 + p, at * half, half, near + (s, False), h) for p, near in enumerate(self.near[:3])]
                found.append((7 + (at >= last // 2), at % (last // 2) * half, half, (1, 1, s, False), h))
            return tuple(found)

        corner = turn_corner(own_x, own_y)
        yield
        chain.pause(corner)
        others, line_rows = range(1, size), (size - 1) * rows
        moves = [(0, (rows + NOTE, s, 0), rows, 0, (s - 1) * rows) for s in others]
        moves += [(0, (rows + NOTE, s, rows), NOTE, 0, line_rows + (s - 1) * NOTE) for s in others]
        moves += [(1, rows + NOTE, rows, 1, s * rows) for s in range(size)]
        line, block = stack_call(
            chain, spot, (line, own), (line_rows + (size - 1) * NOTE, size * rows), tuple(moves)
        )
        first = spread_out(line)
        line = self.along_z(block)
        yield
        first_corner = turn_corner(*first[1:], (size - 1) * NOTE)
        notes = [(p, rows, near + (0, False)) for p, near in enumerate(self.near)]
        for s in others:
            notes += [(4 + p, line_rows + (s - 1) * NOTE, near + (s, False)) for p, near in enumerate(self.near[:3])]
            notes.append((7, line_rows // 2 + (s - 1) * NOTE, (1, 1, s, False)))
        sides.append(([own, own_x, own_y, corner[0], *first, *first_corner], plan(0), tuple(notes)))
        units, count = gate_mine.shape[0], down_low.shape[0]
        ffn_rows = 2 * units + count
        moves = [(0, (rows, s, 0), rows, 0, (s - 1) * rows) for s in others]
        for s in range(size):
            at = s * ffn_rows
            moves += [(1, 0, units, 1, at), (2, 0, units, 1, at + units), (3, 0, count, 1, at + 2 * units)]
        line, block = stack_call(
            chain, spot, (line, gate_mine, gate_came, down_low), (line_rows, size * ffn_rows), tuple(moves)
        )
        across, line = line, self.along_z(block)
        second = spread_out(*chain.pause(first_corner, (across,)))
        yield sides, None
        second_corner = turn_corner(*second[1:])
        sides.append(([own, own_x, own_y, corner[1], *second, *second_corner], plan(1), ()))
        ffn = spread_out(*chain.pause(second_corner, (line,)))
        yield sides, None
        ffn = (*ffn, *turn_corner(*ffn[1:]))
        yield sides, [v.reshape(-1, ffn_rows, v.shape[-1]) for v in ffn]

    def along_z(self, v):
        return lax.all_to_all(v, "z", 0, 0, tiled=True)

    def scatter(self, chain, parts, cuts, groups=1, apart=False):
        if groups > 1:
            came = (self.along_z(flat(parts[0])),)
        else:
            own, to_x, to_y, far_low, far_high = (flat(v) for v in parts)
            by_x, by_y = flip(far_low, "d1"), flip(far_high, "d0")
            yield
            to_x, to_y = yield near_call(chain, to_x, to_y, by_x, by_y)
            came = own, flip(to_x, "d1"), flip(to_y, "d0")
        through = yield came
        outs = line_call(chain, came, self.size, apart, through=through or ())
        count = self.size if apart else 1
        first, *rest = yield outs[:count], outs[count:]
        if groups > 1:
            first, came = lax.all_to_all(first, ("d0", "d1"), 0, 0, tiled=True), ()
        elif apart:
            came = [flip(v, "z", s + 1) for s, v in enumerate(rest)]
        else:
            first, came = self.along_z(first), ()
        more, waits = yield
        yield finish_call(
            chain, self.spot, first, came, 1 if apart else self.size, cuts, 2 * self.chips if more else 0, more, waits
        )

    def spread_gains(self, grad):
        devices = 2 * self.chips
        rows = grad.reshape(2, devices, -1).transpose(1, 0, 2).reshape(devices, -1)
        return self.everyone(jnp.pad(rows, ((0, 0), (0, -rows.shape[1] % 128))))

    def everyone(self, rows):
        return lax.all_to_all(rows, EVERY, 0, 0, tiled=True)


def body(
    inputs, lengths, filters, cotangent, mixer_weight, gate_up_weight, down_weight, norm_gains,
    mixer_first, gate_up_first, down_first, gains_first,
    mixer_second, gate_up_second, down_second, gains_second, mixer_average,
):
    slots, width = inputs.shape
    size = lax.axis_size("z")
    groups = 2 * FF // 256
    cube = lax.axis_size("d0") == 2 and lax.axis_size("d1") == 2 and size == 4
    spot = jnp.stack([lax.axis_index(a) for a in EVERY]).astype(jnp.int32)
    core = spot[3]
    links = (Cube if cube else Whole)(spot, groups)
    units = gate_up_weight.shape[0]
    chain = Chain()

    sums = lengths, swap(lengths)
    source_other, cotangent_other = swap(inputs), swap(cotangent)
    taps = jnp.concatenate([wide(filters), jnp.eye(AR_ORDER, slots, dtype=f32)])
    taps_turned = jnp.roll(taps[:, ::-1], 1 - slots // 4, axis=1)
    taps, taps_turned = (v.reshape(-1, 3, slots) for v in (taps, taps_turned))

    weights = links.gather(
        chain, mixer_weight, gate_up_weight, down_weight, norm_gains, (sums[1], source_other, cotangent_other)
    )
    gains = next(weights)
    tokens = normed_call(chain, spot, inputs, source_other)
    blocks = taps.shape[0]
    cuts, spread = (0, blocks // 3, blocks * 4 // 9, blocks), None
    for at in range(3):
        spread = spread_call(chain, sums, taps_turned, *tokens, cuts[at], cuts[at + 1] - cuts[at], spread)
        sides = next(weights)
    sides, _ = sides
    quarter = sides[0][0][0].shape[1]
    *mixed, left, gains = (*mix_call(chain, spot, spread, 0, *sides[0], gains, size, width), gains)[:4]
    sides, _ = next(weights)
    mixed_own, mixed_other, right = mix_call(chain, spot, spread, 1, *sides[1], gains, size, width, mixed)
    _, ffn = next(weights)

    hidden, *normed_two = hidden_call(chain, inputs, mixed_own, swap(mixed_other), gains)
    tokens = (*normed_two, *(swap(v) for v in normed_two), cotangent, cotangent_other)
    branch_own, branch_other, two_own, two_other, *grad_ffn = ffn_call(
        chain, spot, sums, tokens, ffn, links.ffn_blocks, links.ffn_in, links.ffn_out, size, links.crossed
    )
    if cube:
        grad_ffn = chain.pause(through=grad_ffn)
    ffn_sum = links.scatter(chain, grad_ffn, ((0, units // 2), (units // 2, units // 2), (units, units // 2)), groups)
    ffn_came = next(ffn_sum)
    grad_hidden, grad_low, gains_two = turn_call(
        chain, lengths, hidden, cotangent, two_own, swap(two_other), gains
    )
    grad_other = swap(grad_low)
    rows = mixer_weight.shape[0]
    cuts = (((0,), rows), ((1,), rows))
    grads_of = lambda s: grad_call(
        chain, spot, gains, grad_low, grad_other, spread, s, quarter, links.mixer_blocks, links.mixer_slots[s], size
    )
    first_sum = links.scatter(chain, grads_of(0), cuts, apart=True)
    next(first_sum)
    second_sum = links.scatter(chain, grads_of(1), cuts, apart=True)
    next(second_sum)
    backward = lambda first, steps, one: back_call(
        chain, spot, sums, taps, grad_low, grad_other, (left, right), first, steps, one
    )
    early = blocks // 2
    first_sum.send(next(first_sum))
    one = backward(0, early, ())
    second_sum.send(next(second_sum))
    one_own, one_other = backward(early, blocks - early, one)
    outs, _ = first_sum.send(())
    first_sum.send(outs)
    input_grad, gains_one = last_call(
        chain, spot, grad_hidden, inputs, one_own, swap(one_other), gains, ffn_came
    )
    shard_gains = links.spread_gains(jnp.concatenate([gains_one, gains_two]))
    outs, _ = second_sum.send(())
    first_mine, first_theirs, square = first_sum.send(((), ()))
    chain.pause((shard_gains,))
    next_outs, held = ffn_sum.send((first_theirs, branch_other, *outs))
    first_theirs, branch_other, *outs = held
    ffn_sum.send(next_outs)
    second_sum.send(outs)
    gate_up_mine, gate_up_theirs, shard_down, *squares = ffn_sum.send(((), ()))
    squares.append(square)
    output = output_call(chain, hidden, branch_own, swap(branch_other))
    gate_up_came, first_came = swap(gate_up_theirs), swap(first_theirs)
    second_mine, second_theirs, note = second_sum.send(((*squares, shard_gains), ()))
    second_came = swap(second_theirs)
    mixer = mixer_weight, mixer_first, mixer_second, mixer_average
    gate_up, down = (gate_up_weight, gate_up_first, gate_up_second), (down_weight, down_first, down_second)
    gain = norm_gains, gains_first, gains_second
    if cube:
        (
            mixer_new, mixer_first_new, mixer_second_new, mixer_average_new, gate_up_new, gate_up_first_new,
            gate_up_second_new, down_new, down_first_new, down_second_new, gains_new, gains_first_new, gains_second_new,
            grad_norm,
        ) = adam_call(
            chain, spot, links.everyone(note), mixer, gate_up, down, gain,
            (first_mine, second_mine, first_came, second_came, gate_up_mine, gate_up_came, shard_down, shard_gains),
        )
        grad_norm = grad_norm[0, 0]
    else:
        squares = sum(jnp.sum(v) for v in (*squares, note)) + jnp.sum(shard_gains * shard_gains)
        grad_norm = jnp.sqrt(links.total(squares))
        factor = CLIP_LIMIT / jnp.maximum(grad_norm, CLIP_LIMIT)
        shard_mixer = join(
            jnp.concatenate([first_mine, second_mine], axis=1), jnp.concatenate([first_came, second_came], axis=1), core, 1
        )
        shard_gate_up = join(gate_up_mine, gate_up_came, core)
        step = lambda old, grad: adam_step(old[0], grad * factor, old[1], old[2], RATE_MATRIX, DECAY_MATRIX)
        mixer_new, mixer_first_new, mixer_second_new = step(mixer, shard_mixer)
        gate_up_new, gate_up_first_new, gate_up_second_new = step(gate_up, shard_gate_up)
        down_new, down_first_new, down_second_new = step(down, shard_down)
        gains_new, gains_first_new, gains_second_new = adam_step(
            gain[0], shard_gains * factor, gain[1], gain[2], RATE_GAIN, 0.0
        )
        mixer_average_new = AVERAGE_KEEP * mixer_average + (1.0 - AVERAGE_KEEP) * mixer_new
    return (
        output, input_grad, grad_norm, mixer_new, gate_up_new, down_new, gains_new,
        mixer_first_new, gate_up_first_new, down_first_new, gains_first_new,
        mixer_second_new, gate_up_second_new, down_second_new, gains_second_new, mixer_average_new,
    )


def solution(mesh):
    outer, inner = mesh.shape["dp"], mesh.shape["fsdp"]
    side = math.isqrt(outer)
    if side * side != outer:
        side = 1
    split = jax.sharding.Mesh(
        np.asarray(mesh.devices).reshape(side, outer // side, inner // 2, 2), EVERY
    )
    rows, columns, whole = P(EVERY, None), P(None, EVERY), P()
    return jax.shard_map(
        body,
        mesh=split,
        in_specs=(
            rows, rows, whole, rows, rows, rows, rows, columns,
            rows, rows, rows, columns, rows, rows, rows, columns, rows,
        ),
        out_specs=(
            rows, rows, whole, rows, rows, rows, columns, rows, rows, rows, columns,
            rows, rows, rows, columns, rows,
        ),
        check_vma=False,
    )
```

```python
import functools
import math

import jax
import jax.numpy as jnp
import numpy as np
from jax import lax
from jax.experimental import pallas as pl
from jax.experimental.pallas import tpu as pltpu
from jax.sharding import PartitionSpec as P

bf = jnp.bfloat16
f32 = jnp.float32
FILTERS = 24
AR_ORDER = 3
FF = 2048
STEP = 10
NORM_EPS = 1e-05
CLIP_LIMIT = 1.0
BETA_ONE = 0.9
BETA_TWO = 0.95
ADAM_EPS = 1e-08
RATE_MATRIX = 0.03
RATE_GAIN = 0.5
DECAY_MATRIX = 0.1
AVERAGE_KEEP = 0.9
CHIPS = ("d0", "d1", "z")
EVERY = CHIPS + ("core",)


NT = (((1,), (1,)), ((), ()))
NN = (((1,), (0,)), ((), ()))
TN = (((0,), (0,)), ((), ()))


def dot(a, b, dims=NN):
    return lax.dot_general(a, b, dims, preferred_element_type=f32)


class Chain:
    def __init__(self):
        self.token = None

    def call(self, kernel, name, args, in_specs, out_specs, out_shape, waits=(), through=(), **options):
        count, single = len(args), not isinstance(out_shape, (list, tuple)) and not through
        if single:
            out_specs, out_shape = [out_specs], [out_shape]
        made = len(out_shape)
        aliases = options.pop("input_output_aliases", {})
        aliases = {**aliases, **{count + i: made + i for i in range(len(through))}}
        last = tuple(through) + tuple(waits) + (() if self.token is None else (self.token,))

        def whole(*refs):
            first = count + len(last)
            kernel(*refs[:count], *refs[first : first + made], *refs[first + made + len(through) + 1 :])

        *outs, self.token = pl.pallas_call(
            whole,
            name=name,
            in_specs=list(in_specs) + [anywhere() for _ in last],
            out_specs=list(out_specs) + [anywhere() for _ in through] + [anywhere()],
            out_shape=list(out_shape) + [shaped(v.shape, v.dtype) for v in through] + [shaped((8, 128), f32)],
            input_output_aliases=aliases,
            compiler_params=pltpu.CompilerParams(vmem_limit_bytes=64 << 20),
            cost_estimate=pl.CostEstimate(flops=1, bytes_accessed=1, transcendentals=0),
            **options,
        )(*args, *last)
        return outs[0] if single else outs

    def pause(self, waits=(), through=()):
        return self.call(lambda: None, "pause", (), [], [], [], waits=waits, through=through)


def smem():
    return pl.BlockSpec(memory_space=pltpu.SMEM)


def anywhere():
    return pl.BlockSpec(memory_space=pl.ANY)


def fixed(*shape):
    return pl.BlockSpec(shape, lambda i: (0,) * len(shape))


NOTE = 16


def shaped(shape, dtype):
    return jax.ShapeDtypeStruct(tuple(shape), dtype)


def segment_of(place, ends_ref, group):
    return sum((place >= ends_ref[group, j]).astype(jnp.int32) for j in range(3))


def causal_mask(ends_ref, group, n, transposed):
    down = lax.broadcasted_iota(jnp.int32, (n, 1), 0)
    along = lax.broadcasted_iota(jnp.int32, (1, n), 1)
    one, two = segment_of(down, ends_ref, group), segment_of(along, ends_ref, group)
    order = (down <= along) if transposed else (down >= along)
    return ((one == two) & (one < 3) & order).astype(f32).astype(bf)


def diagonals(row, count):
    wide = jnp.broadcast_to(row, (count, row.shape[-1]))
    return pltpu.roll(wide, 0, 1, stride=1, stride_axis=0).astype(bf)


def spread_kernel(lengths_ref, came_ref, taps_ref, own_ref, other_ref, *refs):
    u_ref, mask, table, ends = refs[-4:]
    n = mask.shape[1]
    q, h, w = n // 4, n // 2, own_ref.shape[1] // 2
    per = taps_ref.shape[1]

    @pl.when(pl.program_id(0) == 0)
    def _():
        find_ends(ends, lengths_ref, came_ref)
        for g in range(2):
            mask[g] = causal_mask(ends, g, n, False)
        table[...] = jnp.zeros_like(table)

    for j in range(per):
        strip = diagonals(taps_ref[0, j : j + 1, :], q)
        for g, tokens in enumerate((own_ref, other_ref)):
            for i in range(4):
                rows, cols = slice(i * q, (i + 1) * q), slice(0, (i + 1) * q)
                table[g, rows, cols] = strip[:, (3 - i) * q :] * mask[g, rows, cols]
            upper = dot(table[g, :h, :h], tokens[:h]).astype(bf)
            lower = dot(table[g, h:, :], tokens[...]).astype(bf)
            for side in range(2):
                cols = slice(side * w, (side + 1) * w)
                u_ref[side, g * n : g * n + h, j * w : (j + 1) * w] = upper[:, cols]
                u_ref[side, g * n + h : (g + 1) * n, j * w : (j + 1) * w] = lower[:, cols]


def find_ends(ends, lengths_ref, came_ref):
    for g, ref in enumerate((lengths_ref, came_ref)):
        total = ref[0, 0]
        ends[g, 0] = total
        for j in range(1, 3):
            total = total + ref[0, j]
            ends[g, j] = total


def spread_call(chain, lengths, taps, own, other, first, steps, into=None):
    blocks, per, n = taps.shape
    w = own.shape[1] // 2
    args = [*lengths, taps, own, other]
    specs = [smem()] * 2 + [pl.BlockSpec((1, per, n), lambda i: (i + first, 0, 0)), fixed(n, 2 * w), fixed(n, 2 * w)]
    options = {}
    if into is not None:
        options = dict(input_output_aliases={len(args): 0})
        args, specs = args + [into], specs + [anywhere()]
    return chain.call(
        spread_kernel, "spread", args, specs,
        pl.BlockSpec((2, 2 * n, per * w), lambda i: (0, 0, i + first)),
        shaped((2, 2 * n, blocks * per * w), bf),
        grid=(steps,),
        scratch_shapes=[pltpu.VMEM((2, n, n), bf), pltpu.VMEM((2, n, n), bf), pltpu.SMEM((2, 3), jnp.int32)],
        **options,
    )


def run_copies(copies):
    for c in copies:
        c.start()
    for c in copies:
        c.wait()


def chip_of(spot_ref, slot, size):
    if isinstance(slot, int):
        return slot
    dy, dx, dz, fixed_z = slot
    return ((spot_ref[0] ^ dy) * 2 + (spot_ref[1] ^ dx)) * size + (dz if fixed_z else spot_ref[2] ^ dz)


def collect(spot_ref, pieces, plan, size, held, sem, columns):
    copies = []
    for at, (piece, row, rows, slot, half) in enumerate(plan):
        place = chip_of(spot_ref, slot, size)
        if half is not None:
            place = place * 2 + (spot_ref[3] ^ half)
        start = pl.multiple_of(place * rows, math.gcd(rows, 512))
        copies.append(
            pltpu.make_async_copy(pieces[piece].at[pl.ds(row, rows)], held.at[pl.ds(start, rows), columns], sem.at[at])
        )
    return copies


def mix_kernel(count, plan, notes, size, width, side, spot_ref, u_ref, *refs):
    pieces, refs = refs[:count], refs[count:]
    first = side == 0
    before, refs = refs[: 0 if first else 2], refs[0 if first else 2 :]
    if not notes:
        gains_ref, refs = refs[0], refs[1:]
    own_ref, other_ref, w_ref, *refs = refs
    if notes:
        gains_ref, refs = refs[0], refs[1:]
    held, u, sem, u_sem, *refs = refs
    tiles = sums = refs[0] if refs else None
    w = held.shape[1]
    filters = held.shape[0] // width
    rows = own_ref.shape[0]
    copies = collect(spot_ref, pieces, plan, size, held, sem, slice(0, w))
    for at, (piece, row, slot) in enumerate(notes):
        copies.append(
            pltpu.make_async_copy(
                pieces[piece].at[pl.ds(row, NOTE)], tiles.at[chip_of(spot_ref, slot, size)], sem.at[len(plan) + at]
            )
        )
    third = filters // 3
    cols = [pl.ds(t * third * w, third * w) for t in range(3)]
    loads = [pltpu.make_async_copy(u_ref.at[side, :, c], u.at[:, c], u_sem.at[t]) for t, c in enumerate(cols)]
    adds = [pltpu.make_async_copy(ref, sums.at[g], u_sem.at[4 + g]) for g, ref in enumerate(before)]
    for c in copies + loads + adds:
        c.start()
    for c in copies:
        c.wait()
    give = pltpu.make_async_copy(held, w_ref, u_sem.at[3])
    give.start()
    if notes:
        lanes = width // len(notes)
        for b in range(width // 128):
            block = jnp.zeros((NOTE, 128), f32)
            for j in range(128 // lanes):
                tile = tiles[b * (128 // lanes) + j].astype(f32)
                block = block + (pltpu.roll(tile, j * lanes, 1) if j else tile)
            gains_ref[:, b * 128 : (b + 1) * 128] = block
    gain = gains_ref[0:1, pl.ds(pl.multiple_of((spot_ref[3] * 2 + side) * w, w), w)]
    result = None
    for t in range(3):
        wide = jnp.concatenate(
            [(held[k * width : (k + 1) * width].astype(f32) * gain).astype(bf) for k in range(t * third, (t + 1) * third)],
            axis=1,
        )
        loads[t].wait()
        part = dot(u[:, cols[t]], wide, NT)
        result = part if t == 0 else result + part
    for g, out in enumerate((own_ref, other_ref)):
        mine = result[g * rows : (g + 1) * rows]
        if not first:
            adds[g].wait()
            mine = mine + sums[g]
        out[...] = mine.astype(out.dtype)
    give.wait()


def mix_call(chain, spot, u, side, pieces, plan, notes, gains, size, width, before=()):
    rows, depth = u.shape[1:]
    w = pieces[0].shape[-1]
    total = depth // w * width
    step = rows // 2
    out = fixed(step, width)
    note = fixed(NOTE, width)
    given = () if notes else (gains,)
    made = 1 - len(given)
    return chain.call(
        functools.partial(mix_kernel, len(pieces), plan, notes, size, width, side), "mix",
        (spot, u, *pieces, *before, *given),
        [smem(), anywhere()] + [anywhere() for _ in (*pieces, *before)] + [note for _ in given],
        [out, out, anywhere()] + [note] * made,
        [shaped((step, width), f32), shaped((step, width), bf if before else f32), shaped((total, w), bf)]
        + [shaped((NOTE, width), f32)] * made,
        grid=(1,),
        scratch_shapes=[
            pltpu.VMEM((total, w), bf), pltpu.VMEM((rows, depth), bf),
            pltpu.SemaphoreType.DMA((len(plan) + len(notes),)), pltpu.SemaphoreType.DMA((6,)),
        ] + [pltpu.VMEM((len(notes), NOTE, 128), bf)] * made + [pltpu.VMEM((2, step, width), f32)] * min(1, len(before)),
    )


def hidden_kernel(source_ref, own_ref, came_ref, gain_ref, hidden_ref, *normed_refs):
    hidden = source_ref[...].astype(f32) + (own_ref[...] + came_ref[...].astype(f32))
    scale = lax.rsqrt(jnp.mean(hidden * hidden, axis=-1, keepdims=True) + NORM_EPS)
    hidden_ref[...] = hidden
    normed = (hidden * scale * gain_ref[1:2]).astype(bf)
    width = normed_refs[0].shape[1]
    for i, ref in enumerate(normed_refs):
        ref[...] = normed[:, i * width : (i + 1) * width]


def hidden_call(chain, source, own, came, gain, parts=2):
    rows, width = source.shape
    block = pl.BlockSpec((rows // parts, width), lambda i: (i, 0))
    thin = pl.BlockSpec((rows // parts, width // 2), lambda i: (i, 0))
    return chain.call(
        hidden_kernel, "hidden", (source, own, came, gain), [block, block, block, fixed(NOTE, width)],
        [block, thin, thin], [shaped((rows, width), f32)] + [shaped((rows, width // 2), bf)] * 2,
        grid=(parts,),
    )


def norm_back(grad, hat, scale, gain):
    weighted = grad * gain
    return scale * (weighted - hat * jnp.mean(weighted * hat, axis=-1, keepdims=True))


def add_rows(ref, values, step):
    total = jnp.sum(values, axis=0, keepdims=True)

    @pl.when(step == 0)
    def _():
        ref[...] = total

    @pl.when(step > 0)
    def _():
        ref[...] += total


def turn_kernel(lengths_ref, hidden_ref, back_ref, own_ref, came_ref, gain_ref, grad_ref, low_ref, gains_ref):
    hidden = hidden_ref[...]
    scale = lax.rsqrt(jnp.mean(hidden * hidden, axis=-1, keepdims=True) + NORM_EPS)
    hat = hidden * scale
    two = own_ref[...] + came_ref[...].astype(f32)
    back = live_rows(back_ref[...].astype(f32), lengths_ref, pl.program_id(0) * hidden.shape[0])
    grad = back + norm_back(two, hat, scale, gain_ref[1:2])
    grad_ref[...] = grad
    low_ref[...] = grad.astype(bf)
    add_rows(gains_ref, two * hat, pl.program_id(0))


def turn_call(chain, lengths, hidden, back, own, came, gain, parts=2):
    rows, width = hidden.shape
    block = pl.BlockSpec((rows // parts, width), lambda i: (i, 0))
    return chain.call(
        turn_kernel, "turn", (lengths, hidden, back, own, came, gain), [smem()] + [block] * 4 + [fixed(NOTE, width)],
        [block, block, fixed(1, width)],
        [shaped((rows, width), f32), shaped((rows, width), bf), shaped((1, width), f32)],
        grid=(parts,),
    )


def output_kernel(hidden_ref, own_ref, came_ref, out_ref):
    out_ref[...] = (hidden_ref[...] + (own_ref[...] + came_ref[...].astype(f32))).astype(bf)


def output_call(chain, hidden, own, came, parts=2):
    rows, width = hidden.shape
    block = pl.BlockSpec((rows // parts, width), lambda i: (i, 0))
    return chain.call(
        output_kernel, "output", (hidden, own, came), [block] * 3, block, shaped((rows, width), bf), grid=(parts,),
    )


def last_kernel(spot_ref, grad_ref, source_ref, own_ref, came_ref, gain_ref, out_ref, one):
    half = own_ref.shape[1]
    core = spot_ref[3]
    one[:, pl.ds(pl.multiple_of(core * half, half), half)] = own_ref[...]
    one[:, pl.ds(pl.multiple_of((1 - core) * half, half), half)] = came_ref[...]
    source = source_ref[...].astype(f32)
    scale = lax.rsqrt(jnp.mean(source * source, axis=-1, keepdims=True) + NORM_EPS)
    out_ref[...] = grad_ref[...] + norm_back(one[...], source * scale, scale, gain_ref[0:1])


def last_call(chain, spot, grad_hidden, source, own, came, gain, parts=2):
    rows, width = source.shape
    block = pl.BlockSpec((rows // parts, width), lambda i: (i, 0))
    thin = pl.BlockSpec((rows // parts, width // 2), lambda i: (i, 0))
    return chain.call(
        last_kernel, "last", (spot, grad_hidden, source, own, came, gain),
        [smem(), block, block, thin, thin, fixed(NOTE, width)], block, shaped((rows, width), f32),
        grid=(parts,), scratch_shapes=[pltpu.VMEM((rows // parts, width), f32)],
    )


def grad_kernel(slots, size, side, spot_ref, gains_ref, own_ref, other_ref, u_ref, *refs):
    outs, (turned, held, sem) = refs[:-3], refs[-3:]
    n, width = own_ref.shape
    w = held.shape[1]
    per = u_ref.shape[2] // w
    step = pl.program_id(0)

    @pl.when(step == 0)
    def _():
        turned[:, :n] = own_ref[...].T
        turned[:, n:] = other_ref[...].T

    gain = gains_ref[0:1, pl.ds(pl.multiple_of((spot_ref[3] * 2 + side) * w, w), w)]
    result = dot(turned[...], u_ref[0])
    for j in range(per):
        at = pl.multiple_of((step * per + j) * width, width)
        held[pl.ds(at, width), :] = (result[:, j * w : (j + 1) * w] * gain).astype(bf)

    @pl.when(step == pl.num_programs(0) - 1)
    def _():
        rows = held.shape[0] // len(slots)
        copies, at = [], 0
        for ref in outs:
            for b in range(ref.shape[0] // rows):
                start = pl.multiple_of(chip_of(spot_ref, slots[at], size) * rows, math.gcd(rows, 512))
                copies.append(
                    pltpu.make_async_copy(held.at[pl.ds(start, rows)], ref.at[pl.ds(b * rows, rows)], sem.at[at])
                )
                at += 1
        run_copies(copies)


def grad_call(chain, spot, gains, own, other, u, side, w, blocks, slots, size, per=9):
    rows, depth = u.shape[1:]
    n, width = own.shape
    count = depth // w
    each = count * width // len(slots)
    return chain.call(
        functools.partial(grad_kernel, slots, size, side), "mixer_grad", (spot, gains, own, other, u),
        [smem(), fixed(NOTE, width), fixed(n, width), fixed(n, width), pl.BlockSpec((1, rows, per * w), lambda i: (side, 0, i))],
        [anywhere() for _ in blocks], [shaped((b * each, w), bf) for b in blocks],
        grid=(count // per,),
        scratch_shapes=[
            pltpu.VMEM((width, rows), bf), pltpu.VMEM((count * width, w), bf), pltpu.SemaphoreType.DMA((len(slots),)),
        ],
    )


def gain_rows(rows_ref, one, two, core, wide):
    devices, half = rows_ref.shape[0], one.shape[1]
    lanes = 2 * half // devices
    if lanes < 1 or 128 % lanes or 2 * lanes > 128:
        return
    wide[...] = jnp.zeros_like(wide)
    wide[:, pl.ds(pl.multiple_of(core * half, half), half)] = jnp.broadcast_to(one, (8, half))
    lane = lax.broadcasted_iota(jnp.int32, (8, 128), 1)
    for i in range(devices):
        block, turn = divmod(i * lanes, 128)
        cols = slice(block * 128, (block + 1) * 128)
        pair = []
        for tile, at in ((wide[:, cols], 0), (jnp.broadcast_to(two[:, cols], (8, 128)), lanes)):
            shift = (at - turn) % 128
            pair.append(pltpu.roll(tile, shift, 1) if shift else tile)
        row = jnp.where(lane < lanes, pair[0], jnp.where(lane < 2 * lanes, pair[1], 0.0))
        rows_ref[i : i + 1, :] = row[:1]


def back_kernel(first, spot_ref, lengths_ref, came_ref, taps_ref, own_ref, other_ref, left_ref, right_ref, *refs):
    if first:
        own_before, other_before, own_hat, other_hat, two_ref, own_out, other_out, gains_ref, rows_ref, wide, *refs = refs
        before = own_before, other_before
    else:
        own_out, other_out, *refs = refs
    mask, low_low, low_high, high, v_low, v_high, ends = refs
    n = mask.shape[1]
    q, h, d = n // 4, n // 2, own_ref.shape[1]
    per = taps_ref.shape[1]

    @pl.when(pl.program_id(0) == 0)
    def _():
        find_ends(ends, lengths_ref, came_ref)
        for g in range(2):
            mask[g] = causal_mask(ends, g, n, True)
        low_low[...] = jnp.zeros_like(low_low)
        high[...] = jnp.zeros_like(high)
        for g, ref in enumerate((own_out, other_out)):
            ref[...] = before[g][...] if first else jnp.zeros_like(ref)

    for j in range(per):
        weight = jnp.concatenate([left_ref[j * d : (j + 1) * d], right_ref[j * d : (j + 1) * d]], axis=1)
        s = diagonals(taps_ref[0, j : j + 1, :], q)
        a = j * h
        for g, grad in enumerate((own_ref, other_ref)):
            v = dot(grad[...], weight).astype(bf)
            v_low[g, a : a + h] = v[:h]
            v_high[g, a : a + h] = v[h:]
            m = mask[g]
            low_low[g, 0:q, a : a + q] = s[:, :q] * m[0:q, 0:q]
            low_low[g, 0:q, a + q : a + h] = s[:, q : 2 * q] * m[0:q, q : 2 * q]
            low_low[g, q:h, a + q : a + h] = s[:, :q] * m[q:h, q:h]
            low_high[g, 0:q, a : a + h] = s[:, 2 * q : 4 * q] * m[0:q, h:]
            low_high[g, q:h, a : a + h] = s[:, q : 3 * q] * m[q:h, h:]
            high[g, 0:q, a : a + h] = s[:, 0 : 2 * q] * m[h : h + q, h:]
            high[g, q:h, a + q : a + h] = s[:, 0:q] * m[h + q :, h + q :]
    for g, out in enumerate((own_out, other_out)):
        out[:h] += dot(low_low[g], v_low[g]) + dot(low_high[g], v_high[g])
        out[h:] += dot(high[g], v_high[g])
    if first:

        @pl.when(pl.program_id(0) == pl.num_programs(0) - 1)
        def _():
            products = own_out[...] * own_hat[...].astype(f32) + other_out[...] * other_hat[...].astype(f32)
            one = jnp.sum(products, axis=0, keepdims=True)
            gains_ref[...] = one
            gain_rows(rows_ref, one, two_ref, spot_ref[3], wide)


def back_call(chain, spot, lengths, taps, own, other, weights, first, steps, before=(), hats=(), two=None, devices=0):
    blocks, per, n = taps.shape
    rows, d = own.shape
    w = weights[0].shape[1]
    width = 2 * w
    scratch = lambda *s: pltpu.VMEM(s, bf)
    weight = pl.BlockSpec((per * d, w), lambda i: (i + first, 0))
    half = fixed(rows, width)
    more = (*before, *hats, two) if before else ()
    outs, shapes = [half] * 2, [shaped((rows, width), f32)] * 2
    scratches = [
        scratch(2, n, n), scratch(2, n // 2, per * n // 2),
        scratch(2, n // 2, per * n // 2), scratch(2, n // 2, per * n // 2),
        scratch(2, per * n // 2, width), scratch(2, per * n // 2, width), pltpu.SMEM((2, 3), jnp.int32),
    ]
    if before:
        outs = outs + [fixed(1, width), fixed(devices, 128)]
        shapes = shapes + [shaped((1, width), f32), shaped((devices, 128), f32)]
        scratches = [pltpu.VMEM((8, 2 * width), f32)] + scratches
    return chain.call(
        functools.partial(back_kernel, first), "spread_back", (spot, *lengths, taps, own, other, *weights, *more),
        [smem()] * 3 + [pl.BlockSpec((1, per, n), lambda i: (i + first, 0, 0)), fixed(rows, d), fixed(rows, d)]
        + [weight, weight] + [fixed(*v.shape) for v in more],
        outs, shapes, grid=(steps,), scratch_shapes=scratches,
    )


def flat(v):
    return v.reshape(-1, v.shape[-1])


def ffn_kernel(count, outs, steps, slots, out_slots, size, crossed, spot_ref, lengths_ref, came_ref, *refs):
    turned = spot_ref[3] if crossed else 0
    tokens, pieces, refs = refs[:6], refs[6 : 6 + count], refs[6 + count :]
    results, grads, (held, dealt, normed, back, sums, sem) = refs[:4], refs[4 : 4 + outs], refs[4 + outs :]
    n = tokens[0].shape[0]
    chips, units, width = held.shape[0], held.shape[1] * 2 // 3, held.shape[2]
    own, half = chips // 2 // steps, units // 2
    step = pl.program_id(0)

    @pl.when(step == 0)
    def _():
        copies, at = [], 0
        for ref in pieces:
            for b in range(ref.shape[0]):
                chip = chip_of(spot_ref, slots[at], size)
                copies.append(
                    pltpu.make_async_copy(ref.at[b, pl.ds(0, units)], held.at[chip, pl.ds(0, units)], sem.at[0, at])
                )
                copies.append(
                    pltpu.make_async_copy(
                        ref.at[b, pl.ds(units, half)], held.at[chip ^ turned, pl.ds(units, half)], sem.at[1, at]
                    )
                )
                at += 1
        for c in copies:
            c.start()
        half_width = tokens[0].shape[1]
        for i in range(2):
            cols = slice(i * half_width, (i + 1) * half_width)
            normed[:n, cols], normed[n:, cols] = tokens[i][...], tokens[2 + i][...]
        back[:n] = live_rows(tokens[4][...].astype(f32), lengths_ref).astype(bf)
        back[n:] = live_rows(tokens[5][...].astype(f32), came_ref).astype(bf)
        for c in copies:
            c.wait()

    w_gate = flat(held[pl.ds(step * own, own), 0:units])
    w_up = flat(held[pl.ds(chips // 2 + step * own, own), 0:units])
    w_down = flat(held[pl.ds(step * 2 * own, 2 * own), units : units + half])
    gate, up = dot(normed[...], w_gate, NT), dot(normed[...], w_up, NT)
    grad_act = dot(back[...], w_down, NT)
    sigma = 1.0 / (1.0 + jnp.exp(-gate))
    swish = gate * sigma
    act = (swish * up).astype(bf)
    grad_gate = (grad_act * up * (sigma * (1.0 + gate * (1.0 - sigma)))).astype(bf)
    grad_up = (grad_act * swish).astype(bf)
    branch = dot(act, w_down)
    two = dot(jnp.concatenate([grad_gate, grad_up], axis=1), jnp.concatenate([w_gate, w_up], axis=0))
    for i, value in enumerate((branch, two)):
        if steps > 1:

            @pl.when(step == 0)
            def _():
                sums[i] = value

            @pl.when((step > 0) & (step < steps - 1))
            def _():
                sums[i] += value

        @pl.when(step == steps - 1)
        def _():
            total = value + sums[i] if steps > 1 else value
            results[2 * i][...] = total[:n]
            results[2 * i + 1][...] = total[n:].astype(bf)

    put = lambda v: v.astype(bf).reshape(own, units, width)
    dealt[pl.ds(step * own, own), 0:units] = put(dot(grad_gate, normed[...], TN))
    dealt[pl.ds(chips // 2 + step * own, own), 0:units] = put(dot(grad_up, normed[...], TN))
    grad_down = dot(act, back[...], TN).astype(bf)
    for b in range(2 * own):
        dealt[(step * 2 * own + b) ^ turned, units : units + half] = grad_down[b * half : (b + 1) * half]

    @pl.when(step == steps - 1)
    def _():
        copies, at = [], 0
        for ref in grads:
            for b in range(ref.shape[0]):
                copies.append(
                    pltpu.make_async_copy(dealt.at[chip_of(spot_ref, out_slots[at], size)], ref.at[b], sem.at[0, at])
                )
                at += 1
        run_copies(copies)


def ffn_call(chain, spot, lengths, tokens, pieces, blocks, slots, out_slots, size, crossed, chunk=1024):
    n, d = tokens[-1].shape
    chips, rows = len(slots), pieces[0].shape[1]
    units = rows * 2 // 3
    steps = chips // 2 * units // chunk
    return chain.call(
        functools.partial(ffn_kernel, len(pieces), len(blocks), steps, slots, out_slots, size, crossed), "ffn",
        (spot, *lengths, *tokens, *pieces),
        [smem()] * 3 + [fixed(*v.shape) for v in tokens] + [anywhere() for _ in pieces],
        [fixed(n, d)] * 4 + [anywhere() for _ in blocks],
        [shaped((n, d), f32), shaped((n, d), bf)] * 2 + [shaped((b, rows, d), bf) for b in blocks],
        grid=(steps,),
        scratch_shapes=[
            pltpu.VMEM((chips, rows, d), bf), pltpu.VMEM((chips, rows, d), bf),
            pltpu.VMEM((2 * n, d), bf), pltpu.VMEM((2 * n, d), bf), pltpu.VMEM((2, 2 * n, d), f32),
            pltpu.SemaphoreType.DMA((2, chips)),
        ],
    )


def normed_kernel(spot_ref, own_ref, other_ref, own_out, other_out, full):
    half = own_out.shape[1]
    cols = pl.ds(pl.multiple_of(spot_ref[3] * half, half), half)
    for ref, out in ((own_ref, own_out), (other_ref, other_out)):
        source = ref[...].astype(f32)
        scale = lax.rsqrt(jnp.mean(source * source, axis=-1, keepdims=True) + NORM_EPS)
        full[...] = (source * scale).astype(bf)
        out[...] = full[:, cols]


def normed_call(chain, spot, own, other, parts=2):
    rows, width = own.shape
    block = pl.BlockSpec((rows // parts, width), lambda i: (i, 0))
    thin = pl.BlockSpec((rows // parts, width // 2), lambda i: (i, 0))
    return chain.call(
        normed_kernel, "normed", (spot, own, other), [smem(), block, block],
        [thin] * 2, [shaped((rows, width // 2), bf)] * 2,
        grid=(parts,), scratch_shapes=[pltpu.VMEM((rows // parts, width), bf)],
    )


def live_rows(values, lengths_ref, first=0):
    total = lengths_ref[0, 0] + lengths_ref[0, 1] + lengths_ref[0, 2]
    place = lax.broadcasted_iota(jnp.int32, (values.shape[0], 1), 0) + first
    return jnp.where(place < total, values, jnp.zeros((), values.dtype))


def pack_kernel(
    spot_ref, mixer_ref, gate_up_ref, down_ref, gains_ref, mixer_mine, mixer_theirs, gate_mine, gate_theirs, down_low, note
):
    half, units, core = mixer_mine.shape[1], gate_mine.shape[0], spot_ref[3]
    for ref, cols, rows, c in ((mixer_mine, half, units, core), (mixer_theirs, half, units, 1 - core)):
        ref[...] = mixer_ref[:, pl.ds(pl.multiple_of(c * half, half), half)].astype(bf)
    for ref, c in ((gate_mine, core), (gate_theirs, 1 - core)):
        ref[:units] = gate_up_ref[pl.ds(pl.multiple_of(c * units, units), units), :].astype(bf)
    count, own = gains_ref.shape
    note[...] = jnp.zeros_like(note)
    note[:count, :own] = gains_ref[...].astype(bf)
    gate_theirs[units:] = jnp.zeros((note.shape[0], gate_theirs.shape[1]), bf)
    gate_theirs[units:, : note.shape[1]] = note[...]
    down_low[...] = down_ref[...].astype(bf)


def pack_call(chain, spot, mixer, gate_up, down, gains):
    (rows, width), (units, _), (half, _) = mixer.shape, gate_up.shape, down.shape
    shapes = [(rows, width // 2)] * 2 + [(units // 2, width), (units // 2 + NOTE, width), (half, width), (NOTE, 128)]
    return chain.call(
        pack_kernel, "pack", (spot, mixer, gate_up, down, gains),
        [smem(), fixed(rows, width), fixed(units, width), fixed(half, width), fixed(*gains.shape)],
        [fixed(*s) for s in shapes], [shaped(s, bf) for s in shapes], grid=(1,),
    )


def block_kernel(own_gains, spot_ref, mine_ref, came_ref, note_ref, gate_ref, all_ref, copies_ref):
    rows, w = mine_ref.shape[0], all_ref.shape[1]
    mine = note_ref[...].astype(f32)
    came = gate_ref[gate_ref.shape[0] - NOTE :, :w].astype(f32)
    turned = lambda v: pltpu.roll(v, own_gains, 1)
    note = jnp.where(spot_ref[3] == 0, mine + turned(came), came + turned(mine)).astype(bf)
    at = 0
    for side in range(2):
        cols = slice(side * w, (side + 1) * w)
        all_ref[at : at + rows] = mine_ref[:, cols]
        all_ref[at + rows : at + 2 * rows] = came_ref[:, cols]
        all_ref[at + 2 * rows : at + 2 * rows + NOTE] = note
        at += 2 * rows + NOTE
    count = 2 * rows + NOTE
    for c in range(copies_ref.shape[0] // count):
        copies_ref[c * count : (c + 1) * count] = all_ref[:count]


def block_call(chain, spot, mine, came, note, gate_came, own_gains, copies, waits):
    rows, width = mine.shape
    w = width // 2
    each = 2 * rows + NOTE
    return chain.call(
        functools.partial(block_kernel, own_gains), "block", (spot, mine, came, note, gate_came),
        [smem()] + [fixed(*v.shape) for v in (mine, came, note, gate_came)],
        [fixed(2 * each, w), fixed(copies * each, w)], [shaped((2 * each, w), bf), shaped((copies * each, w), bf)],
        grid=(1,), waits=waits,
    )


def stack_kernel(count, moves, spot_ref, *refs):
    for i, a, rows, o, b in moves:
        if not isinstance(a, int):
            stride, distance, first = a
            a = pl.multiple_of((spot_ref[2] ^ distance) * stride + first, NOTE)
        refs[count + o][b : b + rows] = refs[i][pl.ds(a, rows)]


def stack_call(chain, spot, arrays, rows, moves, waits=()):
    like = {o: arrays[i] for i, _, _, o, _ in moves}
    shapes = [(r,) + like[o].shape[1:] for o, r in enumerate(rows)]
    return chain.call(
        functools.partial(stack_kernel, len(arrays), moves), "stack", (spot, *arrays),
        [smem()] + [fixed(*v.shape) for v in arrays],
        [fixed(*s) for s in shapes], [shaped(s, like[o].dtype) for o, s in enumerate(shapes)], grid=(1,), waits=waits,
    )


def corner_kernel(cut, extra, x_ref, y_ref, to_x_ref, to_y_ref):
    rows = x_ref.shape[0]
    to_x_ref[:cut] = y_ref[:cut]
    if extra:
        to_x_ref[cut:] = y_ref[rows - extra :]
    to_y_ref[...] = x_ref[cut : rows - extra]


def corner_call(chain, from_x, from_y, extra):
    total, width = from_x.shape
    cut = (total - extra) // 2
    shapes = [(cut + extra, width), (cut, width)]
    return chain.call(
        functools.partial(corner_kernel, cut, extra), "corner", (from_x, from_y), [fixed(total, width)] * 2,
        [fixed(*s) for s in shapes], [shaped(s, bf) for s in shapes], grid=(1,),
    )


def near_kernel(to_x_ref, to_y_ref, by_x_ref, by_y_ref, new_x_ref, new_y_ref):
    new_x_ref[...] = (to_x_ref[...].astype(f32) + by_y_ref[...].astype(f32)).astype(bf)
    new_y_ref[...] = (to_y_ref[...].astype(f32) + by_x_ref[...].astype(f32)).astype(bf)


def near_call(chain, to_x, to_y, by_x, by_y, parts=2, **options):
    rows, width = by_x.shape
    block = (rows // parts, width)
    low, high = pl.BlockSpec(block, lambda i: (i, 0)), pl.BlockSpec(block, lambda i: (i + parts, 0))
    return chain.call(
        near_kernel, "near", (to_x, to_y, by_x, by_y), [high, low, low, low], [high, low],
        [shaped(to_x.shape, bf), shaped(to_y.shape, bf)], grid=(parts,), input_output_aliases={0: 0, 1: 1}, **options,
    )


def line_kernel(count, *refs):
    parts, refs = refs[:count], refs[count:]
    rows = refs[-1].shape[0]

    def total(at):
        result = parts[0][pl.ds(at, rows)].astype(f32)
        for ref in parts[1:]:
            result = result + ref[pl.ds(at, rows)].astype(f32)
        return result

    for s, ref in enumerate(refs):
        ref[...] = total(s * rows).astype(ref.dtype)


def line_call(chain, parts, size, apart, **options):
    quarters = 4 if len(parts) == 1 else 1
    rows, width = parts[0].shape[0] // quarters // size, parts[0].shape[1]
    if apart:
        whole = lambda q: pl.BlockSpec((size * rows, width), lambda i: (q, 0))
        ins = [whole(q) for q in range(quarters)] if quarters > 1 else [whole(0)] * len(parts)
        specs = [fixed(rows, width)] * size
        shapes = [shaped((rows, width), f32)] + [shaped((rows, width), bf)] * (size - 1)
        steps = 1
    else:
        steps = 2
        half = size * rows // steps
        ins = [pl.BlockSpec((half, width), lambda i, q=q: (i + q * steps, 0)) for q in range(quarters)]
        ins = ins if quarters > 1 else ins * len(parts)
        specs, shapes = [pl.BlockSpec((half, width), lambda i: (i, 0))], [shaped((size * rows, width), bf)]
    parts = parts * quarters
    return chain.call(
        functools.partial(line_kernel, len(parts)), "line", parts, ins, specs, shapes, grid=(steps,), **options
    )


def finish_kernel(cuts, count, note, spot_ref, first_ref, *refs):
    came, more, outs, squares_ref, total = (
        refs[:count], refs[count : -len(cuts) - 2], refs[-len(cuts) - 2 : -2], refs[-2], refs[-1]
    )
    rows = total.shape[0]
    result = first_ref[:rows].astype(f32)
    for b in range(1, first_ref.shape[0] // rows):
        result = result + first_ref[b * rows : (b + 1) * rows].astype(f32)
    for ref in came:
        result = result + ref[...].astype(f32)
    total[...] = result
    squares = jnp.sum(result * result, axis=0, keepdims=True)
    if note:
        whole = jnp.sum(squares, axis=1, keepdims=True)
        for ref in more[:-1]:
            whole = whole + jnp.sum(ref[...], axis=1, keepdims=True)
        gains = jnp.sum(more[-1][...], axis=0, keepdims=True)
        squares = jnp.broadcast_to(whole + jnp.sum(gains * gains, axis=1, keepdims=True), squares_ref.shape)
    squares_ref[...] = squares
    for ref, start in zip(outs, cuts):
        rows = ref.shape[0]
        if not isinstance(start, int):
            start = pl.multiple_of((spot_ref[3] ^ start[0]) * rows, rows & -rows)
        ref[...] = total[pl.ds(start, rows), :]


def finish_call(chain, spot, first, came, blocks, cuts, note=0, more=(), waits=()):
    rows, width = first.shape[0] // blocks, first.shape[1]
    shapes = [(r, width) for _, r in cuts] + [(note, 128) if note else (1, width)]
    return chain.call(
        functools.partial(finish_kernel, [c for c, _ in cuts], len(came), note), "finish", (spot, first, *came, *more),
        [smem(), fixed(*first.shape)] + [fixed(rows, width)] * len(came) + [fixed(*v.shape) for v in more],
        [fixed(*s) for s in shapes], [shaped(s, f32) for s in shapes],
        grid=(1,), scratch_shapes=[pltpu.VMEM((rows, width), f32)], waits=waits,
    )


def adam_step(weight, grad, first, second, rate, decay):
    first_new = BETA_ONE * first + (1.0 - BETA_ONE) * grad
    second_new = BETA_TWO * second + (1.0 - BETA_TWO) * grad * grad
    corr_one = 1.0 / (1.0 - BETA_ONE**STEP)
    corr_two = 1.0 / (1.0 - BETA_TWO**STEP)
    update = first_new * (rate * corr_one) / (jnp.sqrt(second_new * corr_two) + ADAM_EPS)
    return (weight * (1.0 - rate * decay) - update, first_new, second_new)


def adam_kernel(spot_ref, note_ref, *refs):
    ins, outs, wide, tall = refs[:21], refs[21:35], refs[35], refs[36]
    mixer, gate_up, down, gains, parts = ins[:4], ins[4:7], ins[7:10], ins[10:13], ins[13:]
    mixer_out, gate_up_out, down_out, gains_out, norm_out = outs[:4], outs[4:7], outs[7:10], outs[10:13], outs[13]
    core, quarter = spot_ref[3], parts[0].shape[1]
    norm = jnp.sqrt(jnp.sum(note_ref[...], axis=0, keepdims=True)[:, :1])
    factor = CLIP_LIMIT / jnp.maximum(norm, CLIP_LIMIT)

    for s in range(2):
        mine = pl.multiple_of(core * 2 * quarter, quarter) + s * quarter
        came = pl.multiple_of((1 - core) * 2 * quarter, quarter) + s * quarter
        wide[:, pl.ds(pl.multiple_of(mine, quarter), quarter)] = parts[s][...]
        wide[:, pl.ds(pl.multiple_of(came, quarter), quarter)] = parts[2 + s][...]
    old, first, second, average = (r[...] for r in mixer)
    new, first, second = adam_step(old, wide[...] * factor, first, second, RATE_MATRIX, DECAY_MATRIX)
    average = AVERAGE_KEEP * average + (1.0 - AVERAGE_KEEP) * new
    for ref, value in zip(mixer_out, (new, first, second, average)):
        ref[...] = value

    @pl.when(pl.program_id(0) == 0)
    def _():
        half = parts[4].shape[0]
        tall[pl.ds(pl.multiple_of(core * half, half), half), :] = parts[4][...]
        tall[pl.ds(pl.multiple_of((1 - core) * half, half), half), :] = parts[5][...]
        own = gains[0].shape[1]
        sums = jnp.sum(parts[7][...], axis=0, keepdims=True)
        gain_grad = jnp.concatenate([sums[:, :own], sums[:, own : 2 * own]])
        for olds, news, grad, rate, decay in (
            (gate_up, gate_up_out, tall[...], RATE_MATRIX, DECAY_MATRIX),
            (down, down_out, parts[6][...], RATE_MATRIX, DECAY_MATRIX),
            (gains, gains_out, gain_grad, RATE_GAIN, 0.0),
        ):
            old, first, second = (r[...] for r in olds)
            scale = factor if rate == RATE_MATRIX else factor[:, :1]
            for ref, value in zip(news, adam_step(old, grad * scale, first, second, rate, decay)):
                ref[...] = value
        norm_out[...] = norm


def adam_call(chain, spot, note, mixer, gate_up, down, gains, parts, blocks=1):
    rows, width = mixer[0].shape
    step = rows // blocks
    block = pl.BlockSpec((step, width), lambda i: (i, 0))
    piece = pl.BlockSpec((step, parts[0].shape[1]), lambda i: (i, 0))
    whole = lambda v: fixed(*v.shape)
    others = [*gate_up, *down, *gains]
    shapes = [v.shape for v in (*mixer, *others)] + [(1, 1)]
    return chain.call(
        adam_kernel, "adam", (spot, note, *mixer, *others, *parts),
        [smem(), whole(note)] + [block] * 4 + [whole(v) for v in others] + [piece] * 4
        + [whole(v) for v in parts[4:]],
        [block] * 4 + [whole(v) for v in others] + [fixed(1, 1)], [shaped(s, f32) for s in shapes],
        grid=(blocks,),
        scratch_shapes=[pltpu.VMEM((step, width), f32), pltpu.VMEM(gate_up[0].shape, f32)],
    )


def flip(v, axis, bits=1):
    size = lax.axis_size(axis)
    return lax.ppermute(v, axis, [(i, i ^ bits) for i in range(size)])


def swap(v):
    return flip(v, "core")


def join(mine, other, core, axis=0):
    return jnp.where(
        core == 0,
        jnp.concatenate([mine, other], axis=axis),
        jnp.concatenate([other, mine], axis=axis),
    )


def part(v, index, axis=0):
    size = v.shape[axis] // 2
    return lax.dynamic_slice_in_dim(v, index * size, size, axis)


def low(v):
    return v.astype(bf)


def wide(v):
    return v.astype(f32)


class Whole:
    crossed = False
    mixer_slots = ((0,), (0,))
    mixer_blocks = (1,)

    def __init__(self, spot, groups):
        self.spot, self.core = spot, spot[3]
        self.size = lax.axis_size("z")
        self.chips = lax.axis_size("d0") * lax.axis_size("d1") * self.size
        self.ffn_in = self.ffn_out = tuple(range(groups))
        self.ffn_blocks = (groups,)

    def gather(self, chain, mixer, gate_up, down, gains, waits):
        def trade(v, axis):
            return join(part(v, self.core, axis), swap(part(v, 1 - self.core, axis)), self.core)

        everything = lambda v: lax.all_gather(v, CHIPS, axis=0, tiled=True)
        mixer_block = trade(low(mixer), 1)
        w, groups = mixer_block.shape[1] // 2, len(self.ffn_in)
        sides = []
        for s in range(2):
            whole = everything(mixer_block[:, s * w : (s + 1) * w])
            sides.append(([whole], ((0, 0, whole.shape[0], 0, None),), ()))
        ffn = [everything(v).reshape(groups, -1, v.shape[1]) for v in (trade(low(gate_up), 0), low(down))]
        ffn = [jnp.concatenate(ffn, axis=1)]
        gains = lax.all_gather(wide(low(gains)), EVERY, axis=1, tiled=True)
        yield jnp.pad(gains, ((0, NOTE - 2), (0, 0)))
        while True:
            yield sides, ffn

    def scatter(self, chain, parts, cuts, groups=1, apart=False):
        grads = parts[0].reshape(groups, -1, parts[0].shape[-1])
        rows = grads.shape[1] * 2 // 3
        if groups > 1:
            shards = [grads[:, :rows], grads[:, rows:]]
        else:
            shards = [grads]
        shards = [wide(lax.psum_scatter(flat(v), CHIPS, scatter_dimension=0, tiled=True)) for v in shards]
        outs = [part(shards[0], self.core), part(shards[0], 1 - self.core)] + shards[1:]
        squares = sum(jnp.sum(v * v, axis=0, keepdims=True) for v in shards)
        if groups == 1:
            yield
            yield ()
        through = yield ()
        yield (), through
        yield
        yield outs + [squares]

    def spread_gains(self, grads, rows):
        one, two = grads
        nothing = jnp.zeros_like(one)
        one = join(one, nothing, self.core, 1)
        return lax.psum_scatter(jnp.concatenate([one, two]), EVERY, scatter_dimension=1, tiled=True)

    def total(self, v):
        return lax.psum(v, EVERY)


class Cube(Whole):
    crossed = True
    near = ((0, 0), (0, 1), (1, 0), (1, 1))

    def __init__(self, spot, groups):
        super().__init__(spot, groups)
        slots = lambda fixed_z: tuple((y, x, s, fixed_z) for y, x in self.near for s in range(self.size))
        self.mixer_slots = slots(False), slots(True)
        self.ffn_in = slots(True)
        self.ffn_out = tuple((y, x, z, True) for z in range(self.size) for y, x in self.near)
        self.mixer_blocks = (self.size,) * 3 + (self.size // 2,) * 2

    def lines(self, block):
        return [flip(block, "z", s) for s in range(1, self.size)]

    def gather(self, chain, mixer, gate_up, down, gains, waits):
        spot = self.spot
        mixer_mine, mixer_theirs, gate_mine, gate_theirs, down_low, note = pack_call(
            chain, spot, mixer, gate_up, down, gains
        )
        gate_came = swap(gate_theirs)
        size = self.size
        own, block = block_call(
            chain, spot, mixer_mine, swap(mixer_theirs), note, gate_came, gains.shape[1], size, waits
        )
        line = self.along_z(block)
        own_x, own_y = flip(own, "d1"), flip(own, "d0")
        yield None
        rows = own.shape[0] // 2 - NOTE
        half = rows // 2
        sides = []

        def spread_out(line):
            return line, flip(line, "d1"), flip(line, "d0")

        def turn_corner(from_x, from_y, extra=0):
            to_x, to_y = corner_call(chain, from_x, from_y, extra)
            return flip(to_x, "d1"), flip(to_y, "d0")

        def plan(side):
            found = [(p, side * (rows + NOTE) + h * half, half, near + (0, False), h) for p, near in enumerate(self.near[:3]) for h in range(2)]
            found += [(3, h * half, half, (1, 1, 0, False), h) for h in range(2)]
            last = (size - 1) * 2
            for at in range(last):
                s, h = at // 2 + 1, at % 2
                found += [(4 + p, at * half, half, near + (s, False), h) for p, near in enumerate(self.near[:3])]
                found.append((7 + (at >= last // 2), at % (last // 2) * half, half, (1, 1, s, False), h))
            return tuple(found)

        corner = turn_corner(own_x, own_y)
        yield
        chain.pause(corner)
        others, line_rows = range(1, size), (size - 1) * rows
        moves = [(0, (rows + NOTE, s, 0), rows, 0, (s - 1) * rows) for s in others]
        moves += [(0, (rows + NOTE, s, rows), NOTE, 0, line_rows + (s - 1) * NOTE) for s in others]
        moves += [(1, rows + NOTE, rows, 1, s * rows) for s in range(size)]
        line, block = stack_call(
            chain, spot, (line, own), (line_rows + (size - 1) * NOTE, size * rows), tuple(moves)
        )
        first = spread_out(line)
        line = self.along_z(block)
        yield
        first_corner = turn_corner(*first[1:], (size - 1) * NOTE)
        notes = [(p, rows, near + (0, False)) for p, near in enumerate(self.near)]
        for s in others:
            notes += [(4 + p, line_rows + (s - 1) * NOTE, near + (s, False)) for p, near in enumerate(self.near[:3])]
            notes.append((7, line_rows // 2 + (s - 1) * NOTE, (1, 1, s, False)))
        sides.append(([own, own_x, own_y, corner[0], *first, *first_corner], plan(0), tuple(notes)))
        units, count = gate_mine.shape[0], down_low.shape[0]
        ffn_rows = 2 * units + count
        moves = [(0, (rows, s, 0), rows, 0, (s - 1) * rows) for s in others]
        for s in range(size):
            at = s * ffn_rows
            moves += [(1, 0, units, 1, at), (2, 0, units, 1, at + units), (3, 0, count, 1, at + 2 * units)]
        line, block = stack_call(
            chain, spot, (line, gate_mine, gate_came, down_low), (line_rows, size * ffn_rows), tuple(moves)
        )
        across, line = line, self.along_z(block)
        second = spread_out(*chain.pause(first_corner, (across,)))
        yield sides, None
        second_corner = turn_corner(*second[1:])
        sides.append(([own, own_x, own_y, corner[1], *second, *second_corner], plan(1), ()))
        ffn = spread_out(*chain.pause(second_corner, (line,)))
        yield sides, None
        ffn = (*ffn, *turn_corner(*ffn[1:]))
        yield sides, [v.reshape(-1, ffn_rows, v.shape[-1]) for v in ffn]

    def along_z(self, v):
        return lax.all_to_all(v, "z", 0, 0, tiled=True)

    def scatter(self, chain, parts, cuts, groups=1, apart=False):
        if groups > 1:
            came = (self.along_z(flat(parts[0])),)
        else:
            own, to_x, to_y, far_low, far_high = (flat(v) for v in parts)
            by_x, by_y = flip(far_low, "d1"), flip(far_high, "d0")
            yield
            to_x, to_y = yield near_call(chain, to_x, to_y, by_x, by_y)
            came = own, flip(to_x, "d1"), flip(to_y, "d0")
        through = yield came
        outs = line_call(chain, came, self.size, apart, through=through or ())
        count = self.size if apart else 1
        first, *rest = yield outs[:count], outs[count:]
        if groups > 1:
            to_x, to_y, far = rest
            far = lax.ppermute(far, ("d0", "d1"), [(i, i ^ 3) for i in range(4)])
            came = flip(to_x, "d1"), flip(to_y, "d0"), far
        elif apart:
            came = [flip(v, "z", s + 1) for s, v in enumerate(rest)]
        else:
            first, came = self.along_z(first), ()
        more, waits = yield
        yield finish_call(
            chain, self.spot, first, came, 1 if apart else self.size, cuts, 2 * self.chips if more else 0, more, waits
        )

    def spread_gains(self, grads, rows):
        return self.everyone(rows)

    def everyone(self, rows):
        return lax.all_to_all(rows, EVERY, 0, 0, tiled=True)


def body(
    inputs, lengths, filters, cotangent, mixer_weight, gate_up_weight, down_weight, norm_gains,
    mixer_first, gate_up_first, down_first, gains_first,
    mixer_second, gate_up_second, down_second, gains_second, mixer_average,
):
    slots, width = inputs.shape
    size = lax.axis_size("z")
    groups = 2 * FF // 256
    cube = lax.axis_size("d0") == 2 and lax.axis_size("d1") == 2 and size == 4
    spot = jnp.stack([lax.axis_index(a) for a in EVERY]).astype(jnp.int32)
    core = spot[3]
    links = (Cube if cube else Whole)(spot, groups)
    units = gate_up_weight.shape[0]
    chain = Chain()

    sums = lengths, swap(lengths)
    source_other, cotangent_other = swap(inputs), swap(cotangent)
    taps = jnp.concatenate([wide(filters), jnp.eye(AR_ORDER, slots, dtype=f32)])
    taps_turned = jnp.roll(taps[:, ::-1], 1 - slots // 4, axis=1)
    taps, taps_turned = (v.reshape(-1, 3, slots) for v in (taps, taps_turned))

    weights = links.gather(
        chain, mixer_weight, gate_up_weight, down_weight, norm_gains, (sums[1], source_other, cotangent_other)
    )
    gains = next(weights)
    tokens = hat_tokens = normed_call(chain, spot, inputs, source_other)
    blocks = taps.shape[0]
    cuts, spread = (0, blocks // 3, blocks * 4 // 9, blocks), None
    for at in range(3):
        spread = spread_call(chain, sums, taps_turned, *tokens, cuts[at], cuts[at + 1] - cuts[at], spread)
        sides = next(weights)
    sides, _ = sides
    quarter = sides[0][0][0].shape[1]
    *mixed, left, gains = (*mix_call(chain, spot, spread, 0, *sides[0], gains, size, width), gains)[:4]
    sides, _ = next(weights)
    mixed_own, mixed_other, right = mix_call(chain, spot, spread, 1, *sides[1], gains, size, width, mixed)
    _, ffn = next(weights)

    hidden, *normed_two = hidden_call(chain, inputs, mixed_own, swap(mixed_other), gains)
    tokens = (*normed_two, *(swap(v) for v in normed_two), cotangent, cotangent_other)
    branch_own, branch_other, two_own, two_other, *grad_ffn = ffn_call(
        chain, spot, sums, tokens, ffn, links.ffn_blocks, links.ffn_in, links.ffn_out, size, links.crossed
    )
    if cube:
        grad_ffn = chain.pause(through=grad_ffn)
    ffn_sum = links.scatter(chain, grad_ffn, ((0, units // 2), (units // 2, units // 2), (units, units // 2)), groups, True)
    ffn_came = next(ffn_sum)
    grad_hidden, grad_low, gains_two = turn_call(
        chain, lengths, hidden, cotangent, two_own, swap(two_other), gains
    )
    grad_other = swap(grad_low)
    rows = mixer_weight.shape[0]
    cuts = (((0,), rows), ((1,), rows))
    grads_of = lambda s: grad_call(
        chain, spot, gains, grad_low, grad_other, spread, s, quarter, links.mixer_blocks, links.mixer_slots[s], size
    )
    first_sum = links.scatter(chain, grads_of(0), cuts, apart=True)
    next(first_sum)
    second_sum = links.scatter(chain, grads_of(1), cuts)
    next(second_sum)
    backward = lambda first, steps, *more: back_call(
        chain, spot, sums, taps, grad_low, grad_other, (left, right), first, steps, *more
    )
    early = blocks // 2
    first_sum.send(next(first_sum))
    one = backward(0, early)
    second_sum.send(next(second_sum))
    one_own, one_other, gains_one, note_rows = backward(
        early, blocks - early, one, hat_tokens, gains_two, 2 * links.chips
    )
    outs, _ = first_sum.send(())
    first_sum.send(outs)
    if cube:
        (note_rows,) = chain.pause(ffn_came, (note_rows,))
    shard_gains = links.spread_gains((gains_one, gains_two), note_rows)
    outs, _ = second_sum.send(())
    chain.pause((shard_gains,))
    first_mine, first_theirs, square = first_sum.send(((), ()))
    first_theirs, branch_other, *outs = chain.pause(through=(first_theirs, branch_other, *outs))
    second_sum.send(outs)
    outs, _ = ffn_sum.send(())
    ffn_sum.send(outs)
    output = output_call(chain, hidden, branch_own, swap(branch_other))
    input_grad = last_call(chain, spot, grad_hidden, inputs, one_own, swap(one_other), gains)
    gate_up_mine, gate_up_theirs, shard_down, *squares = ffn_sum.send(((), ()))
    squares.append(square)
    gate_up_came, first_came = swap(gate_up_theirs), swap(first_theirs)
    second_mine, second_theirs, note = second_sum.send(((*squares, shard_gains), ()))
    second_came = swap(second_theirs)
    mixer = mixer_weight, mixer_first, mixer_second, mixer_average
    gate_up, down = (gate_up_weight, gate_up_first, gate_up_second), (down_weight, down_first, down_second)
    gain = norm_gains, gains_first, gains_second
    if cube:
        (
            mixer_new, mixer_first_new, mixer_second_new, mixer_average_new, gate_up_new, gate_up_first_new,
            gate_up_second_new, down_new, down_first_new, down_second_new, gains_new, gains_first_new, gains_second_new,
            grad_norm,
        ) = adam_call(
            chain, spot, links.everyone(note), mixer, gate_up, down, gain,
            (first_mine, second_mine, first_came, second_came, gate_up_mine, gate_up_came, shard_down, shard_gains),
        )
        grad_norm = grad_norm[0, 0]
    else:
        squares = sum(jnp.sum(v) for v in (*squares, note)) + jnp.sum(shard_gains * shard_gains)
        grad_norm = jnp.sqrt(links.total(squares))
        factor = CLIP_LIMIT / jnp.maximum(grad_norm, CLIP_LIMIT)
        shard_mixer = join(
            jnp.concatenate([first_mine, second_mine], axis=1), jnp.concatenate([first_came, second_came], axis=1), core, 1
        )
        shard_gate_up = join(gate_up_mine, gate_up_came, core)
        step = lambda old, grad: adam_step(old[0], grad * factor, old[1], old[2], RATE_MATRIX, DECAY_MATRIX)
        mixer_new, mixer_first_new, mixer_second_new = step(mixer, shard_mixer)
        gate_up_new, gate_up_first_new, gate_up_second_new = step(gate_up, shard_gate_up)
        down_new, down_first_new, down_second_new = step(down, shard_down)
        gains_new, gains_first_new, gains_second_new = adam_step(
            gain[0], shard_gains * factor, gain[1], gain[2], RATE_GAIN, 0.0
        )
        mixer_average_new = AVERAGE_KEEP * mixer_average + (1.0 - AVERAGE_KEEP) * mixer_new
    return (
        output, input_grad, grad_norm, mixer_new, gate_up_new, down_new, gains_new,
        mixer_first_new, gate_up_first_new, down_first_new, gains_first_new,
        mixer_second_new, gate_up_second_new, down_second_new, gains_second_new, mixer_average_new,
    )


def solution(mesh):
    outer, inner = mesh.shape["dp"], mesh.shape["fsdp"]
    side = math.isqrt(outer)
    if side * side != outer:
        side = 1
    split = jax.sharding.Mesh(
        np.asarray(mesh.devices).reshape(side, outer // side, inner // 2, 2), EVERY
    )
    rows, columns, whole = P(EVERY, None), P(None, EVERY), P()
    return jax.shard_map(
        body,
        mesh=split,
        in_specs=(
            rows, rows, whole, rows, rows, rows, rows, columns,
            rows, rows, rows, columns, rows, rows, rows, columns, rows,
        ),
        out_specs=(
            rows, rows, whole, rows, rows, rows, columns, rows, rows, rows, columns,
            rows, rows, rows, columns, rows,
        ),
        check_vma=False,
    )
```

```python
import functools
import math

import jax
import jax.numpy as jnp
import numpy as np
from jax import lax
from jax.experimental import pallas as pl
from jax.experimental.pallas import tpu as pltpu
from jax.sharding import PartitionSpec as P

bf = jnp.bfloat16
f32 = jnp.float32
FILTERS = 24
AR_ORDER = 3
FF = 2048
STEP = 10
NORM_EPS = 1e-05
CLIP_LIMIT = 1.0
BETA_ONE = 0.9
BETA_TWO = 0.95
ADAM_EPS = 1e-08
RATE_MATRIX = 0.03
RATE_GAIN = 0.5
DECAY_MATRIX = 0.1
AVERAGE_KEEP = 0.9
CHIPS = ("d0", "d1", "z")
EVERY = CHIPS + ("core",)


NT = (((1,), (1,)), ((), ()))
NN = (((1,), (0,)), ((), ()))
TN = (((0,), (0,)), ((), ()))


def dot(a, b, dims=NN):
    return lax.dot_general(a, b, dims, preferred_element_type=f32)


class Chain:
    def __init__(self):
        self.token = None

    def call(self, kernel, name, args, in_specs, out_specs, out_shape, waits=(), through=(), **options):
        count, single = len(args), not isinstance(out_shape, (list, tuple)) and not through
        if single:
            out_specs, out_shape = [out_specs], [out_shape]
        made = len(out_shape)
        aliases = options.pop("input_output_aliases", {})
        aliases = {**aliases, **{count + i: made + i for i in range(len(through))}}
        last = tuple(through) + tuple(waits) + (() if self.token is None else (self.token,))

        def whole(*refs):
            first = count + len(last)
            kernel(*refs[:count], *refs[first : first + made], *refs[first + made + len(through) + 1 :])

        *outs, self.token = pl.pallas_call(
            whole,
            name=name,
            in_specs=list(in_specs) + [anywhere() for _ in last],
            out_specs=list(out_specs) + [anywhere() for _ in through] + [anywhere()],
            out_shape=list(out_shape) + [shaped(v.shape, v.dtype) for v in through] + [shaped((8, 128), f32)],
            input_output_aliases=aliases,
            compiler_params=pltpu.CompilerParams(vmem_limit_bytes=64 << 20),
            cost_estimate=pl.CostEstimate(flops=1, bytes_accessed=1, transcendentals=0),
            **options,
        )(*args, *last)
        return outs[0] if single else outs

    def pause(self, waits=(), through=()):
        return self.call(lambda: None, "pause", (), [], [], [], waits=waits, through=through)


def smem():
    return pl.BlockSpec(memory_space=pltpu.SMEM)


def anywhere():
    return pl.BlockSpec(memory_space=pl.ANY)


def fixed(*shape):
    return pl.BlockSpec(shape, lambda i: (0,) * len(shape))


NOTE = 16


def shaped(shape, dtype):
    return jax.ShapeDtypeStruct(tuple(shape), dtype)


def segment_of(place, ends_ref, group):
    return sum((place >= ends_ref[group, j]).astype(jnp.int32) for j in range(3))


def causal_mask(ends_ref, group, n, transposed):
    down = lax.broadcasted_iota(jnp.int32, (n, 1), 0)
    along = lax.broadcasted_iota(jnp.int32, (1, n), 1)
    one, two = segment_of(down, ends_ref, group), segment_of(along, ends_ref, group)
    order = (down <= along) if transposed else (down >= along)
    return ((one == two) & (one < 3) & order).astype(f32).astype(bf)


def diagonals(row, count):
    wide = jnp.broadcast_to(row, (count, row.shape[-1]))
    return pltpu.roll(wide, 0, 1, stride=1, stride_axis=0).astype(bf)


def spread_kernel(lengths_ref, came_ref, taps_ref, own_ref, other_ref, *refs):
    u_ref, mask, table, ends = refs[-4:]
    n = mask.shape[1]
    q, h, w = n // 4, n // 2, own_ref.shape[1] // 2
    per = taps_ref.shape[1]

    @pl.when(pl.program_id(0) == 0)
    def _():
        find_ends(ends, lengths_ref, came_ref)
        for g in range(2):
            mask[g] = causal_mask(ends, g, n, False)
        table[...] = jnp.zeros_like(table)

    for j in range(per):
        strip = diagonals(taps_ref[0, j : j + 1, :], q)
        for g, tokens in enumerate((own_ref, other_ref)):
            for i in range(4):
                rows, cols = slice(i * q, (i + 1) * q), slice(0, (i + 1) * q)
                table[g, rows, cols] = strip[:, (3 - i) * q :] * mask[g, rows, cols]
            upper = dot(table[g, :h, :h], tokens[:h]).astype(bf)
            lower = dot(table[g, h:, :], tokens[...]).astype(bf)
            for side in range(2):
                cols = slice(side * w, (side + 1) * w)
                u_ref[side, g * n : g * n + h, j * w : (j + 1) * w] = upper[:, cols]
                u_ref[side, g * n + h : (g + 1) * n, j * w : (j + 1) * w] = lower[:, cols]


def find_ends(ends, lengths_ref, came_ref):
    for g, ref in enumerate((lengths_ref, came_ref)):
        total = ref[0, 0]
        ends[g, 0] = total
        for j in range(1, 3):
            total = total + ref[0, j]
            ends[g, j] = total


def spread_call(chain, lengths, taps, own, other, first, steps, into=None):
    blocks, per, n = taps.shape
    w = own.shape[1] // 2
    args = [*lengths, taps, own, other]
    specs = [smem()] * 2 + [pl.BlockSpec((1, per, n), lambda i: (i + first, 0, 0)), fixed(n, 2 * w), fixed(n, 2 * w)]
    options = {}
    if into is not None:
        options = dict(input_output_aliases={len(args): 0})
        args, specs = args + [into], specs + [anywhere()]
    return chain.call(
        spread_kernel, "spread", args, specs,
        pl.BlockSpec((2, 2 * n, per * w), lambda i: (0, 0, i + first)),
        shaped((2, 2 * n, blocks * per * w), bf),
        grid=(steps,),
        scratch_shapes=[pltpu.VMEM((2, n, n), bf), pltpu.VMEM((2, n, n), bf), pltpu.SMEM((2, 3), jnp.int32)],
        **options,
    )


def run_copies(copies):
    for c in copies:
        c.start()
    for c in copies:
        c.wait()


def chip_of(spot_ref, slot, size):
    if isinstance(slot, int):
        return slot
    dy, dx, dz, fixed_z = slot
    return ((spot_ref[0] ^ dy) * 2 + (spot_ref[1] ^ dx)) * size + (dz if fixed_z else spot_ref[2] ^ dz)


def collect(spot_ref, pieces, plan, size, held, sem, columns):
    copies = []
    for at, (piece, row, rows, slot, half) in enumerate(plan):
        place = chip_of(spot_ref, slot, size)
        if half is not None:
            place = place * 2 + (spot_ref[3] ^ half)
        start = pl.multiple_of(place * rows, math.gcd(rows, 512))
        copies.append(
            pltpu.make_async_copy(pieces[piece].at[pl.ds(row, rows)], held.at[pl.ds(start, rows), columns], sem.at[at])
        )
    return copies


def mix_kernel(count, plan, notes, size, width, side, spot_ref, u_ref, *refs):
    pieces, refs = refs[:count], refs[count:]
    first = side == 0
    before, refs = refs[: 0 if first else 2], refs[0 if first else 2 :]
    if not notes:
        gains_ref, refs = refs[0], refs[1:]
    own_ref, other_ref, w_ref, *refs = refs
    if notes:
        gains_ref, refs = refs[0], refs[1:]
    held, u, sem, u_sem, *refs = refs
    tiles = sums = refs[0] if refs else None
    w = held.shape[1]
    filters = held.shape[0] // width
    rows = own_ref.shape[0]
    copies = collect(spot_ref, pieces, plan, size, held, sem, slice(0, w))
    for at, (piece, row, slot) in enumerate(notes):
        copies.append(
            pltpu.make_async_copy(
                pieces[piece].at[pl.ds(row, NOTE)], tiles.at[chip_of(spot_ref, slot, size)], sem.at[len(plan) + at]
            )
        )
    third = filters // 3
    cols = [pl.ds(t * third * w, third * w) for t in range(3)]
    loads = [pltpu.make_async_copy(u_ref.at[side, :, c], u.at[:, c], u_sem.at[t]) for t, c in enumerate(cols)]
    adds = [pltpu.make_async_copy(ref, sums.at[g], u_sem.at[4 + g]) for g, ref in enumerate(before)]
    for c in copies + loads + adds:
        c.start()
    for c in copies:
        c.wait()
    give = pltpu.make_async_copy(held, w_ref, u_sem.at[3])
    give.start()
    if notes:
        lanes = width // len(notes)
        for b in range(width // 128):
            block = jnp.zeros((NOTE, 128), f32)
            for j in range(128 // lanes):
                tile = tiles[b * (128 // lanes) + j].astype(f32)
                block = block + (pltpu.roll(tile, j * lanes, 1) if j else tile)
            gains_ref[:, b * 128 : (b + 1) * 128] = block
    gain = gains_ref[0:1, pl.ds(pl.multiple_of((spot_ref[3] * 2 + side) * w, w), w)]
    result = None
    for t in range(3):
        wide = jnp.concatenate(
            [(held[k * width : (k + 1) * width].astype(f32) * gain).astype(bf) for k in range(t * third, (t + 1) * third)],
            axis=1,
        )
        loads[t].wait()
        part = dot(u[:, cols[t]], wide, NT)
        result = part if t == 0 else result + part
    for g, out in enumerate((own_ref, other_ref)):
        mine = result[g * rows : (g + 1) * rows]
        if not first:
            adds[g].wait()
            mine = mine + sums[g]
        out[...] = mine.astype(out.dtype)
    give.wait()


def mix_call(chain, spot, u, side, pieces, plan, notes, gains, size, width, before=()):
    rows, depth = u.shape[1:]
    w = pieces[0].shape[-1]
    total = depth // w * width
    step = rows // 2
    out = fixed(step, width)
    note = fixed(NOTE, width)
    given = () if notes else (gains,)
    made = 1 - len(given)
    return chain.call(
        functools.partial(mix_kernel, len(pieces), plan, notes, size, width, side), "mix",
        (spot, u, *pieces, *before, *given),
        [smem(), anywhere()] + [anywhere() for _ in (*pieces, *before)] + [note for _ in given],
        [out, out, anywhere()] + [note] * made,
        [shaped((step, width), f32), shaped((step, width), bf if before else f32), shaped((total, w), bf)]
        + [shaped((NOTE, width), f32)] * made,
        grid=(1,),
        scratch_shapes=[
            pltpu.VMEM((total, w), bf), pltpu.VMEM((rows, depth), bf),
            pltpu.SemaphoreType.DMA((len(plan) + len(notes),)), pltpu.SemaphoreType.DMA((6,)),
        ] + [pltpu.VMEM((len(notes), NOTE, 128), bf)] * made + [pltpu.VMEM((2, step, width), f32)] * min(1, len(before)),
    )


def hidden_kernel(source_ref, own_ref, came_ref, gain_ref, hidden_ref, *normed_refs):
    hidden = source_ref[...].astype(f32) + (own_ref[...] + came_ref[...].astype(f32))
    scale = lax.rsqrt(jnp.mean(hidden * hidden, axis=-1, keepdims=True) + NORM_EPS)
    hidden_ref[...] = hidden
    normed = (hidden * scale * gain_ref[1:2]).astype(bf)
    width = normed_refs[0].shape[1]
    for i, ref in enumerate(normed_refs):
        ref[...] = normed[:, i * width : (i + 1) * width]


def hidden_call(chain, source, own, came, gain, parts=2):
    rows, width = source.shape
    block = pl.BlockSpec((rows // parts, width), lambda i: (i, 0))
    thin = pl.BlockSpec((rows // parts, width // 2), lambda i: (i, 0))
    return chain.call(
        hidden_kernel, "hidden", (source, own, came, gain), [block, block, block, fixed(NOTE, width)],
        [block, thin, thin], [shaped((rows, width), f32)] + [shaped((rows, width // 2), bf)] * 2,
        grid=(parts,),
    )


def norm_back(grad, hat, scale, gain):
    weighted = grad * gain
    return scale * (weighted - hat * jnp.mean(weighted * hat, axis=-1, keepdims=True))


def add_rows(ref, values, step):
    total = jnp.sum(values, axis=0, keepdims=True)

    @pl.when(step == 0)
    def _():
        ref[...] = total

    @pl.when(step > 0)
    def _():
        ref[...] += total


def turn_kernel(lengths_ref, hidden_ref, back_ref, own_ref, came_ref, gain_ref, grad_ref, low_ref, gains_ref):
    hidden = hidden_ref[...]
    scale = lax.rsqrt(jnp.mean(hidden * hidden, axis=-1, keepdims=True) + NORM_EPS)
    hat = hidden * scale
    two = own_ref[...] + came_ref[...].astype(f32)
    back = live_rows(back_ref[...].astype(f32), lengths_ref, pl.program_id(0) * hidden.shape[0])
    grad = back + norm_back(two, hat, scale, gain_ref[1:2])
    grad_ref[...] = grad
    low_ref[...] = grad.astype(bf)
    add_rows(gains_ref, two * hat, pl.program_id(0))


def turn_call(chain, lengths, hidden, back, own, came, gain, parts=2):
    rows, width = hidden.shape
    block = pl.BlockSpec((rows // parts, width), lambda i: (i, 0))
    return chain.call(
        turn_kernel, "turn", (lengths, hidden, back, own, came, gain), [smem()] + [block] * 4 + [fixed(NOTE, width)],
        [block, block, fixed(1, width)],
        [shaped((rows, width), f32), shaped((rows, width), bf), shaped((1, width), f32)],
        grid=(parts,),
    )


def output_kernel(hidden_ref, own_ref, came_ref, out_ref):
    out_ref[...] = (hidden_ref[...] + (own_ref[...] + came_ref[...].astype(f32))).astype(bf)


def output_call(chain, hidden, own, came, parts=2):
    rows, width = hidden.shape
    block = pl.BlockSpec((rows // parts, width), lambda i: (i, 0))
    return chain.call(
        output_kernel, "output", (hidden, own, came), [block] * 3, block, shaped((rows, width), bf), grid=(parts,),
    )


def last_kernel(spot_ref, grad_ref, source_ref, own_ref, came_ref, gain_ref, out_ref, one):
    half = own_ref.shape[1]
    core = spot_ref[3]
    one[:, pl.ds(pl.multiple_of(core * half, half), half)] = own_ref[...]
    one[:, pl.ds(pl.multiple_of((1 - core) * half, half), half)] = came_ref[...]
    source = source_ref[...].astype(f32)
    scale = lax.rsqrt(jnp.mean(source * source, axis=-1, keepdims=True) + NORM_EPS)
    out_ref[...] = grad_ref[...] + norm_back(one[...], source * scale, scale, gain_ref[0:1])


def last_call(chain, spot, grad_hidden, source, own, came, gain, parts=2):
    rows, width = source.shape
    block = pl.BlockSpec((rows // parts, width), lambda i: (i, 0))
    thin = pl.BlockSpec((rows // parts, width // 2), lambda i: (i, 0))
    return chain.call(
        last_kernel, "last", (spot, grad_hidden, source, own, came, gain),
        [smem(), block, block, thin, thin, fixed(NOTE, width)], block, shaped((rows, width), f32),
        grid=(parts,), scratch_shapes=[pltpu.VMEM((rows // parts, width), f32)],
    )


def grad_kernel(slots, size, side, spot_ref, gains_ref, own_ref, other_ref, u_ref, *refs):
    outs, (turned, held, sem) = refs[:-3], refs[-3:]
    n, width = own_ref.shape
    w = held.shape[1]
    per = u_ref.shape[2] // w
    step = pl.program_id(0)

    @pl.when(step == 0)
    def _():
        turned[:, :n] = own_ref[...].T
        turned[:, n:] = other_ref[...].T

    gain = gains_ref[0:1, pl.ds(pl.multiple_of((spot_ref[3] * 2 + side) * w, w), w)]
    result = dot(turned[...], u_ref[0])
    for j in range(per):
        at = pl.multiple_of((step * per + j) * width, width)
        held[pl.ds(at, width), :] = (result[:, j * w : (j + 1) * w] * gain).astype(bf)

    @pl.when(step == pl.num_programs(0) - 1)
    def _():
        rows = held.shape[0] // len(slots)
        copies, at = [], 0
        for ref in outs:
            for b in range(ref.shape[0] // rows):
                start = pl.multiple_of(chip_of(spot_ref, slots[at], size) * rows, math.gcd(rows, 512))
                copies.append(
                    pltpu.make_async_copy(held.at[pl.ds(start, rows)], ref.at[pl.ds(b * rows, rows)], sem.at[at])
                )
                at += 1
        run_copies(copies)


def grad_call(chain, spot, gains, own, other, u, side, w, blocks, slots, size, per=9):
    rows, depth = u.shape[1:]
    n, width = own.shape
    count = depth // w
    each = count * width // len(slots)
    return chain.call(
        functools.partial(grad_kernel, slots, size, side), "mixer_grad", (spot, gains, own, other, u),
        [smem(), fixed(NOTE, width), fixed(n, width), fixed(n, width), pl.BlockSpec((1, rows, per * w), lambda i: (side, 0, i))],
        [anywhere() for _ in blocks], [shaped((b * each, w), bf) for b in blocks],
        grid=(count // per,),
        scratch_shapes=[
            pltpu.VMEM((width, rows), bf), pltpu.VMEM((count * width, w), bf), pltpu.SemaphoreType.DMA((len(slots),)),
        ],
    )


def gain_rows(rows_ref, one, two, core, wide):
    devices, half = rows_ref.shape[0], one.shape[1]
    lanes = 2 * half // devices
    if lanes < 1 or 128 % lanes or 2 * lanes > 128:
        return
    wide[...] = jnp.zeros_like(wide)
    wide[:, pl.ds(pl.multiple_of(core * half, half), half)] = jnp.broadcast_to(one, (8, half))
    lane = lax.broadcasted_iota(jnp.int32, (8, 128), 1)
    for i in range(devices):
        block, turn = divmod(i * lanes, 128)
        cols = slice(block * 128, (block + 1) * 128)
        pair = []
        for tile, at in ((wide[:, cols], 0), (jnp.broadcast_to(two[:, cols], (8, 128)), lanes)):
            shift = (at - turn) % 128
            pair.append(pltpu.roll(tile, shift, 1) if shift else tile)
        row = jnp.where(lane < lanes, pair[0], jnp.where(lane < 2 * lanes, pair[1], 0.0))
        rows_ref[i : i + 1, :] = row[:1]


def back_kernel(first, spot_ref, lengths_ref, came_ref, taps_ref, own_ref, other_ref, left_ref, right_ref, *refs):
    if first:
        own_before, other_before, own_hat, other_hat, two_ref, own_out, other_out, gains_ref, rows_ref, wide, *refs = refs
        before = own_before, other_before
    else:
        own_out, other_out, *refs = refs
    mask, low_low, low_high, high, v_low, v_high, ends = refs
    n = mask.shape[1]
    q, h, d = n // 4, n // 2, own_ref.shape[1]
    per = taps_ref.shape[1]

    @pl.when(pl.program_id(0) == 0)
    def _():
        find_ends(ends, lengths_ref, came_ref)
        for g in range(2):
            mask[g] = causal_mask(ends, g, n, True)
        low_low[...] = jnp.zeros_like(low_low)
        high[...] = jnp.zeros_like(high)
        for g, ref in enumerate((own_out, other_out)):
            ref[...] = before[g][...] if first else jnp.zeros_like(ref)

    for j in range(per):
        weight = jnp.concatenate([left_ref[j * d : (j + 1) * d], right_ref[j * d : (j + 1) * d]], axis=1)
        s = diagonals(taps_ref[0, j : j + 1, :], q)
        a = j * h
        for g, grad in enumerate((own_ref, other_ref)):
            v = dot(grad[...], weight).astype(bf)
            v_low[g, a : a + h] = v[:h]
            v_high[g, a : a + h] = v[h:]
            m = mask[g]
            low_low[g, 0:q, a : a + q] = s[:, :q] * m[0:q, 0:q]
            low_low[g, 0:q, a + q : a + h] = s[:, q : 2 * q] * m[0:q, q : 2 * q]
            low_low[g, q:h, a + q : a + h] = s[:, :q] * m[q:h, q:h]
            low_high[g, 0:q, a : a + h] = s[:, 2 * q : 4 * q] * m[0:q, h:]
            low_high[g, q:h, a : a + h] = s[:, q : 3 * q] * m[q:h, h:]
            high[g, 0:q, a : a + h] = s[:, 0 : 2 * q] * m[h : h + q, h:]
            high[g, q:h, a + q : a + h] = s[:, 0:q] * m[h + q :, h + q :]
    for g, out in enumerate((own_out, other_out)):
        out[:h] += dot(low_low[g], v_low[g]) + dot(low_high[g], v_high[g])
        out[h:] += dot(high[g], v_high[g])
    if first:

        @pl.when(pl.program_id(0) == pl.num_programs(0) - 1)
        def _():
            products = own_out[...] * own_hat[...].astype(f32) + other_out[...] * other_hat[...].astype(f32)
            one = jnp.sum(products, axis=0, keepdims=True)
            gains_ref[...] = one
            gain_rows(rows_ref, one, two_ref, spot_ref[3], wide)


def back_call(chain, spot, lengths, taps, own, other, weights, first, steps, before=(), hats=(), two=None, devices=0):
    blocks, per, n = taps.shape
    rows, d = own.shape
    w = weights[0].shape[1]
    width = 2 * w
    scratch = lambda *s: pltpu.VMEM(s, bf)
    weight = pl.BlockSpec((per * d, w), lambda i: (i + first, 0))
    half = fixed(rows, width)
    more = (*before, *hats, two) if before else ()
    outs, shapes = [half] * 2, [shaped((rows, width), f32)] * 2
    scratches = [
        scratch(2, n, n), scratch(2, n // 2, per * n // 2),
        scratch(2, n // 2, per * n // 2), scratch(2, n // 2, per * n // 2),
        scratch(2, per * n // 2, width), scratch(2, per * n // 2, width), pltpu.SMEM((2, 3), jnp.int32),
    ]
    if before:
        outs = outs + [fixed(1, width), fixed(devices, 128)]
        shapes = shapes + [shaped((1, width), f32), shaped((devices, 128), f32)]
        scratches = [pltpu.VMEM((8, 2 * width), f32)] + scratches
    return chain.call(
        functools.partial(back_kernel, first), "spread_back", (spot, *lengths, taps, own, other, *weights, *more),
        [smem()] * 3 + [pl.BlockSpec((1, per, n), lambda i: (i + first, 0, 0)), fixed(rows, d), fixed(rows, d)]
        + [weight, weight] + [fixed(*v.shape) for v in more],
        outs, shapes, grid=(steps,), scratch_shapes=scratches,
    )


def flat(v):
    return v.reshape(-1, v.shape[-1])


def ffn_kernel(count, outs, steps, slots, out_slots, size, crossed, spot_ref, lengths_ref, came_ref, *refs):
    turned = spot_ref[3] if crossed else 0
    tokens, pieces, refs = refs[:6], refs[6 : 6 + count], refs[6 + count :]
    results, grads, (held, dealt, normed, back, sums, sem) = refs[:4], refs[4 : 4 + outs], refs[4 + outs :]
    n = tokens[0].shape[0]
    chips, units, width = held.shape[0], held.shape[1] * 2 // 3, held.shape[2]
    own, half = chips // 2 // steps, units // 2
    step = pl.program_id(0)

    @pl.when(step == 0)
    def _():
        copies, at = [], 0
        for ref in pieces:
            for b in range(ref.shape[0]):
                chip = chip_of(spot_ref, slots[at], size)
                copies.append(
                    pltpu.make_async_copy(ref.at[b, pl.ds(0, units)], held.at[chip, pl.ds(0, units)], sem.at[0, at])
                )
                copies.append(
                    pltpu.make_async_copy(
                        ref.at[b, pl.ds(units, half)], held.at[chip ^ turned, pl.ds(units, half)], sem.at[1, at]
                    )
                )
                at += 1
        for c in copies:
            c.start()
        half_width = tokens[0].shape[1]
        for i in range(2):
            cols = slice(i * half_width, (i + 1) * half_width)
            normed[:n, cols], normed[n:, cols] = tokens[i][...], tokens[2 + i][...]
        back[:n] = live_rows(tokens[4][...].astype(f32), lengths_ref).astype(bf)
        back[n:] = live_rows(tokens[5][...].astype(f32), came_ref).astype(bf)
        for c in copies:
            c.wait()

    w_gate = flat(held[pl.ds(step * own, own), 0:units])
    w_up = flat(held[pl.ds(chips // 2 + step * own, own), 0:units])
    w_down = flat(held[pl.ds(step * 2 * own, 2 * own), units : units + half])
    gate, up = dot(normed[...], w_gate, NT), dot(normed[...], w_up, NT)
    grad_act = dot(back[...], w_down, NT)
    sigma = 1.0 / (1.0 + jnp.exp(-gate))
    swish = gate * sigma
    act = (swish * up).astype(bf)
    grad_gate = (grad_act * up * (sigma * (1.0 + gate * (1.0 - sigma)))).astype(bf)
    grad_up = (grad_act * swish).astype(bf)
    branch = dot(act, w_down)
    two = dot(jnp.concatenate([grad_gate, grad_up], axis=1), jnp.concatenate([w_gate, w_up], axis=0))
    for i, value in enumerate((branch, two)):
        if steps > 1:

            @pl.when(step == 0)
            def _():
                sums[i] = value

            @pl.when((step > 0) & (step < steps - 1))
            def _():
                sums[i] += value

        @pl.when(step == steps - 1)
        def _():
            total = value + sums[i] if steps > 1 else value
            results[2 * i][...] = total[:n]
            results[2 * i + 1][...] = total[n:].astype(bf)

    put = lambda v: v.astype(bf).reshape(own, units, width)
    dealt[pl.ds(step * own, own), 0:units] = put(dot(grad_gate, normed[...], TN))
    dealt[pl.ds(chips // 2 + step * own, own), 0:units] = put(dot(grad_up, normed[...], TN))
    grad_down = dot(act, back[...], TN).astype(bf)
    for b in range(2 * own):
        dealt[(step * 2 * own + b) ^ turned, units : units + half] = grad_down[b * half : (b + 1) * half]

    @pl.when(step == steps - 1)
    def _():
        copies, at = [], 0
        for ref in grads:
            for b in range(ref.shape[0]):
                copies.append(
                    pltpu.make_async_copy(dealt.at[chip_of(spot_ref, out_slots[at], size)], ref.at[b], sem.at[0, at])
                )
                at += 1
        run_copies(copies)


def ffn_call(chain, spot, lengths, tokens, pieces, blocks, slots, out_slots, size, crossed, chunk=1024):
    n, d = tokens[-1].shape
    chips, rows = len(slots), pieces[0].shape[1]
    units = rows * 2 // 3
    steps = chips // 2 * units // chunk
    return chain.call(
        functools.partial(ffn_kernel, len(pieces), len(blocks), steps, slots, out_slots, size, crossed), "ffn",
        (spot, *lengths, *tokens, *pieces),
        [smem()] * 3 + [fixed(*v.shape) for v in tokens] + [anywhere() for _ in pieces],
        [fixed(n, d)] * 4 + [anywhere() for _ in blocks],
        [shaped((n, d), f32), shaped((n, d), bf)] * 2 + [shaped((b, rows, d), bf) for b in blocks],
        grid=(steps,),
        scratch_shapes=[
            pltpu.VMEM((chips, rows, d), bf), pltpu.VMEM((chips, rows, d), bf),
            pltpu.VMEM((2 * n, d), bf), pltpu.VMEM((2 * n, d), bf), pltpu.VMEM((2, 2 * n, d), f32),
            pltpu.SemaphoreType.DMA((2, chips)),
        ],
    )


def normed_kernel(spot_ref, own_ref, other_ref, own_out, other_out, full):
    half = own_out.shape[1]
    cols = pl.ds(pl.multiple_of(spot_ref[3] * half, half), half)
    for ref, out in ((own_ref, own_out), (other_ref, other_out)):
        source = ref[...].astype(f32)
        scale = lax.rsqrt(jnp.mean(source * source, axis=-1, keepdims=True) + NORM_EPS)
        full[...] = (source * scale).astype(bf)
        out[...] = full[:, cols]


def normed_call(chain, spot, own, other, parts=2):
    rows, width = own.shape
    block = pl.BlockSpec((rows // parts, width), lambda i: (i, 0))
    thin = pl.BlockSpec((rows // parts, width // 2), lambda i: (i, 0))
    return chain.call(
        normed_kernel, "normed", (spot, own, other), [smem(), block, block],
        [thin] * 2, [shaped((rows, width // 2), bf)] * 2,
        grid=(parts,), scratch_shapes=[pltpu.VMEM((rows // parts, width), bf)],
    )


def live_rows(values, lengths_ref, first=0):
    total = lengths_ref[0, 0] + lengths_ref[0, 1] + lengths_ref[0, 2]
    place = lax.broadcasted_iota(jnp.int32, (values.shape[0], 1), 0) + first
    return jnp.where(place < total, values, jnp.zeros((), values.dtype))


def pack_kernel(
    spot_ref, mixer_ref, gate_up_ref, down_ref, gains_ref, mixer_mine, mixer_theirs, gate_mine, gate_theirs, down_low, note
):
    half, units, core = mixer_mine.shape[1], gate_mine.shape[0], spot_ref[3]
    for ref, cols, rows, c in ((mixer_mine, half, units, core), (mixer_theirs, half, units, 1 - core)):
        ref[...] = mixer_ref[:, pl.ds(pl.multiple_of(c * half, half), half)].astype(bf)
    for ref, c in ((gate_mine, core), (gate_theirs, 1 - core)):
        ref[:units] = gate_up_ref[pl.ds(pl.multiple_of(c * units, units), units), :].astype(bf)
    count, own = gains_ref.shape
    note[...] = jnp.zeros_like(note)
    note[:count, :own] = gains_ref[...].astype(bf)
    gate_theirs[units:] = jnp.zeros((note.shape[0], gate_theirs.shape[1]), bf)
    gate_theirs[units:, : note.shape[1]] = note[...]
    down_low[...] = down_ref[...].astype(bf)


def pack_call(chain, spot, mixer, gate_up, down, gains):
    (rows, width), (units, _), (half, _) = mixer.shape, gate_up.shape, down.shape
    shapes = [(rows, width // 2)] * 2 + [(units // 2, width), (units // 2 + NOTE, width), (half, width), (NOTE, 128)]
    return chain.call(
        pack_kernel, "pack", (spot, mixer, gate_up, down, gains),
        [smem(), fixed(rows, width), fixed(units, width), fixed(half, width), fixed(*gains.shape)],
        [fixed(*s) for s in shapes], [shaped(s, bf) for s in shapes], grid=(1,),
    )


def block_kernel(own_gains, spot_ref, mine_ref, came_ref, note_ref, gate_ref, all_ref, copies_ref):
    rows, w = mine_ref.shape[0], all_ref.shape[1]
    mine = note_ref[...].astype(f32)
    came = gate_ref[gate_ref.shape[0] - NOTE :, :w].astype(f32)
    turned = lambda v: pltpu.roll(v, own_gains, 1)
    note = jnp.where(spot_ref[3] == 0, mine + turned(came), came + turned(mine)).astype(bf)
    at = 0
    for side in range(2):
        cols = slice(side * w, (side + 1) * w)
        all_ref[at : at + rows] = mine_ref[:, cols]
        all_ref[at + rows : at + 2 * rows] = came_ref[:, cols]
        all_ref[at + 2 * rows : at + 2 * rows + NOTE] = note
        at += 2 * rows + NOTE
    count = 2 * rows + NOTE
    for c in range(copies_ref.shape[0] // count):
        copies_ref[c * count : (c + 1) * count] = all_ref[:count]


def block_call(chain, spot, mine, came, note, gate_came, own_gains, copies, waits):
    rows, width = mine.shape
    w = width // 2
    each = 2 * rows + NOTE
    return chain.call(
        functools.partial(block_kernel, own_gains), "block", (spot, mine, came, note, gate_came),
        [smem()] + [fixed(*v.shape) for v in (mine, came, note, gate_came)],
        [fixed(2 * each, w), fixed(copies * each, w)], [shaped((2 * each, w), bf), shaped((copies * each, w), bf)],
        grid=(1,), waits=waits,
    )


def stack_kernel(count, moves, spot_ref, *refs):
    for i, a, rows, o, b in moves:
        if not isinstance(a, int):
            stride, distance, first = a
            a = pl.multiple_of((spot_ref[2] ^ distance) * stride + first, NOTE)
        refs[count + o][b : b + rows] = refs[i][pl.ds(a, rows)]


def stack_call(chain, spot, arrays, rows, moves, waits=()):
    like = {o: arrays[i] for i, _, _, o, _ in moves}
    shapes = [(r,) + like[o].shape[1:] for o, r in enumerate(rows)]
    return chain.call(
        functools.partial(stack_kernel, len(arrays), moves), "stack", (spot, *arrays),
        [smem()] + [fixed(*v.shape) for v in arrays],
        [fixed(*s) for s in shapes], [shaped(s, like[o].dtype) for o, s in enumerate(shapes)], grid=(1,), waits=waits,
    )


def corner_kernel(cut, extra, x_ref, y_ref, to_x_ref, to_y_ref):
    rows = x_ref.shape[0]
    to_x_ref[:cut] = y_ref[:cut]
    if extra:
        to_x_ref[cut:] = y_ref[rows - extra :]
    to_y_ref[...] = x_ref[cut : rows - extra]


def corner_call(chain, from_x, from_y, extra):
    total, width = from_x.shape
    cut = (total - extra) // 2
    shapes = [(cut + extra, width), (cut, width)]
    return chain.call(
        functools.partial(corner_kernel, cut, extra), "corner", (from_x, from_y), [fixed(total, width)] * 2,
        [fixed(*s) for s in shapes], [shaped(s, bf) for s in shapes], grid=(1,),
    )


def near_kernel(to_x_ref, to_y_ref, by_x_ref, by_y_ref, new_x_ref, new_y_ref):
    new_x_ref[...] = (to_x_ref[...].astype(f32) + by_y_ref[...].astype(f32)).astype(bf)
    new_y_ref[...] = (to_y_ref[...].astype(f32) + by_x_ref[...].astype(f32)).astype(bf)


def near_call(chain, to_x, to_y, by_x, by_y, parts=2, **options):
    rows, width = by_x.shape
    block = (rows // parts, width)
    low, high = pl.BlockSpec(block, lambda i: (i, 0)), pl.BlockSpec(block, lambda i: (i + parts, 0))
    return chain.call(
        near_kernel, "near", (to_x, to_y, by_x, by_y), [high, low, low, low], [high, low],
        [shaped(to_x.shape, bf), shaped(to_y.shape, bf)], grid=(parts,), input_output_aliases={0: 0, 1: 1}, **options,
    )


def line_kernel(count, *refs):
    parts, refs = refs[:count], refs[count:]
    rows = refs[-1].shape[0]

    def total(at):
        result = parts[0][pl.ds(at, rows)].astype(f32)
        for ref in parts[1:]:
            result = result + ref[pl.ds(at, rows)].astype(f32)
        return result

    for s, ref in enumerate(refs):
        ref[...] = total(s * rows).astype(ref.dtype)


def line_call(chain, parts, size, apart, **options):
    quarters = 4 if len(parts) == 1 else 1
    rows, width = parts[0].shape[0] // quarters // size, parts[0].shape[1]
    if apart:
        whole = lambda q: pl.BlockSpec((size * rows, width), lambda i: (q, 0))
        ins = [whole(q) for q in range(quarters)] if quarters > 1 else [whole(0)] * len(parts)
        specs = [fixed(rows, width)] * size
        shapes = [shaped((rows, width), f32)] + [shaped((rows, width), bf)] * (size - 1)
        steps = 1
    else:
        steps = 2
        half = size * rows // steps
        ins = [pl.BlockSpec((half, width), lambda i, q=q: (i + q * steps, 0)) for q in range(quarters)]
        ins = ins if quarters > 1 else ins * len(parts)
        specs, shapes = [pl.BlockSpec((half, width), lambda i: (i, 0))], [shaped((size * rows, width), bf)]
    parts = parts * quarters
    return chain.call(
        functools.partial(line_kernel, len(parts)), "line", parts, ins, specs, shapes, grid=(steps,), **options
    )


def finish_kernel(cuts, count, note, spot_ref, first_ref, *refs):
    came, more, outs, squares_ref, total = (
        refs[:count], refs[count : -len(cuts) - 2], refs[-len(cuts) - 2 : -2], refs[-2], refs[-1]
    )
    rows = total.shape[0]
    result = first_ref[:rows].astype(f32)
    for b in range(1, first_ref.shape[0] // rows):
        result = result + first_ref[b * rows : (b + 1) * rows].astype(f32)
    for ref in came:
        result = result + ref[...].astype(f32)
    total[...] = result
    squares = jnp.sum(result * result, axis=0, keepdims=True)
    if note:
        whole = jnp.sum(squares, axis=1, keepdims=True)
        for ref in more[:-1]:
            whole = whole + jnp.sum(ref[...], axis=1, keepdims=True)
        gains = jnp.sum(more[-1][...], axis=0, keepdims=True)
        squares = jnp.broadcast_to(whole + jnp.sum(gains * gains, axis=1, keepdims=True), squares_ref.shape)
    squares_ref[...] = squares
    for ref, start in zip(outs, cuts):
        rows = ref.shape[0]
        if not isinstance(start, int):
            start = pl.multiple_of((spot_ref[3] ^ start[0]) * rows, rows & -rows)
        ref[...] = total[pl.ds(start, rows), :]


def finish_call(chain, spot, first, came, blocks, cuts, note=0, more=(), waits=()):
    rows, width = first.shape[0] // blocks, first.shape[1]
    shapes = [(r, width) for _, r in cuts] + [(note, 128) if note else (1, width)]
    return chain.call(
        functools.partial(finish_kernel, [c for c, _ in cuts], len(came), note), "finish", (spot, first, *came, *more),
        [smem(), fixed(*first.shape)] + [fixed(rows, width)] * len(came) + [fixed(*v.shape) for v in more],
        [fixed(*s) for s in shapes], [shaped(s, f32) for s in shapes],
        grid=(1,), scratch_shapes=[pltpu.VMEM((rows, width), f32)], waits=waits,
    )


def adam_step(weight, grad, first, second, rate, decay):
    first_new = BETA_ONE * first + (1.0 - BETA_ONE) * grad
    second_new = BETA_TWO * second + (1.0 - BETA_TWO) * grad * grad
    corr_one = 1.0 / (1.0 - BETA_ONE**STEP)
    corr_two = 1.0 / (1.0 - BETA_TWO**STEP)
    update = first_new * (rate * corr_one) / (jnp.sqrt(second_new * corr_two) + ADAM_EPS)
    return (weight * (1.0 - rate * decay) - update, first_new, second_new)


def adam_kernel(spot_ref, note_ref, *refs):
    ins, outs, wide, tall = refs[:21], refs[21:35], refs[35], refs[36]
    mixer, gate_up, down, gains, parts = ins[:4], ins[4:7], ins[7:10], ins[10:13], ins[13:]
    mixer_out, gate_up_out, down_out, gains_out, norm_out = outs[:4], outs[4:7], outs[7:10], outs[10:13], outs[13]
    core, quarter = spot_ref[3], parts[0].shape[1]
    norm = jnp.sqrt(jnp.sum(note_ref[...], axis=0, keepdims=True)[:, :1])
    factor = CLIP_LIMIT / jnp.maximum(norm, CLIP_LIMIT)

    for s in range(2):
        mine = pl.multiple_of(core * 2 * quarter, quarter) + s * quarter
        came = pl.multiple_of((1 - core) * 2 * quarter, quarter) + s * quarter
        wide[:, pl.ds(pl.multiple_of(mine, quarter), quarter)] = parts[s][...]
        wide[:, pl.ds(pl.multiple_of(came, quarter), quarter)] = parts[2 + s][...]
    old, first, second, average = (r[...] for r in mixer)
    new, first, second = adam_step(old, wide[...] * factor, first, second, RATE_MATRIX, DECAY_MATRIX)
    average = AVERAGE_KEEP * average + (1.0 - AVERAGE_KEEP) * new
    for ref, value in zip(mixer_out, (new, first, second, average)):
        ref[...] = value

    @pl.when(pl.program_id(0) == 0)
    def _():
        half = parts[4].shape[0]
        tall[pl.ds(pl.multiple_of(core * half, half), half), :] = parts[4][...]
        tall[pl.ds(pl.multiple_of((1 - core) * half, half), half), :] = parts[5][...]
        own = gains[0].shape[1]
        sums = jnp.sum(parts[7][...], axis=0, keepdims=True)
        gain_grad = jnp.concatenate([sums[:, :own], sums[:, own : 2 * own]])
        for olds, news, grad, rate, decay in (
            (gate_up, gate_up_out, tall[...], RATE_MATRIX, DECAY_MATRIX),
            (down, down_out, parts[6][...], RATE_MATRIX, DECAY_MATRIX),
            (gains, gains_out, gain_grad, RATE_GAIN, 0.0),
        ):
            old, first, second = (r[...] for r in olds)
            scale = factor if rate == RATE_MATRIX else factor[:, :1]
            for ref, value in zip(news, adam_step(old, grad * scale, first, second, rate, decay)):
                ref[...] = value
        norm_out[...] = norm


def adam_call(chain, spot, note, mixer, gate_up, down, gains, parts, blocks=2):
    rows, width = mixer[0].shape
    step = rows // blocks
    block = pl.BlockSpec((step, width), lambda i: (i, 0))
    piece = pl.BlockSpec((step, parts[0].shape[1]), lambda i: (i, 0))
    whole = lambda v: fixed(*v.shape)
    others = [*gate_up, *down, *gains]
    shapes = [v.shape for v in (*mixer, *others)] + [(1, 1)]
    return chain.call(
        adam_kernel, "adam", (spot, note, *mixer, *others, *parts),
        [smem(), whole(note)] + [block] * 4 + [whole(v) for v in others] + [piece] * 4
        + [whole(v) for v in parts[4:]],
        [block] * 4 + [whole(v) for v in others] + [fixed(1, 1)], [shaped(s, f32) for s in shapes],
        grid=(blocks,),
        scratch_shapes=[pltpu.VMEM((step, width), f32), pltpu.VMEM(gate_up[0].shape, f32)],
    )


def flip(v, axis, bits=1):
    size = lax.axis_size(axis)
    return lax.ppermute(v, axis, [(i, i ^ bits) for i in range(size)])


def swap(v):
    return flip(v, "core")


def join(mine, other, core, axis=0):
    return jnp.where(
        core == 0,
        jnp.concatenate([mine, other], axis=axis),
        jnp.concatenate([other, mine], axis=axis),
    )


def part(v, index, axis=0):
    size = v.shape[axis] // 2
    return lax.dynamic_slice_in_dim(v, index * size, size, axis)


def low(v):
    return v.astype(bf)


def wide(v):
    return v.astype(f32)


class Whole:
    crossed = False
    mixer_slots = ((0,), (0,))
    mixer_blocks = (1,)

    def __init__(self, spot, groups):
        self.spot, self.core = spot, spot[3]
        self.size = lax.axis_size("z")
        self.chips = lax.axis_size("d0") * lax.axis_size("d1") * self.size
        self.ffn_in = self.ffn_out = tuple(range(groups))
        self.ffn_blocks = (groups,)

    def gather(self, chain, mixer, gate_up, down, gains, waits):
        def trade(v, axis):
            return join(part(v, self.core, axis), swap(part(v, 1 - self.core, axis)), self.core)

        everything = lambda v: lax.all_gather(v, CHIPS, axis=0, tiled=True)
        mixer_block = trade(low(mixer), 1)
        w, groups = mixer_block.shape[1] // 2, len(self.ffn_in)
        sides = []
        for s in range(2):
            whole = everything(mixer_block[:, s * w : (s + 1) * w])
            sides.append(([whole], ((0, 0, whole.shape[0], 0, None),), ()))
        ffn = [everything(v).reshape(groups, -1, v.shape[1]) for v in (trade(low(gate_up), 0), low(down))]
        ffn = [jnp.concatenate(ffn, axis=1)]
        gains = lax.all_gather(wide(low(gains)), EVERY, axis=1, tiled=True)
        yield jnp.pad(gains, ((0, NOTE - 2), (0, 0)))
        while True:
            yield sides, ffn

    def scatter(self, chain, parts, cuts, groups=1, apart=False):
        grads = parts[0].reshape(groups, -1, parts[0].shape[-1])
        rows = grads.shape[1] * 2 // 3
        if groups > 1:
            shards = [grads[:, :rows], grads[:, rows:]]
        else:
            shards = [grads]
        shards = [wide(lax.psum_scatter(flat(v), CHIPS, scatter_dimension=0, tiled=True)) for v in shards]
        outs = [part(shards[0], self.core), part(shards[0], 1 - self.core)] + shards[1:]
        squares = sum(jnp.sum(v * v, axis=0, keepdims=True) for v in shards)
        if groups == 1:
            yield
            yield ()
        through = yield ()
        yield (), through
        yield
        yield outs + [squares]

    def spread_gains(self, grads, rows):
        one, two = grads
        nothing = jnp.zeros_like(one)
        one = join(one, nothing, self.core, 1)
        return lax.psum_scatter(jnp.concatenate([one, two]), EVERY, scatter_dimension=1, tiled=True)

    def total(self, v):
        return lax.psum(v, EVERY)


class Cube(Whole):
    crossed = True
    near = ((0, 0), (0, 1), (1, 0), (1, 1))

    def __init__(self, spot, groups):
        super().__init__(spot, groups)
        slots = lambda fixed_z: tuple((y, x, s, fixed_z) for y, x in self.near for s in range(self.size))
        self.mixer_slots = slots(False), slots(True)
        self.ffn_in = slots(True)
        self.ffn_out = tuple((y, x, z, True) for z in range(self.size) for y, x in self.near)
        self.mixer_blocks = (self.size,) * 3 + (self.size // 2,) * 2

    def lines(self, block):
        return [flip(block, "z", s) for s in range(1, self.size)]

    def gather(self, chain, mixer, gate_up, down, gains, waits):
        spot = self.spot
        mixer_mine, mixer_theirs, gate_mine, gate_theirs, down_low, note = pack_call(
            chain, spot, mixer, gate_up, down, gains
        )
        gate_came = swap(gate_theirs)
        size = self.size
        own, block = block_call(
            chain, spot, mixer_mine, swap(mixer_theirs), note, gate_came, gains.shape[1], size, waits
        )
        line = self.along_z(block)
        own_x, own_y = flip(own, "d1"), flip(own, "d0")
        yield None
        rows = own.shape[0] // 2 - NOTE
        half = rows // 2
        sides = []

        def spread_out(line):
            return line, flip(line, "d1"), flip(line, "d0")

        def turn_corner(from_x, from_y, extra=0):
            to_x, to_y = corner_call(chain, from_x, from_y, extra)
            return flip(to_x, "d1"), flip(to_y, "d0")

        def plan(side):
            found = [(p, side * (rows + NOTE) + h * half, half, near + (0, False), h) for p, near in enumerate(self.near[:3]) for h in range(2)]
            found += [(3, h * half, half, (1, 1, 0, False), h) for h in range(2)]
            last = (size - 1) * 2
            for at in range(last):
                s, h = at // 2 + 1, at % 2
                found += [(4 + p, at * half, half, near + (s, False), h) for p, near in enumerate(self.near[:3])]
                found.append((7 + (at >= last // 2), at % (last // 2) * half, half, (1, 1, s, False), h))
            return tuple(found)

        corner = turn_corner(own_x, own_y)
        yield
        chain.pause(corner)
        others, line_rows = range(1, size), (size - 1) * rows
        moves = [(0, (rows + NOTE, s, 0), rows, 0, (s - 1) * rows) for s in others]
        moves += [(0, (rows + NOTE, s, rows), NOTE, 0, line_rows + (s - 1) * NOTE) for s in others]
        moves += [(1, rows + NOTE, rows, 1, s * rows) for s in range(size)]
        line, block = stack_call(
            chain, spot, (line, own), (line_rows + (size - 1) * NOTE, size * rows), tuple(moves)
        )
        first = spread_out(line)
        line = self.along_z(block)
        yield
        first_corner = turn_corner(*first[1:], (size - 1) * NOTE)
        notes = [(p, rows, near + (0, False)) for p, near in enumerate(self.near)]
        for s in others:
            notes += [(4 + p, line_rows + (s - 1) * NOTE, near + (s, False)) for p, near in enumerate(self.near[:3])]
            notes.append((7, line_rows // 2 + (s - 1) * NOTE, (1, 1, s, False)))
        sides.append(([own, own_x, own_y, corner[0], *first, *first_corner], plan(0), tuple(notes)))
        units, count = gate_mine.shape[0], down_low.shape[0]
        ffn_rows = 2 * units + count
        moves = [(0, (rows, s, 0), rows, 0, (s - 1) * rows) for s in others]
        for s in range(size):
            at = s * ffn_rows
            moves += [(1, 0, units, 1, at), (2, 0, units, 1, at + units), (3, 0, count, 1, at + 2 * units)]
        line, block = stack_call(
            chain, spot, (line, gate_mine, gate_came, down_low), (line_rows, size * ffn_rows), tuple(moves)
        )
        across, line = line, self.along_z(block)
        second = spread_out(*chain.pause(first_corner, (across,)))
        yield sides, None
        second_corner = turn_corner(*second[1:])
        sides.append(([own, own_x, own_y, corner[1], *second, *second_corner], plan(1), ()))
        ffn = spread_out(*chain.pause(second_corner, (line,)))
        yield sides, None
        ffn = (*ffn, *turn_corner(*ffn[1:]))
        yield sides, [v.reshape(-1, ffn_rows, v.shape[-1]) for v in ffn]

    def along_z(self, v):
        return lax.all_to_all(v, "z", 0, 0, tiled=True)

    def scatter(self, chain, parts, cuts, groups=1, apart=False):
        if groups > 1:
            came = (self.along_z(flat(parts[0])),)
        else:
            own, to_x, to_y, far_low, far_high = (flat(v) for v in parts)
            by_x, by_y = flip(far_low, "d1"), flip(far_high, "d0")
            yield
            to_x, to_y = yield near_call(chain, to_x, to_y, by_x, by_y)
            came = own, flip(to_x, "d1"), flip(to_y, "d0")
        through = yield came
        outs = line_call(chain, came, self.size, apart, through=through or ())
        count = self.size if apart else 1
        first, *rest = yield outs[:count], outs[count:]
        if groups > 1:
            to_x, to_y, far = rest
            far = lax.ppermute(far, ("d0", "d1"), [(i, i ^ 3) for i in range(4)])
            came = flip(to_x, "d1"), flip(to_y, "d0"), far
        elif apart:
            came = [flip(v, "z", s + 1) for s, v in enumerate(rest)]
        else:
            first, came = self.along_z(first), ()
        more, waits = yield
        yield finish_call(
            chain, self.spot, first, came, 1 if apart else self.size, cuts, 2 * self.chips if more else 0, more, waits
        )

    def spread_gains(self, grads, rows):
        return self.everyone(rows)

    def everyone(self, rows):
        return lax.all_to_all(rows, EVERY, 0, 0, tiled=True)


def body(
    inputs, lengths, filters, cotangent, mixer_weight, gate_up_weight, down_weight, norm_gains,
    mixer_first, gate_up_first, down_first, gains_first,
    mixer_second, gate_up_second, down_second, gains_second, mixer_average,
):
    slots, width = inputs.shape
    size = lax.axis_size("z")
    groups = 2 * FF // 256
    cube = lax.axis_size("d0") == 2 and lax.axis_size("d1") == 2 and size == 4
    spot = jnp.stack([lax.axis_index(a) for a in EVERY]).astype(jnp.int32)
    core = spot[3]
    links = (Cube if cube else Whole)(spot, groups)
    units = gate_up_weight.shape[0]
    chain = Chain()

    sums = lengths, swap(lengths)
    source_other, cotangent_other = swap(inputs), swap(cotangent)
    taps = jnp.concatenate([wide(filters), jnp.eye(AR_ORDER, slots, dtype=f32)])
    taps_turned = jnp.roll(taps[:, ::-1], 1 - slots // 4, axis=1)
    taps, taps_turned = (v.reshape(-1, 3, slots) for v in (taps, taps_turned))

    weights = links.gather(
        chain, mixer_weight, gate_up_weight, down_weight, norm_gains, (sums[1], source_other, cotangent_other)
    )
    gains = next(weights)
    tokens = hat_tokens = normed_call(chain, spot, inputs, source_other)
    blocks = taps.shape[0]
    cuts, spread = (0, blocks // 3, blocks * 4 // 9, blocks), None
    for at in range(3):
        spread = spread_call(chain, sums, taps_turned, *tokens, cuts[at], cuts[at + 1] - cuts[at], spread)
        sides = next(weights)
    sides, _ = sides
    quarter = sides[0][0][0].shape[1]
    *mixed, left, gains = (*mix_call(chain, spot, spread, 0, *sides[0], gains, size, width), gains)[:4]
    sides, _ = next(weights)
    mixed_own, mixed_other, right = mix_call(chain, spot, spread, 1, *sides[1], gains, size, width, mixed)
    _, ffn = next(weights)

    hidden, *normed_two = hidden_call(chain, inputs, mixed_own, swap(mixed_other), gains)
    tokens = (*normed_two, *(swap(v) for v in normed_two), cotangent, cotangent_other)
    branch_own, branch_other, two_own, two_other, *grad_ffn = ffn_call(
        chain, spot, sums, tokens, ffn, links.ffn_blocks, links.ffn_in, links.ffn_out, size, links.crossed
    )
    if cube:
        grad_ffn = chain.pause(through=grad_ffn)
    ffn_sum = links.scatter(chain, grad_ffn, ((0, units // 2), (units // 2, units // 2), (units, units // 2)), groups, True)
    ffn_came = next(ffn_sum)
    grad_hidden, grad_low, gains_two = turn_call(
        chain, lengths, hidden, cotangent, two_own, swap(two_other), gains
    )
    grad_other = swap(grad_low)
    rows = mixer_weight.shape[0]
    cuts = (((0,), rows), ((1,), rows))
    grads_of = lambda s: grad_call(
        chain, spot, gains, grad_low, grad_other, spread, s, quarter, links.mixer_blocks, links.mixer_slots[s], size
    )
    first_sum = links.scatter(chain, grads_of(0), cuts, apart=True)
    next(first_sum)
    second_sum = links.scatter(chain, grads_of(1), cuts)
    next(second_sum)
    backward = lambda first, steps, *more: back_call(
        chain, spot, sums, taps, grad_low, grad_other, (left, right), first, steps, *more
    )
    early = blocks // 2
    first_sum.send(next(first_sum))
    one = backward(0, early)
    second_sum.send(next(second_sum))
    one_own, one_other, gains_one, note_rows = backward(
        early, blocks - early, one, hat_tokens, gains_two, 2 * links.chips
    )
    outs, _ = first_sum.send(())
    first_sum.send(outs)
    if cube:
        (note_rows,) = chain.pause(ffn_came, (note_rows,))
    shard_gains = links.spread_gains((gains_one, gains_two), note_rows)
    outs, _ = second_sum.send(())
    chain.pause((shard_gains,))
    first_mine, first_theirs, square = first_sum.send(((), ()))
    first_theirs, branch_other, *outs = chain.pause(through=(first_theirs, branch_other, *outs))
    second_sum.send(outs)
    outs, _ = ffn_sum.send(())
    ffn_sum.send(outs)
    output = output_call(chain, hidden, branch_own, swap(branch_other))
    input_grad = last_call(chain, spot, grad_hidden, inputs, one_own, swap(one_other), gains)
    gate_up_mine, gate_up_theirs, shard_down, *squares = ffn_sum.send(((), ()))
    squares.append(square)
    gate_up_came, first_came = swap(gate_up_theirs), swap(first_theirs)
    second_mine, second_theirs, note = second_sum.send(((*squares, shard_gains), ()))
    second_came = swap(second_theirs)
    mixer = mixer_weight, mixer_first, mixer_second, mixer_average
    gate_up, down = (gate_up_weight, gate_up_first, gate_up_second), (down_weight, down_first, down_second)
    gain = norm_gains, gains_first, gains_second
    if cube:
        (
            mixer_new, mixer_first_new, mixer_second_new, mixer_average_new, gate_up_new, gate_up_first_new,
            gate_up_second_new, down_new, down_first_new, down_second_new, gains_new, gains_first_new, gains_second_new,
            grad_norm,
        ) = adam_call(
            chain, spot, links.everyone(note), mixer, gate_up, down, gain,
            (first_mine, second_mine, first_came, second_came, gate_up_mine, gate_up_came, shard_down, shard_gains),
        )
        grad_norm = grad_norm[0, 0]
    else:
        squares = sum(jnp.sum(v) for v in (*squares, note)) + jnp.sum(shard_gains * shard_gains)
        grad_norm = jnp.sqrt(links.total(squares))
        factor = CLIP_LIMIT / jnp.maximum(grad_norm, CLIP_LIMIT)
        shard_mixer = join(
            jnp.concatenate([first_mine, second_mine], axis=1), jnp.concatenate([first_came, second_came], axis=1), core, 1
        )
        shard_gate_up = join(gate_up_mine, gate_up_came, core)
        step = lambda old, grad: adam_step(old[0], grad * factor, old[1], old[2], RATE_MATRIX, DECAY_MATRIX)
        mixer_new, mixer_first_new, mixer_second_new = step(mixer, shard_mixer)
        gate_up_new, gate_up_first_new, gate_up_second_new = step(gate_up, shard_gate_up)
        down_new, down_first_new, down_second_new = step(down, shard_down)
        gains_new, gains_first_new, gains_second_new = adam_step(
            gain[0], shard_gains * factor, gain[1], gain[2], RATE_GAIN, 0.0
        )
        mixer_average_new = AVERAGE_KEEP * mixer_average + (1.0 - AVERAGE_KEEP) * mixer_new
    return (
        output, input_grad, grad_norm, mixer_new, gate_up_new, down_new, gains_new,
        mixer_first_new, gate_up_first_new, down_first_new, gains_first_new,
        mixer_second_new, gate_up_second_new, down_second_new, gains_second_new, mixer_average_new,
    )


def solution(mesh):
    outer, inner = mesh.shape["dp"], mesh.shape["fsdp"]
    side = math.isqrt(outer)
    if side * side != outer:
        side = 1
    split = jax.sharding.Mesh(
        np.asarray(mesh.devices).reshape(side, outer // side, inner // 2, 2), EVERY
    )
    rows, columns, whole = P(EVERY, None), P(None, EVERY), P()
    return jax.shard_map(
        body,
        mesh=split,
        in_specs=(
            rows, rows, whole, rows, rows, rows, rows, columns,
            rows, rows, rows, columns, rows, rows, rows, columns, rows,
        ),
        out_specs=(
            rows, rows, whole, rows, rows, rows, columns, rows, rows, rows, columns,
            rows, rows, rows, columns, rows,
        ),
        check_vma=False,
    )
```

```python
import functools
import math

import jax
import jax.numpy as jnp
import numpy as np
from jax import lax
from jax.experimental import pallas as pl
from jax.experimental.pallas import tpu as pltpu
from jax.sharding import PartitionSpec as P

bf = jnp.bfloat16
f32 = jnp.float32
FILTERS = 24
AR_ORDER = 3
FF = 2048
STEP = 10
NORM_EPS = 1e-05
CLIP_LIMIT = 1.0
BETA_ONE = 0.9
BETA_TWO = 0.95
ADAM_EPS = 1e-08
RATE_MATRIX = 0.03
RATE_GAIN = 0.5
DECAY_MATRIX = 0.1
AVERAGE_KEEP = 0.9
CHIPS = ("d0", "d1", "z")
EVERY = CHIPS + ("core",)


NT = (((1,), (1,)), ((), ()))
NN = (((1,), (0,)), ((), ()))
TN = (((0,), (0,)), ((), ()))


def dot(a, b, dims=NN):
    return lax.dot_general(a, b, dims, preferred_element_type=f32)


class Chain:
    def __init__(self):
        self.token = None

    def call(self, kernel, name, args, in_specs, out_specs, out_shape, waits=(), through=(), **options):
        count, single = len(args), not isinstance(out_shape, (list, tuple)) and not through
        if single:
            out_specs, out_shape = [out_specs], [out_shape]
        made = len(out_shape)
        aliases = options.pop("input_output_aliases", {})
        aliases = {**aliases, **{count + i: made + i for i in range(len(through))}}
        last = tuple(through) + tuple(waits) + (() if self.token is None else (self.token,))

        def whole(*refs):
            first = count + len(last)
            kernel(*refs[:count], *refs[first : first + made], *refs[first + made + len(through) + 1 :])

        *outs, self.token = pl.pallas_call(
            whole,
            name=name,
            in_specs=list(in_specs) + [anywhere() for _ in last],
            out_specs=list(out_specs) + [anywhere() for _ in through] + [anywhere()],
            out_shape=list(out_shape) + [shaped(v.shape, v.dtype) for v in through] + [shaped((8, 128), f32)],
            input_output_aliases=aliases,
            compiler_params=pltpu.CompilerParams(vmem_limit_bytes=64 << 20),
            cost_estimate=pl.CostEstimate(flops=1, bytes_accessed=1, transcendentals=0),
            **options,
        )(*args, *last)
        return outs[0] if single else outs

    def pause(self, waits=(), through=()):
        return self.call(lambda: None, "pause", (), [], [], [], waits=waits, through=through)


def smem():
    return pl.BlockSpec(memory_space=pltpu.SMEM)


def anywhere():
    return pl.BlockSpec(memory_space=pl.ANY)


def fixed(*shape):
    return pl.BlockSpec(shape, lambda i: (0,) * len(shape))


NOTE = 16


def shaped(shape, dtype):
    return jax.ShapeDtypeStruct(tuple(shape), dtype)


def segment_of(place, ends_ref, group):
    return sum((place >= ends_ref[group, j]).astype(jnp.int32) for j in range(3))


def causal_mask(ends_ref, group, n, transposed):
    down = lax.broadcasted_iota(jnp.int32, (n, 1), 0)
    along = lax.broadcasted_iota(jnp.int32, (1, n), 1)
    one, two = segment_of(down, ends_ref, group), segment_of(along, ends_ref, group)
    order = (down <= along) if transposed else (down >= along)
    return ((one == two) & (one < 3) & order).astype(f32).astype(bf)


def diagonals(row, count):
    wide = jnp.broadcast_to(row, (count, row.shape[-1]))
    return pltpu.roll(wide, 0, 1, stride=1, stride_axis=0).astype(bf)


def spread_kernel(lengths_ref, came_ref, taps_ref, own_ref, other_ref, *refs):
    u_ref, mask, table, ends = refs[-4:]
    n = mask.shape[1]
    q, h, w = n // 4, n // 2, own_ref.shape[1] // 2
    per = taps_ref.shape[1]

    @pl.when(pl.program_id(0) == 0)
    def _():
        find_ends(ends, lengths_ref, came_ref)
        for g in range(2):
            mask[g] = causal_mask(ends, g, n, False)
        table[...] = jnp.zeros_like(table)

    for j in range(per):
        strip = diagonals(taps_ref[0, j : j + 1, :], q)
        for g, tokens in enumerate((own_ref, other_ref)):
            for i in range(4):
                rows, cols = slice(i * q, (i + 1) * q), slice(0, (i + 1) * q)
                table[g, rows, cols] = strip[:, (3 - i) * q :] * mask[g, rows, cols]
            upper = dot(table[g, :h, :h], tokens[:h]).astype(bf)
            lower = dot(table[g, h:, :], tokens[...]).astype(bf)
            for side in range(2):
                cols = slice(side * w, (side + 1) * w)
                u_ref[side, g * n : g * n + h, j * w : (j + 1) * w] = upper[:, cols]
                u_ref[side, g * n + h : (g + 1) * n, j * w : (j + 1) * w] = lower[:, cols]


def find_ends(ends, lengths_ref, came_ref):
    for g, ref in enumerate((lengths_ref, came_ref)):
        total = ref[0, 0]
        ends[g, 0] = total
        for j in range(1, 3):
            total = total + ref[0, j]
            ends[g, j] = total


def spread_call(chain, lengths, taps, own, other, first, steps, into=None):
    blocks, per, n = taps.shape
    w = own.shape[1] // 2
    args = [*lengths, taps, own, other]
    specs = [smem()] * 2 + [pl.BlockSpec((1, per, n), lambda i: (i + first, 0, 0)), fixed(n, 2 * w), fixed(n, 2 * w)]
    options = {}
    if into is not None:
        options = dict(input_output_aliases={len(args): 0})
        args, specs = args + [into], specs + [anywhere()]
    return chain.call(
        spread_kernel, "spread", args, specs,
        pl.BlockSpec((2, 2 * n, per * w), lambda i: (0, 0, i + first)),
        shaped((2, 2 * n, blocks * per * w), bf),
        grid=(steps,),
        scratch_shapes=[pltpu.VMEM((2, n, n), bf), pltpu.VMEM((2, n, n), bf), pltpu.SMEM((2, 3), jnp.int32)],
        **options,
    )


def run_copies(copies):
    for c in copies:
        c.start()
    for c in copies:
        c.wait()


def chip_of(spot_ref, slot, size):
    if isinstance(slot, int):
        return slot
    dy, dx, dz, fixed_z = slot
    return ((spot_ref[0] ^ dy) * 2 + (spot_ref[1] ^ dx)) * size + (dz if fixed_z else spot_ref[2] ^ dz)


def collect(spot_ref, pieces, plan, size, held, sem, columns):
    copies = []
    for at, (piece, row, rows, slot, half) in enumerate(plan):
        place = chip_of(spot_ref, slot, size)
        if half is not None:
            place = place * 2 + (spot_ref[3] ^ half)
        start = pl.multiple_of(place * rows, math.gcd(rows, 512))
        copies.append(
            pltpu.make_async_copy(pieces[piece].at[pl.ds(row, rows)], held.at[pl.ds(start, rows), columns], sem.at[at])
        )
    return copies


def mix_kernel(count, plan, notes, size, width, side, spot_ref, u_ref, *refs):
    pieces, refs = refs[:count], refs[count:]
    first = side == 0
    before, refs = refs[: 0 if first else 2], refs[0 if first else 2 :]
    if not notes:
        gains_ref, refs = refs[0], refs[1:]
    own_ref, other_ref, w_ref, *refs = refs
    if notes:
        gains_ref, refs = refs[0], refs[1:]
    held, u, sem, u_sem, *refs = refs
    *refs, result = refs
    tiles = sums = refs[0] if refs else None
    w = held.shape[1]
    filters = held.shape[0] // width
    rows = own_ref.shape[0]
    copies = collect(spot_ref, pieces, plan, size, held, sem, slice(0, w))
    for at, (piece, row, slot) in enumerate(notes):
        copies.append(
            pltpu.make_async_copy(
                pieces[piece].at[pl.ds(row, NOTE)], tiles.at[chip_of(spot_ref, slot, size)], sem.at[len(plan) + at]
            )
        )
    third = filters // 3
    cols = [pl.ds(t * third * w, third * w) for t in range(3)]
    loads = [pltpu.make_async_copy(u_ref.at[side, :, c], u.at[:, c], u_sem.at[t]) for t, c in enumerate(cols)]
    adds = [pltpu.make_async_copy(ref, sums.at[g], u_sem.at[4 + g]) for g, ref in enumerate(before)]
    for c in copies + loads + adds:
        c.start()
    for c in copies:
        c.wait()
    give = pltpu.make_async_copy(held, w_ref, u_sem.at[3])
    give.start()
    if notes:
        lanes = width // len(notes)
        for b in range(width // 128):
            block = jnp.zeros((NOTE, 128), f32)
            for j in range(128 // lanes):
                tile = tiles[b * (128 // lanes) + j].astype(f32)
                block = block + (pltpu.roll(tile, j * lanes, 1) if j else tile)
            gains_ref[:, b * 128 : (b + 1) * 128] = block
    gain = gains_ref[0:1, pl.ds(pl.multiple_of((spot_ref[3] * 2 + side) * w, w), w)]
    result[...] = jnp.zeros_like(result)

    @pl.loop(0, 3)
    def _(t):
        pltpu.make_async_copy(u_ref.at[side, :, pl.ds(0, third * w)], u.at[:, pl.ds(0, third * w)], u_sem.at[t]).wait()
        first_row = pl.multiple_of(t * third * width, width)
        wide = jnp.concatenate(
            [(held[pl.ds(first_row + k * width, width), :].astype(f32) * gain).astype(bf) for k in range(third)], axis=1
        )
        result[...] += dot(u[:, pl.ds(pl.multiple_of(t * third * w, w), third * w)], wide, NT)

    for g, out in enumerate((own_ref, other_ref)):
        mine = result[g * rows : (g + 1) * rows]
        if not first:
            adds[g].wait()
            mine = mine + sums[g]
        out[...] = mine.astype(out.dtype)
    give.wait()


def mix_call(chain, spot, u, side, pieces, plan, notes, gains, size, width, before=()):
    rows, depth = u.shape[1:]
    w = pieces[0].shape[-1]
    total = depth // w * width
    step = rows // 2
    out = fixed(step, width)
    note = fixed(NOTE, width)
    given = () if notes else (gains,)
    made = 1 - len(given)
    return chain.call(
        functools.partial(mix_kernel, len(pieces), plan, notes, size, width, side), "mix",
        (spot, u, *pieces, *before, *given),
        [smem(), anywhere()] + [anywhere() for _ in (*pieces, *before)] + [note for _ in given],
        [out, out, anywhere()] + [note] * made,
        [shaped((step, width), f32), shaped((step, width), bf if before else f32), shaped((total, w), bf)]
        + [shaped((NOTE, width), f32)] * made,
        grid=(1,),
        scratch_shapes=[
            pltpu.VMEM((total, w), bf), pltpu.VMEM((rows, depth), bf),
            pltpu.SemaphoreType.DMA((len(plan) + len(notes),)), pltpu.SemaphoreType.DMA((6,)),
        ] + [pltpu.VMEM((len(notes), NOTE, 128), bf)] * made + [pltpu.VMEM((2, step, width), f32)] * min(1, len(before))
        + [pltpu.VMEM((rows, width), f32)],
    )


def hidden_kernel(source_ref, own_ref, came_ref, gain_ref, hidden_ref, *normed_refs):
    hidden = source_ref[...].astype(f32) + (own_ref[...] + came_ref[...].astype(f32))
    scale = lax.rsqrt(jnp.mean(hidden * hidden, axis=-1, keepdims=True) + NORM_EPS)
    hidden_ref[...] = hidden
    normed = (hidden * scale * gain_ref[1:2]).astype(bf)
    width = normed_refs[0].shape[1]
    for i, ref in enumerate(normed_refs):
        ref[...] = normed[:, i * width : (i + 1) * width]


def hidden_call(chain, source, own, came, gain, parts=2):
    rows, width = source.shape
    block = pl.BlockSpec((rows // parts, width), lambda i: (i, 0))
    thin = pl.BlockSpec((rows // parts, width // 2), lambda i: (i, 0))
    return chain.call(
        hidden_kernel, "hidden", (source, own, came, gain), [block, block, block, fixed(NOTE, width)],
        [block, thin, thin], [shaped((rows, width), f32)] + [shaped((rows, width // 2), bf)] * 2,
        grid=(parts,),
    )


def norm_back(grad, hat, scale, gain):
    weighted = grad * gain
    return scale * (weighted - hat * jnp.mean(weighted * hat, axis=-1, keepdims=True))


def add_rows(ref, values, step):
    total = jnp.sum(values, axis=0, keepdims=True)

    @pl.when(step == 0)
    def _():
        ref[...] = total

    @pl.when(step > 0)
    def _():
        ref[...] += total


def turn_kernel(lengths_ref, hidden_ref, back_ref, own_ref, came_ref, gain_ref, grad_ref, low_ref, gains_ref):
    hidden = hidden_ref[...]
    scale = lax.rsqrt(jnp.mean(hidden * hidden, axis=-1, keepdims=True) + NORM_EPS)
    hat = hidden * scale
    two = own_ref[...] + came_ref[...].astype(f32)
    back = live_rows(back_ref[...].astype(f32), lengths_ref, pl.program_id(0) * hidden.shape[0])
    grad = back + norm_back(two, hat, scale, gain_ref[1:2])
    grad_ref[...] = grad
    low_ref[...] = grad.astype(bf)
    add_rows(gains_ref, two * hat, pl.program_id(0))


def turn_call(chain, lengths, hidden, back, own, came, gain, parts=2):
    rows, width = hidden.shape
    block = pl.BlockSpec((rows // parts, width), lambda i: (i, 0))
    return chain.call(
        turn_kernel, "turn", (lengths, hidden, back, own, came, gain), [smem()] + [block] * 4 + [fixed(NOTE, width)],
        [block, block, fixed(1, width)],
        [shaped((rows, width), f32), shaped((rows, width), bf), shaped((1, width), f32)],
        grid=(parts,),
    )


def output_kernel(hidden_ref, own_ref, came_ref, out_ref):
    out_ref[...] = (hidden_ref[...] + (own_ref[...] + came_ref[...].astype(f32))).astype(bf)


def output_call(chain, hidden, own, came, parts=2):
    rows, width = hidden.shape
    block = pl.BlockSpec((rows // parts, width), lambda i: (i, 0))
    return chain.call(
        output_kernel, "output", (hidden, own, came), [block] * 3, block, shaped((rows, width), bf), grid=(parts,),
    )


def last_kernel(spot_ref, grad_ref, source_ref, own_ref, came_ref, gain_ref, out_ref, one):
    half = own_ref.shape[1]
    core = spot_ref[3]
    one[:, pl.ds(pl.multiple_of(core * half, half), half)] = own_ref[...]
    one[:, pl.ds(pl.multiple_of((1 - core) * half, half), half)] = came_ref[...]
    source = source_ref[...].astype(f32)
    scale = lax.rsqrt(jnp.mean(source * source, axis=-1, keepdims=True) + NORM_EPS)
    out_ref[...] = grad_ref[...] + norm_back(one[...], source * scale, scale, gain_ref[0:1])


def last_call(chain, spot, grad_hidden, source, own, came, gain, parts=2):
    rows, width = source.shape
    block = pl.BlockSpec((rows // parts, width), lambda i: (i, 0))
    thin = pl.BlockSpec((rows // parts, width // 2), lambda i: (i, 0))
    return chain.call(
        last_kernel, "last", (spot, grad_hidden, source, own, came, gain),
        [smem(), block, block, thin, thin, fixed(NOTE, width)], block, shaped((rows, width), f32),
        grid=(parts,), scratch_shapes=[pltpu.VMEM((rows // parts, width), f32)],
    )


def grad_kernel(slots, size, side, spot_ref, gains_ref, own_ref, other_ref, u_ref, *refs):
    outs, (turned, held, sem) = refs[:-3], refs[-3:]
    n, width = own_ref.shape
    w = held.shape[1]
    per = u_ref.shape[2] // w
    step = pl.program_id(0)

    @pl.when(step == 0)
    def _():
        turned[:, :n] = own_ref[...].T
        turned[:, n:] = other_ref[...].T

    gain = gains_ref[0:1, pl.ds(pl.multiple_of((spot_ref[3] * 2 + side) * w, w), w)]
    result = dot(turned[...], u_ref[0])
    for j in range(per):
        at = pl.multiple_of((step * per + j) * width, width)
        held[pl.ds(at, width), :] = (result[:, j * w : (j + 1) * w] * gain).astype(bf)

    @pl.when(step == pl.num_programs(0) - 1)
    def _():
        rows = held.shape[0] // len(slots)
        copies, at = [], 0
        for ref in outs:
            for b in range(ref.shape[0] // rows):
                start = pl.multiple_of(chip_of(spot_ref, slots[at], size) * rows, math.gcd(rows, 512))
                copies.append(
                    pltpu.make_async_copy(held.at[pl.ds(start, rows)], ref.at[pl.ds(b * rows, rows)], sem.at[at])
                )
                at += 1
        run_copies(copies)


def grad_call(chain, spot, gains, own, other, u, side, w, blocks, slots, size, per=9):
    rows, depth = u.shape[1:]
    n, width = own.shape
    count = depth // w
    each = count * width // len(slots)
    return chain.call(
        functools.partial(grad_kernel, slots, size, side), "mixer_grad", (spot, gains, own, other, u),
        [smem(), fixed(NOTE, width), fixed(n, width), fixed(n, width), pl.BlockSpec((1, rows, per * w), lambda i: (side, 0, i))],
        [anywhere() for _ in blocks], [shaped((b * each, w), bf) for b in blocks],
        grid=(count // per,),
        scratch_shapes=[
            pltpu.VMEM((width, rows), bf), pltpu.VMEM((count * width, w), bf), pltpu.SemaphoreType.DMA((len(slots),)),
        ],
    )


def gain_rows(rows_ref, one, two, core, wide):
    devices, half = rows_ref.shape[0], one.shape[1]
    lanes = 2 * half // devices
    if lanes < 1 or 128 % lanes or 2 * lanes > 128:
        return
    wide[...] = jnp.zeros_like(wide)
    wide[:, pl.ds(pl.multiple_of(core * half, half), half)] = jnp.broadcast_to(one, (8, half))
    lane = lax.broadcasted_iota(jnp.int32, (8, 128), 1)
    for i in range(devices):
        block, turn = divmod(i * lanes, 128)
        cols = slice(block * 128, (block + 1) * 128)
        pair = []
        for tile, at in ((wide[:, cols], 0), (jnp.broadcast_to(two[:, cols], (8, 128)), lanes)):
            shift = (at - turn) % 128
            pair.append(pltpu.roll(tile, shift, 1) if shift else tile)
        row = jnp.where(lane < lanes, pair[0], jnp.where(lane < 2 * lanes, pair[1], 0.0))
        rows_ref[i : i + 1, :] = row[:1]


def back_kernel(first, spot_ref, lengths_ref, came_ref, taps_ref, own_ref, other_ref, left_ref, right_ref, *refs):
    if first:
        own_before, other_before, own_hat, other_hat, two_ref, own_out, other_out, gains_ref, rows_ref, wide, *refs = refs
        before = own_before, other_before
    else:
        own_out, other_out, *refs = refs
    mask, low_low, low_high, high, v_low, v_high, ends = refs
    n = mask.shape[1]
    q, h, d = n // 4, n // 2, own_ref.shape[1]
    per = taps_ref.shape[1]

    @pl.when(pl.program_id(0) == 0)
    def _():
        find_ends(ends, lengths_ref, came_ref)
        for g in range(2):
            mask[g] = causal_mask(ends, g, n, True)
        low_low[...] = jnp.zeros_like(low_low)
        high[...] = jnp.zeros_like(high)
        for g, ref in enumerate((own_out, other_out)):
            ref[...] = before[g][...] if first else jnp.zeros_like(ref)

    for j in range(per):
        weight = jnp.concatenate([left_ref[j * d : (j + 1) * d], right_ref[j * d : (j + 1) * d]], axis=1)
        s = diagonals(taps_ref[0, j : j + 1, :], q)
        a = j * h
        for g, grad in enumerate((own_ref, other_ref)):
            v = dot(grad[...], weight).astype(bf)
            v_low[g, a : a + h] = v[:h]
            v_high[g, a : a + h] = v[h:]
            m = mask[g]
            low_low[g, 0:q, a : a + q] = s[:, :q] * m[0:q, 0:q]
            low_low[g, 0:q, a + q : a + h] = s[:, q : 2 * q] * m[0:q, q : 2 * q]
            low_low[g, q:h, a + q : a + h] = s[:, :q] * m[q:h, q:h]
            low_high[g, 0:q, a : a + h] = s[:, 2 * q : 4 * q] * m[0:q, h:]
            low_high[g, q:h, a : a + h] = s[:, q : 3 * q] * m[q:h, h:]
            high[g, 0:q, a : a + h] = s[:, 0 : 2 * q] * m[h : h + q, h:]
            high[g, q:h, a + q : a + h] = s[:, 0:q] * m[h + q :, h + q :]
    for g, out in enumerate((own_out, other_out)):
        out[:h] += dot(low_low[g], v_low[g]) + dot(low_high[g], v_high[g])
        out[h:] += dot(high[g], v_high[g])
    if first:

        @pl.when(pl.program_id(0) == pl.num_programs(0) - 1)
        def _():
            products = own_out[...] * own_hat[...].astype(f32) + other_out[...] * other_hat[...].astype(f32)
            one = jnp.sum(products, axis=0, keepdims=True)
            gains_ref[...] = one
            gain_rows(rows_ref, one, two_ref, spot_ref[3], wide)


def back_call(chain, spot, lengths, taps, own, other, weights, first, steps, before=(), hats=(), two=None, devices=0):
    blocks, per, n = taps.shape
    rows, d = own.shape
    w = weights[0].shape[1]
    width = 2 * w
    scratch = lambda *s: pltpu.VMEM(s, bf)
    weight = pl.BlockSpec((per * d, w), lambda i: (i + first, 0))
    half = fixed(rows, width)
    more = (*before, *hats, two) if before else ()
    outs, shapes = [half] * 2, [shaped((rows, width), f32)] * 2
    scratches = [
        scratch(2, n, n), scratch(2, n // 2, per * n // 2),
        scratch(2, n // 2, per * n // 2), scratch(2, n // 2, per * n // 2),
        scratch(2, per * n // 2, width), scratch(2, per * n // 2, width), pltpu.SMEM((2, 3), jnp.int32),
    ]
    if before:
        outs = outs + [fixed(1, width), fixed(devices, 128)]
        shapes = shapes + [shaped((1, width), f32), shaped((devices, 128), f32)]
        scratches = [pltpu.VMEM((8, 2 * width), f32)] + scratches
    return chain.call(
        functools.partial(back_kernel, first), "spread_back", (spot, *lengths, taps, own, other, *weights, *more),
        [smem()] * 3 + [pl.BlockSpec((1, per, n), lambda i: (i + first, 0, 0)), fixed(rows, d), fixed(rows, d)]
        + [weight, weight] + [fixed(*v.shape) for v in more],
        outs, shapes, grid=(steps,), scratch_shapes=scratches,
    )


def flat(v):
    return v.reshape(-1, v.shape[-1])


def ffn_kernel(count, outs, steps, slots, out_slots, size, crossed, spot_ref, lengths_ref, came_ref, *refs):
    turned = spot_ref[3] if crossed else 0
    tokens, pieces, refs = refs[:6], refs[6 : 6 + count], refs[6 + count :]
    results, grads, (held, dealt, normed, back, sums, sem) = refs[:4], refs[4 : 4 + outs], refs[4 + outs :]
    n = tokens[0].shape[0]
    chips, units, width = held.shape[0], held.shape[1] * 2 // 3, held.shape[2]
    own, half = chips // 2 // steps, units // 2
    step = pl.program_id(0)

    @pl.when(step == 0)
    def _():
        copies, at = [], 0
        for ref in pieces:
            for b in range(ref.shape[0]):
                chip = chip_of(spot_ref, slots[at], size)
                copies.append(
                    pltpu.make_async_copy(ref.at[b, pl.ds(0, units)], held.at[chip, pl.ds(0, units)], sem.at[0, at])
                )
                copies.append(
                    pltpu.make_async_copy(
                        ref.at[b, pl.ds(units, half)], held.at[chip ^ turned, pl.ds(units, half)], sem.at[1, at]
                    )
                )
                at += 1
        for c in copies:
            c.start()
        half_width = tokens[0].shape[1]
        for i in range(2):
            cols = slice(i * half_width, (i + 1) * half_width)
            normed[:n, cols], normed[n:, cols] = tokens[i][...], tokens[2 + i][...]
        back[:n] = live_rows(tokens[4][...].astype(f32), lengths_ref).astype(bf)
        back[n:] = live_rows(tokens[5][...].astype(f32), came_ref).astype(bf)
        for c in copies:
            c.wait()

    w_gate = flat(held[pl.ds(step * own, own), 0:units])
    w_up = flat(held[pl.ds(chips // 2 + step * own, own), 0:units])
    w_down = flat(held[pl.ds(step * 2 * own, 2 * own), units : units + half])
    gate, up = dot(normed[...], w_gate, NT), dot(normed[...], w_up, NT)
    grad_act = dot(back[...], w_down, NT)
    sigma = 1.0 / (1.0 + jnp.exp(-gate))
    swish = gate * sigma
    act = (swish * up).astype(bf)
    grad_gate = (grad_act * up * (sigma * (1.0 + gate * (1.0 - sigma)))).astype(bf)
    grad_up = (grad_act * swish).astype(bf)
    branch = dot(act, w_down)
    two = dot(jnp.concatenate([grad_gate, grad_up], axis=1), jnp.concatenate([w_gate, w_up], axis=0))
    for i, value in enumerate((branch, two)):
        if steps > 1:

            @pl.when(step == 0)
            def _():
                sums[i] = value

            @pl.when((step > 0) & (step < steps - 1))
            def _():
                sums[i] += value

        @pl.when(step == steps - 1)
        def _():
            total = value + sums[i] if steps > 1 else value
            results[2 * i][...] = total[:n]
            results[2 * i + 1][...] = total[n:].astype(bf)

    put = lambda v: v.astype(bf).reshape(own, units, width)
    dealt[pl.ds(step * own, own), 0:units] = put(dot(grad_gate, normed[...], TN))
    dealt[pl.ds(chips // 2 + step * own, own), 0:units] = put(dot(grad_up, normed[...], TN))
    grad_down = dot(act, back[...], TN).astype(bf)
    for b in range(2 * own):
        dealt[(step * 2 * own + b) ^ turned, units : units + half] = grad_down[b * half : (b + 1) * half]

    @pl.when(step == steps - 1)
    def _():
        copies, at = [], 0
        for ref in grads:
            for b in range(ref.shape[0]):
                copies.append(
                    pltpu.make_async_copy(dealt.at[chip_of(spot_ref, out_slots[at], size)], ref.at[b], sem.at[0, at])
                )
                at += 1
        run_copies(copies)


def ffn_call(chain, spot, lengths, tokens, pieces, blocks, slots, out_slots, size, crossed, chunk=512):
    n, d = tokens[-1].shape
    chips, rows = len(slots), pieces[0].shape[1]
    units = rows * 2 // 3
    steps = chips // 2 * units // chunk
    return chain.call(
        functools.partial(ffn_kernel, len(pieces), len(blocks), steps, slots, out_slots, size, crossed), "ffn",
        (spot, *lengths, *tokens, *pieces),
        [smem()] * 3 + [fixed(*v.shape) for v in tokens] + [anywhere() for _ in pieces],
        [fixed(n, d)] * 4 + [anywhere() for _ in blocks],
        [shaped((n, d), f32), shaped((n, d), bf)] * 2 + [shaped((b, rows, d), bf) for b in blocks],
        grid=(steps,),
        scratch_shapes=[
            pltpu.VMEM((chips, rows, d), bf), pltpu.VMEM((chips, rows, d), bf),
            pltpu.VMEM((2 * n, d), bf), pltpu.VMEM((2 * n, d), bf), pltpu.VMEM((2, 2 * n, d), f32),
            pltpu.SemaphoreType.DMA((2, chips)),
        ],
    )


def normed_kernel(spot_ref, own_ref, other_ref, own_out, other_out, full):
    half = own_out.shape[1]
    cols = pl.ds(pl.multiple_of(spot_ref[3] * half, half), half)
    for ref, out in ((own_ref, own_out), (other_ref, other_out)):
        source = ref[...].astype(f32)
        scale = lax.rsqrt(jnp.mean(source * source, axis=-1, keepdims=True) + NORM_EPS)
        full[...] = (source * scale).astype(bf)
        out[...] = full[:, cols]


def normed_call(chain, spot, own, other, parts=2):
    rows, width = own.shape
    block = pl.BlockSpec((rows // parts, width), lambda i: (i, 0))
    thin = pl.BlockSpec((rows // parts, width // 2), lambda i: (i, 0))
    return chain.call(
        normed_kernel, "normed", (spot, own, other), [smem(), block, block],
        [thin] * 2, [shaped((rows, width // 2), bf)] * 2,
        grid=(parts,), scratch_shapes=[pltpu.VMEM((rows // parts, width), bf)],
    )


def live_rows(values, lengths_ref, first=0):
    total = lengths_ref[0, 0] + lengths_ref[0, 1] + lengths_ref[0, 2]
    place = lax.broadcasted_iota(jnp.int32, (values.shape[0], 1), 0) + first
    return jnp.where(place < total, values, jnp.zeros((), values.dtype))


def pack_kernel(
    spot_ref, mixer_ref, gate_up_ref, down_ref, gains_ref, mixer_mine, mixer_theirs, gate_mine, gate_theirs, down_low, note
):
    half, units, core = mixer_mine.shape[1], gate_mine.shape[0], spot_ref[3]
    for ref, cols, rows, c in ((mixer_mine, half, units, core), (mixer_theirs, half, units, 1 - core)):
        ref[...] = mixer_ref[:, pl.ds(pl.multiple_of(c * half, half), half)].astype(bf)
    for ref, c in ((gate_mine, core), (gate_theirs, 1 - core)):
        ref[:units] = gate_up_ref[pl.ds(pl.multiple_of(c * units, units), units), :].astype(bf)
    count, own = gains_ref.shape
    note[...] = jnp.zeros_like(note)
    note[:count, :own] = gains_ref[...].astype(bf)
    gate_theirs[units:] = jnp.zeros((note.shape[0], gate_theirs.shape[1]), bf)
    gate_theirs[units:, : note.shape[1]] = note[...]
    down_low[...] = down_ref[...].astype(bf)


def pack_call(chain, spot, mixer, gate_up, down, gains):
    (rows, width), (units, _), (half, _) = mixer.shape, gate_up.shape, down.shape
    shapes = [(rows, width // 2)] * 2 + [(units // 2, width), (units // 2 + NOTE, width), (half, width), (NOTE, 128)]
    return chain.call(
        pack_kernel, "pack", (spot, mixer, gate_up, down, gains),
        [smem(), fixed(rows, width), fixed(units, width), fixed(half, width), fixed(*gains.shape)],
        [fixed(*s) for s in shapes], [shaped(s, bf) for s in shapes], grid=(1,),
    )


def block_kernel(own_gains, spot_ref, mine_ref, came_ref, note_ref, gate_ref, all_ref, copies_ref):
    rows, w = mine_ref.shape[0], all_ref.shape[1]
    mine = note_ref[...].astype(f32)
    came = gate_ref[gate_ref.shape[0] - NOTE :, :w].astype(f32)
    turned = lambda v: pltpu.roll(v, own_gains, 1)
    note = jnp.where(spot_ref[3] == 0, mine + turned(came), came + turned(mine)).astype(bf)
    at = 0
    for side in range(2):
        cols = slice(side * w, (side + 1) * w)
        all_ref[at : at + rows] = mine_ref[:, cols]
        all_ref[at + rows : at + 2 * rows] = came_ref[:, cols]
        all_ref[at + 2 * rows : at + 2 * rows + NOTE] = note
        at += 2 * rows + NOTE
    count = 2 * rows + NOTE
    for c in range(copies_ref.shape[0] // count):
        copies_ref[c * count : (c + 1) * count] = all_ref[:count]


def block_call(chain, spot, mine, came, note, gate_came, own_gains, copies, waits):
    rows, width = mine.shape
    w = width // 2
    each = 2 * rows + NOTE
    return chain.call(
        functools.partial(block_kernel, own_gains), "block", (spot, mine, came, note, gate_came),
        [smem()] + [fixed(*v.shape) for v in (mine, came, note, gate_came)],
        [fixed(2 * each, w), fixed(copies * each, w)], [shaped((2 * each, w), bf), shaped((copies * each, w), bf)],
        grid=(1,), waits=waits,
    )


def stack_kernel(count, moves, spot_ref, *refs):
    for i, a, rows, o, b in moves:
        if not isinstance(a, int):
            stride, distance, first = a
            a = pl.multiple_of((spot_ref[2] ^ distance) * stride + first, NOTE)
        refs[count + o][b : b + rows] = refs[i][pl.ds(a, rows)]


def stack_call(chain, spot, arrays, rows, moves, waits=()):
    like = {o: arrays[i] for i, _, _, o, _ in moves}
    shapes = [(r,) + like[o].shape[1:] for o, r in enumerate(rows)]
    return chain.call(
        functools.partial(stack_kernel, len(arrays), moves), "stack", (spot, *arrays),
        [smem()] + [fixed(*v.shape) for v in arrays],
        [fixed(*s) for s in shapes], [shaped(s, like[o].dtype) for o, s in enumerate(shapes)], grid=(1,), waits=waits,
    )


def corner_kernel(cut, extra, x_ref, y_ref, to_x_ref, to_y_ref):
    rows = x_ref.shape[0]
    to_x_ref[:cut] = y_ref[:cut]
    if extra:
        to_x_ref[cut:] = y_ref[rows - extra :]
    to_y_ref[...] = x_ref[cut : rows - extra]


def corner_call(chain, from_x, from_y, extra):
    total, width = from_x.shape
    cut = (total - extra) // 2
    shapes = [(cut + extra, width), (cut, width)]
    return chain.call(
        functools.partial(corner_kernel, cut, extra), "corner", (from_x, from_y), [fixed(total, width)] * 2,
        [fixed(*s) for s in shapes], [shaped(s, bf) for s in shapes], grid=(1,),
    )


def near_kernel(to_x_ref, to_y_ref, by_x_ref, by_y_ref, new_x_ref, new_y_ref):
    new_x_ref[...] = (to_x_ref[...].astype(f32) + by_y_ref[...].astype(f32)).astype(bf)
    new_y_ref[...] = (to_y_ref[...].astype(f32) + by_x_ref[...].astype(f32)).astype(bf)


def near_call(chain, to_x, to_y, by_x, by_y, parts=2, **options):
    rows, width = by_x.shape
    block = (rows // parts, width)
    low, high = pl.BlockSpec(block, lambda i: (i, 0)), pl.BlockSpec(block, lambda i: (i + parts, 0))
    return chain.call(
        near_kernel, "near", (to_x, to_y, by_x, by_y), [high, low, low, low], [high, low],
        [shaped(to_x.shape, bf), shaped(to_y.shape, bf)], grid=(parts,), input_output_aliases={0: 0, 1: 1}, **options,
    )


def line_kernel(count, *refs):
    parts, refs = refs[:count], refs[count:]
    rows = refs[-1].shape[0]

    def total(at):
        result = parts[0][pl.ds(at, rows)].astype(f32)
        for ref in parts[1:]:
            result = result + ref[pl.ds(at, rows)].astype(f32)
        return result

    for s, ref in enumerate(refs):
        ref[...] = total(s * rows).astype(ref.dtype)


def line_call(chain, parts, size, apart, **options):
    quarters = 4 if len(parts) == 1 else 1
    rows, width = parts[0].shape[0] // quarters // size, parts[0].shape[1]
    if apart:
        whole = lambda q: pl.BlockSpec((size * rows, width), lambda i: (q, 0))
        ins = [whole(q) for q in range(quarters)] if quarters > 1 else [whole(0)] * len(parts)
        specs = [fixed(rows, width)] * size
        shapes = [shaped((rows, width), f32)] + [shaped((rows, width), bf)] * (size - 1)
        steps = 1
    else:
        steps = 2
        half = size * rows // steps
        ins = [pl.BlockSpec((half, width), lambda i, q=q: (i + q * steps, 0)) for q in range(quarters)]
        ins = ins if quarters > 1 else ins * len(parts)
        specs, shapes = [pl.BlockSpec((half, width), lambda i: (i, 0))], [shaped((size * rows, width), bf)]
    parts = parts * quarters
    return chain.call(
        functools.partial(line_kernel, len(parts)), "line", parts, ins, specs, shapes, grid=(steps,), **options
    )


def finish_kernel(cuts, count, note, spot_ref, first_ref, *refs):
    came, more, outs, squares_ref, total = (
        refs[:count], refs[count : -len(cuts) - 2], refs[-len(cuts) - 2 : -2], refs[-2], refs[-1]
    )
    rows = total.shape[0]
    result = first_ref[:rows].astype(f32)
    for b in range(1, first_ref.shape[0] // rows):
        result = result + first_ref[b * rows : (b + 1) * rows].astype(f32)
    for ref in came:
        result = result + ref[...].astype(f32)
    total[...] = result
    squares = jnp.sum(result * result, axis=0, keepdims=True)
    if note:
        whole = jnp.sum(squares, axis=1, keepdims=True)
        for ref in more[:-1]:
            whole = whole + jnp.sum(ref[...], axis=1, keepdims=True)
        gains = jnp.sum(more[-1][...], axis=0, keepdims=True)
        squares = jnp.broadcast_to(whole + jnp.sum(gains * gains, axis=1, keepdims=True), squares_ref.shape)
    squares_ref[...] = squares
    for ref, start in zip(outs, cuts):
        rows = ref.shape[0]
        if not isinstance(start, int):
            start = pl.multiple_of((spot_ref[3] ^ start[0]) * rows, rows & -rows)
        ref[...] = total[pl.ds(start, rows), :]


def finish_call(chain, spot, first, came, blocks, cuts, note=0, more=(), waits=()):
    rows, width = first.shape[0] // blocks, first.shape[1]
    shapes = [(r, width) for _, r in cuts] + [(note, 128) if note else (1, width)]
    return chain.call(
        functools.partial(finish_kernel, [c for c, _ in cuts], len(came), note), "finish", (spot, first, *came, *more),
        [smem(), fixed(*first.shape)] + [fixed(rows, width)] * len(came) + [fixed(*v.shape) for v in more],
        [fixed(*s) for s in shapes], [shaped(s, f32) for s in shapes],
        grid=(1,), scratch_shapes=[pltpu.VMEM((rows, width), f32)], waits=waits,
    )


def adam_step(weight, grad, first, second, rate, decay):
    first_new = BETA_ONE * first + (1.0 - BETA_ONE) * grad
    second_new = BETA_TWO * second + (1.0 - BETA_TWO) * grad * grad
    corr_one = 1.0 / (1.0 - BETA_ONE**STEP)
    corr_two = 1.0 / (1.0 - BETA_TWO**STEP)
    update = first_new * (rate * corr_one) / (jnp.sqrt(second_new * corr_two) + ADAM_EPS)
    return (weight * (1.0 - rate * decay) - update, first_new, second_new)


def adam_kernel(spot_ref, note_ref, *refs):
    ins, outs, wide, tall = refs[:21], refs[21:35], refs[35], refs[36]
    mixer, gate_up, down, gains, parts = ins[:4], ins[4:7], ins[7:10], ins[10:13], ins[13:]
    mixer_out, gate_up_out, down_out, gains_out, norm_out = outs[:4], outs[4:7], outs[7:10], outs[10:13], outs[13]
    core, quarter = spot_ref[3], parts[0].shape[1]
    norm = jnp.sqrt(jnp.sum(note_ref[...], axis=0, keepdims=True)[:, :1])
    factor = CLIP_LIMIT / jnp.maximum(norm, CLIP_LIMIT)

    rows, step = mixer[0].shape[0], wide.shape[0]

    @pl.loop(0, rows // step)
    def _(i):
        at = pl.ds(pl.multiple_of(i * step, step & -step), step)
        for s in range(2):
            mine = pl.multiple_of(core * 2 * quarter, quarter) + s * quarter
            came = pl.multiple_of((1 - core) * 2 * quarter, quarter) + s * quarter
            wide[:, pl.ds(pl.multiple_of(mine, quarter), quarter)] = parts[s][at]
            wide[:, pl.ds(pl.multiple_of(came, quarter), quarter)] = parts[2 + s][at]
        old, first, second, average = (r[at] for r in mixer)
        new, first, second = adam_step(old, wide[...] * factor, first, second, RATE_MATRIX, DECAY_MATRIX)
        average = AVERAGE_KEEP * average + (1.0 - AVERAGE_KEEP) * new
        for ref, value in zip(mixer_out, (new, first, second, average)):
            ref[at] = value

    @pl.when(pl.program_id(0) == 0)
    def _():
        half = parts[4].shape[0]
        tall[pl.ds(pl.multiple_of(core * half, half), half), :] = parts[4][...]
        tall[pl.ds(pl.multiple_of((1 - core) * half, half), half), :] = parts[5][...]
        own = gains[0].shape[1]
        sums = jnp.sum(parts[7][...], axis=0, keepdims=True)
        gain_grad = jnp.concatenate([sums[:, :own], sums[:, own : 2 * own]])
        for olds, news, grad, rate, decay in (
            (gate_up, gate_up_out, tall[...], RATE_MATRIX, DECAY_MATRIX),
            (down, down_out, parts[6][...], RATE_MATRIX, DECAY_MATRIX),
            (gains, gains_out, gain_grad, RATE_GAIN, 0.0),
        ):
            old, first, second = (r[...] for r in olds)
            scale = factor if rate == RATE_MATRIX else factor[:, :1]
            for ref, value in zip(news, adam_step(old, grad * scale, first, second, rate, decay)):
                ref[...] = value
        norm_out[...] = norm


def adam_call(chain, spot, note, mixer, gate_up, down, gains, parts, blocks=1):
    rows, width = mixer[0].shape
    step = rows // blocks
    block = pl.BlockSpec((step, width), lambda i: (i, 0))
    piece = pl.BlockSpec((step, parts[0].shape[1]), lambda i: (i, 0))
    whole = lambda v: fixed(*v.shape)
    others = [*gate_up, *down, *gains]
    shapes = [v.shape for v in (*mixer, *others)] + [(1, 1)]
    return chain.call(
        adam_kernel, "adam", (spot, note, *mixer, *others, *parts),
        [smem(), whole(note)] + [block] * 4 + [whole(v) for v in others] + [piece] * 4
        + [whole(v) for v in parts[4:]],
        [block] * 4 + [whole(v) for v in others] + [fixed(1, 1)], [shaped(s, f32) for s in shapes],
        grid=(blocks,),
        scratch_shapes=[pltpu.VMEM((step // 3, width), f32), pltpu.VMEM(gate_up[0].shape, f32)],
    )


def flip(v, axis, bits=1):
    size = lax.axis_size(axis)
    return lax.ppermute(v, axis, [(i, i ^ bits) for i in range(size)])


def swap(v):
    return flip(v, "core")


def join(mine, other, core, axis=0):
    return jnp.where(
        core == 0,
        jnp.concatenate([mine, other], axis=axis),
        jnp.concatenate([other, mine], axis=axis),
    )


def part(v, index, axis=0):
    size = v.shape[axis] // 2
    return lax.dynamic_slice_in_dim(v, index * size, size, axis)


def low(v):
    return v.astype(bf)


def wide(v):
    return v.astype(f32)


class Whole:
    crossed = False
    mixer_slots = ((0,), (0,))
    mixer_blocks = (1,)

    def __init__(self, spot, groups):
        self.spot, self.core = spot, spot[3]
        self.size = lax.axis_size("z")
        self.chips = lax.axis_size("d0") * lax.axis_size("d1") * self.size
        self.ffn_in = self.ffn_out = tuple(range(groups))
        self.ffn_blocks = (groups,)

    def gather(self, chain, mixer, gate_up, down, gains, waits):
        def trade(v, axis):
            return join(part(v, self.core, axis), swap(part(v, 1 - self.core, axis)), self.core)

        everything = lambda v: lax.all_gather(v, CHIPS, axis=0, tiled=True)
        mixer_block = trade(low(mixer), 1)
        w, groups = mixer_block.shape[1] // 2, len(self.ffn_in)
        sides = []
        for s in range(2):
            whole = everything(mixer_block[:, s * w : (s + 1) * w])
            sides.append(([whole], ((0, 0, whole.shape[0], 0, None),), ()))
        ffn = [everything(v).reshape(groups, -1, v.shape[1]) for v in (trade(low(gate_up), 0), low(down))]
        ffn = [jnp.concatenate(ffn, axis=1)]
        gains = lax.all_gather(wide(low(gains)), EVERY, axis=1, tiled=True)
        yield jnp.pad(gains, ((0, NOTE - 2), (0, 0)))
        while True:
            yield sides, ffn

    def scatter(self, chain, parts, cuts, groups=1, apart=False):
        grads = parts[0].reshape(groups, -1, parts[0].shape[-1])
        rows = grads.shape[1] * 2 // 3
        if groups > 1:
            shards = [grads[:, :rows], grads[:, rows:]]
        else:
            shards = [grads]
        shards = [wide(lax.psum_scatter(flat(v), CHIPS, scatter_dimension=0, tiled=True)) for v in shards]
        outs = [part(shards[0], self.core), part(shards[0], 1 - self.core)] + shards[1:]
        squares = sum(jnp.sum(v * v, axis=0, keepdims=True) for v in shards)
        if groups == 1:
            yield
            yield ()
        through = yield ()
        yield (), through
        yield
        yield outs + [squares]

    def spread_gains(self, grads, rows):
        one, two = grads
        nothing = jnp.zeros_like(one)
        one = join(one, nothing, self.core, 1)
        return lax.psum_scatter(jnp.concatenate([one, two]), EVERY, scatter_dimension=1, tiled=True)

    def total(self, v):
        return lax.psum(v, EVERY)


class Cube(Whole):
    crossed = True
    near = ((0, 0), (0, 1), (1, 0), (1, 1))

    def __init__(self, spot, groups):
        super().__init__(spot, groups)
        slots = lambda fixed_z: tuple((y, x, s, fixed_z) for y, x in self.near for s in range(self.size))
        self.mixer_slots = slots(False), slots(True)
        self.ffn_in = slots(True)
        self.ffn_out = tuple((y, x, z, True) for z in range(self.size) for y, x in self.near)
        self.mixer_blocks = (self.size,) * 3 + (self.size // 2,) * 2

    def lines(self, block):
        return [flip(block, "z", s) for s in range(1, self.size)]

    def gather(self, chain, mixer, gate_up, down, gains, waits):
        spot = self.spot
        mixer_mine, mixer_theirs, gate_mine, gate_theirs, down_low, note = pack_call(
            chain, spot, mixer, gate_up, down, gains
        )
        gate_came = swap(gate_theirs)
        size = self.size
        own, block = block_call(
            chain, spot, mixer_mine, swap(mixer_theirs), note, gate_came, gains.shape[1], size, waits
        )
        line = self.along_z(block)
        own_x, own_y = flip(own, "d1"), flip(own, "d0")
        yield None
        rows = own.shape[0] // 2 - NOTE
        half = rows // 2
        sides = []

        def spread_out(line):
            return line, flip(line, "d1"), flip(line, "d0")

        def turn_corner(from_x, from_y, extra=0):
            to_x, to_y = corner_call(chain, from_x, from_y, extra)
            return flip(to_x, "d1"), flip(to_y, "d0")

        def plan(side):
            found = [(p, side * (rows + NOTE) + h * half, half, near + (0, False), h) for p, near in enumerate(self.near[:3]) for h in range(2)]
            found += [(3, h * half, half, (1, 1, 0, False), h) for h in range(2)]
            last = (size - 1) * 2
            for at in range(last):
                s, h = at // 2 + 1, at % 2
                found += [(4 + p, at * half, half, near + (s, False), h) for p, near in enumerate(self.near[:3])]
                found.append((7 + (at >= last // 2), at % (last // 2) * half, half, (1, 1, s, False), h))
            return tuple(found)

        corner = turn_corner(own_x, own_y)
        yield
        chain.pause(corner)
        others, line_rows = range(1, size), (size - 1) * rows
        moves = [(0, (rows + NOTE, s, 0), rows, 0, (s - 1) * rows) for s in others]
        moves += [(0, (rows + NOTE, s, rows), NOTE, 0, line_rows + (s - 1) * NOTE) for s in others]
        moves += [(1, rows + NOTE, rows, 1, s * rows) for s in range(size)]
        line, block = stack_call(
            chain, spot, (line, own), (line_rows + (size - 1) * NOTE, size * rows), tuple(moves)
        )
        first = spread_out(line)
        line = self.along_z(block)
        yield
        first_corner = turn_corner(*first[1:], (size - 1) * NOTE)
        notes = [(p, rows, near + (0, False)) for p, near in enumerate(self.near)]
        for s in others:
            notes += [(4 + p, line_rows + (s - 1) * NOTE, near + (s, False)) for p, near in enumerate(self.near[:3])]
            notes.append((7, line_rows // 2 + (s - 1) * NOTE, (1, 1, s, False)))
        sides.append(([own, own_x, own_y, corner[0], *first, *first_corner], plan(0), tuple(notes)))
        units, count = gate_mine.shape[0], down_low.shape[0]
        ffn_rows = 2 * units + count
        moves = [(0, (rows, s, 0), rows, 0, (s - 1) * rows) for s in others]
        for s in range(size):
            at = s * ffn_rows
            moves += [(1, 0, units, 1, at), (2, 0, units, 1, at + units), (3, 0, count, 1, at + 2 * units)]
        line, block = stack_call(
            chain, spot, (line, gate_mine, gate_came, down_low), (line_rows, size * ffn_rows), tuple(moves)
        )
        across, line = line, self.along_z(block)
        second = spread_out(*chain.pause(first_corner, (across,)))
        yield sides, None
        second_corner = turn_corner(*second[1:])
        sides.append(([own, own_x, own_y, corner[1], *second, *second_corner], plan(1), ()))
        ffn = spread_out(*chain.pause(second_corner, (line,)))
        yield sides, None
        ffn = (*ffn, *turn_corner(*ffn[1:]))
        yield sides, [v.reshape(-1, ffn_rows, v.shape[-1]) for v in ffn]

    def along_z(self, v):
        return lax.all_to_all(v, "z", 0, 0, tiled=True)

    def scatter(self, chain, parts, cuts, groups=1, apart=False):
        if groups > 1:
            came = (self.along_z(flat(parts[0])),)
        else:
            own, to_x, to_y, far_low, far_high = (flat(v) for v in parts)
            by_x, by_y = flip(far_low, "d1"), flip(far_high, "d0")
            yield
            to_x, to_y = yield near_call(chain, to_x, to_y, by_x, by_y)
            came = own, flip(to_x, "d1"), flip(to_y, "d0")
        through = yield came
        outs = line_call(chain, came, self.size, apart, through=through or ())
        count = self.size if apart else 1
        first, *rest = yield outs[:count], outs[count:]
        if groups > 1:
            to_x, to_y, far = rest
            far = lax.ppermute(far, ("d0", "d1"), [(i, i ^ 3) for i in range(4)])
            came = flip(to_x, "d1"), flip(to_y, "d0"), far
        elif apart:
            came = [flip(v, "z", s + 1) for s, v in enumerate(rest)]
        else:
            first, came = self.along_z(first), ()
        more, waits = yield
        yield finish_call(
            chain, self.spot, first, came, 1 if apart else self.size, cuts, 2 * self.chips if more else 0, more, waits
        )

    def spread_gains(self, grads, rows):
        return self.everyone(rows)

    def everyone(self, rows):
        return lax.all_to_all(rows, EVERY, 0, 0, tiled=True)


def body(
    inputs, lengths, filters, cotangent, mixer_weight, gate_up_weight, down_weight, norm_gains,
    mixer_first, gate_up_first, down_first, gains_first,
    mixer_second, gate_up_second, down_second, gains_second, mixer_average,
):
    slots, width = inputs.shape
    size = lax.axis_size("z")
    groups = 2 * FF // 256
    cube = lax.axis_size("d0") == 2 and lax.axis_size("d1") == 2 and size == 4
    spot = jnp.stack([lax.axis_index(a) for a in EVERY]).astype(jnp.int32)
    core = spot[3]
    links = (Cube if cube else Whole)(spot, groups)
    units = gate_up_weight.shape[0]
    chain = Chain()

    sums = lengths, swap(lengths)
    source_other, cotangent_other = swap(inputs), swap(cotangent)
    taps = jnp.concatenate([wide(filters), jnp.eye(AR_ORDER, slots, dtype=f32)])
    taps_turned = jnp.roll(taps[:, ::-1], 1 - slots // 4, axis=1)
    taps, taps_turned = (v.reshape(-1, 3, slots) for v in (taps, taps_turned))

    weights = links.gather(
        chain, mixer_weight, gate_up_weight, down_weight, norm_gains, (sums[1], source_other, cotangent_other)
    )
    gains = next(weights)
    tokens = hat_tokens = normed_call(chain, spot, inputs, source_other)
    blocks = taps.shape[0]
    cuts, spread = (0, blocks // 3, blocks * 4 // 9, blocks), None
    for at in range(3):
        spread = spread_call(chain, sums, taps_turned, *tokens, cuts[at], cuts[at + 1] - cuts[at], spread)
        sides = next(weights)
    sides, _ = sides
    quarter = sides[0][0][0].shape[1]
    *mixed, left, gains = (*mix_call(chain, spot, spread, 0, *sides[0], gains, size, width), gains)[:4]
    sides, _ = next(weights)
    mixed_own, mixed_other, right = mix_call(chain, spot, spread, 1, *sides[1], gains, size, width, mixed)
    _, ffn = next(weights)

    hidden, *normed_two = hidden_call(chain, inputs, mixed_own, swap(mixed_other), gains)
    tokens = (*normed_two, *(swap(v) for v in normed_two), cotangent, cotangent_other)
    branch_own, branch_other, two_own, two_other, *grad_ffn = ffn_call(
        chain, spot, sums, tokens, ffn, links.ffn_blocks, links.ffn_in, links.ffn_out, size, links.crossed
    )
    if cube:
        grad_ffn = chain.pause(through=grad_ffn)
    ffn_sum = links.scatter(chain, grad_ffn, ((0, units // 2), (units // 2, units // 2), (units, units // 2)), groups, True)
    ffn_came = next(ffn_sum)
    grad_hidden, grad_low, gains_two = turn_call(
        chain, lengths, hidden, cotangent, two_own, swap(two_other), gains
    )
    grad_other = swap(grad_low)
    rows = mixer_weight.shape[0]
    cuts = (((0,), rows), ((1,), rows))
    grads_of = lambda s: grad_call(
        chain, spot, gains, grad_low, grad_other, spread, s, quarter, links.mixer_blocks, links.mixer_slots[s], size
    )
    first_sum = links.scatter(chain, grads_of(0), cuts, apart=True)
    next(first_sum)
    second_sum = links.scatter(chain, grads_of(1), cuts)
    next(second_sum)
    backward = lambda first, steps, *more: back_call(
        chain, spot, sums, taps, grad_low, grad_other, (left, right), first, steps, *more
    )
    early = blocks // 2
    first_sum.send(next(first_sum))
    one = backward(0, early)
    second_sum.send(next(second_sum))
    one_own, one_other, gains_one, note_rows = backward(
        early, blocks - early, one, hat_tokens, gains_two, 2 * links.chips
    )
    outs, _ = first_sum.send(())
    first_sum.send(outs)
    if cube:
        (note_rows,) = chain.pause(ffn_came, (note_rows,))
    shard_gains = links.spread_gains((gains_one, gains_two), note_rows)
    outs, _ = second_sum.send(())
    chain.pause((shard_gains,))
    first_mine, first_theirs, square = first_sum.send(((), ()))
    first_theirs, branch_other, *outs = chain.pause(through=(first_theirs, branch_other, *outs))
    second_sum.send(outs)
    outs, _ = ffn_sum.send(())
    ffn_sum.send(outs)
    output = output_call(chain, hidden, branch_own, swap(branch_other))
    input_grad = last_call(chain, spot, grad_hidden, inputs, one_own, swap(one_other), gains)
    gate_up_mine, gate_up_theirs, shard_down, *squares = ffn_sum.send(((), ()))
    squares.append(square)
    gate_up_came, first_came = swap(gate_up_theirs), swap(first_theirs)
    second_mine, second_theirs, note = second_sum.send(((*squares, shard_gains), ()))
    second_came = swap(second_theirs)
    mixer = mixer_weight, mixer_first, mixer_second, mixer_average
    gate_up, down = (gate_up_weight, gate_up_first, gate_up_second), (down_weight, down_first, down_second)
    gain = norm_gains, gains_first, gains_second
    if cube:
        (
            mixer_new, mixer_first_new, mixer_second_new, mixer_average_new, gate_up_new, gate_up_first_new,
            gate_up_second_new, down_new, down_first_new, down_second_new, gains_new, gains_first_new, gains_second_new,
            grad_norm,
        ) = adam_call(
            chain, spot, links.everyone(note), mixer, gate_up, down, gain,
            (first_mine, second_mine, first_came, second_came, gate_up_mine, gate_up_came, shard_down, shard_gains),
        )
        grad_norm = grad_norm[0, 0]
    else:
        squares = sum(jnp.sum(v) for v in (*squares, note)) + jnp.sum(shard_gains * shard_gains)
        grad_norm = jnp.sqrt(links.total(squares))
        factor = CLIP_LIMIT / jnp.maximum(grad_norm, CLIP_LIMIT)
        shard_mixer = join(
            jnp.concatenate([first_mine, second_mine], axis=1), jnp.concatenate([first_came, second_came], axis=1), core, 1
        )
        shard_gate_up = join(gate_up_mine, gate_up_came, core)
        step = lambda old, grad: adam_step(old[0], grad * factor, old[1], old[2], RATE_MATRIX, DECAY_MATRIX)
        mixer_new, mixer_first_new, mixer_second_new = step(mixer, shard_mixer)
        gate_up_new, gate_up_first_new, gate_up_second_new = step(gate_up, shard_gate_up)
        down_new, down_first_new, down_second_new = step(down, shard_down)
        gains_new, gains_first_new, gains_second_new = adam_step(
            gain[0], shard_gains * factor, gain[1], gain[2], RATE_GAIN, 0.0
        )
        mixer_average_new = AVERAGE_KEEP * mixer_average + (1.0 - AVERAGE_KEEP) * mixer_new
    return (
        output, input_grad, grad_norm, mixer_new, gate_up_new, down_new, gains_new,
        mixer_first_new, gate_up_first_new, down_first_new, gains_first_new,
        mixer_second_new, gate_up_second_new, down_second_new, gains_second_new, mixer_average_new,
    )


def solution(mesh):
    outer, inner = mesh.shape["dp"], mesh.shape["fsdp"]
    side = math.isqrt(outer)
    if side * side != outer:
        side = 1
    split = jax.sharding.Mesh(
        np.asarray(mesh.devices).reshape(side, outer // side, inner // 2, 2), EVERY
    )
    rows, columns, whole = P(EVERY, None), P(None, EVERY), P()
    return jax.shard_map(
        body,
        mesh=split,
        in_specs=(
            rows, rows, whole, rows, rows, rows, rows, columns,
            rows, rows, rows, columns, rows, rows, rows, columns, rows,
        ),
        out_specs=(
            rows, rows, whole, rows, rows, rows, columns, rows, rows, rows, columns,
            rows, rows, rows, columns, rows,
        ),
        check_vma=False,
    )
```

```python
import functools
import math

import jax
import jax.numpy as jnp
import numpy as np
from jax import lax
from jax.experimental import pallas as pl
from jax.experimental.pallas import tpu as pltpu
from jax.sharding import PartitionSpec as P

bf = jnp.bfloat16
f32 = jnp.float32
FILTERS = 24
AR_ORDER = 3
FF = 2048
STEP = 10
NORM_EPS = 1e-05
CLIP_LIMIT = 1.0
BETA_ONE = 0.9
BETA_TWO = 0.95
ADAM_EPS = 1e-08
RATE_MATRIX = 0.03
RATE_GAIN = 0.5
DECAY_MATRIX = 0.1
AVERAGE_KEEP = 0.9
CHIPS = ("d0", "d1", "z")
EVERY = CHIPS + ("core",)


NT = (((1,), (1,)), ((), ()))
NN = (((1,), (0,)), ((), ()))
TN = (((0,), (0,)), ((), ()))


def dot(a, b, dims=NN):
    return lax.dot_general(a, b, dims, preferred_element_type=f32)


class Chain:
    def __init__(self):
        self.token = None

    def call(self, kernel, name, args, in_specs, out_specs, out_shape, waits=(), through=(), **options):
        count, single = len(args), not isinstance(out_shape, (list, tuple)) and not through
        if single:
            out_specs, out_shape = [out_specs], [out_shape]
        made = len(out_shape)
        aliases = options.pop("input_output_aliases", {})
        aliases = {**aliases, **{count + i: made + i for i in range(len(through))}}
        last = tuple(through) + tuple(waits) + (() if self.token is None else (self.token,))

        def whole(*refs):
            first = count + len(last)
            kernel(*refs[:count], *refs[first : first + made], *refs[first + made + len(through) + 1 :])

        *outs, self.token = pl.pallas_call(
            whole,
            name=name,
            in_specs=list(in_specs) + [anywhere() for _ in last],
            out_specs=list(out_specs) + [anywhere() for _ in through] + [anywhere()],
            out_shape=list(out_shape) + [shaped(v.shape, v.dtype) for v in through] + [shaped((8, 128), f32)],
            input_output_aliases=aliases,
            compiler_params=pltpu.CompilerParams(vmem_limit_bytes=64 << 20),
            cost_estimate=pl.CostEstimate(flops=1, bytes_accessed=1, transcendentals=0),
            **options,
        )(*args, *last)
        return outs[0] if single else outs

    def pause(self, waits=(), through=()):
        return self.call(lambda: None, "pause", (), [], [], [], waits=waits, through=through)


def smem():
    return pl.BlockSpec(memory_space=pltpu.SMEM)


def anywhere():
    return pl.BlockSpec(memory_space=pl.ANY)


def fixed(*shape):
    return pl.BlockSpec(shape, lambda i: (0,) * len(shape))


NOTE = 16


def shaped(shape, dtype):
    return jax.ShapeDtypeStruct(tuple(shape), dtype)


def segment_of(place, ends_ref, group):
    return sum((place >= ends_ref[group, j]).astype(jnp.int32) for j in range(3))


def causal_mask(ends_ref, group, n, transposed):
    down = lax.broadcasted_iota(jnp.int32, (n, 1), 0)
    along = lax.broadcasted_iota(jnp.int32, (1, n), 1)
    one, two = segment_of(down, ends_ref, group), segment_of(along, ends_ref, group)
    order = (down <= along) if transposed else (down >= along)
    return ((one == two) & (one < 3) & order).astype(f32).astype(bf)


def diagonals(row, count):
    wide = jnp.broadcast_to(row, (count, row.shape[-1]))
    return pltpu.roll(wide, 0, 1, stride=1, stride_axis=0).astype(bf)


def spread_kernel(lengths_ref, came_ref, taps_ref, own_ref, other_ref, *refs):
    u_ref, mask, table, ends = refs[-4:]
    n = mask.shape[1]
    q, h, w = n // 4, n // 2, own_ref.shape[1] // 2
    per = taps_ref.shape[1]

    @pl.when(pl.program_id(0) == 0)
    def _():
        find_ends(ends, lengths_ref, came_ref)
        for g in range(2):
            mask[g] = causal_mask(ends, g, n, False)
        table[...] = jnp.zeros_like(table)

    @pl.loop(0, per)
    def _(j):
        at = pl.multiple_of(j * w, w)
        strip = diagonals(taps_ref[0, pl.ds(j, 1), :], q)
        for g, tokens in enumerate((own_ref, other_ref)):
            for i in range(4):
                rows, cols = slice(i * q, (i + 1) * q), slice(0, (i + 1) * q)
                table[g, rows, cols] = strip[:, (3 - i) * q :] * mask[g, rows, cols]
            upper = dot(table[g, :h, :h], tokens[:h]).astype(bf)
            lower = dot(table[g, h:, :], tokens[...]).astype(bf)
            for side in range(2):
                cols = slice(side * w, (side + 1) * w)
                u_ref[side, g * n : g * n + h, pl.ds(at, w)] = upper[:, cols]
                u_ref[side, g * n + h : (g + 1) * n, pl.ds(at, w)] = lower[:, cols]


def find_ends(ends, lengths_ref, came_ref):
    for g, ref in enumerate((lengths_ref, came_ref)):
        total = ref[0, 0]
        ends[g, 0] = total
        for j in range(1, 3):
            total = total + ref[0, j]
            ends[g, j] = total


def spread_call(chain, lengths, taps, own, other, first, steps, into=None):
    blocks, per, n = taps.shape
    w = own.shape[1] // 2
    args = [*lengths, taps, own, other]
    specs = [smem()] * 2 + [pl.BlockSpec((1, per, n), lambda i: (i + first, 0, 0)), fixed(n, 2 * w), fixed(n, 2 * w)]
    options = {}
    if into is not None:
        options = dict(input_output_aliases={len(args): 0})
        args, specs = args + [into], specs + [anywhere()]
    return chain.call(
        spread_kernel, "spread", args, specs,
        pl.BlockSpec((2, 2 * n, per * w), lambda i: (0, 0, i + first)),
        shaped((2, 2 * n, blocks * per * w), bf),
        grid=(steps,),
        scratch_shapes=[pltpu.VMEM((2, n, n), bf), pltpu.VMEM((2, n, n), bf), pltpu.SMEM((2, 3), jnp.int32)],
        **options,
    )


def run_copies(copies):
    for c in copies:
        c.start()
    for c in copies:
        c.wait()


def chip_of(spot_ref, slot, size):
    if isinstance(slot, int):
        return slot
    dy, dx, dz, fixed_z = slot
    return ((spot_ref[0] ^ dy) * 2 + (spot_ref[1] ^ dx)) * size + (dz if fixed_z else spot_ref[2] ^ dz)


def collect(spot_ref, pieces, plan, size, held, sem, columns):
    copies = []
    for at, (piece, row, rows, slot, half) in enumerate(plan):
        place = chip_of(spot_ref, slot, size)
        if half is not None:
            place = place * 2 + (spot_ref[3] ^ half)
        start = pl.multiple_of(place * rows, math.gcd(rows, 512))
        copies.append(
            pltpu.make_async_copy(pieces[piece].at[pl.ds(row, rows)], held.at[pl.ds(start, rows), columns], sem.at[at])
        )
    return copies


def mix_kernel(count, plan, notes, size, width, side, spot_ref, u_ref, *refs):
    pieces, refs = refs[:count], refs[count:]
    first = side == 0
    before, refs = refs[: 0 if first else 2], refs[0 if first else 2 :]
    if not notes:
        gains_ref, refs = refs[0], refs[1:]
    own_ref, other_ref, w_ref, *refs = refs
    if notes:
        gains_ref, refs = refs[0], refs[1:]
    held, u, sem, u_sem, *refs = refs
    *refs, result = refs
    tiles = sums = refs[0] if refs else None
    w = held.shape[1]
    filters = held.shape[0] // width
    rows = own_ref.shape[0]
    copies = collect(spot_ref, pieces, plan, size, held, sem, slice(0, w))
    for at, (piece, row, slot) in enumerate(notes):
        copies.append(
            pltpu.make_async_copy(
                pieces[piece].at[pl.ds(row, NOTE)], tiles.at[chip_of(spot_ref, slot, size)], sem.at[len(plan) + at]
            )
        )
    third = filters // 3
    cols = [pl.ds(t * third * w, third * w) for t in range(3)]
    loads = [pltpu.make_async_copy(u_ref.at[side, :, c], u.at[:, c], u_sem.at[t]) for t, c in enumerate(cols)]
    adds = [pltpu.make_async_copy(ref, sums.at[g], u_sem.at[4 + g]) for g, ref in enumerate(before)]
    for c in copies + loads + adds:
        c.start()
    for c in copies:
        c.wait()
    give = pltpu.make_async_copy(held, w_ref, u_sem.at[3])
    give.start()
    if notes:
        lanes = width // len(notes)
        for b in range(width // 128):
            block = jnp.zeros((NOTE, 128), f32)
            for j in range(128 // lanes):
                tile = tiles[b * (128 // lanes) + j].astype(f32)
                block = block + (pltpu.roll(tile, j * lanes, 1) if j else tile)
            gains_ref[:, b * 128 : (b + 1) * 128] = block
    gain = gains_ref[0:1, pl.ds(pl.multiple_of((spot_ref[3] * 2 + side) * w, w), w)]
    result[...] = jnp.zeros_like(result)

    @pl.loop(0, 3)
    def _(t):
        pltpu.make_async_copy(u_ref.at[side, :, pl.ds(0, third * w)], u.at[:, pl.ds(0, third * w)], u_sem.at[t]).wait()
        first_row = pl.multiple_of(t * third * width, width)
        wide = jnp.concatenate(
            [(held[pl.ds(first_row + k * width, width), :].astype(f32) * gain).astype(bf) for k in range(third)], axis=1
        )
        result[...] += dot(u[:, pl.ds(pl.multiple_of(t * third * w, w), third * w)], wide, NT)

    for g, out in enumerate((own_ref, other_ref)):
        mine = result[g * rows : (g + 1) * rows]
        if not first:
            adds[g].wait()
            mine = mine + sums[g]
        out[...] = mine.astype(out.dtype)
    give.wait()


def mix_call(chain, spot, u, side, pieces, plan, notes, gains, size, width, before=()):
    rows, depth = u.shape[1:]
    w = pieces[0].shape[-1]
    total = depth // w * width
    step = rows // 2
    out = fixed(step, width)
    note = fixed(NOTE, width)
    given = () if notes else (gains,)
    made = 1 - len(given)
    return chain.call(
        functools.partial(mix_kernel, len(pieces), plan, notes, size, width, side), "mix",
        (spot, u, *pieces, *before, *given),
        [smem(), anywhere()] + [anywhere() for _ in (*pieces, *before)] + [note for _ in given],
        [out, out, anywhere()] + [note] * made,
        [shaped((step, width), f32), shaped((step, width), bf if before else f32), shaped((total, w), bf)]
        + [shaped((NOTE, width), f32)] * made,
        grid=(1,),
        scratch_shapes=[
            pltpu.VMEM((total, w), bf), pltpu.VMEM((rows, depth), bf),
            pltpu.SemaphoreType.DMA((len(plan) + len(notes),)), pltpu.SemaphoreType.DMA((6,)),
        ] + [pltpu.VMEM((len(notes), NOTE, 128), bf)] * made + [pltpu.VMEM((2, step, width), f32)] * min(1, len(before))
        + [pltpu.VMEM((rows, width), f32)],
    )


def hidden_kernel(source_ref, own_ref, came_ref, gain_ref, hidden_ref, *normed_refs):
    hidden = source_ref[...].astype(f32) + (own_ref[...] + came_ref[...].astype(f32))
    scale = lax.rsqrt(jnp.mean(hidden * hidden, axis=-1, keepdims=True) + NORM_EPS)
    hidden_ref[...] = hidden
    normed = (hidden * scale * gain_ref[1:2]).astype(bf)
    width = normed_refs[0].shape[1]
    for i, ref in enumerate(normed_refs):
        ref[...] = normed[:, i * width : (i + 1) * width]


def hidden_call(chain, source, own, came, gain, parts=2):
    rows, width = source.shape
    block = pl.BlockSpec((rows // parts, width), lambda i: (i, 0))
    thin = pl.BlockSpec((rows // parts, width // 2), lambda i: (i, 0))
    return chain.call(
        hidden_kernel, "hidden", (source, own, came, gain), [block, block, block, fixed(NOTE, width)],
        [block, thin, thin], [shaped((rows, width), f32)] + [shaped((rows, width // 2), bf)] * 2,
        grid=(parts,),
    )


def norm_back(grad, hat, scale, gain):
    weighted = grad * gain
    return scale * (weighted - hat * jnp.mean(weighted * hat, axis=-1, keepdims=True))


def add_rows(ref, values, step):
    total = jnp.sum(values, axis=0, keepdims=True)

    @pl.when(step == 0)
    def _():
        ref[...] = total

    @pl.when(step > 0)
    def _():
        ref[...] += total


def turn_kernel(lengths_ref, hidden_ref, back_ref, own_ref, came_ref, gain_ref, grad_ref, low_ref, gains_ref):
    hidden = hidden_ref[...]
    scale = lax.rsqrt(jnp.mean(hidden * hidden, axis=-1, keepdims=True) + NORM_EPS)
    hat = hidden * scale
    two = own_ref[...] + came_ref[...].astype(f32)
    back = live_rows(back_ref[...].astype(f32), lengths_ref, pl.program_id(0) * hidden.shape[0])
    grad = back + norm_back(two, hat, scale, gain_ref[1:2])
    grad_ref[...] = grad
    low_ref[...] = grad.astype(bf)
    add_rows(gains_ref, two * hat, pl.program_id(0))


def turn_call(chain, lengths, hidden, back, own, came, gain, parts=2):
    rows, width = hidden.shape
    block = pl.BlockSpec((rows // parts, width), lambda i: (i, 0))
    return chain.call(
        turn_kernel, "turn", (lengths, hidden, back, own, came, gain), [smem()] + [block] * 4 + [fixed(NOTE, width)],
        [block, block, fixed(1, width)],
        [shaped((rows, width), f32), shaped((rows, width), bf), shaped((1, width), f32)],
        grid=(parts,),
    )


def output_kernel(hidden_ref, own_ref, came_ref, out_ref):
    out_ref[...] = (hidden_ref[...] + (own_ref[...] + came_ref[...].astype(f32))).astype(bf)


def output_call(chain, hidden, own, came, parts=2):
    rows, width = hidden.shape
    block = pl.BlockSpec((rows // parts, width), lambda i: (i, 0))
    return chain.call(
        output_kernel, "output", (hidden, own, came), [block] * 3, block, shaped((rows, width), bf), grid=(parts,),
    )


def last_kernel(spot_ref, grad_ref, source_ref, own_ref, came_ref, gain_ref, out_ref, one):
    half = own_ref.shape[1]
    core = spot_ref[3]
    one[:, pl.ds(pl.multiple_of(core * half, half), half)] = own_ref[...]
    one[:, pl.ds(pl.multiple_of((1 - core) * half, half), half)] = came_ref[...]
    source = source_ref[...].astype(f32)
    scale = lax.rsqrt(jnp.mean(source * source, axis=-1, keepdims=True) + NORM_EPS)
    out_ref[...] = grad_ref[...] + norm_back(one[...], source * scale, scale, gain_ref[0:1])


def last_call(chain, spot, grad_hidden, source, own, came, gain, parts=2):
    rows, width = source.shape
    block = pl.BlockSpec((rows // parts, width), lambda i: (i, 0))
    thin = pl.BlockSpec((rows // parts, width // 2), lambda i: (i, 0))
    return chain.call(
        last_kernel, "last", (spot, grad_hidden, source, own, came, gain),
        [smem(), block, block, thin, thin, fixed(NOTE, width)], block, shaped((rows, width), f32),
        grid=(parts,), scratch_shapes=[pltpu.VMEM((rows // parts, width), f32)],
    )


def grad_kernel(slots, size, side, spot_ref, gains_ref, own_ref, other_ref, u_ref, *refs):
    outs, (turned, held, sem) = refs[:-3], refs[-3:]
    n, width = own_ref.shape
    w = held.shape[1]
    per = u_ref.shape[2] // w
    step = pl.program_id(0)

    @pl.when(step == 0)
    def _():
        turned[:, :n] = own_ref[...].T
        turned[:, n:] = other_ref[...].T

    gain = gains_ref[0:1, pl.ds(pl.multiple_of((spot_ref[3] * 2 + side) * w, w), w)]
    result = dot(turned[...], u_ref[0])
    for j in range(per):
        at = pl.multiple_of((step * per + j) * width, width)
        held[pl.ds(at, width), :] = (result[:, j * w : (j + 1) * w] * gain).astype(bf)

    @pl.when(step == pl.num_programs(0) - 1)
    def _():
        rows = held.shape[0] // len(slots)
        copies, at = [], 0
        for ref in outs:
            for b in range(ref.shape[0] // rows):
                start = pl.multiple_of(chip_of(spot_ref, slots[at], size) * rows, math.gcd(rows, 512))
                copies.append(
                    pltpu.make_async_copy(held.at[pl.ds(start, rows)], ref.at[pl.ds(b * rows, rows)], sem.at[at])
                )
                at += 1
        run_copies(copies)


def grad_call(chain, spot, gains, own, other, u, side, w, blocks, slots, size, per=9):
    rows, depth = u.shape[1:]
    n, width = own.shape
    count = depth // w
    each = count * width // len(slots)
    return chain.call(
        functools.partial(grad_kernel, slots, size, side), "mixer_grad", (spot, gains, own, other, u),
        [smem(), fixed(NOTE, width), fixed(n, width), fixed(n, width), pl.BlockSpec((1, rows, per * w), lambda i: (side, 0, i))],
        [anywhere() for _ in blocks], [shaped((b * each, w), bf) for b in blocks],
        grid=(count // per,),
        scratch_shapes=[
            pltpu.VMEM((width, rows), bf), pltpu.VMEM((count * width, w), bf), pltpu.SemaphoreType.DMA((len(slots),)),
        ],
    )


def gain_rows(rows_ref, one, two, core, wide):
    devices, half = rows_ref.shape[0], one.shape[1]
    lanes = 2 * half // devices
    if lanes < 1 or 128 % lanes or 2 * lanes > 128:
        return
    wide[...] = jnp.zeros_like(wide)
    wide[:, pl.ds(pl.multiple_of(core * half, half), half)] = jnp.broadcast_to(one, (8, half))
    lane = lax.broadcasted_iota(jnp.int32, (8, 128), 1)
    for i in range(devices):
        block, turn = divmod(i * lanes, 128)
        cols = slice(block * 128, (block + 1) * 128)
        pair = []
        for tile, at in ((wide[:, cols], 0), (jnp.broadcast_to(two[:, cols], (8, 128)), lanes)):
            shift = (at - turn) % 128
            pair.append(pltpu.roll(tile, shift, 1) if shift else tile)
        row = jnp.where(lane < lanes, pair[0], jnp.where(lane < 2 * lanes, pair[1], 0.0))
        rows_ref[i : i + 1, :] = row[:1]


def back_kernel(first, spot_ref, lengths_ref, came_ref, taps_ref, own_ref, other_ref, left_ref, right_ref, *refs):
    if first:
        own_before, other_before, own_hat, other_hat, two_ref, own_out, other_out, gains_ref, rows_ref, wide, *refs = refs
        before = own_before, other_before
    else:
        own_out, other_out, *refs = refs
    mask, low_low, low_high, high, v_low, v_high, ends = refs
    n = mask.shape[1]
    q, h, d = n // 4, n // 2, own_ref.shape[1]
    per = taps_ref.shape[1]

    @pl.when(pl.program_id(0) == 0)
    def _():
        find_ends(ends, lengths_ref, came_ref)
        for g in range(2):
            mask[g] = causal_mask(ends, g, n, True)
        low_low[...] = jnp.zeros_like(low_low)
        high[...] = jnp.zeros_like(high)
        for g, ref in enumerate((own_out, other_out)):
            ref[...] = before[g][...] if first else jnp.zeros_like(ref)

    for j in range(per):
        weight = jnp.concatenate([left_ref[j * d : (j + 1) * d], right_ref[j * d : (j + 1) * d]], axis=1)
        s = diagonals(taps_ref[0, j : j + 1, :], q)
        a = j * h
        for g, grad in enumerate((own_ref, other_ref)):
            v = dot(grad[...], weight).astype(bf)
            v_low[g, a : a + h] = v[:h]
            v_high[g, a : a + h] = v[h:]
            m = mask[g]
            low_low[g, 0:q, a : a + q] = s[:, :q] * m[0:q, 0:q]
            low_low[g, 0:q, a + q : a + h] = s[:, q : 2 * q] * m[0:q, q : 2 * q]
            low_low[g, q:h, a + q : a + h] = s[:, :q] * m[q:h, q:h]
            low_high[g, 0:q, a : a + h] = s[:, 2 * q : 4 * q] * m[0:q, h:]
            low_high[g, q:h, a : a + h] = s[:, q : 3 * q] * m[q:h, h:]
            high[g, 0:q, a : a + h] = s[:, 0 : 2 * q] * m[h : h + q, h:]
            high[g, q:h, a + q : a + h] = s[:, 0:q] * m[h + q :, h + q :]
    for g, out in enumerate((own_out, other_out)):
        out[:h] += dot(low_low[g], v_low[g]) + dot(low_high[g], v_high[g])
        out[h:] += dot(high[g], v_high[g])
    if first:

        @pl.when(pl.program_id(0) == pl.num_programs(0) - 1)
        def _():
            products = own_out[...] * own_hat[...].astype(f32) + other_out[...] * other_hat[...].astype(f32)
            one = jnp.sum(products, axis=0, keepdims=True)
            gains_ref[...] = one
            gain_rows(rows_ref, one, two_ref, spot_ref[3], wide)


def back_call(chain, spot, lengths, taps, own, other, weights, first, steps, before=(), hats=(), two=None, devices=0):
    blocks, per, n = taps.shape
    rows, d = own.shape
    w = weights[0].shape[1]
    width = 2 * w
    scratch = lambda *s: pltpu.VMEM(s, bf)
    weight = pl.BlockSpec((per * d, w), lambda i: (i + first, 0))
    half = fixed(rows, width)
    more = (*before, *hats, two) if before else ()
    outs, shapes = [half] * 2, [shaped((rows, width), f32)] * 2
    scratches = [
        scratch(2, n, n), scratch(2, n // 2, per * n // 2),
        scratch(2, n // 2, per * n // 2), scratch(2, n // 2, per * n // 2),
        scratch(2, per * n // 2, width), scratch(2, per * n // 2, width), pltpu.SMEM((2, 3), jnp.int32),
    ]
    if before:
        outs = outs + [fixed(1, width), fixed(devices, 128)]
        shapes = shapes + [shaped((1, width), f32), shaped((devices, 128), f32)]
        scratches = [pltpu.VMEM((8, 2 * width), f32)] + scratches
    return chain.call(
        functools.partial(back_kernel, first), "spread_back", (spot, *lengths, taps, own, other, *weights, *more),
        [smem()] * 3 + [pl.BlockSpec((1, per, n), lambda i: (i + first, 0, 0)), fixed(rows, d), fixed(rows, d)]
        + [weight, weight] + [fixed(*v.shape) for v in more],
        outs, shapes, grid=(steps,), scratch_shapes=scratches,
    )


def flat(v):
    return v.reshape(-1, v.shape[-1])


def ffn_kernel(count, outs, steps, slots, out_slots, size, crossed, spot_ref, lengths_ref, came_ref, *refs):
    turned = spot_ref[3] if crossed else 0
    tokens, pieces, refs = refs[:6], refs[6 : 6 + count], refs[6 + count :]
    results, grads, (held, dealt, normed, back, sums, sem, token_sem) = refs[:4], refs[4 : 4 + outs], refs[4 + outs :]
    n = tokens[-1].shape[0]
    chips, units, width = held.shape[0], held.shape[1] * 2 // 3, held.shape[2]
    own, half = chips // 2 // steps, units // 2
    step = pl.program_id(0)

    @pl.when(step == 0)
    def _():
        half_width = tokens[0].shape[1]
        copies, at = [], 0
        for g in range(2):
            rows = pl.ds(g * n, n)
            for i in range(2):
                cols = pl.ds(i * half_width, half_width)
                copies.append(pltpu.make_async_copy(tokens[2 * g + i], normed.at[rows, cols], token_sem.at[2 * g + i]))
            copies.append(pltpu.make_async_copy(tokens[4 + g], back.at[rows], token_sem.at[4 + g]))
        for ref in pieces:
            for b in range(ref.shape[0]):
                chip = chip_of(spot_ref, slots[at], size)
                copies.append(
                    pltpu.make_async_copy(ref.at[b, pl.ds(0, units)], held.at[chip, pl.ds(0, units)], sem.at[0, at])
                )
                copies.append(
                    pltpu.make_async_copy(
                        ref.at[b, pl.ds(units, half)], held.at[chip ^ turned, pl.ds(units, half)], sem.at[1, at]
                    )
                )
                at += 1
        for c in copies:
            c.start()
        for c in copies[:6]:
            c.wait()
        for g, ref in enumerate((lengths_ref, came_ref)):
            back[g * n : (g + 1) * n] = live_rows(back[g * n : (g + 1) * n].astype(f32), ref).astype(bf)
        for c in copies[6:]:
            c.wait()

    w_gate = flat(held[pl.ds(step * own, own), 0:units])
    w_up = flat(held[pl.ds(chips // 2 + step * own, own), 0:units])
    w_down = flat(held[pl.ds(step * 2 * own, 2 * own), units : units + half])
    gate, up = dot(normed[...], w_gate, NT), dot(normed[...], w_up, NT)
    grad_act = dot(back[...], w_down, NT)
    sigma = 1.0 / (1.0 + jnp.exp(-gate))
    swish = gate * sigma
    act = (swish * up).astype(bf)
    grad_gate = (grad_act * up * (sigma * (1.0 + gate * (1.0 - sigma)))).astype(bf)
    grad_up = (grad_act * swish).astype(bf)
    put = lambda v: v.astype(bf).reshape(own, units, width)
    dealt[pl.ds(step * own, own), 0:units] = put(dot(grad_gate, normed[...], TN))
    dealt[pl.ds(chips // 2 + step * own, own), 0:units] = put(dot(grad_up, normed[...], TN))
    grad_down = dot(act, back[...], TN).astype(bf)
    for b in range(2 * own):
        dealt[(step * 2 * own + b) ^ turned, units : units + half] = grad_down[b * half : (b + 1) * half]

    def deal():
        copies, at = [], 0
        for ref in grads:
            for b in range(ref.shape[0]):
                chip = chip_of(spot_ref, out_slots[at], size)
                copies.append(pltpu.make_async_copy(dealt.at[chip], ref.at[b], sem.at[0, at]))
                at += 1
        return copies

    @pl.when(step == steps - 1)
    def _():
        for c in deal():
            c.start()

    branch = dot(act, w_down)
    two = dot(jnp.concatenate([grad_gate, grad_up], axis=1), jnp.concatenate([w_gate, w_up], axis=0))
    for i, value in enumerate((branch, two)):
        if steps > 1:

            @pl.when(step == 0)
            def _():
                sums[i] = value

            @pl.when((step > 0) & (step < steps - 1))
            def _():
                sums[i] += value

        @pl.when(step == steps - 1)
        def _():
            total = value + sums[i] if steps > 1 else value
            results[2 * i][...] = total[:n]
            results[2 * i + 1][...] = total[n:].astype(bf)

    @pl.when(step == steps - 1)
    def _():
        for c in deal():
            c.wait()


def ffn_call(chain, spot, lengths, tokens, pieces, blocks, slots, out_slots, size, crossed, chunk=1024):
    n, d = tokens[-1].shape
    chips, rows = len(slots), pieces[0].shape[1]
    units = rows * 2 // 3
    steps = chips // 2 * units // chunk
    return chain.call(
        functools.partial(ffn_kernel, len(pieces), len(blocks), steps, slots, out_slots, size, crossed), "ffn",
        (spot, *lengths, *tokens, *pieces),
        [smem()] * 3 + [anywhere() for _ in (*tokens, *pieces)],
        [fixed(n, d)] * 4 + [anywhere() for _ in blocks],
        [shaped((n, d), f32), shaped((n, d), bf)] * 2 + [shaped((b, rows, d), bf) for b in blocks],
        grid=(steps,),
        scratch_shapes=[
            pltpu.VMEM((chips, rows, d), bf), pltpu.VMEM((chips, rows, d), bf),
            pltpu.VMEM((2 * n, d), bf), pltpu.VMEM((2 * n, d), bf), pltpu.VMEM((2, 2 * n, d), f32),
            pltpu.SemaphoreType.DMA((2, chips)), pltpu.SemaphoreType.DMA((6,)),
        ],
    )


def normed_kernel(spot_ref, own_ref, other_ref, own_out, other_out, full):
    half = own_out.shape[1]
    cols = pl.ds(pl.multiple_of(spot_ref[3] * half, half), half)
    for ref, out in ((own_ref, own_out), (other_ref, other_out)):
        source = ref[...].astype(f32)
        scale = lax.rsqrt(jnp.mean(source * source, axis=-1, keepdims=True) + NORM_EPS)
        full[...] = (source * scale).astype(bf)
        out[...] = full[:, cols]


def normed_call(chain, spot, own, other, parts=2):
    rows, width = own.shape
    block = pl.BlockSpec((rows // parts, width), lambda i: (i, 0))
    thin = pl.BlockSpec((rows // parts, width // 2), lambda i: (i, 0))
    return chain.call(
        normed_kernel, "normed", (spot, own, other), [smem(), block, block],
        [thin] * 2, [shaped((rows, width // 2), bf)] * 2,
        grid=(parts,), scratch_shapes=[pltpu.VMEM((rows // parts, width), bf)],
    )


def live_rows(values, lengths_ref, first=0):
    total = lengths_ref[0, 0] + lengths_ref[0, 1] + lengths_ref[0, 2]
    place = lax.broadcasted_iota(jnp.int32, (values.shape[0], 1), 0) + first
    return jnp.where(place < total, values, jnp.zeros((), values.dtype))


def pack_kernel(
    spot_ref, mixer_ref, gate_up_ref, down_ref, gains_ref, mixer_mine, mixer_theirs, gate_mine, gate_theirs, down_low, note
):
    half, units, core = mixer_mine.shape[1], gate_mine.shape[0], spot_ref[3]
    for ref, cols, rows, c in ((mixer_mine, half, units, core), (mixer_theirs, half, units, 1 - core)):
        ref[...] = mixer_ref[:, pl.ds(pl.multiple_of(c * half, half), half)].astype(bf)
    for ref, c in ((gate_mine, core), (gate_theirs, 1 - core)):
        ref[:units] = gate_up_ref[pl.ds(pl.multiple_of(c * units, units), units), :].astype(bf)
    count, own = gains_ref.shape
    note[...] = jnp.zeros_like(note)
    note[:count, :own] = gains_ref[...].astype(bf)
    gate_theirs[units:] = jnp.zeros((note.shape[0], gate_theirs.shape[1]), bf)
    gate_theirs[units:, : note.shape[1]] = note[...]
    down_low[...] = down_ref[...].astype(bf)


def pack_call(chain, spot, mixer, gate_up, down, gains):
    (rows, width), (units, _), (half, _) = mixer.shape, gate_up.shape, down.shape
    shapes = [(rows, width // 2)] * 2 + [(units // 2, width), (units // 2 + NOTE, width), (half, width), (NOTE, 128)]
    return chain.call(
        pack_kernel, "pack", (spot, mixer, gate_up, down, gains),
        [smem(), fixed(rows, width), fixed(units, width), fixed(half, width), fixed(*gains.shape)],
        [fixed(*s) for s in shapes], [shaped(s, bf) for s in shapes], grid=(1,),
    )


def block_kernel(own_gains, spot_ref, mine_ref, came_ref, note_ref, gate_ref, all_ref, copies_ref):
    rows, w = mine_ref.shape[0], all_ref.shape[1]
    mine = note_ref[...].astype(f32)
    came = gate_ref[gate_ref.shape[0] - NOTE :, :w].astype(f32)
    turned = lambda v: pltpu.roll(v, own_gains, 1)
    note = jnp.where(spot_ref[3] == 0, mine + turned(came), came + turned(mine)).astype(bf)
    at = 0
    for side in range(2):
        cols = slice(side * w, (side + 1) * w)
        all_ref[at : at + rows] = mine_ref[:, cols]
        all_ref[at + rows : at + 2 * rows] = came_ref[:, cols]
        all_ref[at + 2 * rows : at + 2 * rows + NOTE] = note
        at += 2 * rows + NOTE
    count = 2 * rows + NOTE
    for c in range(copies_ref.shape[0] // count):
        copies_ref[c * count : (c + 1) * count] = all_ref[:count]


def block_call(chain, spot, mine, came, note, gate_came, own_gains, copies, waits):
    rows, width = mine.shape
    w = width // 2
    each = 2 * rows + NOTE
    return chain.call(
        functools.partial(block_kernel, own_gains), "block", (spot, mine, came, note, gate_came),
        [smem()] + [fixed(*v.shape) for v in (mine, came, note, gate_came)],
        [fixed(2 * each, w), fixed(copies * each, w)], [shaped((2 * each, w), bf), shaped((copies * each, w), bf)],
        grid=(1,), waits=waits,
    )


def stack_kernel(count, moves, spot_ref, *refs):
    for i, a, rows, o, b in moves:
        if not isinstance(a, int):
            stride, distance, first = a
            a = pl.multiple_of((spot_ref[2] ^ distance) * stride + first, NOTE)
        refs[count + o][b : b + rows] = refs[i][pl.ds(a, rows)]


def stack_call(chain, spot, arrays, rows, moves, waits=()):
    like = {o: arrays[i] for i, _, _, o, _ in moves}
    shapes = [(r,) + like[o].shape[1:] for o, r in enumerate(rows)]
    return chain.call(
        functools.partial(stack_kernel, len(arrays), moves), "stack", (spot, *arrays),
        [smem()] + [fixed(*v.shape) for v in arrays],
        [fixed(*s) for s in shapes], [shaped(s, like[o].dtype) for o, s in enumerate(shapes)], grid=(1,), waits=waits,
    )


def corner_kernel(cut, extra, x_ref, y_ref, to_x_ref, to_y_ref):
    rows = x_ref.shape[0]
    to_x_ref[:cut] = y_ref[:cut]
    if extra:
        to_x_ref[cut:] = y_ref[rows - extra :]
    to_y_ref[...] = x_ref[cut : rows - extra]


def corner_call(chain, from_x, from_y, extra):
    total, width = from_x.shape
    cut = (total - extra) // 2
    shapes = [(cut + extra, width), (cut, width)]
    return chain.call(
        functools.partial(corner_kernel, cut, extra), "corner", (from_x, from_y), [fixed(total, width)] * 2,
        [fixed(*s) for s in shapes], [shaped(s, bf) for s in shapes], grid=(1,),
    )


def near_kernel(to_x_ref, to_y_ref, by_x_ref, by_y_ref, new_x_ref, new_y_ref):
    new_x_ref[...] = (to_x_ref[...].astype(f32) + by_y_ref[...].astype(f32)).astype(bf)
    new_y_ref[...] = (to_y_ref[...].astype(f32) + by_x_ref[...].astype(f32)).astype(bf)


def near_call(chain, to_x, to_y, by_x, by_y, parts=2, **options):
    rows, width = by_x.shape
    block = (rows // parts, width)
    low, high = pl.BlockSpec(block, lambda i: (i, 0)), pl.BlockSpec(block, lambda i: (i + parts, 0))
    return chain.call(
        near_kernel, "near", (to_x, to_y, by_x, by_y), [high, low, low, low], [high, low],
        [shaped(to_x.shape, bf), shaped(to_y.shape, bf)], grid=(parts,), input_output_aliases={0: 0, 1: 1}, **options,
    )


def line_kernel(count, *refs):
    parts, refs = refs[:count], refs[count:]
    rows = refs[-1].shape[0]

    def total(at):
        result = parts[0][pl.ds(at, rows)].astype(f32)
        for ref in parts[1:]:
            result = result + ref[pl.ds(at, rows)].astype(f32)
        return result

    for s, ref in enumerate(refs):
        ref[...] = total(s * rows).astype(ref.dtype)


def line_call(chain, parts, size, apart, **options):
    quarters = 4 if len(parts) == 1 else 1
    rows, width = parts[0].shape[0] // quarters // size, parts[0].shape[1]
    if apart:
        whole = lambda q: pl.BlockSpec((size * rows, width), lambda i: (q, 0))
        ins = [whole(q) for q in range(quarters)] if quarters > 1 else [whole(0)] * len(parts)
        specs = [fixed(rows, width)] * size
        shapes = [shaped((rows, width), f32)] + [shaped((rows, width), bf)] * (size - 1)
        steps = 1
    else:
        steps = 2
        half = size * rows // steps
        ins = [pl.BlockSpec((half, width), lambda i, q=q: (i + q * steps, 0)) for q in range(quarters)]
        ins = ins if quarters > 1 else ins * len(parts)
        specs, shapes = [pl.BlockSpec((half, width), lambda i: (i, 0))], [shaped((size * rows, width), bf)]
    parts = parts * quarters
    return chain.call(
        functools.partial(line_kernel, len(parts)), "line", parts, ins, specs, shapes, grid=(steps,), **options
    )


def finish_kernel(cuts, count, note, spot_ref, first_ref, *refs):
    came, more, outs, squares_ref, total = (
        refs[:count], refs[count : -len(cuts) - 2], refs[-len(cuts) - 2 : -2], refs[-2], refs[-1]
    )
    rows = total.shape[0]
    result = first_ref[:rows].astype(f32)
    for b in range(1, first_ref.shape[0] // rows):
        result = result + first_ref[b * rows : (b + 1) * rows].astype(f32)
    for ref in came:
        result = result + ref[...].astype(f32)
    total[...] = result
    squares = jnp.sum(result * result, axis=0, keepdims=True)
    if note:
        whole = jnp.sum(squares, axis=1, keepdims=True)
        for ref in more[:-1]:
            whole = whole + jnp.sum(ref[...], axis=1, keepdims=True)
        gains = jnp.sum(more[-1][...], axis=0, keepdims=True)
        squares = jnp.broadcast_to(whole + jnp.sum(gains * gains, axis=1, keepdims=True), squares_ref.shape)
    squares_ref[...] = squares
    for ref, start in zip(outs, cuts):
        rows = ref.shape[0]
        if not isinstance(start, int):
            start = pl.multiple_of((spot_ref[3] ^ start[0]) * rows, rows & -rows)
        ref[...] = total[pl.ds(start, rows), :]


def finish_call(chain, spot, first, came, blocks, cuts, note=0, more=(), waits=()):
    rows, width = first.shape[0] // blocks, first.shape[1]
    shapes = [(r, width) for _, r in cuts] + [(note, 128) if note else (1, width)]
    return chain.call(
        functools.partial(finish_kernel, [c for c, _ in cuts], len(came), note), "finish", (spot, first, *came, *more),
        [smem(), fixed(*first.shape)] + [fixed(rows, width)] * len(came) + [fixed(*v.shape) for v in more],
        [fixed(*s) for s in shapes], [shaped(s, f32) for s in shapes],
        grid=(1,), scratch_shapes=[pltpu.VMEM((rows, width), f32)], waits=waits,
    )


def adam_step(weight, grad, first, second, rate, decay):
    first_new = BETA_ONE * first + (1.0 - BETA_ONE) * grad
    second_new = BETA_TWO * second + (1.0 - BETA_TWO) * grad * grad
    corr_one = 1.0 / (1.0 - BETA_ONE**STEP)
    corr_two = 1.0 / (1.0 - BETA_TWO**STEP)
    update = first_new * (rate * corr_one) / (jnp.sqrt(second_new * corr_two) + ADAM_EPS)
    return (weight * (1.0 - rate * decay) - update, first_new, second_new)


def adam_kernel(spot_ref, note_ref, *refs):
    ins, outs, wide, tall = refs[:21], refs[21:35], refs[35], refs[36]
    mixer, gate_up, down, gains, parts = ins[:4], ins[4:7], ins[7:10], ins[10:13], ins[13:]
    mixer_out, gate_up_out, down_out, gains_out, norm_out = outs[:4], outs[4:7], outs[7:10], outs[10:13], outs[13]
    core, quarter = spot_ref[3], parts[0].shape[1]
    norm = jnp.sqrt(jnp.sum(note_ref[...], axis=0, keepdims=True)[:, :1])
    factor = CLIP_LIMIT / jnp.maximum(norm, CLIP_LIMIT)

    rows, step = mixer[0].shape[0], wide.shape[0]

    @pl.loop(0, rows // step)
    def _(i):
        at = pl.ds(pl.multiple_of(i * step, step & -step), step)
        for s in range(2):
            mine = pl.multiple_of(core * 2 * quarter, quarter) + s * quarter
            came = pl.multiple_of((1 - core) * 2 * quarter, quarter) + s * quarter
            wide[:, pl.ds(pl.multiple_of(mine, quarter), quarter)] = parts[s][at]
            wide[:, pl.ds(pl.multiple_of(came, quarter), quarter)] = parts[2 + s][at]
        old, first, second, average = (r[at] for r in mixer)
        new, first, second = adam_step(old, wide[...] * factor, first, second, RATE_MATRIX, DECAY_MATRIX)
        average = AVERAGE_KEEP * average + (1.0 - AVERAGE_KEEP) * new
        for ref, value in zip(mixer_out, (new, first, second, average)):
            ref[at] = value

    @pl.when(pl.program_id(0) == 0)
    def _():
        half = parts[4].shape[0]
        tall[pl.ds(pl.multiple_of(core * half, half), half), :] = parts[4][...]
        tall[pl.ds(pl.multiple_of((1 - core) * half, half), half), :] = parts[5][...]
        own = gains[0].shape[1]
        sums = jnp.sum(parts[7][...], axis=0, keepdims=True)
        gain_grad = jnp.concatenate([sums[:, :own], sums[:, own : 2 * own]])
        for olds, news, grad, rate, decay in (
            (gate_up, gate_up_out, tall[...], RATE_MATRIX, DECAY_MATRIX),
            (down, down_out, parts[6][...], RATE_MATRIX, DECAY_MATRIX),
            (gains, gains_out, gain_grad, RATE_GAIN, 0.0),
        ):
            old, first, second = (r[...] for r in olds)
            scale = factor if rate == RATE_MATRIX else factor[:, :1]
            for ref, value in zip(news, adam_step(old, grad * scale, first, second, rate, decay)):
                ref[...] = value
        norm_out[...] = norm


def adam_call(chain, spot, note, mixer, gate_up, down, gains, parts, blocks=1):
    rows, width = mixer[0].shape
    step = rows // blocks
    block = pl.BlockSpec((step, width), lambda i: (i, 0))
    piece = pl.BlockSpec((step, parts[0].shape[1]), lambda i: (i, 0))
    whole = lambda v: fixed(*v.shape)
    others = [*gate_up, *down, *gains]
    shapes = [v.shape for v in (*mixer, *others)] + [(1, 1)]
    return chain.call(
        adam_kernel, "adam", (spot, note, *mixer, *others, *parts),
        [smem(), whole(note)] + [block] * 4 + [whole(v) for v in others] + [piece] * 4
        + [whole(v) for v in parts[4:]],
        [block] * 4 + [whole(v) for v in others] + [fixed(1, 1)], [shaped(s, f32) for s in shapes],
        grid=(blocks,),
        scratch_shapes=[pltpu.VMEM((step // 3, width), f32), pltpu.VMEM(gate_up[0].shape, f32)],
    )


def flip(v, axis, bits=1):
    size = lax.axis_size(axis)
    return lax.ppermute(v, axis, [(i, i ^ bits) for i in range(size)])


def swap(v):
    return flip(v, "core")


def join(mine, other, core, axis=0):
    return jnp.where(
        core == 0,
        jnp.concatenate([mine, other], axis=axis),
        jnp.concatenate([other, mine], axis=axis),
    )


def part(v, index, axis=0):
    size = v.shape[axis] // 2
    return lax.dynamic_slice_in_dim(v, index * size, size, axis)


def low(v):
    return v.astype(bf)


def wide(v):
    return v.astype(f32)


class Whole:
    crossed = False
    mixer_slots = ((0,), (0,))
    mixer_blocks = (1,)

    def __init__(self, spot, groups):
        self.spot, self.core = spot, spot[3]
        self.size = lax.axis_size("z")
        self.chips = lax.axis_size("d0") * lax.axis_size("d1") * self.size
        self.ffn_in = self.ffn_out = tuple(range(groups))
        self.ffn_blocks = (groups,)

    def gather(self, chain, mixer, gate_up, down, gains, waits):
        def trade(v, axis):
            return join(part(v, self.core, axis), swap(part(v, 1 - self.core, axis)), self.core)

        everything = lambda v: lax.all_gather(v, CHIPS, axis=0, tiled=True)
        mixer_block = trade(low(mixer), 1)
        w, groups = mixer_block.shape[1] // 2, len(self.ffn_in)
        sides = []
        for s in range(2):
            whole = everything(mixer_block[:, s * w : (s + 1) * w])
            sides.append(([whole], ((0, 0, whole.shape[0], 0, None),), ()))
        ffn = [everything(v).reshape(groups, -1, v.shape[1]) for v in (trade(low(gate_up), 0), low(down))]
        ffn = [jnp.concatenate(ffn, axis=1)]
        gains = lax.all_gather(wide(low(gains)), EVERY, axis=1, tiled=True)
        yield jnp.pad(gains, ((0, NOTE - 2), (0, 0)))
        while True:
            yield sides, ffn

    def scatter(self, chain, parts, cuts, groups=1, apart=False):
        grads = parts[0].reshape(groups, -1, parts[0].shape[-1])
        rows = grads.shape[1] * 2 // 3
        if groups > 1:
            shards = [grads[:, :rows], grads[:, rows:]]
        else:
            shards = [grads]
        shards = [wide(lax.psum_scatter(flat(v), CHIPS, scatter_dimension=0, tiled=True)) for v in shards]
        outs = [part(shards[0], self.core), part(shards[0], 1 - self.core)] + shards[1:]
        squares = sum(jnp.sum(v * v, axis=0, keepdims=True) for v in shards)
        if groups == 1:
            yield
            yield ()
        through = yield ()
        yield (), through
        yield
        yield outs + [squares]

    def spread_gains(self, grads, rows):
        one, two = grads
        nothing = jnp.zeros_like(one)
        one = join(one, nothing, self.core, 1)
        return lax.psum_scatter(jnp.concatenate([one, two]), EVERY, scatter_dimension=1, tiled=True)

    def total(self, v):
        return lax.psum(v, EVERY)


class Cube(Whole):
    crossed = True
    near = ((0, 0), (0, 1), (1, 0), (1, 1))

    def __init__(self, spot, groups):
        super().__init__(spot, groups)
        slots = lambda fixed_z: tuple((y, x, s, fixed_z) for y, x in self.near for s in range(self.size))
        self.mixer_slots = slots(False), slots(True)
        self.ffn_in = slots(True)
        self.ffn_out = tuple((y, x, z, True) for z in range(self.size) for y, x in self.near)
        self.mixer_blocks = (self.size,) * 3 + (self.size // 2,) * 2

    def lines(self, block):
        return [flip(block, "z", s) for s in range(1, self.size)]

    def gather(self, chain, mixer, gate_up, down, gains, waits):
        spot = self.spot
        mixer_mine, mixer_theirs, gate_mine, gate_theirs, down_low, note = pack_call(
            chain, spot, mixer, gate_up, down, gains
        )
        gate_came = swap(gate_theirs)
        size = self.size
        own, block = block_call(
            chain, spot, mixer_mine, swap(mixer_theirs), note, gate_came, gains.shape[1], size, waits
        )
        line = self.along_z(block)
        own_x, own_y = flip(own, "d1"), flip(own, "d0")
        yield None
        rows = own.shape[0] // 2 - NOTE
        half = rows // 2
        sides = []

        def spread_out(line):
            return line, flip(line, "d1"), flip(line, "d0")

        def turn_corner(from_x, from_y, extra=0):
            to_x, to_y = corner_call(chain, from_x, from_y, extra)
            return flip(to_x, "d1"), flip(to_y, "d0")

        def plan(side):
            found = [(p, side * (rows + NOTE) + h * half, half, near + (0, False), h) for p, near in enumerate(self.near[:3]) for h in range(2)]
            found += [(3, h * half, half, (1, 1, 0, False), h) for h in range(2)]
            last = (size - 1) * 2
            for at in range(last):
                s, h = at // 2 + 1, at % 2
                found += [(4 + p, at * half, half, near + (s, False), h) for p, near in enumerate(self.near[:3])]
                found.append((7 + (at >= last // 2), at % (last // 2) * half, half, (1, 1, s, False), h))
            return tuple(found)

        corner = turn_corner(own_x, own_y)
        yield
        chain.pause(corner)
        others, line_rows = range(1, size), (size - 1) * rows
        moves = [(0, (rows + NOTE, s, 0), rows, 0, (s - 1) * rows) for s in others]
        moves += [(0, (rows + NOTE, s, rows), NOTE, 0, line_rows + (s - 1) * NOTE) for s in others]
        moves += [(1, rows + NOTE, rows, 1, s * rows) for s in range(size)]
        line, block = stack_call(
            chain, spot, (line, own), (line_rows + (size - 1) * NOTE, size * rows), tuple(moves)
        )
        first = spread_out(line)
        line = self.along_z(block)
        yield
        first_corner = turn_corner(*first[1:], (size - 1) * NOTE)
        notes = [(p, rows, near + (0, False)) for p, near in enumerate(self.near)]
        for s in others:
            notes += [(4 + p, line_rows + (s - 1) * NOTE, near + (s, False)) for p, near in enumerate(self.near[:3])]
            notes.append((7, line_rows // 2 + (s - 1) * NOTE, (1, 1, s, False)))
        sides.append(([own, own_x, own_y, corner[0], *first, *first_corner], plan(0), tuple(notes)))
        units, count = gate_mine.shape[0], down_low.shape[0]
        ffn_rows = 2 * units + count
        moves = [(0, (rows, s, 0), rows, 0, (s - 1) * rows) for s in others]
        for s in range(size):
            at = s * ffn_rows
            moves += [(1, 0, units, 1, at), (2, 0, units, 1, at + units), (3, 0, count, 1, at + 2 * units)]
        line, block = stack_call(
            chain, spot, (line, gate_mine, gate_came, down_low), (line_rows, size * ffn_rows), tuple(moves)
        )
        across, line = line, self.along_z(block)
        second = spread_out(*chain.pause(first_corner, (across,)))
        yield sides, None
        second_corner = turn_corner(*second[1:])
        sides.append(([own, own_x, own_y, corner[1], *second, *second_corner], plan(1), ()))
        ffn = spread_out(*chain.pause(second_corner, (line,)))
        yield sides, None
        ffn = (*ffn, *turn_corner(*ffn[1:]))
        yield sides, [v.reshape(-1, ffn_rows, v.shape[-1]) for v in ffn]

    def along_z(self, v):
        return lax.all_to_all(v, "z", 0, 0, tiled=True)

    def scatter(self, chain, parts, cuts, groups=1, apart=False):
        if groups > 1:
            came = (self.along_z(flat(parts[0])),)
        else:
            own, to_x, to_y, far_low, far_high = (flat(v) for v in parts)
            by_x, by_y = flip(far_low, "d1"), flip(far_high, "d0")
            yield
            to_x, to_y = yield near_call(chain, to_x, to_y, by_x, by_y)
            came = own, flip(to_x, "d1"), flip(to_y, "d0")
        through = yield came
        outs = line_call(chain, came, self.size, apart, through=through or ())
        count = self.size if apart else 1
        first, *rest = yield outs[:count], outs[count:]
        if groups > 1:
            to_x, to_y, far = rest
            far = lax.ppermute(far, ("d0", "d1"), [(i, i ^ 3) for i in range(4)])
            came = flip(to_x, "d1"), flip(to_y, "d0"), far
        elif apart:
            came = [flip(v, "z", s + 1) for s, v in enumerate(rest)]
        else:
            first, came = self.along_z(first), ()
        more, waits = yield
        yield finish_call(
            chain, self.spot, first, came, 1 if apart else self.size, cuts, 2 * self.chips if more else 0, more, waits
        )

    def spread_gains(self, grads, rows):
        return self.everyone(rows)

    def everyone(self, rows):
        return lax.all_to_all(rows, EVERY, 0, 0, tiled=True)


def body(
    inputs, lengths, filters, cotangent, mixer_weight, gate_up_weight, down_weight, norm_gains,
    mixer_first, gate_up_first, down_first, gains_first,
    mixer_second, gate_up_second, down_second, gains_second, mixer_average,
):
    slots, width = inputs.shape
    size = lax.axis_size("z")
    groups = 2 * FF // 256
    cube = lax.axis_size("d0") == 2 and lax.axis_size("d1") == 2 and size == 4
    spot = jnp.stack([lax.axis_index(a) for a in EVERY]).astype(jnp.int32)
    core = spot[3]
    links = (Cube if cube else Whole)(spot, groups)
    units = gate_up_weight.shape[0]
    chain = Chain()

    sums = lengths, swap(lengths)
    source_other, cotangent_other = swap(inputs), swap(cotangent)
    taps = jnp.concatenate([wide(filters), jnp.eye(AR_ORDER, slots, dtype=f32)])
    taps_turned = jnp.roll(taps[:, ::-1], 1 - slots // 4, axis=1)
    taps, taps_turned = (v.reshape(-1, 3, slots) for v in (taps, taps_turned))

    weights = links.gather(
        chain, mixer_weight, gate_up_weight, down_weight, norm_gains, (sums[1], source_other, cotangent_other)
    )
    gains = next(weights)
    tokens = hat_tokens = normed_call(chain, spot, inputs, source_other)
    blocks = taps.shape[0]
    cuts, spread = (0, blocks // 3, blocks * 4 // 9, blocks), None
    for at in range(3):
        spread = spread_call(chain, sums, taps_turned, *tokens, cuts[at], cuts[at + 1] - cuts[at], spread)
        sides = next(weights)
    sides, _ = sides
    quarter = sides[0][0][0].shape[1]
    *mixed, left, gains = (*mix_call(chain, spot, spread, 0, *sides[0], gains, size, width), gains)[:4]
    sides, _ = next(weights)
    mixed_own, mixed_other, right = mix_call(chain, spot, spread, 1, *sides[1], gains, size, width, mixed)
    _, ffn = next(weights)

    hidden, *normed_two = hidden_call(chain, inputs, mixed_own, swap(mixed_other), gains)
    tokens = (*normed_two, *(swap(v) for v in normed_two), cotangent, cotangent_other)
    branch_own, branch_other, two_own, two_other, *grad_ffn = ffn_call(
        chain, spot, sums, tokens, ffn, links.ffn_blocks, links.ffn_in, links.ffn_out, size, links.crossed
    )
    if cube:
        grad_ffn = chain.pause(through=grad_ffn)
    ffn_sum = links.scatter(chain, grad_ffn, ((0, units // 2), (units // 2, units // 2), (units, units // 2)), groups, True)
    ffn_came = next(ffn_sum)
    grad_hidden, grad_low, gains_two = turn_call(
        chain, lengths, hidden, cotangent, two_own, swap(two_other), gains
    )
    grad_other = swap(grad_low)
    rows = mixer_weight.shape[0]
    cuts = (((0,), rows), ((1,), rows))
    grads_of = lambda s: grad_call(
        chain, spot, gains, grad_low, grad_other, spread, s, quarter, links.mixer_blocks, links.mixer_slots[s], size
    )
    first_sum = links.scatter(chain, grads_of(0), cuts, apart=True)
    next(first_sum)
    second_sum = links.scatter(chain, grads_of(1), cuts)
    next(second_sum)
    backward = lambda first, steps, *more: back_call(
        chain, spot, sums, taps, grad_low, grad_other, (left, right), first, steps, *more
    )
    early = blocks // 2
    first_sum.send(next(first_sum))
    one = backward(0, early)
    second_sum.send(next(second_sum))
    one_own, one_other, gains_one, note_rows = backward(
        early, blocks - early, one, hat_tokens, gains_two, 2 * links.chips
    )
    outs, _ = first_sum.send(())
    first_sum.send(outs)
    if cube:
        (note_rows,) = chain.pause(ffn_came, (note_rows,))
    shard_gains = links.spread_gains((gains_one, gains_two), note_rows)
    outs, _ = second_sum.send(())
    chain.pause((shard_gains,))
    first_mine, first_theirs, square = first_sum.send(((), ()))
    first_theirs, branch_other, *outs = chain.pause(through=(first_theirs, branch_other, *outs))
    second_sum.send(outs)
    outs, _ = ffn_sum.send(())
    ffn_sum.send(outs)
    output = output_call(chain, hidden, branch_own, swap(branch_other))
    input_grad = last_call(chain, spot, grad_hidden, inputs, one_own, swap(one_other), gains)
    gate_up_mine, gate_up_theirs, shard_down, *squares = ffn_sum.send(((), ()))
    squares.append(square)
    gate_up_came, first_came = swap(gate_up_theirs), swap(first_theirs)
    second_mine, second_theirs, note = second_sum.send(((*squares, shard_gains), ()))
    second_came = swap(second_theirs)
    mixer = mixer_weight, mixer_first, mixer_second, mixer_average
    gate_up, down = (gate_up_weight, gate_up_first, gate_up_second), (down_weight, down_first, down_second)
    gain = norm_gains, gains_first, gains_second
    if cube:
        (
            mixer_new, mixer_first_new, mixer_second_new, mixer_average_new, gate_up_new, gate_up_first_new,
            gate_up_second_new, down_new, down_first_new, down_second_new, gains_new, gains_first_new, gains_second_new,
            grad_norm,
        ) = adam_call(
            chain, spot, links.everyone(note), mixer, gate_up, down, gain,
            (first_mine, second_mine, first_came, second_came, gate_up_mine, gate_up_came, shard_down, shard_gains),
        )
        grad_norm = grad_norm[0, 0]
    else:
        squares = sum(jnp.sum(v) for v in (*squares, note)) + jnp.sum(shard_gains * shard_gains)
        grad_norm = jnp.sqrt(links.total(squares))
        factor = CLIP_LIMIT / jnp.maximum(grad_norm, CLIP_LIMIT)
        shard_mixer = join(
            jnp.concatenate([first_mine, second_mine], axis=1), jnp.concatenate([first_came, second_came], axis=1), core, 1
        )
        shard_gate_up = join(gate_up_mine, gate_up_came, core)
        step = lambda old, grad: adam_step(old[0], grad * factor, old[1], old[2], RATE_MATRIX, DECAY_MATRIX)
        mixer_new, mixer_first_new, mixer_second_new = step(mixer, shard_mixer)
        gate_up_new, gate_up_first_new, gate_up_second_new = step(gate_up, shard_gate_up)
        down_new, down_first_new, down_second_new = step(down, shard_down)
        gains_new, gains_first_new, gains_second_new = adam_step(
            gain[0], shard_gains * factor, gain[1], gain[2], RATE_GAIN, 0.0
        )
        mixer_average_new = AVERAGE_KEEP * mixer_average + (1.0 - AVERAGE_KEEP) * mixer_new
    return (
        output, input_grad, grad_norm, mixer_new, gate_up_new, down_new, gains_new,
        mixer_first_new, gate_up_first_new, down_first_new, gains_first_new,
        mixer_second_new, gate_up_second_new, down_second_new, gains_second_new, mixer_average_new,
    )


def solution(mesh):
    outer, inner = mesh.shape["dp"], mesh.shape["fsdp"]
    side = math.isqrt(outer)
    if side * side != outer:
        side = 1
    split = jax.sharding.Mesh(
        np.asarray(mesh.devices).reshape(side, outer // side, inner // 2, 2), EVERY
    )
    rows, columns, whole = P(EVERY, None), P(None, EVERY), P()
    return jax.shard_map(
        body,
        mesh=split,
        in_specs=(
            rows, rows, whole, rows, rows, rows, rows, columns,
            rows, rows, rows, columns, rows, rows, rows, columns, rows,
        ),
        out_specs=(
            rows, rows, whole, rows, rows, rows, columns, rows, rows, rows, columns,
            rows, rows, rows, columns, rows,
        ),
        check_vma=False,
    )
```

```python
import functools
import math

import jax
import jax.numpy as jnp
import numpy as np
from jax import lax
from jax.experimental import pallas as pl
from jax.experimental.pallas import tpu as pltpu
from jax.sharding import PartitionSpec as P

bf = jnp.bfloat16
f32 = jnp.float32
FILTERS = 24
AR_ORDER = 3
FF = 2048
STEP = 10
NORM_EPS = 1e-05
CLIP_LIMIT = 1.0
BETA_ONE = 0.9
BETA_TWO = 0.95
ADAM_EPS = 1e-08
RATE_MATRIX = 0.03
RATE_GAIN = 0.5
DECAY_MATRIX = 0.1
AVERAGE_KEEP = 0.9
CHIPS = ("d0", "d1", "z")
EVERY = CHIPS + ("core",)


NT = (((1,), (1,)), ((), ()))
NN = (((1,), (0,)), ((), ()))
TN = (((0,), (0,)), ((), ()))


def dot(a, b, dims=NN):
    return lax.dot_general(a, b, dims, preferred_element_type=f32)


class Chain:
    def __init__(self):
        self.token = None

    def call(self, kernel, name, args, in_specs, out_specs, out_shape, waits=(), through=(), **options):
        count, single = len(args), not isinstance(out_shape, (list, tuple)) and not through
        if single:
            out_specs, out_shape = [out_specs], [out_shape]
        made = len(out_shape)
        aliases = options.pop("input_output_aliases", {})
        aliases = {**aliases, **{count + i: made + i for i in range(len(through))}}
        last = tuple(through) + tuple(waits) + (() if self.token is None else (self.token,))

        def whole(*refs):
            first = count + len(last)
            kernel(*refs[:count], *refs[first : first + made], *refs[first + made + len(through) + 1 :])

        *outs, self.token = pl.pallas_call(
            whole,
            name=name,
            in_specs=list(in_specs) + [anywhere() for _ in last],
            out_specs=list(out_specs) + [anywhere() for _ in through] + [anywhere()],
            out_shape=list(out_shape) + [shaped(v.shape, v.dtype) for v in through] + [shaped((8, 128), f32)],
            input_output_aliases=aliases,
            compiler_params=pltpu.CompilerParams(vmem_limit_bytes=64 << 20),
            cost_estimate=pl.CostEstimate(flops=1, bytes_accessed=1, transcendentals=0),
            **options,
        )(*args, *last)
        return outs[0] if single else outs

    def pause(self, waits=(), through=()):
        return self.call(lambda: None, "pause", (), [], [], [], waits=waits, through=through)


def smem():
    return pl.BlockSpec(memory_space=pltpu.SMEM)


def anywhere():
    return pl.BlockSpec(memory_space=pl.ANY)


def fixed(*shape):
    return pl.BlockSpec(shape, lambda i: (0,) * len(shape))


NOTE = 16


def shaped(shape, dtype):
    return jax.ShapeDtypeStruct(tuple(shape), dtype)


def segment_of(place, ends_ref, group):
    return sum((place >= ends_ref[group, j]).astype(jnp.int32) for j in range(3))


def causal_mask(ends_ref, group, n, transposed):
    down = lax.broadcasted_iota(jnp.int32, (n, 1), 0)
    along = lax.broadcasted_iota(jnp.int32, (1, n), 1)
    one, two = segment_of(down, ends_ref, group), segment_of(along, ends_ref, group)
    order = (down <= along) if transposed else (down >= along)
    return ((one == two) & (one < 3) & order).astype(f32).astype(bf)


def diagonals(row, count):
    wide = jnp.broadcast_to(row, (count, row.shape[-1]))
    return pltpu.roll(wide, 0, 1, stride=1, stride_axis=0).astype(bf)


def spread_kernel(lengths_ref, came_ref, taps_ref, own_ref, other_ref, *refs):
    u_ref, mask, table, ends = refs[-4:]
    n = mask.shape[1]
    q, h, w = n // 4, n // 2, own_ref.shape[1] // 2
    per = taps_ref.shape[1]

    @pl.when(pl.program_id(0) == 0)
    def _():
        find_ends(ends, lengths_ref, came_ref)
        for g in range(2):
            mask[g] = causal_mask(ends, g, n, False)
        table[...] = jnp.zeros_like(table)

    @pl.loop(0, per)
    def _(j):
        at = pl.multiple_of(j * w, w)
        strip = diagonals(taps_ref[0, pl.ds(j, 1), :], q)
        for g, tokens in enumerate((own_ref, other_ref)):
            for i in range(4):
                rows, cols = slice(i * q, (i + 1) * q), slice(0, (i + 1) * q)
                table[g, rows, cols] = strip[:, (3 - i) * q :] * mask[g, rows, cols]
            upper = dot(table[g, :h, :h], tokens[:h]).astype(bf)
            lower = dot(table[g, h:, :], tokens[...]).astype(bf)
            for side in range(2):
                cols = slice(side * w, (side + 1) * w)
                u_ref[side, g * n : g * n + h, pl.ds(at, w)] = upper[:, cols]
                u_ref[side, g * n + h : (g + 1) * n, pl.ds(at, w)] = lower[:, cols]


def find_ends(ends, lengths_ref, came_ref):
    for g, ref in enumerate((lengths_ref, came_ref)):
        total = ref[0, 0]
        ends[g, 0] = total
        for j in range(1, 3):
            total = total + ref[0, j]
            ends[g, j] = total


def spread_call(chain, lengths, taps, own, other, first, steps, into=None):
    blocks, per, n = taps.shape
    w = own.shape[1] // 2
    args = [*lengths, taps, own, other]
    specs = [smem()] * 2 + [pl.BlockSpec((1, per, n), lambda i: (i + first, 0, 0)), fixed(n, 2 * w), fixed(n, 2 * w)]
    options = {}
    if into is not None:
        options = dict(input_output_aliases={len(args): 0})
        args, specs = args + [into], specs + [anywhere()]
    return chain.call(
        spread_kernel, "spread", args, specs,
        pl.BlockSpec((2, 2 * n, per * w), lambda i: (0, 0, i + first)),
        shaped((2, 2 * n, blocks * per * w), bf),
        grid=(steps,),
        scratch_shapes=[pltpu.VMEM((2, n, n), bf), pltpu.VMEM((2, n, n), bf), pltpu.SMEM((2, 3), jnp.int32)],
        **options,
    )


def run_copies(copies):
    for c in copies:
        c.start()
    for c in copies:
        c.wait()


def chip_of(spot_ref, slot, size):
    if isinstance(slot, int):
        return slot
    dy, dx, dz, fixed_z = slot
    return ((spot_ref[0] ^ dy) * 2 + (spot_ref[1] ^ dx)) * size + (dz if fixed_z else spot_ref[2] ^ dz)


def collect(spot_ref, pieces, plan, size, held, sem, columns):
    copies = []
    for at, (piece, row, rows, slot, half) in enumerate(plan):
        place = chip_of(spot_ref, slot, size)
        if half is not None:
            place = place * 2 + (spot_ref[3] ^ half)
        start = pl.multiple_of(place * rows, math.gcd(rows, 512))
        copies.append(
            pltpu.make_async_copy(pieces[piece].at[pl.ds(row, rows)], held.at[pl.ds(start, rows), columns], sem.at[at])
        )
    return copies


def mix_kernel(count, plan, notes, size, width, side, spot_ref, u_ref, *refs):
    pieces, refs = refs[:count], refs[count:]
    first = side == 0
    before, refs = refs[: 0 if first else 2], refs[0 if first else 2 :]
    if not notes:
        gains_ref, refs = refs[0], refs[1:]
    own_ref, other_ref, w_ref, *refs = refs
    if notes:
        gains_ref, refs = refs[0], refs[1:]
    held, u, sem, u_sem, *refs = refs
    *refs, result = refs
    tiles = sums = refs[0] if refs else None
    w = held.shape[1]
    filters = held.shape[0] // width
    rows = own_ref.shape[0]
    copies = collect(spot_ref, pieces, plan, size, held, sem, slice(0, w))
    for at, (piece, row, slot) in enumerate(notes):
        copies.append(
            pltpu.make_async_copy(
                pieces[piece].at[pl.ds(row, NOTE)], tiles.at[chip_of(spot_ref, slot, size)], sem.at[len(plan) + at]
            )
        )
    third = filters // 3
    cols = [pl.ds(t * third * w, third * w) for t in range(3)]
    loads = [pltpu.make_async_copy(u_ref.at[side, :, c], u.at[:, c], u_sem.at[t]) for t, c in enumerate(cols)]
    adds = [pltpu.make_async_copy(ref, sums.at[g], u_sem.at[4 + g]) for g, ref in enumerate(before)]
    for c in copies + loads + adds:
        c.start()
    for c in copies:
        c.wait()
    give = pltpu.make_async_copy(held, w_ref, u_sem.at[3])
    give.start()
    if notes:
        lanes = width // len(notes)
        for b in range(width // 128):
            block = jnp.zeros((NOTE, 128), f32)
            for j in range(128 // lanes):
                tile = tiles[b * (128 // lanes) + j].astype(f32)
                block = block + (pltpu.roll(tile, j * lanes, 1) if j else tile)
            gains_ref[:, b * 128 : (b + 1) * 128] = block
    gain = gains_ref[0:1, pl.ds(pl.multiple_of((spot_ref[3] * 2 + side) * w, w), w)]
    result[...] = jnp.zeros_like(result)

    @pl.loop(0, 3)
    def _(t):
        pltpu.make_async_copy(u_ref.at[side, :, pl.ds(0, third * w)], u.at[:, pl.ds(0, third * w)], u_sem.at[t]).wait()
        first_row = pl.multiple_of(t * third * width, width)
        wide = jnp.concatenate(
            [(held[pl.ds(first_row + k * width, width), :].astype(f32) * gain).astype(bf) for k in range(third)], axis=1
        )
        result[...] += dot(u[:, pl.ds(pl.multiple_of(t * third * w, w), third * w)], wide, NT)

    for g, out in enumerate((own_ref, other_ref)):
        mine = result[g * rows : (g + 1) * rows]
        if not first:
            adds[g].wait()
            mine = mine + sums[g]
        out[...] = mine.astype(out.dtype)
    give.wait()


def mix_call(chain, spot, u, side, pieces, plan, notes, gains, size, width, before=()):
    rows, depth = u.shape[1:]
    w = pieces[0].shape[-1]
    total = depth // w * width
    step = rows // 2
    out = fixed(step, width)
    note = fixed(NOTE, width)
    given = () if notes else (gains,)
    made = 1 - len(given)
    return chain.call(
        functools.partial(mix_kernel, len(pieces), plan, notes, size, width, side), "mix",
        (spot, u, *pieces, *before, *given),
        [smem(), anywhere()] + [anywhere() for _ in (*pieces, *before)] + [note for _ in given],
        [out, out, anywhere()] + [note] * made,
        [shaped((step, width), f32), shaped((step, width), bf if before else f32), shaped((total, w), bf)]
        + [shaped((NOTE, width), f32)] * made,
        grid=(1,),
        scratch_shapes=[
            pltpu.VMEM((total, w), bf), pltpu.VMEM((rows, depth), bf),
            pltpu.SemaphoreType.DMA((len(plan) + len(notes),)), pltpu.SemaphoreType.DMA((6,)),
        ] + [pltpu.VMEM((len(notes), NOTE, 128), bf)] * made + [pltpu.VMEM((2, step, width), f32)] * min(1, len(before))
        + [pltpu.VMEM((rows, width), f32)],
    )


def hidden_kernel(source_ref, own_ref, came_ref, gain_ref, hidden_ref, *normed_refs):
    hidden = source_ref[...].astype(f32) + (own_ref[...] + came_ref[...].astype(f32))
    scale = lax.rsqrt(jnp.mean(hidden * hidden, axis=-1, keepdims=True) + NORM_EPS)
    hidden_ref[...] = hidden
    normed = (hidden * scale * gain_ref[1:2]).astype(bf)
    width = normed_refs[0].shape[1]
    for i, ref in enumerate(normed_refs):
        ref[...] = normed[:, i * width : (i + 1) * width]


def hidden_call(chain, source, own, came, gain, parts=2):
    rows, width = source.shape
    block = pl.BlockSpec((rows // parts, width), lambda i: (i, 0))
    thin = pl.BlockSpec((rows // parts, width // 2), lambda i: (i, 0))
    return chain.call(
        hidden_kernel, "hidden", (source, own, came, gain), [block, block, block, fixed(NOTE, width)],
        [block, thin, thin], [shaped((rows, width), f32)] + [shaped((rows, width // 2), bf)] * 2,
        grid=(parts,),
    )


def norm_back(grad, hat, scale, gain):
    weighted = grad * gain
    return scale * (weighted - hat * jnp.mean(weighted * hat, axis=-1, keepdims=True))


def add_rows(ref, values, step):
    total = jnp.sum(values, axis=0, keepdims=True)

    @pl.when(step == 0)
    def _():
        ref[...] = total

    @pl.when(step > 0)
    def _():
        ref[...] += total


def turn_kernel(lengths_ref, hidden_ref, back_ref, own_ref, came_ref, gain_ref, grad_ref, low_ref, gains_ref):
    hidden = hidden_ref[...]
    scale = lax.rsqrt(jnp.mean(hidden * hidden, axis=-1, keepdims=True) + NORM_EPS)
    hat = hidden * scale
    two = own_ref[...] + came_ref[...].astype(f32)
    back = live_rows(back_ref[...].astype(f32), lengths_ref, pl.program_id(0) * hidden.shape[0])
    grad = back + norm_back(two, hat, scale, gain_ref[1:2])
    grad_ref[...] = grad
    low_ref[...] = grad.astype(bf)
    add_rows(gains_ref, two * hat, pl.program_id(0))


def turn_call(chain, lengths, hidden, back, own, came, gain, parts=2):
    rows, width = hidden.shape
    block = pl.BlockSpec((rows // parts, width), lambda i: (i, 0))
    return chain.call(
        turn_kernel, "turn", (lengths, hidden, back, own, came, gain), [smem()] + [block] * 4 + [fixed(NOTE, width)],
        [block, block, fixed(1, width)],
        [shaped((rows, width), f32), shaped((rows, width), bf), shaped((1, width), f32)],
        grid=(parts,),
    )


def output_kernel(hidden_ref, own_ref, came_ref, out_ref):
    out_ref[...] = (hidden_ref[...] + (own_ref[...] + came_ref[...].astype(f32))).astype(bf)


def output_call(chain, hidden, own, came, parts=2):
    rows, width = hidden.shape
    block = pl.BlockSpec((rows // parts, width), lambda i: (i, 0))
    return chain.call(
        output_kernel, "output", (hidden, own, came), [block] * 3, block, shaped((rows, width), bf), grid=(parts,),
    )


def last_kernel(spot_ref, grad_ref, source_ref, own_ref, came_ref, gain_ref, out_ref, one):
    half = own_ref.shape[1]
    core = spot_ref[3]
    one[:, pl.ds(pl.multiple_of(core * half, half), half)] = own_ref[...]
    one[:, pl.ds(pl.multiple_of((1 - core) * half, half), half)] = came_ref[...]
    source = source_ref[...].astype(f32)
    scale = lax.rsqrt(jnp.mean(source * source, axis=-1, keepdims=True) + NORM_EPS)
    out_ref[...] = grad_ref[...] + norm_back(one[...], source * scale, scale, gain_ref[0:1])


def last_call(chain, spot, grad_hidden, source, own, came, gain, parts=2):
    rows, width = source.shape
    block = pl.BlockSpec((rows // parts, width), lambda i: (i, 0))
    thin = pl.BlockSpec((rows // parts, width // 2), lambda i: (i, 0))
    return chain.call(
        last_kernel, "last", (spot, grad_hidden, source, own, came, gain),
        [smem(), block, block, thin, thin, fixed(NOTE, width)], block, shaped((rows, width), f32),
        grid=(parts,), scratch_shapes=[pltpu.VMEM((rows // parts, width), f32)],
    )


def grad_kernel(slots, size, side, spot_ref, gains_ref, own_ref, other_ref, u_ref, *refs):
    outs, (turned, held, sem) = refs[:-3], refs[-3:]
    n, width = own_ref.shape
    w = held.shape[1]
    per = u_ref.shape[2] // w
    step = pl.program_id(0)

    @pl.when(step == 0)
    def _():
        turned[:, :n] = own_ref[...].T
        turned[:, n:] = other_ref[...].T

    gain = gains_ref[0:1, pl.ds(pl.multiple_of((spot_ref[3] * 2 + side) * w, w), w)]
    result = dot(turned[...], u_ref[0])
    for j in range(per):
        at = pl.multiple_of((step * per + j) * width, width)
        held[pl.ds(at, width), :] = (result[:, j * w : (j + 1) * w] * gain).astype(bf)

    @pl.when(step == pl.num_programs(0) - 1)
    def _():
        rows = held.shape[0] // len(slots)
        copies, at = [], 0
        for ref in outs:
            for b in range(ref.shape[0] // rows):
                start = pl.multiple_of(chip_of(spot_ref, slots[at], size) * rows, math.gcd(rows, 512))
                copies.append(
                    pltpu.make_async_copy(held.at[pl.ds(start, rows)], ref.at[pl.ds(b * rows, rows)], sem.at[at])
                )
                at += 1
        run_copies(copies)


def grad_call(chain, spot, gains, own, other, u, side, w, blocks, slots, size, per=9):
    rows, depth = u.shape[1:]
    n, width = own.shape
    count = depth // w
    each = count * width // len(slots)
    return chain.call(
        functools.partial(grad_kernel, slots, size, side), "mixer_grad", (spot, gains, own, other, u),
        [smem(), fixed(NOTE, width), fixed(n, width), fixed(n, width), pl.BlockSpec((1, rows, per * w), lambda i: (side, 0, i))],
        [anywhere() for _ in blocks], [shaped((b * each, w), bf) for b in blocks],
        grid=(count // per,),
        scratch_shapes=[
            pltpu.VMEM((width, rows), bf), pltpu.VMEM((count * width, w), bf), pltpu.SemaphoreType.DMA((len(slots),)),
        ],
    )


def gain_rows(rows_ref, one, two, core, wide):
    devices, half = rows_ref.shape[0], one.shape[1]
    lanes = 2 * half // devices
    if lanes < 1 or 128 % lanes or 2 * lanes > 128:
        return
    wide[...] = jnp.zeros_like(wide)
    wide[:, pl.ds(pl.multiple_of(core * half, half), half)] = jnp.broadcast_to(one, (8, half))
    lane = lax.broadcasted_iota(jnp.int32, (8, 128), 1)
    for i in range(devices):
        block, turn = divmod(i * lanes, 128)
        cols = slice(block * 128, (block + 1) * 128)
        pair = []
        for tile, at in ((wide[:, cols], 0), (jnp.broadcast_to(two[:, cols], (8, 128)), lanes)):
            shift = (at - turn) % 128
            pair.append(pltpu.roll(tile, shift, 1) if shift else tile)
        row = jnp.where(lane < lanes, pair[0], jnp.where(lane < 2 * lanes, pair[1], 0.0))
        rows_ref[i : i + 1, :] = row[:1]


def back_kernel(first, spot_ref, lengths_ref, came_ref, taps_ref, own_ref, other_ref, left_ref, right_ref, *refs):
    if first:
        own_before, other_before, own_hat, other_hat, two_ref, own_out, other_out, gains_ref, rows_ref, wide, *refs = refs
        before = own_before, other_before
    else:
        own_out, other_out, *refs = refs
    mask, low_low, low_high, high, v_low, v_high, ends = refs
    n = mask.shape[1]
    q, h, d = n // 4, n // 2, own_ref.shape[1]
    per = taps_ref.shape[1]

    @pl.when(pl.program_id(0) == 0)
    def _():
        find_ends(ends, lengths_ref, came_ref)
        for g in range(2):
            mask[g] = causal_mask(ends, g, n, True)
        low_low[...] = jnp.zeros_like(low_low)
        high[...] = jnp.zeros_like(high)
        for g, ref in enumerate((own_out, other_out)):
            ref[...] = before[g][...] if first else jnp.zeros_like(ref)

    for j in range(per):
        weight = jnp.concatenate([left_ref[j * d : (j + 1) * d], right_ref[j * d : (j + 1) * d]], axis=1)
        s = diagonals(taps_ref[0, j : j + 1, :], q)
        a = j * h
        for g, grad in enumerate((own_ref, other_ref)):
            v = dot(grad[...], weight).astype(bf)
            v_low[g, a : a + h] = v[:h]
            v_high[g, a : a + h] = v[h:]
            m = mask[g]
            low_low[g, 0:q, a : a + q] = s[:, :q] * m[0:q, 0:q]
            low_low[g, 0:q, a + q : a + h] = s[:, q : 2 * q] * m[0:q, q : 2 * q]
            low_low[g, q:h, a + q : a + h] = s[:, :q] * m[q:h, q:h]
            low_high[g, 0:q, a : a + h] = s[:, 2 * q : 4 * q] * m[0:q, h:]
            low_high[g, q:h, a : a + h] = s[:, q : 3 * q] * m[q:h, h:]
            high[g, 0:q, a : a + h] = s[:, 0 : 2 * q] * m[h : h + q, h:]
            high[g, q:h, a + q : a + h] = s[:, 0:q] * m[h + q :, h + q :]
    for g, out in enumerate((own_out, other_out)):
        out[:h] += dot(low_low[g], v_low[g]) + dot(low_high[g], v_high[g])
        out[h:] += dot(high[g], v_high[g])
    if first:

        @pl.when(pl.program_id(0) == pl.num_programs(0) - 1)
        def _():
            products = own_out[...] * own_hat[...].astype(f32) + other_out[...] * other_hat[...].astype(f32)
            one = jnp.sum(products, axis=0, keepdims=True)
            gains_ref[...] = one
            gain_rows(rows_ref, one, two_ref, spot_ref[3], wide)


def back_call(chain, spot, lengths, taps, own, other, weights, first, steps, before=(), hats=(), two=None, devices=0):
    blocks, per, n = taps.shape
    rows, d = own.shape
    w = weights[0].shape[1]
    width = 2 * w
    scratch = lambda *s: pltpu.VMEM(s, bf)
    weight = pl.BlockSpec((per * d, w), lambda i: (i + first, 0))
    half = fixed(rows, width)
    more = (*before, *hats, two) if before else ()
    outs, shapes = [half] * 2, [shaped((rows, width), f32)] * 2
    scratches = [
        scratch(2, n, n), scratch(2, n // 2, per * n // 2),
        scratch(2, n // 2, per * n // 2), scratch(2, n // 2, per * n // 2),
        scratch(2, per * n // 2, width), scratch(2, per * n // 2, width), pltpu.SMEM((2, 3), jnp.int32),
    ]
    if before:
        outs = outs + [fixed(1, width), fixed(devices, 128)]
        shapes = shapes + [shaped((1, width), f32), shaped((devices, 128), f32)]
        scratches = [pltpu.VMEM((8, 2 * width), f32)] + scratches
    return chain.call(
        functools.partial(back_kernel, first), "spread_back", (spot, *lengths, taps, own, other, *weights, *more),
        [smem()] * 3 + [pl.BlockSpec((1, per, n), lambda i: (i + first, 0, 0)), fixed(rows, d), fixed(rows, d)]
        + [weight, weight] + [fixed(*v.shape) for v in more],
        outs, shapes, grid=(steps,), scratch_shapes=scratches,
    )


def flat(v):
    return v.reshape(-1, v.shape[-1])


def ffn_kernel(count, outs, steps, slots, out_slots, size, crossed, spot_ref, lengths_ref, came_ref, *refs):
    turned = spot_ref[3] if crossed else 0
    tokens, pieces, refs = refs[:6], refs[6 : 6 + count], refs[6 + count :]
    results, grads, (held, dealt, normed, back, sums, sem, token_sem) = refs[:4], refs[4 : 4 + outs], refs[4 + outs :]
    n = tokens[-1].shape[0]
    chips, units, width = held.shape[0], held.shape[1] * 2 // 3, held.shape[2]
    own, half = chips // 2 // steps, units // 2
    step = pl.program_id(0)

    @pl.when(step == 0)
    def _():
        half_width = tokens[0].shape[1]
        copies, at = [], 0
        for g in range(2):
            rows = pl.ds(g * n, n)
            for i in range(2):
                cols = pl.ds(i * half_width, half_width)
                copies.append(pltpu.make_async_copy(tokens[2 * g + i], normed.at[rows, cols], token_sem.at[2 * g + i]))
            copies.append(pltpu.make_async_copy(tokens[4 + g], back.at[rows], token_sem.at[4 + g]))
        for ref in pieces:
            for b in range(ref.shape[0]):
                chip = chip_of(spot_ref, slots[at], size)
                copies.append(
                    pltpu.make_async_copy(ref.at[b, pl.ds(0, units)], held.at[chip, pl.ds(0, units)], sem.at[0, at])
                )
                copies.append(
                    pltpu.make_async_copy(
                        ref.at[b, pl.ds(units, half)], held.at[chip ^ turned, pl.ds(units, half)], sem.at[1, at]
                    )
                )
                at += 1
        for c in copies:
            c.start()
        for c in copies[:6]:
            c.wait()
        for g, ref in enumerate((lengths_ref, came_ref)):
            back[g * n : (g + 1) * n] = live_rows(back[g * n : (g + 1) * n].astype(f32), ref).astype(bf)
        for c in copies[6:]:
            c.wait()

    w_gate = flat(held[pl.ds(step * own, own), 0:units])
    w_up = flat(held[pl.ds(chips // 2 + step * own, own), 0:units])
    w_down = flat(held[pl.ds(step * 2 * own, 2 * own), units : units + half])
    gate, up = dot(normed[...], w_gate, NT), dot(normed[...], w_up, NT)
    grad_act = dot(back[...], w_down, NT)
    sigma = 1.0 / (1.0 + jnp.exp(-gate))
    swish = gate * sigma
    act = (swish * up).astype(bf)
    grad_gate = (grad_act * up * (sigma * (1.0 + gate * (1.0 - sigma)))).astype(bf)
    grad_up = (grad_act * swish).astype(bf)
    put = lambda v: v.astype(bf).reshape(own, units, width)
    dealt[pl.ds(step * own, own), 0:units] = put(dot(grad_gate, normed[...], TN))
    dealt[pl.ds(chips // 2 + step * own, own), 0:units] = put(dot(grad_up, normed[...], TN))
    grad_down = dot(act, back[...], TN).astype(bf)
    for b in range(2 * own):
        dealt[(step * 2 * own + b) ^ turned, units : units + half] = grad_down[b * half : (b + 1) * half]

    def deal():
        copies, at = [], 0
        for ref in grads:
            for b in range(ref.shape[0]):
                chip = chip_of(spot_ref, out_slots[at], size)
                copies.append(pltpu.make_async_copy(dealt.at[chip], ref.at[b], sem.at[0, at]))
                at += 1
        return copies

    @pl.when(step == steps - 1)
    def _():
        for c in deal():
            c.start()

    branch = dot(act, w_down)
    two = dot(jnp.concatenate([grad_gate, grad_up], axis=1), jnp.concatenate([w_gate, w_up], axis=0))
    for i, value in enumerate((branch, two)):
        if steps > 1:

            @pl.when(step == 0)
            def _():
                sums[i] = value

            @pl.when((step > 0) & (step < steps - 1))
            def _():
                sums[i] += value

        @pl.when(step == steps - 1)
        def _():
            total = value + sums[i] if steps > 1 else value
            results[2 * i][...] = total[:n]
            results[2 * i + 1][...] = total[n:].astype(bf)

    @pl.when(step == steps - 1)
    def _():
        for c in deal():
            c.wait()


def ffn_call(chain, spot, lengths, tokens, pieces, blocks, slots, out_slots, size, crossed, chunk=1024):
    n, d = tokens[-1].shape
    chips, rows = len(slots), pieces[0].shape[1]
    units = rows * 2 // 3
    steps = chips // 2 * units // chunk
    return chain.call(
        functools.partial(ffn_kernel, len(pieces), len(blocks), steps, slots, out_slots, size, crossed), "ffn",
        (spot, *lengths, *tokens, *pieces),
        [smem()] * 3 + [anywhere() for _ in (*tokens, *pieces)],
        [fixed(n, d)] * 4 + [anywhere() for _ in blocks],
        [shaped((n, d), f32), shaped((n, d), bf)] * 2 + [shaped((b, rows, d), bf) for b in blocks],
        grid=(steps,),
        scratch_shapes=[
            pltpu.VMEM((chips, rows, d), bf), pltpu.VMEM((chips, rows, d), bf),
            pltpu.VMEM((2 * n, d), bf), pltpu.VMEM((2 * n, d), bf), pltpu.VMEM((2, 2 * n, d), f32),
            pltpu.SemaphoreType.DMA((2, chips)), pltpu.SemaphoreType.DMA((6,)),
        ],
    )


def normed_kernel(spot_ref, own_ref, other_ref, own_out, other_out, full):
    half = own_out.shape[1]
    cols = pl.ds(pl.multiple_of(spot_ref[3] * half, half), half)
    for ref, out in ((own_ref, own_out), (other_ref, other_out)):
        source = ref[...].astype(f32)
        scale = lax.rsqrt(jnp.mean(source * source, axis=-1, keepdims=True) + NORM_EPS)
        full[...] = (source * scale).astype(bf)
        out[...] = full[:, cols]


def normed_call(chain, spot, own, other, parts=2):
    rows, width = own.shape
    block = pl.BlockSpec((rows // parts, width), lambda i: (i, 0))
    thin = pl.BlockSpec((rows // parts, width // 2), lambda i: (i, 0))
    return chain.call(
        normed_kernel, "normed", (spot, own, other), [smem(), block, block],
        [thin] * 2, [shaped((rows, width // 2), bf)] * 2,
        grid=(parts,), scratch_shapes=[pltpu.VMEM((rows // parts, width), bf)],
    )


def live_rows(values, lengths_ref, first=0):
    total = lengths_ref[0, 0] + lengths_ref[0, 1] + lengths_ref[0, 2]
    place = lax.broadcasted_iota(jnp.int32, (values.shape[0], 1), 0) + first
    return jnp.where(place < total, values, jnp.zeros((), values.dtype))


def pack_kernel(
    spot_ref, mixer_ref, gate_up_ref, down_ref, gains_ref, mixer_mine, mixer_theirs, gate_mine, gate_theirs, down_low, note
):
    half, units, core = mixer_mine.shape[1], gate_mine.shape[0], spot_ref[3]
    for ref, cols, rows, c in ((mixer_mine, half, units, core), (mixer_theirs, half, units, 1 - core)):
        ref[...] = mixer_ref[:, pl.ds(pl.multiple_of(c * half, half), half)].astype(bf)
    for ref, c in ((gate_mine, core), (gate_theirs, 1 - core)):
        ref[:units] = gate_up_ref[pl.ds(pl.multiple_of(c * units, units), units), :].astype(bf)
    count, own = gains_ref.shape
    note[...] = jnp.zeros_like(note)
    note[:count, :own] = gains_ref[...].astype(bf)
    gate_theirs[units:] = jnp.zeros((note.shape[0], gate_theirs.shape[1]), bf)
    gate_theirs[units:, : note.shape[1]] = note[...]
    down_low[...] = down_ref[...].astype(bf)


def pack_call(chain, spot, mixer, gate_up, down, gains):
    (rows, width), (units, _), (half, _) = mixer.shape, gate_up.shape, down.shape
    shapes = [(rows, width // 2)] * 2 + [(units // 2, width), (units // 2 + NOTE, width), (half, width), (NOTE, 128)]
    return chain.call(
        pack_kernel, "pack", (spot, mixer, gate_up, down, gains),
        [smem(), fixed(rows, width), fixed(units, width), fixed(half, width), fixed(*gains.shape)],
        [fixed(*s) for s in shapes], [shaped(s, bf) for s in shapes], grid=(1,),
    )


def block_kernel(own_gains, spot_ref, mine_ref, came_ref, note_ref, gate_ref, all_ref, copies_ref):
    rows, w = mine_ref.shape[0], all_ref.shape[1]
    mine = note_ref[...].astype(f32)
    came = gate_ref[gate_ref.shape[0] - NOTE :, :w].astype(f32)
    turned = lambda v: pltpu.roll(v, own_gains, 1)
    note = jnp.where(spot_ref[3] == 0, mine + turned(came), came + turned(mine)).astype(bf)
    at = 0
    for side in range(2):
        cols = slice(side * w, (side + 1) * w)
        all_ref[at : at + rows] = mine_ref[:, cols]
        all_ref[at + rows : at + 2 * rows] = came_ref[:, cols]
        all_ref[at + 2 * rows : at + 2 * rows + NOTE] = note
        at += 2 * rows + NOTE
    count = 2 * rows + NOTE
    for c in range(copies_ref.shape[0] // count):
        copies_ref[c * count : (c + 1) * count] = all_ref[:count]


def block_call(chain, spot, mine, came, note, gate_came, own_gains, copies, waits):
    rows, width = mine.shape
    w = width // 2
    each = 2 * rows + NOTE
    return chain.call(
        functools.partial(block_kernel, own_gains), "block", (spot, mine, came, note, gate_came),
        [smem()] + [fixed(*v.shape) for v in (mine, came, note, gate_came)],
        [fixed(2 * each, w), fixed(copies * each, w)], [shaped((2 * each, w), bf), shaped((copies * each, w), bf)],
        grid=(1,), waits=waits,
    )


def stack_kernel(count, moves, spot_ref, *refs):
    for i, a, rows, o, b in moves:
        if not isinstance(a, int):
            stride, distance, first = a
            a = pl.multiple_of((spot_ref[2] ^ distance) * stride + first, NOTE)
        refs[count + o][b : b + rows] = refs[i][pl.ds(a, rows)]


def stack_call(chain, spot, arrays, rows, moves, through=()):
    like = {o: arrays[i] for i, _, _, o, _ in moves}
    shapes = [(r,) + like[o].shape[1:] for o, r in enumerate(rows)]
    return chain.call(
        functools.partial(stack_kernel, len(arrays), moves), "stack", (spot, *arrays),
        [smem()] + [fixed(*v.shape) for v in arrays],
        [fixed(*s) for s in shapes], [shaped(s, like[o].dtype) for o, s in enumerate(shapes)], grid=(1,), through=through,
    )


def corner_kernel(cut, extra, x_ref, y_ref, to_x_ref, to_y_ref):
    rows = x_ref.shape[0]
    to_x_ref[:cut] = y_ref[:cut]
    if extra:
        to_x_ref[cut:] = y_ref[rows - extra :]
    to_y_ref[...] = x_ref[cut : rows - extra]


def whole_corner_kernel(x_ref, y_ref, to_x_ref, to_y_ref):
    to_x_ref[...] = y_ref[...]
    to_y_ref[...] = x_ref[...]


def corner_call(chain, from_x, from_y, extra):
    total, width = from_x.shape
    cut = (total - extra) // 2
    shapes = [(cut + extra, width), (cut, width)]
    ins, kernel = [fixed(total, width)] * 2, functools.partial(corner_kernel, cut, extra)
    if not extra:
        ins = [pl.BlockSpec((cut, width), lambda i: (1, 0)), pl.BlockSpec((cut, width), lambda i: (0, 0))]
        kernel = whole_corner_kernel
    return chain.call(
        kernel, "corner", (from_x, from_y), ins,
        [fixed(*s) for s in shapes], [shaped(s, bf) for s in shapes], grid=(1,),
    )


def near_kernel(to_x_ref, to_y_ref, by_x_ref, by_y_ref, new_x_ref, new_y_ref):
    new_x_ref[...] = (to_x_ref[...].astype(f32) + by_y_ref[...].astype(f32)).astype(bf)
    new_y_ref[...] = (to_y_ref[...].astype(f32) + by_x_ref[...].astype(f32)).astype(bf)


def near_call(chain, to_x, to_y, by_x, by_y, parts=2, **options):
    rows, width = by_x.shape
    block = (rows // parts, width)
    low, high = pl.BlockSpec(block, lambda i: (i, 0)), pl.BlockSpec(block, lambda i: (i + parts, 0))
    return chain.call(
        near_kernel, "near", (to_x, to_y, by_x, by_y), [high, low, low, low], [high, low],
        [shaped(to_x.shape, bf), shaped(to_y.shape, bf)], grid=(parts,), input_output_aliases={0: 0, 1: 1}, **options,
    )


def line_kernel(count, *refs):
    parts, refs = refs[:count], refs[count:]
    rows = refs[-1].shape[0]

    def total(at):
        result = parts[0][pl.ds(at, rows)].astype(f32)
        for ref in parts[1:]:
            result = result + ref[pl.ds(at, rows)].astype(f32)
        return result

    for s, ref in enumerate(refs):
        ref[...] = total(s * rows).astype(ref.dtype)


def line_call(chain, parts, size, apart, **options):
    quarters = 4 if len(parts) == 1 else 1
    rows, width = parts[0].shape[0] // quarters // size, parts[0].shape[1]
    if apart:
        whole = lambda q: pl.BlockSpec((size * rows, width), lambda i: (q, 0))
        ins = [whole(q) for q in range(quarters)] if quarters > 1 else [whole(0)] * len(parts)
        specs = [fixed(rows, width)] * size
        shapes = [shaped((rows, width), f32)] + [shaped((rows, width), bf)] * (size - 1)
        steps = 1
    else:
        steps = 2
        half = size * rows // steps
        ins = [pl.BlockSpec((half, width), lambda i, q=q: (i + q * steps, 0)) for q in range(quarters)]
        ins = ins if quarters > 1 else ins * len(parts)
        specs, shapes = [pl.BlockSpec((half, width), lambda i: (i, 0))], [shaped((size * rows, width), bf)]
    parts = parts * quarters
    return chain.call(
        functools.partial(line_kernel, len(parts)), "line", parts, ins, specs, shapes, grid=(steps,), **options
    )


def finish_kernel(cuts, count, note, spot_ref, first_ref, *refs):
    came, more, outs, squares_ref, total = (
        refs[:count], refs[count : -len(cuts) - 2], refs[-len(cuts) - 2 : -2], refs[-2], refs[-1]
    )
    rows = total.shape[0]
    result = first_ref[:rows].astype(f32)
    for b in range(1, first_ref.shape[0] // rows):
        result = result + first_ref[b * rows : (b + 1) * rows].astype(f32)
    for ref in came:
        result = result + ref[...].astype(f32)
    total[...] = result
    squares = jnp.sum(result * result, axis=0, keepdims=True)
    if note:
        whole = jnp.sum(squares, axis=1, keepdims=True)
        for ref in more[:-1]:
            whole = whole + jnp.sum(ref[...], axis=1, keepdims=True)
        gains = jnp.sum(more[-1][...], axis=0, keepdims=True)
        squares = jnp.broadcast_to(whole + jnp.sum(gains * gains, axis=1, keepdims=True), squares_ref.shape)
    squares_ref[...] = squares
    for ref, start in zip(outs, cuts):
        rows = ref.shape[0]
        if not isinstance(start, int):
            start = pl.multiple_of((spot_ref[3] ^ start[0]) * rows, rows & -rows)
        ref[...] = total[pl.ds(start, rows), :]


def finish_call(chain, spot, first, came, blocks, cuts, note=0, more=(), waits=()):
    rows, width = first.shape[0] // blocks, first.shape[1]
    shapes = [(r, width) for _, r in cuts] + [(note, 128) if note else (1, width)]
    return chain.call(
        functools.partial(finish_kernel, [c for c, _ in cuts], len(came), note), "finish", (spot, first, *came, *more),
        [smem(), fixed(*first.shape)] + [fixed(rows, width)] * len(came) + [fixed(*v.shape) for v in more],
        [fixed(*s) for s in shapes], [shaped(s, f32) for s in shapes],
        grid=(1,), scratch_shapes=[pltpu.VMEM((rows, width), f32)], waits=waits,
    )


def adam_step(weight, grad, first, second, rate, decay):
    first_new = BETA_ONE * first + (1.0 - BETA_ONE) * grad
    second_new = BETA_TWO * second + (1.0 - BETA_TWO) * grad * grad
    corr_one = 1.0 / (1.0 - BETA_ONE**STEP)
    corr_two = 1.0 / (1.0 - BETA_TWO**STEP)
    update = first_new * (rate * corr_one) / (jnp.sqrt(second_new * corr_two) + ADAM_EPS)
    return (weight * (1.0 - rate * decay) - update, first_new, second_new)


def adam_kernel(spot_ref, note_ref, *refs):
    ins, outs, wide, tall = refs[:21], refs[21:35], refs[35], refs[36]
    mixer, gate_up, down, gains, parts = ins[:4], ins[4:7], ins[7:10], ins[10:13], ins[13:]
    mixer_out, gate_up_out, down_out, gains_out, norm_out = outs[:4], outs[4:7], outs[7:10], outs[10:13], outs[13]
    core, quarter = spot_ref[3], parts[0].shape[1]
    norm = jnp.sqrt(jnp.sum(note_ref[...], axis=0, keepdims=True)[:, :1])
    factor = CLIP_LIMIT / jnp.maximum(norm, CLIP_LIMIT)

    rows, step = mixer[0].shape[0], wide.shape[0]

    @pl.loop(0, rows // step)
    def _(i):
        at = pl.ds(pl.multiple_of(i * step, step & -step), step)
        for s in range(2):
            mine = pl.multiple_of(core * 2 * quarter, quarter) + s * quarter
            came = pl.multiple_of((1 - core) * 2 * quarter, quarter) + s * quarter
            wide[:, pl.ds(pl.multiple_of(mine, quarter), quarter)] = parts[s][at]
            wide[:, pl.ds(pl.multiple_of(came, quarter), quarter)] = parts[2 + s][at]
        old, first, second, average = (r[at] for r in mixer)
        new, first, second = adam_step(old, wide[...] * factor, first, second, RATE_MATRIX, DECAY_MATRIX)
        average = AVERAGE_KEEP * average + (1.0 - AVERAGE_KEEP) * new
        for ref, value in zip(mixer_out, (new, first, second, average)):
            ref[at] = value

    @pl.when(pl.program_id(0) == 0)
    def _():
        half = parts[4].shape[0]
        tall[pl.ds(pl.multiple_of(core * half, half), half), :] = parts[4][...]
        tall[pl.ds(pl.multiple_of((1 - core) * half, half), half), :] = parts[5][...]
        own = gains[0].shape[1]
        sums = jnp.sum(parts[7][...], axis=0, keepdims=True)
        gain_grad = jnp.concatenate([sums[:, :own], sums[:, own : 2 * own]])
        for olds, news, grad, rate, decay in (
            (gate_up, gate_up_out, tall[...], RATE_MATRIX, DECAY_MATRIX),
            (down, down_out, parts[6][...], RATE_MATRIX, DECAY_MATRIX),
            (gains, gains_out, gain_grad, RATE_GAIN, 0.0),
        ):
            old, first, second = (r[...] for r in olds)
            scale = factor if rate == RATE_MATRIX else factor[:, :1]
            for ref, value in zip(news, adam_step(old, grad * scale, first, second, rate, decay)):
                ref[...] = value
        norm_out[...] = norm


def adam_call(chain, spot, note, mixer, gate_up, down, gains, parts, blocks=1):
    rows, width = mixer[0].shape
    step = rows // blocks
    block = pl.BlockSpec((step, width), lambda i: (i, 0))
    piece = pl.BlockSpec((step, parts[0].shape[1]), lambda i: (i, 0))
    whole = lambda v: fixed(*v.shape)
    others = [*gate_up, *down, *gains]
    shapes = [v.shape for v in (*mixer, *others)] + [(1, 1)]
    return chain.call(
        adam_kernel, "adam", (spot, note, *mixer, *others, *parts),
        [smem(), whole(note)] + [block] * 4 + [whole(v) for v in others] + [piece] * 4
        + [whole(v) for v in parts[4:]],
        [block] * 4 + [whole(v) for v in others] + [fixed(1, 1)], [shaped(s, f32) for s in shapes],
        grid=(blocks,),
        scratch_shapes=[pltpu.VMEM((step // 3, width), f32), pltpu.VMEM(gate_up[0].shape, f32)],
    )


def flip(v, axis, bits=1):
    size = lax.axis_size(axis)
    return lax.ppermute(v, axis, [(i, i ^ bits) for i in range(size)])


def swap(v):
    return flip(v, "core")


def join(mine, other, core, axis=0):
    return jnp.where(
        core == 0,
        jnp.concatenate([mine, other], axis=axis),
        jnp.concatenate([other, mine], axis=axis),
    )


def part(v, index, axis=0):
    size = v.shape[axis] // 2
    return lax.dynamic_slice_in_dim(v, index * size, size, axis)


def low(v):
    return v.astype(bf)


def wide(v):
    return v.astype(f32)


class Whole:
    crossed = False
    mixer_slots = ((0,), (0,))
    mixer_blocks = (1,)

    def __init__(self, spot, groups):
        self.spot, self.core = spot, spot[3]
        self.size = lax.axis_size("z")
        self.chips = lax.axis_size("d0") * lax.axis_size("d1") * self.size
        self.ffn_in = self.ffn_out = tuple(range(groups))
        self.ffn_blocks = (groups,)

    def gather(self, chain, mixer, gate_up, down, gains, waits):
        def trade(v, axis):
            return join(part(v, self.core, axis), swap(part(v, 1 - self.core, axis)), self.core)

        everything = lambda v: lax.all_gather(v, CHIPS, axis=0, tiled=True)
        mixer_block = trade(low(mixer), 1)
        w, groups = mixer_block.shape[1] // 2, len(self.ffn_in)
        sides = []
        for s in range(2):
            whole = everything(mixer_block[:, s * w : (s + 1) * w])
            sides.append(([whole], ((0, 0, whole.shape[0], 0, None),), ()))
        ffn = [everything(v).reshape(groups, -1, v.shape[1]) for v in (trade(low(gate_up), 0), low(down))]
        ffn = [jnp.concatenate(ffn, axis=1)]
        gains = lax.all_gather(wide(low(gains)), EVERY, axis=1, tiled=True)
        yield jnp.pad(gains, ((0, NOTE - 2), (0, 0)))
        while True:
            yield sides, ffn

    def scatter(self, chain, parts, cuts, groups=1, apart=False):
        grads = parts[0].reshape(groups, -1, parts[0].shape[-1])
        rows = grads.shape[1] * 2 // 3
        if groups > 1:
            shards = [grads[:, :rows], grads[:, rows:]]
        else:
            shards = [grads]
        shards = [wide(lax.psum_scatter(flat(v), CHIPS, scatter_dimension=0, tiled=True)) for v in shards]
        outs = [part(shards[0], self.core), part(shards[0], 1 - self.core)] + shards[1:]
        squares = sum(jnp.sum(v * v, axis=0, keepdims=True) for v in shards)
        if groups == 1:
            yield
            yield ()
        through = yield ()
        yield (), through
        yield
        yield outs + [squares]

    def spread_gains(self, grads, rows):
        one, two = grads
        nothing = jnp.zeros_like(one)
        one = join(one, nothing, self.core, 1)
        return lax.psum_scatter(jnp.concatenate([one, two]), EVERY, scatter_dimension=1, tiled=True)

    def total(self, v):
        return lax.psum(v, EVERY)


class Cube(Whole):
    crossed = True
    near = ((0, 0), (0, 1), (1, 0), (1, 1))

    def __init__(self, spot, groups):
        super().__init__(spot, groups)
        slots = lambda fixed_z: tuple((y, x, s, fixed_z) for y, x in self.near for s in range(self.size))
        self.mixer_slots = slots(False), slots(True)
        self.ffn_in = slots(True)
        self.ffn_out = tuple((y, x, z, True) for z in range(self.size) for y, x in self.near)
        self.mixer_blocks = (self.size,) * 3 + (self.size // 2,) * 2

    def lines(self, block):
        return [flip(block, "z", s) for s in range(1, self.size)]

    def gather(self, chain, mixer, gate_up, down, gains, waits):
        spot = self.spot
        mixer_mine, mixer_theirs, gate_mine, gate_theirs, down_low, note = pack_call(
            chain, spot, mixer, gate_up, down, gains
        )
        gate_came = swap(gate_theirs)
        size = self.size
        own, block = block_call(
            chain, spot, mixer_mine, swap(mixer_theirs), note, gate_came, gains.shape[1], size, waits
        )
        line = self.along_z(block)
        own_x, own_y = flip(own, "d1"), flip(own, "d0")
        rows = own.shape[0] // 2 - NOTE
        units, count = gate_mine.shape[0], down_low.shape[0]
        ffn_rows = 2 * units + count
        moves = [(0, rows + NOTE, rows, 0, s * rows) for s in range(size)]
        for s in range(size):
            at = s * ffn_rows
            moves += [(1, 0, units, 1, at), (2, 0, units, 1, at + units), (3, 0, count, 1, at + 2 * units)]
        second_block, ffn_block = stack_call(
            chain, spot, (own, gate_mine, gate_came, down_low), (size * rows, size * ffn_rows), tuple(moves)
        )
        yield None
        half = rows // 2
        sides = []

        def spread_out(line):
            return line, flip(line, "d1"), flip(line, "d0")

        def turn_corner(from_x, from_y, extra=0):
            to_x, to_y = corner_call(chain, from_x, from_y, extra)
            return flip(to_x, "d1"), flip(to_y, "d0")

        def plan(side):
            found = [(p, side * (rows + NOTE) + h * half, half, near + (0, False), h) for p, near in enumerate(self.near[:3]) for h in range(2)]
            found += [(3, h * half, half, (1, 1, 0, False), h) for h in range(2)]
            last = (size - 1) * 2
            for at in range(last):
                s, h = at // 2 + 1, at % 2
                found += [(4 + p, at * half, half, near + (s, False), h) for p, near in enumerate(self.near[:3])]
                found.append((7 + (at >= last // 2), at % (last // 2) * half, half, (1, 1, s, False), h))
            return tuple(found)

        corner = turn_corner(own_x, own_y)
        yield
        chain.pause(corner)
        others, line_rows = range(1, size), (size - 1) * rows
        moves = [(0, (rows + NOTE, s, 0), rows, 0, (s - 1) * rows) for s in others]
        moves += [(0, (rows + NOTE, s, rows), NOTE, 0, line_rows + (s - 1) * NOTE) for s in others]
        line, block = stack_call(
            chain, spot, (line,), (line_rows + (size - 1) * NOTE,), tuple(moves), through=(second_block,)
        )
        first = spread_out(line)
        line = self.along_z(block)
        yield
        first_corner = turn_corner(*first[1:], (size - 1) * NOTE)
        notes = [(p, rows, near + (0, False)) for p, near in enumerate(self.near)]
        for s in others:
            notes += [(4 + p, line_rows + (s - 1) * NOTE, near + (s, False)) for p, near in enumerate(self.near[:3])]
            notes.append((7, line_rows // 2 + (s - 1) * NOTE, (1, 1, s, False)))
        sides.append(([own, own_x, own_y, corner[0], *first, *first_corner], plan(0), tuple(notes)))
        moves = [(0, (rows, s, 0), rows, 0, (s - 1) * rows) for s in others]
        line, block = stack_call(chain, spot, (line,), (line_rows,), tuple(moves), through=(ffn_block,))
        across, line = line, self.along_z(block)
        second = spread_out(*chain.pause(first_corner, (across,)))
        yield sides, None
        second_corner = turn_corner(*second[1:])
        sides.append(([own, own_x, own_y, corner[1], *second, *second_corner], plan(1), ()))
        ffn = spread_out(*chain.pause(second_corner, (line,)))
        yield sides, None
        ffn = (*ffn, *turn_corner(*ffn[1:]))
        yield sides, [v.reshape(-1, ffn_rows, v.shape[-1]) for v in ffn]

    def along_z(self, v):
        return lax.all_to_all(v, "z", 0, 0, tiled=True)

    def scatter(self, chain, parts, cuts, groups=1, apart=False):
        if groups > 1:
            came = (self.along_z(flat(parts[0])),)
        else:
            own, to_x, to_y, far_low, far_high = (flat(v) for v in parts)
            by_x, by_y = flip(far_low, "d1"), flip(far_high, "d0")
            yield
            to_x, to_y = yield near_call(chain, to_x, to_y, by_x, by_y)
            came = own, flip(to_x, "d1"), flip(to_y, "d0")
        through = yield came
        outs = line_call(chain, came, self.size, apart, through=through or ())
        count = self.size if apart else 1
        first, *rest = yield outs[:count], outs[count:]
        if groups > 1:
            to_x, to_y, far = rest
            far = lax.ppermute(far, ("d0", "d1"), [(i, i ^ 3) for i in range(4)])
            came = flip(to_x, "d1"), flip(to_y, "d0"), far
        elif apart:
            came = [flip(v, "z", s + 1) for s, v in enumerate(rest)]
        else:
            first, came = self.along_z(first), ()
        more, waits = yield
        yield finish_call(
            chain, self.spot, first, came, 1 if apart else self.size, cuts, 2 * self.chips if more else 0, more, waits
        )

    def spread_gains(self, grads, rows):
        return self.everyone(rows)

    def everyone(self, rows):
        return lax.all_to_all(rows, EVERY, 0, 0, tiled=True)


def body(
    inputs, lengths, filters, cotangent, mixer_weight, gate_up_weight, down_weight, norm_gains,
    mixer_first, gate_up_first, down_first, gains_first,
    mixer_second, gate_up_second, down_second, gains_second, mixer_average,
):
    slots, width = inputs.shape
    size = lax.axis_size("z")
    groups = 2 * FF // 256
    cube = lax.axis_size("d0") == 2 and lax.axis_size("d1") == 2 and size == 4
    spot = jnp.stack([lax.axis_index(a) for a in EVERY]).astype(jnp.int32)
    core = spot[3]
    links = (Cube if cube else Whole)(spot, groups)
    units = gate_up_weight.shape[0]
    chain = Chain()

    sums = lengths, swap(lengths)
    source_other, cotangent_other = swap(inputs), swap(cotangent)
    taps = jnp.concatenate([wide(filters), jnp.eye(AR_ORDER, slots, dtype=f32)])
    taps_turned = jnp.roll(taps[:, ::-1], 1 - slots // 4, axis=1)
    taps, taps_turned = (v.reshape(-1, 3, slots) for v in (taps, taps_turned))

    weights = links.gather(
        chain, mixer_weight, gate_up_weight, down_weight, norm_gains, (sums[1], source_other, cotangent_other)
    )
    gains = next(weights)
    tokens = hat_tokens = normed_call(chain, spot, inputs, source_other)
    blocks = taps.shape[0]
    cuts, spread = (0, blocks * 2 // 9, blocks // 3, blocks), None
    for at in range(3):
        spread = spread_call(chain, sums, taps_turned, *tokens, cuts[at], cuts[at + 1] - cuts[at], spread)
        sides = next(weights)
    sides, _ = sides
    quarter = sides[0][0][0].shape[1]
    *mixed, left, gains = (*mix_call(chain, spot, spread, 0, *sides[0], gains, size, width), gains)[:4]
    sides, _ = next(weights)
    mixed_own, mixed_other, right = mix_call(chain, spot, spread, 1, *sides[1], gains, size, width, mixed)
    _, ffn = next(weights)

    hidden, *normed_two = hidden_call(chain, inputs, mixed_own, swap(mixed_other), gains)
    tokens = (*normed_two, *(swap(v) for v in normed_two), cotangent, cotangent_other)
    branch_own, branch_other, two_own, two_other, *grad_ffn = ffn_call(
        chain, spot, sums, tokens, ffn, links.ffn_blocks, links.ffn_in, links.ffn_out, size, links.crossed
    )
    if cube:
        grad_ffn = chain.pause(through=grad_ffn)
    ffn_sum = links.scatter(chain, grad_ffn, ((0, units // 2), (units // 2, units // 2), (units, units // 2)), groups, True)
    ffn_came = next(ffn_sum)
    grad_hidden, grad_low, gains_two = turn_call(
        chain, lengths, hidden, cotangent, two_own, swap(two_other), gains
    )
    grad_other = swap(grad_low)
    rows = mixer_weight.shape[0]
    cuts = (((0,), rows), ((1,), rows))
    grads_of = lambda s: grad_call(
        chain, spot, gains, grad_low, grad_other, spread, s, quarter, links.mixer_blocks, links.mixer_slots[s], size
    )
    first_sum = links.scatter(chain, grads_of(0), cuts, apart=True)
    next(first_sum)
    second_sum = links.scatter(chain, grads_of(1), cuts)
    next(second_sum)
    backward = lambda first, steps, *more: back_call(
        chain, spot, sums, taps, grad_low, grad_other, (left, right), first, steps, *more
    )
    early = blocks // 2
    first_sum.send(next(first_sum))
    one = backward(0, early)
    second_sum.send(next(second_sum))
    one_own, one_other, gains_one, note_rows = backward(
        early, blocks - early, one, hat_tokens, gains_two, 2 * links.chips
    )
    outs, _ = first_sum.send(())
    first_sum.send(outs)
    if cube:
        (note_rows,) = chain.pause(ffn_came, (note_rows,))
    shard_gains = links.spread_gains((gains_one, gains_two), note_rows)
    outs, _ = second_sum.send(())
    chain.pause((shard_gains,))
    first_mine, first_theirs, square = first_sum.send(((), ()))
    first_theirs, branch_other, *outs = chain.pause(through=(first_theirs, branch_other, *outs))
    second_sum.send(outs)
    outs, _ = ffn_sum.send(())
    ffn_sum.send(outs)
    output = output_call(chain, hidden, branch_own, swap(branch_other))
    input_grad = last_call(chain, spot, grad_hidden, inputs, one_own, swap(one_other), gains)
    gate_up_mine, gate_up_theirs, shard_down, *squares = ffn_sum.send(((), ()))
    squares.append(square)
    gate_up_came, first_came = swap(gate_up_theirs), swap(first_theirs)
    second_mine, second_theirs, note = second_sum.send(((*squares, shard_gains), ()))
    second_came = swap(second_theirs)
    mixer = mixer_weight, mixer_first, mixer_second, mixer_average
    gate_up, down = (gate_up_weight, gate_up_first, gate_up_second), (down_weight, down_first, down_second)
    gain = norm_gains, gains_first, gains_second
    if cube:
        (
            mixer_new, mixer_first_new, mixer_second_new, mixer_average_new, gate_up_new, gate_up_first_new,
            gate_up_second_new, down_new, down_first_new, down_second_new, gains_new, gains_first_new, gains_second_new,
            grad_norm,
        ) = adam_call(
            chain, spot, links.everyone(note), mixer, gate_up, down, gain,
            (first_mine, second_mine, first_came, second_came, gate_up_mine, gate_up_came, shard_down, shard_gains),
        )
        grad_norm = grad_norm[0, 0]
    else:
        squares = sum(jnp.sum(v) for v in (*squares, note)) + jnp.sum(shard_gains * shard_gains)
        grad_norm = jnp.sqrt(links.total(squares))
        factor = CLIP_LIMIT / jnp.maximum(grad_norm, CLIP_LIMIT)
        shard_mixer = join(
            jnp.concatenate([first_mine, second_mine], axis=1), jnp.concatenate([first_came, second_came], axis=1), core, 1
        )
        shard_gate_up = join(gate_up_mine, gate_up_came, core)
        step = lambda old, grad: adam_step(old[0], grad * factor, old[1], old[2], RATE_MATRIX, DECAY_MATRIX)
        mixer_new, mixer_first_new, mixer_second_new = step(mixer, shard_mixer)
        gate_up_new, gate_up_first_new, gate_up_second_new = step(gate_up, shard_gate_up)
        down_new, down_first_new, down_second_new = step(down, shard_down)
        gains_new, gains_first_new, gains_second_new = adam_step(
            gain[0], shard_gains * factor, gain[1], gain[2], RATE_GAIN, 0.0
        )
        mixer_average_new = AVERAGE_KEEP * mixer_average + (1.0 - AVERAGE_KEEP) * mixer_new
    return (
        output, input_grad, grad_norm, mixer_new, gate_up_new, down_new, gains_new,
        mixer_first_new, gate_up_first_new, down_first_new, gains_first_new,
        mixer_second_new, gate_up_second_new, down_second_new, gains_second_new, mixer_average_new,
    )


def solution(mesh):
    outer, inner = mesh.shape["dp"], mesh.shape["fsdp"]
    side = math.isqrt(outer)
    if side * side != outer:
        side = 1
    split = jax.sharding.Mesh(
        np.asarray(mesh.devices).reshape(side, outer // side, inner // 2, 2), EVERY
    )
    rows, columns, whole = P(EVERY, None), P(None, EVERY), P()
    return jax.shard_map(
        body,
        mesh=split,
        in_specs=(
            rows, rows, whole, rows, rows, rows, rows, columns,
            rows, rows, rows, columns, rows, rows, rows, columns, rows,
        ),
        out_specs=(
            rows, rows, whole, rows, rows, rows, columns, rows, rows, rows, columns,
            rows, rows, rows, columns, rows,
        ),
        check_vma=False,
    )
```

```python
import functools
import math

import jax
import jax.numpy as jnp
import numpy as np
from jax import lax
from jax.experimental import pallas as pl
from jax.experimental.pallas import tpu as pltpu
from jax.sharding import PartitionSpec as P

bf = jnp.bfloat16
f32 = jnp.float32
FILTERS = 24
AR_ORDER = 3
FF = 2048
STEP = 10
NORM_EPS = 1e-05
CLIP_LIMIT = 1.0
BETA_ONE = 0.9
BETA_TWO = 0.95
ADAM_EPS = 1e-08
RATE_MATRIX = 0.03
RATE_GAIN = 0.5
DECAY_MATRIX = 0.1
AVERAGE_KEEP = 0.9
CHIPS = ("d0", "d1", "z")
EVERY = CHIPS + ("core",)


NT = (((1,), (1,)), ((), ()))
NN = (((1,), (0,)), ((), ()))
TN = (((0,), (0,)), ((), ()))


def dot(a, b, dims=NN):
    return lax.dot_general(a, b, dims, preferred_element_type=f32)


class Chain:
    def __init__(self):
        self.token = None

    def call(self, kernel, name, args, in_specs, out_specs, out_shape, waits=(), through=(), **options):
        count, single = len(args), not isinstance(out_shape, (list, tuple)) and not through
        if single:
            out_specs, out_shape = [out_specs], [out_shape]
        made = len(out_shape)
        aliases = options.pop("input_output_aliases", {})
        aliases = {**aliases, **{count + i: made + i for i in range(len(through))}}
        last = tuple(through) + tuple(waits) + (() if self.token is None else (self.token,))

        def whole(*refs):
            first = count + len(last)
            kernel(*refs[:count], *refs[first : first + made], *refs[first + made + len(through) + 1 :])

        *outs, self.token = pl.pallas_call(
            whole,
            name=name,
            in_specs=list(in_specs) + [anywhere() for _ in last],
            out_specs=list(out_specs) + [anywhere() for _ in through] + [anywhere()],
            out_shape=list(out_shape) + [shaped(v.shape, v.dtype) for v in through] + [shaped((8, 128), f32)],
            input_output_aliases=aliases,
            compiler_params=pltpu.CompilerParams(vmem_limit_bytes=64 << 20),
            cost_estimate=pl.CostEstimate(flops=1, bytes_accessed=1, transcendentals=0),
            **options,
        )(*args, *last)
        return outs[0] if single else outs

    def pause(self, waits=(), through=()):
        return self.call(lambda: None, "pause", (), [], [], [], waits=waits, through=through)


def smem():
    return pl.BlockSpec(memory_space=pltpu.SMEM)


def anywhere():
    return pl.BlockSpec(memory_space=pl.ANY)


def fixed(*shape):
    return pl.BlockSpec(shape, lambda i: (0,) * len(shape))


NOTE = 16


def shaped(shape, dtype):
    return jax.ShapeDtypeStruct(tuple(shape), dtype)


def segment_of(place, ends_ref, group):
    return sum((place >= ends_ref[group, j]).astype(jnp.int32) for j in range(3))


def causal_mask(ends_ref, group, n, transposed):
    down = lax.broadcasted_iota(jnp.int32, (n, 1), 0)
    along = lax.broadcasted_iota(jnp.int32, (1, n), 1)
    one, two = segment_of(down, ends_ref, group), segment_of(along, ends_ref, group)
    order = (down <= along) if transposed else (down >= along)
    return ((one == two) & (one < 3) & order).astype(f32).astype(bf)


def diagonals(row, count):
    wide = jnp.broadcast_to(row, (count, row.shape[-1]))
    return pltpu.roll(wide, 0, 1, stride=1, stride_axis=0).astype(bf)


def spread_kernel(lengths_ref, came_ref, taps_ref, own_ref, other_ref, *refs):
    u_ref, mask, table, ends = refs[-4:]
    n = mask.shape[1]
    q, h, w = n // 4, n // 2, own_ref.shape[1] // 2
    per = taps_ref.shape[1]

    @pl.when(pl.program_id(0) == 0)
    def _():
        find_ends(ends, lengths_ref, came_ref)
        for g in range(2):
            mask[g] = causal_mask(ends, g, n, False)
        table[...] = jnp.zeros_like(table)

    @pl.loop(0, per)
    def _(j):
        at = pl.multiple_of(j * w, w)
        strip = diagonals(taps_ref[0, pl.ds(j, 1), :], q)
        for g, tokens in enumerate((own_ref, other_ref)):
            for i in range(4):
                rows, cols = slice(i * q, (i + 1) * q), slice(0, (i + 1) * q)
                table[g, rows, cols] = strip[:, (3 - i) * q :] * mask[g, rows, cols]
            upper = dot(table[g, :h, :h], tokens[:h]).astype(bf)
            lower = dot(table[g, h:, :], tokens[...]).astype(bf)
            for side in range(2):
                cols = slice(side * w, (side + 1) * w)
                u_ref[side, g * n : g * n + h, pl.ds(at, w)] = upper[:, cols]
                u_ref[side, g * n + h : (g + 1) * n, pl.ds(at, w)] = lower[:, cols]


def find_ends(ends, lengths_ref, came_ref):
    for g, ref in enumerate((lengths_ref, came_ref)):
        total = ref[0, 0]
        ends[g, 0] = total
        for j in range(1, 3):
            total = total + ref[0, j]
            ends[g, j] = total


def spread_call(chain, lengths, taps, own, other, first, steps, into=None):
    blocks, per, n = taps.shape
    w = own.shape[1] // 2
    args = [*lengths, taps, own, other]
    specs = [smem()] * 2 + [pl.BlockSpec((1, per, n), lambda i: (i + first, 0, 0)), fixed(n, 2 * w), fixed(n, 2 * w)]
    options = {}
    if into is not None:
        options = dict(input_output_aliases={len(args): 0})
        args, specs = args + [into], specs + [anywhere()]
    return chain.call(
        spread_kernel, "spread", args, specs,
        pl.BlockSpec((2, 2 * n, per * w), lambda i: (0, 0, i + first)),
        shaped((2, 2 * n, blocks * per * w), bf),
        grid=(steps,),
        scratch_shapes=[pltpu.VMEM((2, n, n), bf), pltpu.VMEM((2, n, n), bf), pltpu.SMEM((2, 3), jnp.int32)],
        **options,
    )


def run_copies(copies):
    for c in copies:
        c.start()
    for c in copies:
        c.wait()


def chip_of(spot_ref, slot, size):
    if isinstance(slot, int):
        return slot
    dy, dx, dz, fixed_z = slot
    return ((spot_ref[0] ^ dy) * 2 + (spot_ref[1] ^ dx)) * size + (dz if fixed_z else spot_ref[2] ^ dz)


def collect(spot_ref, pieces, plan, size, held, sem, columns):
    copies = []
    for at, (piece, row, rows, slot, half) in enumerate(plan):
        place = chip_of(spot_ref, slot, size)
        if half is not None:
            place = place * 2 + (spot_ref[3] ^ half)
        start = pl.multiple_of(place * rows, math.gcd(rows, 512))
        copies.append(
            pltpu.make_async_copy(pieces[piece].at[pl.ds(row, rows)], held.at[pl.ds(start, rows), columns], sem.at[at])
        )
    return copies


def mix_kernel(count, plan, notes, size, width, side, spot_ref, u_ref, *refs):
    pieces, refs = refs[:count], refs[count:]
    first = side == 0
    before, refs = refs[: 0 if first else 2], refs[0 if first else 2 :]
    if not notes:
        gains_ref, refs = refs[0], refs[1:]
    own_ref, other_ref, w_ref, *refs = refs
    if notes:
        gains_ref, refs = refs[0], refs[1:]
    held, u, sem, u_sem, *refs = refs
    *refs, result = refs
    tiles = sums = refs[0] if refs else None
    w = held.shape[1]
    filters = held.shape[0] // width
    rows = own_ref.shape[0]
    copies = collect(spot_ref, pieces, plan, size, held, sem, slice(0, w))
    for at, (piece, row, slot) in enumerate(notes):
        copies.append(
            pltpu.make_async_copy(
                pieces[piece].at[pl.ds(row, NOTE)], tiles.at[chip_of(spot_ref, slot, size)], sem.at[len(plan) + at]
            )
        )
    third = filters // 3
    cols = [pl.ds(t * third * w, third * w) for t in range(3)]
    loads = [pltpu.make_async_copy(u_ref.at[side, :, c], u.at[:, c], u_sem.at[t]) for t, c in enumerate(cols)]
    adds = [pltpu.make_async_copy(ref, sums.at[g], u_sem.at[4 + g]) for g, ref in enumerate(before)]
    for c in copies + loads + adds:
        c.start()
    for c in copies:
        c.wait()
    give = pltpu.make_async_copy(held, w_ref, u_sem.at[3])
    give.start()
    if notes:
        lanes = width // len(notes)
        for b in range(width // 128):
            block = jnp.zeros((NOTE, 128), f32)
            for j in range(128 // lanes):
                tile = tiles[b * (128 // lanes) + j].astype(f32)
                block = block + (pltpu.roll(tile, j * lanes, 1) if j else tile)
            gains_ref[:, b * 128 : (b + 1) * 128] = block
    gain = gains_ref[0:1, pl.ds(pl.multiple_of((spot_ref[3] * 2 + side) * w, w), w)]
    result[...] = jnp.zeros_like(result)

    @pl.loop(0, 3)
    def _(t):
        pltpu.make_async_copy(u_ref.at[side, :, pl.ds(0, third * w)], u.at[:, pl.ds(0, third * w)], u_sem.at[t]).wait()
        first_row = pl.multiple_of(t * third * width, width)
        wide = jnp.concatenate(
            [(held[pl.ds(first_row + k * width, width), :].astype(f32) * gain).astype(bf) for k in range(third)], axis=1
        )
        result[...] += dot(u[:, pl.ds(pl.multiple_of(t * third * w, w), third * w)], wide, NT)

    for g, out in enumerate((own_ref, other_ref)):
        mine = result[g * rows : (g + 1) * rows]
        if not first:
            adds[g].wait()
            mine = mine + sums[g]
        out[...] = mine.astype(out.dtype)
    give.wait()


def mix_call(chain, spot, u, side, pieces, plan, notes, gains, size, width, before=()):
    rows, depth = u.shape[1:]
    w = pieces[0].shape[-1]
    total = depth // w * width
    step = rows // 2
    out = fixed(step, width)
    note = fixed(NOTE, width)
    given = () if notes else (gains,)
    made = 1 - len(given)
    return chain.call(
        functools.partial(mix_kernel, len(pieces), plan, notes, size, width, side), "mix",
        (spot, u, *pieces, *before, *given),
        [smem(), anywhere()] + [anywhere() for _ in (*pieces, *before)] + [note for _ in given],
        [out, out, anywhere()] + [note] * made,
        [shaped((step, width), f32), shaped((step, width), bf if before else f32), shaped((total, w), bf)]
        + [shaped((NOTE, width), f32)] * made,
        grid=(1,),
        scratch_shapes=[
            pltpu.VMEM((total, w), bf), pltpu.VMEM((rows, depth), bf),
            pltpu.SemaphoreType.DMA((len(plan) + len(notes),)), pltpu.SemaphoreType.DMA((6,)),
        ] + [pltpu.VMEM((len(notes), NOTE, 128), bf)] * made + [pltpu.VMEM((2, step, width), f32)] * min(1, len(before))
        + [pltpu.VMEM((rows, width), f32)],
    )


def hidden_kernel(source_ref, own_ref, came_ref, gain_ref, hidden_ref, *normed_refs):
    hidden = source_ref[...].astype(f32) + (own_ref[...] + came_ref[...].astype(f32))
    scale = lax.rsqrt(jnp.mean(hidden * hidden, axis=-1, keepdims=True) + NORM_EPS)
    hidden_ref[...] = hidden
    normed = (hidden * scale * gain_ref[1:2]).astype(bf)
    width = normed_refs[0].shape[1]
    for i, ref in enumerate(normed_refs):
        ref[...] = normed[:, i * width : (i + 1) * width]


def hidden_call(chain, source, own, came, gain, parts=2):
    rows, width = source.shape
    block = pl.BlockSpec((rows // parts, width), lambda i: (i, 0))
    thin = pl.BlockSpec((rows // parts, width // 2), lambda i: (i, 0))
    return chain.call(
        hidden_kernel, "hidden", (source, own, came, gain), [block, block, block, fixed(NOTE, width)],
        [block, thin, thin], [shaped((rows, width), f32)] + [shaped((rows, width // 2), bf)] * 2,
        grid=(parts,),
    )


def norm_back(grad, hat, scale, gain):
    weighted = grad * gain
    return scale * (weighted - hat * jnp.mean(weighted * hat, axis=-1, keepdims=True))


def add_rows(ref, values, step):
    total = jnp.sum(values, axis=0, keepdims=True)

    @pl.when(step == 0)
    def _():
        ref[...] = total

    @pl.when(step > 0)
    def _():
        ref[...] += total


def turn_kernel(lengths_ref, hidden_ref, back_ref, own_ref, came_ref, gain_ref, grad_ref, low_ref, gains_ref):
    hidden = hidden_ref[...]
    scale = lax.rsqrt(jnp.mean(hidden * hidden, axis=-1, keepdims=True) + NORM_EPS)
    hat = hidden * scale
    two = own_ref[...] + came_ref[...].astype(f32)
    back = live_rows(back_ref[...].astype(f32), lengths_ref, pl.program_id(0) * hidden.shape[0])
    grad = back + norm_back(two, hat, scale, gain_ref[1:2])
    grad_ref[...] = grad
    low_ref[...] = grad.astype(bf)
    add_rows(gains_ref, two * hat, pl.program_id(0))


def turn_call(chain, lengths, hidden, back, own, came, gain, parts=2):
    rows, width = hidden.shape
    block = pl.BlockSpec((rows // parts, width), lambda i: (i, 0))
    return chain.call(
        turn_kernel, "turn", (lengths, hidden, back, own, came, gain), [smem()] + [block] * 4 + [fixed(NOTE, width)],
        [block, block, fixed(1, width)],
        [shaped((rows, width), f32), shaped((rows, width), bf), shaped((1, width), f32)],
        grid=(parts,),
    )


def output_kernel(hidden_ref, own_ref, came_ref, out_ref):
    out_ref[...] = (hidden_ref[...] + (own_ref[...] + came_ref[...].astype(f32))).astype(bf)


def output_call(chain, hidden, own, came, parts=2):
    rows, width = hidden.shape
    block = pl.BlockSpec((rows // parts, width), lambda i: (i, 0))
    return chain.call(
        output_kernel, "output", (hidden, own, came), [block] * 3, block, shaped((rows, width), bf), grid=(parts,),
    )


def last_kernel(spot_ref, grad_ref, source_ref, own_ref, came_ref, gain_ref, out_ref, one):
    half = own_ref.shape[1]
    core = spot_ref[3]
    one[:, pl.ds(pl.multiple_of(core * half, half), half)] = own_ref[...]
    one[:, pl.ds(pl.multiple_of((1 - core) * half, half), half)] = came_ref[...]
    source = source_ref[...].astype(f32)
    scale = lax.rsqrt(jnp.mean(source * source, axis=-1, keepdims=True) + NORM_EPS)
    out_ref[...] = grad_ref[...] + norm_back(one[...], source * scale, scale, gain_ref[0:1])


def last_call(chain, spot, grad_hidden, source, own, came, gain, parts=2):
    rows, width = source.shape
    block = pl.BlockSpec((rows // parts, width), lambda i: (i, 0))
    thin = pl.BlockSpec((rows // parts, width // 2), lambda i: (i, 0))
    return chain.call(
        last_kernel, "last", (spot, grad_hidden, source, own, came, gain),
        [smem(), block, block, thin, thin, fixed(NOTE, width)], block, shaped((rows, width), f32),
        grid=(parts,), scratch_shapes=[pltpu.VMEM((rows // parts, width), f32)],
    )


def grad_kernel(slots, size, side, spot_ref, gains_ref, own_ref, other_ref, u_ref, *refs):
    outs, (turned, held, sem) = refs[:-3], refs[-3:]
    n, width = own_ref.shape
    w = held.shape[1]
    per = u_ref.shape[2] // w
    step = pl.program_id(0)

    @pl.when(step == 0)
    def _():
        turned[:, :n] = own_ref[...].T
        turned[:, n:] = other_ref[...].T

    gain = gains_ref[0:1, pl.ds(pl.multiple_of((spot_ref[3] * 2 + side) * w, w), w)]
    result = dot(turned[...], u_ref[0])
    for j in range(per):
        at = pl.multiple_of((step * per + j) * width, width)
        held[pl.ds(at, width), :] = (result[:, j * w : (j + 1) * w] * gain).astype(bf)

    @pl.when(step == pl.num_programs(0) - 1)
    def _():
        rows = held.shape[0] // len(slots)
        copies, at = [], 0
        for ref in outs:
            for b in range(ref.shape[0] // rows):
                start = pl.multiple_of(chip_of(spot_ref, slots[at], size) * rows, math.gcd(rows, 512))
                copies.append(
                    pltpu.make_async_copy(held.at[pl.ds(start, rows)], ref.at[pl.ds(b * rows, rows)], sem.at[at])
                )
                at += 1
        run_copies(copies)


def grad_call(chain, spot, gains, own, other, u, side, w, blocks, slots, size, per=9):
    rows, depth = u.shape[1:]
    n, width = own.shape
    count = depth // w
    each = count * width // len(slots)
    return chain.call(
        functools.partial(grad_kernel, slots, size, side), "mixer_grad", (spot, gains, own, other, u),
        [smem(), fixed(NOTE, width), fixed(n, width), fixed(n, width), pl.BlockSpec((1, rows, per * w), lambda i: (side, 0, i))],
        [anywhere() for _ in blocks], [shaped((b * each, w), bf) for b in blocks],
        grid=(count // per,),
        scratch_shapes=[
            pltpu.VMEM((width, rows), bf), pltpu.VMEM((count * width, w), bf), pltpu.SemaphoreType.DMA((len(slots),)),
        ],
    )


def gain_rows(rows_ref, one, two, core, wide):
    devices, half = rows_ref.shape[0], one.shape[1]
    lanes = 2 * half // devices
    if lanes < 1 or 128 % lanes or 2 * lanes > 128:
        return
    wide[...] = jnp.zeros_like(wide)
    wide[:, pl.ds(pl.multiple_of(core * half, half), half)] = jnp.broadcast_to(one, (8, half))
    lane = lax.broadcasted_iota(jnp.int32, (8, 128), 1)
    for i in range(devices):
        block, turn = divmod(i * lanes, 128)
        cols = slice(block * 128, (block + 1) * 128)
        pair = []
        for tile, at in ((wide[:, cols], 0), (jnp.broadcast_to(two[:, cols], (8, 128)), lanes)):
            shift = (at - turn) % 128
            pair.append(pltpu.roll(tile, shift, 1) if shift else tile)
        row = jnp.where(lane < lanes, pair[0], jnp.where(lane < 2 * lanes, pair[1], 0.0))
        rows_ref[i : i + 1, :] = row[:1]


def back_kernel(first, spot_ref, lengths_ref, came_ref, taps_ref, own_ref, other_ref, left_ref, right_ref, *refs):
    if first:
        own_before, other_before, own_hat, other_hat, two_ref, own_out, other_out, gains_ref, rows_ref, wide, *refs = refs
        before = own_before, other_before
    else:
        own_out, other_out, *refs = refs
    mask, low_low, low_high, high, v_low, v_high, ends = refs
    n = mask.shape[1]
    q, h, d = n // 4, n // 2, own_ref.shape[1]
    per = taps_ref.shape[1]

    @pl.when(pl.program_id(0) == 0)
    def _():
        find_ends(ends, lengths_ref, came_ref)
        for g in range(2):
            mask[g] = causal_mask(ends, g, n, True)
        low_low[...] = jnp.zeros_like(low_low)
        high[...] = jnp.zeros_like(high)
        for g, ref in enumerate((own_out, other_out)):
            ref[...] = before[g][...] if first else jnp.zeros_like(ref)

    for j in range(per):
        weight = jnp.concatenate([left_ref[j * d : (j + 1) * d], right_ref[j * d : (j + 1) * d]], axis=1)
        s = diagonals(taps_ref[0, j : j + 1, :], q)
        a = j * h
        for g, grad in enumerate((own_ref, other_ref)):
            v = dot(grad[...], weight).astype(bf)
            v_low[g, a : a + h] = v[:h]
            v_high[g, a : a + h] = v[h:]
            m = mask[g]
            low_low[g, 0:q, a : a + q] = s[:, :q] * m[0:q, 0:q]
            low_low[g, 0:q, a + q : a + h] = s[:, q : 2 * q] * m[0:q, q : 2 * q]
            low_low[g, q:h, a + q : a + h] = s[:, :q] * m[q:h, q:h]
            low_high[g, 0:q, a : a + h] = s[:, 2 * q : 4 * q] * m[0:q, h:]
            low_high[g, q:h, a : a + h] = s[:, q : 3 * q] * m[q:h, h:]
            high[g, 0:q, a : a + h] = s[:, 0 : 2 * q] * m[h : h + q, h:]
            high[g, q:h, a + q : a + h] = s[:, 0:q] * m[h + q :, h + q :]
    for g, out in enumerate((own_out, other_out)):
        out[:h] += dot(low_low[g], v_low[g]) + dot(low_high[g], v_high[g])
        out[h:] += dot(high[g], v_high[g])
    if first:

        @pl.when(pl.program_id(0) == pl.num_programs(0) - 1)
        def _():
            products = own_out[...] * own_hat[...].astype(f32) + other_out[...] * other_hat[...].astype(f32)
            one = jnp.sum(products, axis=0, keepdims=True)
            gains_ref[...] = one
            gain_rows(rows_ref, one, two_ref, spot_ref[3], wide)


def back_call(chain, spot, lengths, taps, own, other, weights, first, steps, before=(), hats=(), two=None, devices=0):
    blocks, per, n = taps.shape
    rows, d = own.shape
    w = weights[0].shape[1]
    width = 2 * w
    scratch = lambda *s: pltpu.VMEM(s, bf)
    weight = pl.BlockSpec((per * d, w), lambda i: (i + first, 0))
    half = fixed(rows, width)
    more = (*before, *hats, two) if before else ()
    outs, shapes = [half] * 2, [shaped((rows, width), f32)] * 2
    scratches = [
        scratch(2, n, n), scratch(2, n // 2, per * n // 2),
        scratch(2, n // 2, per * n // 2), scratch(2, n // 2, per * n // 2),
        scratch(2, per * n // 2, width), scratch(2, per * n // 2, width), pltpu.SMEM((2, 3), jnp.int32),
    ]
    if before:
        outs = outs + [fixed(1, width), fixed(devices, 128)]
        shapes = shapes + [shaped((1, width), f32), shaped((devices, 128), f32)]
        scratches = [pltpu.VMEM((8, 2 * width), f32)] + scratches
    return chain.call(
        functools.partial(back_kernel, first), "spread_back", (spot, *lengths, taps, own, other, *weights, *more),
        [smem()] * 3 + [pl.BlockSpec((1, per, n), lambda i: (i + first, 0, 0)), fixed(rows, d), fixed(rows, d)]
        + [weight, weight] + [fixed(*v.shape) for v in more],
        outs, shapes, grid=(steps,), scratch_shapes=scratches,
    )


def flat(v):
    return v.reshape(-1, v.shape[-1])


def ffn_kernel(count, outs, steps, slots, out_slots, size, crossed, spot_ref, lengths_ref, came_ref, *refs):
    turned = spot_ref[3] if crossed else 0
    tokens, pieces, refs = refs[:6], refs[6 : 6 + count], refs[6 + count :]
    results, grads, (held, dealt, normed, back, sums, sem, token_sem) = refs[:4], refs[4 : 4 + outs], refs[4 + outs :]
    n = tokens[-1].shape[0]
    chips, units, width = held.shape[0], held.shape[1] * 2 // 3, held.shape[2]
    own, half = chips // 2 // steps, units // 2
    step = pl.program_id(0)

    @pl.when(step == 0)
    def _():
        half_width = tokens[0].shape[1]
        copies, at = [], 0
        for g in range(2):
            rows = pl.ds(g * n, n)
            for i in range(2):
                cols = pl.ds(i * half_width, half_width)
                copies.append(pltpu.make_async_copy(tokens[2 * g + i], normed.at[rows, cols], token_sem.at[2 * g + i]))
            copies.append(pltpu.make_async_copy(tokens[4 + g], back.at[rows], token_sem.at[4 + g]))
        for ref in pieces:
            for b in range(ref.shape[0]):
                chip = chip_of(spot_ref, slots[at], size)
                copies.append(
                    pltpu.make_async_copy(ref.at[b, pl.ds(0, units)], held.at[chip, pl.ds(0, units)], sem.at[0, at])
                )
                copies.append(
                    pltpu.make_async_copy(
                        ref.at[b, pl.ds(units, half)], held.at[chip ^ turned, pl.ds(units, half)], sem.at[1, at]
                    )
                )
                at += 1
        for c in copies:
            c.start()
        for c in copies[:6]:
            c.wait()
        for g, ref in enumerate((lengths_ref, came_ref)):
            back[g * n : (g + 1) * n] = live_rows(back[g * n : (g + 1) * n].astype(f32), ref).astype(bf)
        for c in copies[6:]:
            c.wait()

    w_gate = flat(held[pl.ds(step * own, own), 0:units])
    w_up = flat(held[pl.ds(chips // 2 + step * own, own), 0:units])
    w_down = flat(held[pl.ds(step * 2 * own, 2 * own), units : units + half])
    gate, up = dot(normed[...], w_gate, NT), dot(normed[...], w_up, NT)
    grad_act = dot(back[...], w_down, NT)
    sigma = 1.0 / (1.0 + jnp.exp(-gate))
    swish = gate * sigma
    act = (swish * up).astype(bf)
    grad_gate = (grad_act * up * (sigma * (1.0 + gate * (1.0 - sigma)))).astype(bf)
    grad_up = (grad_act * swish).astype(bf)
    put = lambda v: v.astype(bf).reshape(own, units, width)
    dealt[pl.ds(step * own, own), 0:units] = put(dot(grad_gate, normed[...], TN))
    dealt[pl.ds(chips // 2 + step * own, own), 0:units] = put(dot(grad_up, normed[...], TN))
    grad_down = dot(act, back[...], TN).astype(bf)
    for b in range(2 * own):
        dealt[(step * 2 * own + b) ^ turned, units : units + half] = grad_down[b * half : (b + 1) * half]

    def deal():
        copies, at = [], 0
        for ref in grads:
            for b in range(ref.shape[0]):
                chip = chip_of(spot_ref, out_slots[at], size)
                copies.append(pltpu.make_async_copy(dealt.at[chip], ref.at[b], sem.at[0, at]))
                at += 1
        return copies

    @pl.when(step == steps - 1)
    def _():
        for c in deal():
            c.start()

    branch = dot(act, w_down)
    two = dot(jnp.concatenate([grad_gate, grad_up], axis=1), jnp.concatenate([w_gate, w_up], axis=0))
    for i, value in enumerate((branch, two)):
        if steps > 1:

            @pl.when(step == 0)
            def _():
                sums[i] = value

            @pl.when((step > 0) & (step < steps - 1))
            def _():
                sums[i] += value

        @pl.when(step == steps - 1)
        def _():
            total = value + sums[i] if steps > 1 else value
            results[2 * i][...] = total[:n]
            results[2 * i + 1][...] = total[n:].astype(bf)

    @pl.when(step == steps - 1)
    def _():
        for c in deal():
            c.wait()


def ffn_call(chain, spot, lengths, tokens, pieces, blocks, slots, out_slots, size, crossed, chunk=1024):
    n, d = tokens[-1].shape
    chips, rows = len(slots), pieces[0].shape[1]
    units = rows * 2 // 3
    steps = chips // 2 * units // chunk
    return chain.call(
        functools.partial(ffn_kernel, len(pieces), len(blocks), steps, slots, out_slots, size, crossed), "ffn",
        (spot, *lengths, *tokens, *pieces),
        [smem()] * 3 + [anywhere() for _ in (*tokens, *pieces)],
        [fixed(n, d)] * 4 + [anywhere() for _ in blocks],
        [shaped((n, d), f32), shaped((n, d), bf)] * 2 + [shaped((b, rows, d), bf) for b in blocks],
        grid=(steps,),
        scratch_shapes=[
            pltpu.VMEM((chips, rows, d), bf), pltpu.VMEM((chips, rows, d), bf),
            pltpu.VMEM((2 * n, d), bf), pltpu.VMEM((2 * n, d), bf), pltpu.VMEM((2, 2 * n, d), f32),
            pltpu.SemaphoreType.DMA((2, chips)), pltpu.SemaphoreType.DMA((6,)),
        ],
    )


def normed_kernel(spot_ref, own_ref, other_ref, own_out, other_out, full):
    half = own_out.shape[1]
    cols = pl.ds(pl.multiple_of(spot_ref[3] * half, half), half)
    for ref, out in ((own_ref, own_out), (other_ref, other_out)):
        source = ref[...].astype(f32)
        scale = lax.rsqrt(jnp.mean(source * source, axis=-1, keepdims=True) + NORM_EPS)
        full[...] = (source * scale).astype(bf)
        out[...] = full[:, cols]


def normed_call(chain, spot, own, other, parts=2):
    rows, width = own.shape
    block = pl.BlockSpec((rows // parts, width), lambda i: (i, 0))
    thin = pl.BlockSpec((rows // parts, width // 2), lambda i: (i, 0))
    return chain.call(
        normed_kernel, "normed", (spot, own, other), [smem(), block, block],
        [thin] * 2, [shaped((rows, width // 2), bf)] * 2,
        grid=(parts,), scratch_shapes=[pltpu.VMEM((rows // parts, width), bf)],
    )


def live_rows(values, lengths_ref, first=0):
    total = lengths_ref[0, 0] + lengths_ref[0, 1] + lengths_ref[0, 2]
    place = lax.broadcasted_iota(jnp.int32, (values.shape[0], 1), 0) + first
    return jnp.where(place < total, values, jnp.zeros((), values.dtype))


def pack_kernel(
    spot_ref, mixer_ref, gate_up_ref, down_ref, gains_ref, mixer_mine, mixer_theirs, gate_mine, gate_theirs, down_low, note
):
    half, units, core = mixer_mine.shape[1], gate_mine.shape[0], spot_ref[3]
    for ref, cols, rows, c in ((mixer_mine, half, units, core), (mixer_theirs, half, units, 1 - core)):
        ref[...] = mixer_ref[:, pl.ds(pl.multiple_of(c * half, half), half)].astype(bf)
    for ref, c in ((gate_mine, core), (gate_theirs, 1 - core)):
        ref[:units] = gate_up_ref[pl.ds(pl.multiple_of(c * units, units), units), :].astype(bf)
    count, own = gains_ref.shape
    note[...] = jnp.zeros_like(note)
    note[:count, :own] = gains_ref[...].astype(bf)
    gate_theirs[units:] = jnp.zeros((note.shape[0], gate_theirs.shape[1]), bf)
    gate_theirs[units:, : note.shape[1]] = note[...]
    down_low[...] = down_ref[...].astype(bf)


def pack_call(chain, spot, mixer, gate_up, down, gains):
    (rows, width), (units, _), (half, _) = mixer.shape, gate_up.shape, down.shape
    shapes = [(rows, width // 2)] * 2 + [(units // 2, width), (units // 2 + NOTE, width), (half, width), (NOTE, 128)]
    return chain.call(
        pack_kernel, "pack", (spot, mixer, gate_up, down, gains),
        [smem(), fixed(rows, width), fixed(units, width), fixed(half, width), fixed(*gains.shape)],
        [fixed(*s) for s in shapes], [shaped(s, bf) for s in shapes], grid=(1,),
    )


def block_kernel(own_gains, spot_ref, mine_ref, came_ref, note_ref, gate_ref, all_ref, copies_ref):
    rows, w = mine_ref.shape[0], all_ref.shape[1]
    mine = note_ref[...].astype(f32)
    came = gate_ref[gate_ref.shape[0] - NOTE :, :w].astype(f32)
    turned = lambda v: pltpu.roll(v, own_gains, 1)
    note = jnp.where(spot_ref[3] == 0, mine + turned(came), came + turned(mine)).astype(bf)
    at = 0
    for side in range(2):
        cols = slice(side * w, (side + 1) * w)
        all_ref[at : at + rows] = mine_ref[:, cols]
        all_ref[at + rows : at + 2 * rows] = came_ref[:, cols]
        all_ref[at + 2 * rows : at + 2 * rows + NOTE] = note
        at += 2 * rows + NOTE
    count = 2 * rows + NOTE
    for c in range(copies_ref.shape[0] // count):
        copies_ref[c * count : (c + 1) * count] = all_ref[:count]


def block_call(chain, spot, mine, came, note, gate_came, own_gains, copies, waits):
    rows, width = mine.shape
    w = width // 2
    each = 2 * rows + NOTE
    return chain.call(
        functools.partial(block_kernel, own_gains), "block", (spot, mine, came, note, gate_came),
        [smem()] + [fixed(*v.shape) for v in (mine, came, note, gate_came)],
        [fixed(2 * each, w), fixed(copies * each, w)], [shaped((2 * each, w), bf), shaped((copies * each, w), bf)],
        grid=(1,), waits=waits,
    )


def stack_kernel(count, moves, spot_ref, *refs):
    for i, a, rows, o, b in moves:
        if not isinstance(a, int):
            stride, distance, first = a
            a = pl.multiple_of((spot_ref[2] ^ distance) * stride + first, NOTE)
        refs[count + o][b : b + rows] = refs[i][pl.ds(a, rows)]


def stack_call(chain, spot, arrays, rows, moves, through=()):
    like = {o: arrays[i] for i, _, _, o, _ in moves}
    shapes = [(r,) + like[o].shape[1:] for o, r in enumerate(rows)]
    return chain.call(
        functools.partial(stack_kernel, len(arrays), moves), "stack", (spot, *arrays),
        [smem()] + [fixed(*v.shape) for v in arrays],
        [fixed(*s) for s in shapes], [shaped(s, like[o].dtype) for o, s in enumerate(shapes)], grid=(1,), through=through,
    )


def corner_kernel(cut, extra, x_ref, y_ref, to_x_ref, to_y_ref):
    rows = x_ref.shape[0]
    to_x_ref[:cut] = y_ref[:cut]
    if extra:
        to_x_ref[cut:] = y_ref[rows - extra :]
    to_y_ref[...] = x_ref[cut : rows - extra]


def whole_corner_kernel(x_ref, y_ref, to_x_ref, to_y_ref):
    to_x_ref[...] = y_ref[...]
    to_y_ref[...] = x_ref[...]


def corner_call(chain, from_x, from_y, extra):
    total, width = from_x.shape
    cut = (total - extra) // 2
    shapes = [(cut + extra, width), (cut, width)]
    ins, kernel = [fixed(total, width)] * 2, functools.partial(corner_kernel, cut, extra)
    if not extra:
        ins = [pl.BlockSpec((cut, width), lambda i: (1, 0)), pl.BlockSpec((cut, width), lambda i: (0, 0))]
        kernel = whole_corner_kernel
    return chain.call(
        kernel, "corner", (from_x, from_y), ins,
        [fixed(*s) for s in shapes], [shaped(s, bf) for s in shapes], grid=(1,),
    )


def near_kernel(to_x_ref, to_y_ref, by_x_ref, by_y_ref, new_x_ref, new_y_ref):
    new_x_ref[...] = (to_x_ref[...].astype(f32) + by_y_ref[...].astype(f32)).astype(bf)
    new_y_ref[...] = (to_y_ref[...].astype(f32) + by_x_ref[...].astype(f32)).astype(bf)


def near_call(chain, to_x, to_y, by_x, by_y, parts=2, **options):
    rows, width = by_x.shape
    block = (rows // parts, width)
    low, high = pl.BlockSpec(block, lambda i: (i, 0)), pl.BlockSpec(block, lambda i: (i + parts, 0))
    return chain.call(
        near_kernel, "near", (to_x, to_y, by_x, by_y), [high, low, low, low], [high, low],
        [shaped(to_x.shape, bf), shaped(to_y.shape, bf)], grid=(parts,), input_output_aliases={0: 0, 1: 1}, **options,
    )


def line_kernel(count, *refs):
    parts, refs = refs[:count], refs[count:]
    rows = refs[-1].shape[0]

    def total(at):
        result = parts[0][pl.ds(at, rows)].astype(f32)
        for ref in parts[1:]:
            result = result + ref[pl.ds(at, rows)].astype(f32)
        return result

    for s, ref in enumerate(refs):
        ref[...] = total(s * rows).astype(ref.dtype)


def line_call(chain, parts, size, apart, **options):
    quarters = 4 if len(parts) == 1 else 1
    rows, width = parts[0].shape[0] // quarters // size, parts[0].shape[1]
    if apart:
        whole = lambda q: pl.BlockSpec((size * rows, width), lambda i: (q, 0))
        ins = [whole(q) for q in range(quarters)] if quarters > 1 else [whole(0)] * len(parts)
        specs = [fixed(rows, width)] * size
        shapes = [shaped((rows, width), f32)] + [shaped((rows, width), bf)] * (size - 1)
        steps = 1
    else:
        steps = 2
        half = size * rows // steps
        ins = [pl.BlockSpec((half, width), lambda i, q=q: (i + q * steps, 0)) for q in range(quarters)]
        ins = ins if quarters > 1 else ins * len(parts)
        specs, shapes = [pl.BlockSpec((half, width), lambda i: (i, 0))], [shaped((size * rows, width), bf)]
    parts = parts * quarters
    return chain.call(
        functools.partial(line_kernel, len(parts)), "line", parts, ins, specs, shapes, grid=(steps,), **options
    )


def finish_kernel(cuts, count, note, spot_ref, first_ref, *refs):
    came, more, outs, squares_ref, total = (
        refs[:count], refs[count : -len(cuts) - 2], refs[-len(cuts) - 2 : -2], refs[-2], refs[-1]
    )
    rows = total.shape[0]
    result = first_ref[:rows].astype(f32)
    for b in range(1, first_ref.shape[0] // rows):
        result = result + first_ref[b * rows : (b + 1) * rows].astype(f32)
    for ref in came:
        result = result + ref[...].astype(f32)
    total[...] = result
    squares = jnp.sum(result * result, axis=0, keepdims=True)
    if note:
        whole = jnp.sum(squares, axis=1, keepdims=True)
        for ref in more[:-1]:
            whole = whole + jnp.sum(ref[...], axis=1, keepdims=True)
        gains = jnp.sum(more[-1][...], axis=0, keepdims=True)
        squares = jnp.broadcast_to(whole + jnp.sum(gains * gains, axis=1, keepdims=True), squares_ref.shape)
    squares_ref[...] = squares
    for ref, start in zip(outs, cuts):
        rows = ref.shape[0]
        if not isinstance(start, int):
            start = pl.multiple_of((spot_ref[3] ^ start[0]) * rows, rows & -rows)
        ref[...] = total[pl.ds(start, rows), :]


def finish_call(chain, spot, first, came, blocks, cuts, note=0, more=(), waits=()):
    rows, width = first.shape[0] // blocks, first.shape[1]
    shapes = [(r, width) for _, r in cuts] + [(note, 128) if note else (1, width)]
    return chain.call(
        functools.partial(finish_kernel, [c for c, _ in cuts], len(came), note), "finish", (spot, first, *came, *more),
        [smem(), fixed(*first.shape)] + [fixed(rows, width)] * len(came) + [fixed(*v.shape) for v in more],
        [fixed(*s) for s in shapes], [shaped(s, f32) for s in shapes],
        grid=(1,), scratch_shapes=[pltpu.VMEM((rows, width), f32)], waits=waits,
    )


def adam_step(weight, grad, first, second, rate, decay):
    first_new = BETA_ONE * first + (1.0 - BETA_ONE) * grad
    second_new = BETA_TWO * second + (1.0 - BETA_TWO) * grad * grad
    corr_one = 1.0 / (1.0 - BETA_ONE**STEP)
    corr_two = 1.0 / (1.0 - BETA_TWO**STEP)
    update = first_new * (rate * corr_one) / (jnp.sqrt(second_new * corr_two) + ADAM_EPS)
    return (weight * (1.0 - rate * decay) - update, first_new, second_new)


def adam_kernel(spot_ref, note_ref, *refs):
    ins, outs, wide, tall = refs[:21], refs[21:35], refs[35], refs[36]
    mixer, gate_up, down, gains, parts = ins[:4], ins[4:7], ins[7:10], ins[10:13], ins[13:]
    mixer_out, gate_up_out, down_out, gains_out, norm_out = outs[:4], outs[4:7], outs[7:10], outs[10:13], outs[13]
    core, quarter = spot_ref[3], parts[0].shape[1]
    norm = jnp.sqrt(jnp.sum(note_ref[...], axis=0, keepdims=True)[:, :1])
    factor = CLIP_LIMIT / jnp.maximum(norm, CLIP_LIMIT)

    rows, step = mixer[0].shape[0], wide.shape[0]

    @pl.loop(0, rows // step)
    def _(i):
        at = pl.ds(pl.multiple_of(i * step, step & -step), step)
        for s in range(2):
            mine = pl.multiple_of(core * 2 * quarter, quarter) + s * quarter
            came = pl.multiple_of((1 - core) * 2 * quarter, quarter) + s * quarter
            wide[:, pl.ds(pl.multiple_of(mine, quarter), quarter)] = parts[s][at]
            wide[:, pl.ds(pl.multiple_of(came, quarter), quarter)] = parts[2 + s][at]
        old, first, second, average = (r[at] for r in mixer)
        new, first, second = adam_step(old, wide[...] * factor, first, second, RATE_MATRIX, DECAY_MATRIX)
        average = AVERAGE_KEEP * average + (1.0 - AVERAGE_KEEP) * new
        for ref, value in zip(mixer_out, (new, first, second, average)):
            ref[at] = value

    @pl.when(pl.program_id(0) == 0)
    def _():
        half = parts[4].shape[0]
        tall[pl.ds(pl.multiple_of(core * half, half), half), :] = parts[4][...]
        tall[pl.ds(pl.multiple_of((1 - core) * half, half), half), :] = parts[5][...]
        own = gains[0].shape[1]
        sums = jnp.sum(parts[7][...], axis=0, keepdims=True)
        gain_grad = jnp.concatenate([sums[:, :own], sums[:, own : 2 * own]])
        for olds, news, grad, rate, decay in (
            (gate_up, gate_up_out, tall[...], RATE_MATRIX, DECAY_MATRIX),
            (down, down_out, parts[6][...], RATE_MATRIX, DECAY_MATRIX),
            (gains, gains_out, gain_grad, RATE_GAIN, 0.0),
        ):
            old, first, second = (r[...] for r in olds)
            scale = factor if rate == RATE_MATRIX else factor[:, :1]
            for ref, value in zip(news, adam_step(old, grad * scale, first, second, rate, decay)):
                ref[...] = value
        norm_out[...] = norm


def adam_call(chain, spot, note, mixer, gate_up, down, gains, parts, blocks=1):
    rows, width = mixer[0].shape
    step = rows // blocks
    block = pl.BlockSpec((step, width), lambda i: (i, 0))
    piece = pl.BlockSpec((step, parts[0].shape[1]), lambda i: (i, 0))
    whole = lambda v: fixed(*v.shape)
    others = [*gate_up, *down, *gains]
    shapes = [v.shape for v in (*mixer, *others)] + [(1, 1)]
    return chain.call(
        adam_kernel, "adam", (spot, note, *mixer, *others, *parts),
        [smem(), whole(note)] + [block] * 4 + [whole(v) for v in others] + [piece] * 4
        + [whole(v) for v in parts[4:]],
        [block] * 4 + [whole(v) for v in others] + [fixed(1, 1)], [shaped(s, f32) for s in shapes],
        grid=(blocks,),
        scratch_shapes=[pltpu.VMEM((step // 3, width), f32), pltpu.VMEM(gate_up[0].shape, f32)],
    )


def flip(v, axis, bits=1):
    size = lax.axis_size(axis)
    return lax.ppermute(v, axis, [(i, i ^ bits) for i in range(size)])


def swap(v):
    return flip(v, "core")


def join(mine, other, core, axis=0):
    return jnp.where(
        core == 0,
        jnp.concatenate([mine, other], axis=axis),
        jnp.concatenate([other, mine], axis=axis),
    )


def part(v, index, axis=0):
    size = v.shape[axis] // 2
    return lax.dynamic_slice_in_dim(v, index * size, size, axis)


def low(v):
    return v.astype(bf)


def wide(v):
    return v.astype(f32)


class Whole:
    crossed = False
    mixer_slots = ((0,), (0,))
    mixer_blocks = (1,)

    def __init__(self, spot, groups):
        self.spot, self.core = spot, spot[3]
        self.size = lax.axis_size("z")
        self.chips = lax.axis_size("d0") * lax.axis_size("d1") * self.size
        self.ffn_in = self.ffn_out = tuple(range(groups))
        self.ffn_blocks = (groups,)

    def gather(self, chain, mixer, gate_up, down, gains, waits):
        def trade(v, axis):
            return join(part(v, self.core, axis), swap(part(v, 1 - self.core, axis)), self.core)

        everything = lambda v: lax.all_gather(v, CHIPS, axis=0, tiled=True)
        mixer_block = trade(low(mixer), 1)
        w, groups = mixer_block.shape[1] // 2, len(self.ffn_in)
        sides = []
        for s in range(2):
            whole = everything(mixer_block[:, s * w : (s + 1) * w])
            sides.append(([whole], ((0, 0, whole.shape[0], 0, None),), ()))
        ffn = [everything(v).reshape(groups, -1, v.shape[1]) for v in (trade(low(gate_up), 0), low(down))]
        ffn = [jnp.concatenate(ffn, axis=1)]
        gains = lax.all_gather(wide(low(gains)), EVERY, axis=1, tiled=True)
        yield jnp.pad(gains, ((0, NOTE - 2), (0, 0)))
        while True:
            yield sides, ffn

    def scatter(self, chain, parts, cuts, groups=1, apart=False):
        grads = parts[0].reshape(groups, -1, parts[0].shape[-1])
        rows = grads.shape[1] * 2 // 3
        if groups > 1:
            shards = [grads[:, :rows], grads[:, rows:]]
        else:
            shards = [grads]
        shards = [wide(lax.psum_scatter(flat(v), CHIPS, scatter_dimension=0, tiled=True)) for v in shards]
        outs = [part(shards[0], self.core), part(shards[0], 1 - self.core)] + shards[1:]
        squares = sum(jnp.sum(v * v, axis=0, keepdims=True) for v in shards)
        if groups == 1:
            yield
            yield ()
        through = yield ()
        yield (), through
        yield
        yield outs + [squares]

    def spread_gains(self, grads, rows):
        one, two = grads
        nothing = jnp.zeros_like(one)
        one = join(one, nothing, self.core, 1)
        return lax.psum_scatter(jnp.concatenate([one, two]), EVERY, scatter_dimension=1, tiled=True)

    def total(self, v):
        return lax.psum(v, EVERY)


class Cube(Whole):
    crossed = True
    near = ((0, 0), (0, 1), (1, 0), (1, 1))

    def __init__(self, spot, groups):
        super().__init__(spot, groups)
        slots = lambda fixed_z: tuple((y, x, s, fixed_z) for y, x in self.near for s in range(self.size))
        self.mixer_slots = slots(False), slots(True)
        self.ffn_in = slots(True)
        self.ffn_out = tuple((y, x, z, True) for z in range(self.size) for y, x in self.near)
        self.mixer_blocks = (self.size,) * 3 + (self.size // 2,) * 2

    def lines(self, block):
        return [flip(block, "z", s) for s in range(1, self.size)]

    def gather(self, chain, mixer, gate_up, down, gains, waits):
        spot = self.spot
        mixer_mine, mixer_theirs, gate_mine, gate_theirs, down_low, note = pack_call(
            chain, spot, mixer, gate_up, down, gains
        )
        gate_came = swap(gate_theirs)
        size = self.size
        own, block = block_call(
            chain, spot, mixer_mine, swap(mixer_theirs), note, gate_came, gains.shape[1], size, waits
        )
        line = self.along_z(block)
        own_x, own_y = flip(own, "d1"), flip(own, "d0")
        rows = own.shape[0] // 2 - NOTE
        units, count = gate_mine.shape[0], down_low.shape[0]
        ffn_rows = 2 * units + count
        moves = [(0, rows + NOTE, rows, 0, s * rows) for s in range(size)]
        for s in range(size):
            at = s * ffn_rows
            moves += [(1, 0, units, 1, at), (2, 0, units, 1, at + units), (3, 0, count, 1, at + 2 * units)]
        second_block, ffn_block = stack_call(
            chain, spot, (own, gate_mine, gate_came, down_low), (size * rows, size * ffn_rows), tuple(moves)
        )
        yield None
        half = rows // 2
        sides = []

        def spread_out(line):
            return line, flip(line, "d1"), flip(line, "d0")

        def turn_corner(from_x, from_y, extra=0):
            to_x, to_y = corner_call(chain, from_x, from_y, extra)
            return flip(to_x, "d1"), flip(to_y, "d0")

        def plan(side):
            found = [(p, side * (rows + NOTE) + h * half, half, near + (0, False), h) for p, near in enumerate(self.near[:3]) for h in range(2)]
            found += [(3, h * half, half, (1, 1, 0, False), h) for h in range(2)]
            last = (size - 1) * 2
            for at in range(last):
                s, h = at // 2 + 1, at % 2
                found += [(4 + p, at * half, half, near + (s, False), h) for p, near in enumerate(self.near[:3])]
                found.append((7 + (at >= last // 2), at % (last // 2) * half, half, (1, 1, s, False), h))
            return tuple(found)

        corner = turn_corner(own_x, own_y)
        yield
        chain.pause(corner)
        others, line_rows = range(1, size), (size - 1) * rows
        moves = [(0, (rows + NOTE, s, 0), rows, 0, (s - 1) * rows) for s in others]
        moves += [(0, (rows + NOTE, s, rows), NOTE, 0, line_rows + (s - 1) * NOTE) for s in others]
        line, block = stack_call(
            chain, spot, (line,), (line_rows + (size - 1) * NOTE,), tuple(moves), through=(second_block,)
        )
        first = spread_out(line)
        line = self.along_z(block)
        yield
        first_corner = turn_corner(*first[1:], (size - 1) * NOTE)
        notes = [(p, rows, near + (0, False)) for p, near in enumerate(self.near)]
        for s in others:
            notes += [(4 + p, line_rows + (s - 1) * NOTE, near + (s, False)) for p, near in enumerate(self.near[:3])]
            notes.append((7, line_rows // 2 + (s - 1) * NOTE, (1, 1, s, False)))
        sides.append(([own, own_x, own_y, corner[0], *first, *first_corner], plan(0), tuple(notes)))
        moves = [(0, (rows, s, 0), rows, 0, (s - 1) * rows) for s in others]
        line, block = stack_call(chain, spot, (line,), (line_rows,), tuple(moves), through=(ffn_block,))
        across, line = line, self.along_z(block)
        second = spread_out(*chain.pause(first_corner, (across,)))
        yield sides, None
        second_corner = turn_corner(*second[1:])
        sides.append(([own, own_x, own_y, corner[1], *second, *second_corner], plan(1), ()))
        ffn = spread_out(*chain.pause(second_corner, (line,)))
        yield sides, None
        ffn = (*ffn, *turn_corner(*ffn[1:]))
        yield sides, [v.reshape(-1, ffn_rows, v.shape[-1]) for v in ffn]

    def along_z(self, v):
        return lax.all_to_all(v, "z", 0, 0, tiled=True)

    def scatter(self, chain, parts, cuts, groups=1, apart=False):
        if groups > 1:
            came = (self.along_z(flat(parts[0])),)
        else:
            own, to_x, to_y, far_low, far_high = (flat(v) for v in parts)
            by_x, by_y = flip(far_low, "d1"), flip(far_high, "d0")
            yield
            to_x, to_y = yield near_call(chain, to_x, to_y, by_x, by_y)
            came = own, flip(to_x, "d1"), flip(to_y, "d0")
        through = yield came
        outs = line_call(chain, came, self.size, apart, through=through or ())
        count = self.size if apart else 1
        first, *rest = yield outs[:count], outs[count:]
        if groups > 1:
            to_x, to_y, far = rest
            far = lax.ppermute(far, ("d0", "d1"), [(i, i ^ 3) for i in range(4)])
            came = flip(to_x, "d1"), flip(to_y, "d0"), far
        elif apart:
            came = [flip(v, "z", s + 1) for s, v in enumerate(rest)]
        else:
            first, came = self.along_z(first), ()
        more, waits = yield
        yield finish_call(
            chain, self.spot, first, came, 1 if apart else self.size, cuts, 2 * self.chips if more else 0, more, waits
        )

    def spread_gains(self, grads, rows):
        return self.everyone(rows)

    def everyone(self, rows):
        return lax.all_to_all(rows, EVERY, 0, 0, tiled=True)


def body(
    inputs, lengths, filters, cotangent, mixer_weight, gate_up_weight, down_weight, norm_gains,
    mixer_first, gate_up_first, down_first, gains_first,
    mixer_second, gate_up_second, down_second, gains_second, mixer_average,
):
    slots, width = inputs.shape
    size = lax.axis_size("z")
    groups = 2 * FF // 256
    cube = lax.axis_size("d0") == 2 and lax.axis_size("d1") == 2 and size == 4
    spot = jnp.stack([lax.axis_index(a) for a in EVERY]).astype(jnp.int32)
    core = spot[3]
    links = (Cube if cube else Whole)(spot, groups)
    units = gate_up_weight.shape[0]
    chain = Chain()

    sums = lengths, swap(lengths)
    source_other, cotangent_other = swap(inputs), swap(cotangent)
    taps = jnp.concatenate([wide(filters), jnp.eye(AR_ORDER, slots, dtype=f32)])
    taps_turned = jnp.roll(taps[:, ::-1], 1 - slots // 4, axis=1)
    taps, taps_turned = (v.reshape(-1, 3, slots) for v in (taps, taps_turned))

    weights = links.gather(
        chain, mixer_weight, gate_up_weight, down_weight, norm_gains, (sums[1], source_other, cotangent_other)
    )
    gains = next(weights)
    tokens = hat_tokens = normed_call(chain, spot, inputs, source_other)
    blocks = taps.shape[0]
    cuts, spread = (0, blocks // 9, blocks * 2 // 9, blocks), None
    for at in range(3):
        spread = spread_call(chain, sums, taps_turned, *tokens, cuts[at], cuts[at + 1] - cuts[at], spread)
        sides = next(weights)
    sides, _ = sides
    quarter = sides[0][0][0].shape[1]
    *mixed, left, gains = (*mix_call(chain, spot, spread, 0, *sides[0], gains, size, width), gains)[:4]
    sides, _ = next(weights)
    mixed_own, mixed_other, right = mix_call(chain, spot, spread, 1, *sides[1], gains, size, width, mixed)
    _, ffn = next(weights)

    hidden, *normed_two = hidden_call(chain, inputs, mixed_own, swap(mixed_other), gains)
    tokens = (*normed_two, *(swap(v) for v in normed_two), cotangent, cotangent_other)
    branch_own, branch_other, two_own, two_other, *grad_ffn = ffn_call(
        chain, spot, sums, tokens, ffn, links.ffn_blocks, links.ffn_in, links.ffn_out, size, links.crossed
    )
    if cube:
        grad_ffn = chain.pause(through=grad_ffn)
    ffn_sum = links.scatter(chain, grad_ffn, ((0, units // 2), (units // 2, units // 2), (units, units // 2)), groups, True)
    ffn_came = next(ffn_sum)
    grad_hidden, grad_low, gains_two = turn_call(
        chain, lengths, hidden, cotangent, two_own, swap(two_other), gains
    )
    grad_other = swap(grad_low)
    rows = mixer_weight.shape[0]
    cuts = (((0,), rows), ((1,), rows))
    grads_of = lambda s: grad_call(
        chain, spot, gains, grad_low, grad_other, spread, s, quarter, links.mixer_blocks, links.mixer_slots[s], size
    )
    first_sum = links.scatter(chain, grads_of(0), cuts, apart=True)
    next(first_sum)
    second_sum = links.scatter(chain, grads_of(1), cuts)
    next(second_sum)
    backward = lambda first, steps, *more: back_call(
        chain, spot, sums, taps, grad_low, grad_other, (left, right), first, steps, *more
    )
    early = blocks // 2
    first_sum.send(next(first_sum))
    one = backward(0, early)
    second_sum.send(next(second_sum))
    one_own, one_other, gains_one, note_rows = backward(
        early, blocks - early, one, hat_tokens, gains_two, 2 * links.chips
    )
    outs, _ = first_sum.send(())
    first_sum.send(outs)
    if cube:
        (note_rows,) = chain.pause(ffn_came, (note_rows,))
    shard_gains = links.spread_gains((gains_one, gains_two), note_rows)
    outs, _ = second_sum.send(())
    chain.pause((shard_gains,))
    first_mine, first_theirs, square = first_sum.send(((), ()))
    first_theirs, branch_other, *outs = chain.pause(through=(first_theirs, branch_other, *outs))
    second_sum.send(outs)
    outs, _ = ffn_sum.send(())
    ffn_sum.send(outs)
    output = output_call(chain, hidden, branch_own, swap(branch_other))
    input_grad = last_call(chain, spot, grad_hidden, inputs, one_own, swap(one_other), gains)
    gate_up_mine, gate_up_theirs, shard_down, *squares = ffn_sum.send(((), ()))
    squares.append(square)
    gate_up_came, first_came = swap(gate_up_theirs), swap(first_theirs)
    second_mine, second_theirs, note = second_sum.send(((*squares, shard_gains), ()))
    second_came = swap(second_theirs)
    mixer = mixer_weight, mixer_first, mixer_second, mixer_average
    gate_up, down = (gate_up_weight, gate_up_first, gate_up_second), (down_weight, down_first, down_second)
    gain = norm_gains, gains_first, gains_second
    if cube:
        (
            mixer_new, mixer_first_new, mixer_second_new, mixer_average_new, gate_up_new, gate_up_first_new,
            gate_up_second_new, down_new, down_first_new, down_second_new, gains_new, gains_first_new, gains_second_new,
            grad_norm,
        ) = adam_call(
            chain, spot, links.everyone(note), mixer, gate_up, down, gain,
            (first_mine, second_mine, first_came, second_came, gate_up_mine, gate_up_came, shard_down, shard_gains),
        )
        grad_norm = grad_norm[0, 0]
    else:
        squares = sum(jnp.sum(v) for v in (*squares, note)) + jnp.sum(shard_gains * shard_gains)
        grad_norm = jnp.sqrt(links.total(squares))
        factor = CLIP_LIMIT / jnp.maximum(grad_norm, CLIP_LIMIT)
        shard_mixer = join(
            jnp.concatenate([first_mine, second_mine], axis=1), jnp.concatenate([first_came, second_came], axis=1), core, 1
        )
        shard_gate_up = join(gate_up_mine, gate_up_came, core)
        step = lambda old, grad: adam_step(old[0], grad * factor, old[1], old[2], RATE_MATRIX, DECAY_MATRIX)
        mixer_new, mixer_first_new, mixer_second_new = step(mixer, shard_mixer)
        gate_up_new, gate_up_first_new, gate_up_second_new = step(gate_up, shard_gate_up)
        down_new, down_first_new, down_second_new = step(down, shard_down)
        gains_new, gains_first_new, gains_second_new = adam_step(
            gain[0], shard_gains * factor, gain[1], gain[2], RATE_GAIN, 0.0
        )
        mixer_average_new = AVERAGE_KEEP * mixer_average + (1.0 - AVERAGE_KEEP) * mixer_new
    return (
        output, input_grad, grad_norm, mixer_new, gate_up_new, down_new, gains_new,
        mixer_first_new, gate_up_first_new, down_first_new, gains_first_new,
        mixer_second_new, gate_up_second_new, down_second_new, gains_second_new, mixer_average_new,
    )


def solution(mesh):
    outer, inner = mesh.shape["dp"], mesh.shape["fsdp"]
    side = math.isqrt(outer)
    if side * side != outer:
        side = 1
    split = jax.sharding.Mesh(
        np.asarray(mesh.devices).reshape(side, outer // side, inner // 2, 2), EVERY
    )
    rows, columns, whole = P(EVERY, None), P(None, EVERY), P()
    return jax.shard_map(
        body,
        mesh=split,
        in_specs=(
            rows, rows, whole, rows, rows, rows, rows, columns,
            rows, rows, rows, columns, rows, rows, rows, columns, rows,
        ),
        out_specs=(
            rows, rows, whole, rows, rows, rows, columns, rows, rows, rows, columns,
            rows, rows, rows, columns, rows,
        ),
        check_vma=False,
    )
```
